32 devices in a mesh: seq: 4 (over z), wsh: 8 (over y, x, core).
Axes of the slice: x: 2, y: 2, z: 4, core: 2. Of those that a mesh axis runs over, the one named last changes fastest.
Arguments:
- inputs: bfloat16 [8, 2048, 1536], P('wsh', 'seq'), may hold values from -6 to 6
- cotangent: bfloat16 [8, 2048, 1536], P('wsh', 'seq'), may hold values from -6 to 6
- w_in: float32 [1536, 6400], P('wsh'), may hold values from -0.15625 to 0.15625
- w_dt: float32 [1536, 48], P('wsh'), may hold values from -0.15625 to 0.15625
- w_out: float32 [3072, 1536], P('wsh'), may hold values from -0.109375 to 0.109375
- gain_pre: float32 [1536], P('wsh'), may hold values from 0.5 to 1.5
- gain_norm: float32 [3072], P('wsh'), may hold values from 0.5 to 1.5
- conv_param: float32 [5, 3328], P(None, 'wsh'), may hold values from -0.5 to 0.5
- head_param: float32 [3, 48], P(None, 'wsh'), may hold values from -6.5 to 3, as said below
- first_w_in: float32 [1536, 6400], P('wsh')
- second_w_in: float32 [1536, 6400], P('wsh'), as said below
- first_w_dt: float32 [1536, 48], P('wsh')
- second_w_dt: float32 [1536, 48], P('wsh'), as said below
- first_w_out: float32 [3072, 1536], P('wsh')
- second_w_out: float32 [3072, 1536], P('wsh'), as said below
- first_gain_pre: float32 [1536], P('wsh')
- second_gain_pre: float32 [1536], P('wsh'), as said below
- first_gain_norm: float32 [3072], P('wsh')
- second_gain_norm: float32 [3072], P('wsh'), as said below
- first_conv: float32 [5, 3328], P(None, 'wsh')
- second_conv: float32 [5, 3328], P(None, 'wsh'), as said below
- first_head: float32 [3, 48], P(None, 'wsh')
- second_head: float32 [3, 48], P(None, 'wsh'), as said below
Outputs:
- block_out: bfloat16 [8, 2048, 1536], P('wsh', 'seq')
- input_grad: float32 [8, 2048, 1536], P('wsh', 'seq')
- grad_w_in: float32 [1536, 6400], P('wsh')
- grad_w_dt: float32 [1536, 48], P('wsh')
- grad_w_out: float32 [3072, 1536], P('wsh')
- grad_gain_pre: float32 [1536], P('wsh')
- grad_gain_norm: float32 [3072], P('wsh')
- grad_conv: float32 [5, 3328], P(None, 'wsh')
- grad_head: float32 [3, 48], P(None, 'wsh')
- next_w_in: float32 [1536, 6400], P('wsh')
- next_w_dt: float32 [1536, 48], P('wsh')
- next_w_out: float32 [3072, 1536], P('wsh')
- next_gain_pre: float32 [1536], P('wsh')
- next_gain_norm: float32 [3072], P('wsh')
- next_conv: float32 [5, 3328], P(None, 'wsh')
- next_head: float32 [3, 48], P(None, 'wsh')
- next_first_w_in: float32 [1536, 6400], P('wsh')
- next_second_w_in: float32 [1536, 6400], P('wsh')
- next_first_w_dt: float32 [1536, 48], P('wsh')
- next_second_w_dt: float32 [1536, 48], P('wsh')
- next_first_w_out: float32 [3072, 1536], P('wsh')
- next_second_w_out: float32 [3072, 1536], P('wsh')
- next_first_gain_pre: float32 [1536], P('wsh')
- next_second_gain_pre: float32 [1536], P('wsh')
- next_first_gain_norm: float32 [3072], P('wsh')
- next_second_gain_norm: float32 [3072], P('wsh')
- next_first_conv: float32 [5, 3328], P(None, 'wsh')
- next_second_conv: float32 [5, 3328], P(None, 'wsh')
- next_first_head: float32 [3, 48], P(None, 'wsh')
- next_second_head: float32 [3, 48], P(None, 'wsh')
The draws below stay inside these ranges and needn't reach their ends.
Inputs may be any that keep to these rules, and one draw needn't show every extreme that they name: `head_param`: row 0 lies between 0 and log 16, row 1 between -6.5 and -2.5, row 2 between 0.5 and 1.5. `second_w_in`: Positive. `second_w_dt`: Positive. `second_w_out`: Positive. `second_gain_pre`: Positive. `second_gain_norm`: Positive. `second_conv`: Positive. `second_head`: Positive.
All inputs are finite; a program needn't handle non-finite values.
Results may differ from the reference program's by a relative error of at most 0.014.
The reference program's roundings to bfloat16 on the way count: a program that leaves them out, or rounds other values in their place, can miss the bound.
Values may be sent and summed in bfloat16 or wider, within the bound.
A program may use at most 256 MiB of HBM per device.

```python
import math
import jax
import jax.numpy as jnp
from jax import lax

D = 1536
HEADS = 48
HEAD_DIM = 64
STATE = 128
CONV_WIDTH = 4
SPAN = 256
STEP = 2
INNER = 3072
PROJ = 6400
CONV_CH = 3328
SEQ_LEN = 2048
SEQS = 8
TOTAL_TOK = 16384


def sample_first(key, array_shape, factor):
    typical = factor * math.sqrt(TOTAL_TOK)
    return 0.05 * typical * jax.random.normal(key, array_shape, jnp.float32)


def sample_second(key, array_shape, factor):
    typical = factor * math.sqrt(TOTAL_TOK)
    spread = jnp.exp(jax.random.uniform(key, array_shape, jnp.float32, math.log(0.25), math.log(4.0)))
    return 0.001 * typical * typical * spread


def draw_head_param(key, part):
    subkeys = jax.random.split(key, 3)
    log_decay = jnp.log(jax.random.uniform(subkeys[0], (HEADS,), jnp.float32, 1.0, 16.0))
    step_bias = jax.random.uniform(subkeys[1], (HEADS,), jnp.float32, -6.5, -2.5)
    skip_gain = jax.random.uniform(subkeys[2], (HEADS,), jnp.float32, 0.5, 1.5)
    return jnp.stack([log_decay, step_bias, skip_gain])


def draw_first_w_in(key, part):
    return sample_first(key, (D, PROJ), 0.5)


def draw_second_w_in(key, part):
    return sample_second(key, (D, PROJ), 0.5)


def draw_first_w_dt(key, part):
    return sample_first(key, (D, HEADS), 0.5)


def draw_second_w_dt(key, part):
    return sample_second(key, (D, HEADS), 0.5)


def draw_first_w_out(key, part):
    return sample_first(key, (INNER, D), 1.0)


def draw_second_w_out(key, part):
    return sample_second(key, (INNER, D), 1.0)


def draw_first_gain_pre(key, part):
    return sample_first(key, (D,), 1.0)


def draw_second_gain_pre(key, part):
    return sample_second(key, (D,), 1.0)


def draw_first_gain_norm(key, part):
    return sample_first(key, (INNER,), 0.7)


def draw_second_gain_norm(key, part):
    return sample_second(key, (INNER,), 0.7)


def draw_first_conv(key, part):
    return sample_first(key, (CONV_WIDTH + 1, CONV_CH), 0.5)


def draw_second_conv(key, part):
    return sample_second(key, (CONV_WIDTH + 1, CONV_CH), 0.5)


def draw_first_head(key, part):
    return sample_first(key, (3, HEADS), 3.0)


def draw_second_head(key, part):
    return sample_second(key, (3, HEADS), 3.0)


def steps_of(rng, shape, pieces, least, largest):
    def one(position, shards_of):
        steps = jax.random.uniform(jax.random.fold_in(jax.random.fold_in(rng, 6), position), (shards_of,), jnp.float32, least / len(pieces), largest / len(pieces))
        return jnp.repeat(jnp.exp(steps), shape[position] // shards_of).reshape((-1,) + (1,) * (len(shape) - position - 1))

    gain = one(*pieces[0])
    for cut in pieces[1:]:
        gain = gain * one(*cut)
    return gain


def bell_draw(stream_key, shape, scale, bound, shards=(), held_as=jnp.bfloat16):
    entries = jax.random.normal(stream_key, shape, jnp.float32) * scale
    if len(shards) > 0:
        entries = steps_of(stream_key, shape, shards, -0.22, 0.18) * entries
    return jnp.clip(entries, min=-bound, max=bound).astype(held_as)


def setup_inputs(seed: int = 0) -> dict:
    key_list = jax.random.split(jax.random.key(seed), 24)
    return {
        "inputs": bell_draw(key_list[0], (SEQS, SEQ_LEN, D), 1.0, 6.0, ((0, 8), (1, 4))),
        "cotangent": bell_draw(key_list[1], (SEQS, SEQ_LEN, D), 1.0, 6.0, ((0, 8), (1, 4))),
        "w_in": bell_draw(key_list[2], (D, PROJ), D ** -0.5, 0.15625, ((0, 8),), jnp.float32),
        "w_dt": bell_draw(key_list[3], (D, HEADS), D ** -0.5, 0.15625, ((0, 8),), jnp.float32),
        "w_out": bell_draw(key_list[4], (INNER, D), INNER ** -0.5, 0.109375, ((0, 8),), jnp.float32),
        "gain_pre": jnp.clip(1.0 + 0.1 * jax.random.normal(key_list[5], (D,), jnp.float32), 0.5, 1.5),
        "gain_norm": jnp.clip(1.0 + 0.1 * jax.random.normal(key_list[6], (INNER,), jnp.float32), 0.5, 1.5),
        "conv_param": jnp.clip(jax.random.uniform(key_list[7], (CONV_WIDTH + 1, CONV_CH), jnp.float32, -0.5, 0.5) * steps_of(key_list[7], (CONV_WIDTH + 1, CONV_CH), ((1, 8),), -0.4, 0.0), -0.5, 0.5),
        "head_param": draw_head_param(jax.random.fold_in(key_list[23], 71), 0),
        "first_w_in": draw_first_w_in(jax.random.fold_in(key_list[23], 71), 0),
        "second_w_in": draw_second_w_in(jax.random.fold_in(key_list[23], 71), 0),
        "first_w_dt": draw_first_w_dt(jax.random.fold_in(key_list[23], 71), 0),
        "second_w_dt": draw_second_w_dt(jax.random.fold_in(key_list[23], 71), 0),
        "first_w_out": draw_first_w_out(jax.random.fold_in(key_list[23], 71), 0),
        "second_w_out": draw_second_w_out(jax.random.fold_in(key_list[23], 71), 0),
        "first_gain_pre": draw_first_gain_pre(jax.random.fold_in(key_list[23], 71), 0),
        "second_gain_pre": draw_second_gain_pre(jax.random.fold_in(key_list[23], 71), 0),
        "first_gain_norm": draw_first_gain_norm(jax.random.fold_in(key_list[23], 71), 0),
        "second_gain_norm": draw_second_gain_norm(jax.random.fold_in(key_list[23], 71), 0),
        "first_conv": draw_first_conv(jax.random.fold_in(key_list[23], 71), 0),
        "second_conv": draw_second_conv(jax.random.fold_in(key_list[23], 71), 0),
        "first_head": draw_first_head(jax.random.fold_in(key_list[23], 71), 0),
        "second_head": draw_second_head(jax.random.fold_in(key_list[23], 71), 0),
    }


norm_eps = 1e-05
beta_one = 0.9
beta_two = 0.999
adam_eps = 1e-08
rate_matrix = 0.01
rate_gain = 0.4
rate_conv = 0.1
rate_head = 1.0
weight_decay = 0.1
highest = lax.Precision.HIGHEST

@jax.custom_vjp
def low(v):
    return lax.optimization_barrier(v.astype(jnp.bfloat16)).astype(jnp.float32)

@jax.custom_vjp
def low_back(v):
    return v

def low_keep(v):
    return (low(v), None)

def low_pass(kept, grad):
    return (grad,)

def back_keep(v):
    return (v, None)

def back_low(kept, grad):
    return (low(grad),)
low.defvjp(low_keep, low_pass)
low_back.defvjp(back_keep, back_low)

def product(left_side, right_side):
    return jnp.dot(left_side, right_side, precision=highest, preferred_element_type=jnp.float32)

def segment_sums(log_rates):
    length = log_rates.shape[-1]
    row_ids = jnp.arange(length)[:, None]
    col_ids = jnp.arange(length)[None, :]
    spread = jnp.where(row_ids > col_ids, log_rates[..., :, None], jnp.zeros((), log_rates.dtype))
    partial_sums = jnp.cumsum(spread, axis=-2)
    return jnp.where(row_ids >= col_ids, partial_sums, jnp.full((), -jnp.inf, log_rates.dtype))

def state_space(values, step_sizes, decay_rate, in_map, out_map):
    length, head_count, head_width = values.shape
    blocks = length // SPAN
    log_rates = (step_sizes * decay_rate).reshape(blocks, SPAN, head_count).transpose(2, 0, 1)
    inflow = (values * step_sizes[:, :, None]).reshape(blocks, SPAN, head_count, head_width)
    in_blocks = in_map.reshape(blocks, SPAN, -1)
    out_blocks = out_map.reshape(blocks, SPAN, -1)
    running = jnp.cumsum(log_rates, axis=-1)
    within = jnp.exp(segment_sums(log_rates))
    intersection = jnp.einsum('cln,csn->cls', out_blocks, in_blocks, precision=highest)
    mixing = within * intersection[None]
    diagonal = jnp.einsum('hcls,cshp->clhp', mixing, inflow, precision=highest)
    tail_decay = jnp.exp(running[:, :, -1:] - running)
    weighted = inflow * tail_decay.transpose(1, 2, 0)[..., None]
    end_states = jnp.einsum('csn,cshp->chpn', in_blocks, weighted, precision=highest)
    totals = jnp.concatenate([jnp.zeros((head_count, 1), running.dtype), running[:, :, -1]], axis=1)
    across = jnp.exp(segment_sums(totals))
    starts = jnp.concatenate([jnp.zeros((1,) + end_states.shape[1:], end_states.dtype), end_states], axis=0)
    carried = jnp.einsum('hzc,chpn->zhpn', across, starts, precision=highest)[:-1]
    entering = jnp.exp(running).transpose(1, 2, 0)[..., None]
    offdiag = jnp.einsum('cln,chpn->clhp', out_blocks, carried, precision=highest) * entering
    return (diagonal + offdiag).reshape(length, head_count, head_width)

def convolve(signal, kernel):
    length = signal.shape[0]
    padded = jnp.pad(signal, ((CONV_WIDTH - 1, 0), (0, 0)))
    summed = jnp.broadcast_to(kernel[CONV_WIDTH], signal.shape)
    for offset in range(CONV_WIDTH):
        summed = summed + padded[offset:offset + length] * kernel[offset]
    return jax.nn.silu(summed)

def layer_forward(params, inputs_seq):
    w_in, w_dt, w_out, gain_pre, gain_norm, conv_param, head_param = params
    inv_rms = lax.rsqrt(lax.optimization_barrier(jnp.mean(inputs_seq * inputs_seq, axis=-1, keepdims=True)) + norm_eps)
    normed = low(inputs_seq * inv_rms * low(gain_pre))
    projected = product(normed, low(w_in))
    gate_vals = low_back(projected[:, :INNER])
    signal = low(low_back(projected[:, INNER:]))
    raw_step = low(low_back(product(normed, low(w_dt))))
    convolved = convolve(signal, low(conv_param))
    head_vals = low(head_param)
    length = inputs_seq.shape[0]
    head_inputs = convolved[:, :INNER].reshape(length, HEADS, HEAD_DIM)
    step_sizes = jax.nn.softplus(raw_step + head_vals[1])
    decay_rate = -jnp.exp(head_vals[0])
    scanned = state_space(head_inputs, step_sizes, decay_rate, convolved[:, INNER:INNER + STATE], convolved[:, INNER + STATE:])
    scanned = scanned + head_vals[2][None, :, None] * head_inputs
    scanned = low(low_back(scanned.reshape(length, INNER)))
    gated_vals = scanned * jax.nn.silu(gate_vals)
    normed_out = low(gated_vals * lax.rsqrt(lax.optimization_barrier(jnp.mean(gated_vals * gated_vals, axis=-1, keepdims=True)) + norm_eps) * low(gain_norm))
    return inputs_seq + product(normed_out, low(w_out))

def adam_update(weights, gradient, first_moment, second_moment, step_rate, decay_amount):
    next_first = beta_one * first_moment + (1.0 - beta_one) * gradient
    next_second = beta_two * second_moment + (1.0 - beta_two) * gradient * gradient
    corrected = next_first / (1.0 - beta_one ** STEP) / (jnp.sqrt(next_second / (1.0 - beta_two ** STEP)) + adam_eps)
    return (weights - step_rate * (corrected + decay_amount * weights), next_first, next_second)

def reference(inputs, cotangent, w_in, w_dt, w_out, gain_pre, gain_norm, conv_param, head_param, first_w_in, second_w_in, first_w_dt, second_w_dt, first_w_out, second_w_out, first_gain_pre, second_gain_pre, first_gain_norm, second_gain_norm, first_conv, second_conv, first_head, second_head):
    params = (w_in, w_dt, w_out, gain_pre, gain_norm, conv_param, head_param)

    def one_sequence(totals, seq_pair):
        seq_in, seq_cot = seq_pair
        outputs, pullback = jax.vjp(layer_forward, params, seq_in.astype(jnp.float32))
        gradients, in_grad = pullback(seq_cot.astype(jnp.float32))
        return (jax.tree.map(jnp.add, totals, gradients), (outputs.astype(jnp.bfloat16), in_grad))
    totals, (block_out, input_grad) = lax.scan(one_sequence, jax.tree.map(jnp.zeros_like, params), (inputs, cotangent))
    step_rates = (rate_matrix, rate_matrix, rate_matrix, rate_gain, rate_gain, rate_conv, rate_head)
    decays = (weight_decay, weight_decay, weight_decay, 0.0, 0.0, 0.0, 0.0)
    firsts = (first_w_in, first_w_dt, first_w_out, first_gain_pre, first_gain_norm, first_conv, first_head)
    seconds = (second_w_in, second_w_dt, second_w_out, second_gain_pre, second_gain_norm, second_conv, second_head)
    updated = [adam_update(weights, gradient, first_moment, second_moment, step_rate, decay_amount) for weights, gradient, first_moment, second_moment, step_rate, decay_amount in zip(params, totals, firsts, seconds, step_rates, decays)]
    new_params = tuple((entry[0] for entry in updated))
    moments = []
    for entry in updated:
        moments.append(entry[1])
        moments.append(entry[2])
    return (block_out, input_grad) + tuple(totals) + new_params + tuple(moments)
```

```python
import functools

import jax
import jax.numpy as jnp
from jax import lax
from jax.experimental import pallas as pl
from jax.experimental.pallas import tpu as pltpu
from jax.sharding import PartitionSpec as P

D = 1536
HEADS = 48
HEAD_DIM = 64
STATE = 128
CONV_WIDTH = 4
STEP = 2
INNER = 3072
CONV_CH = 3328
BLOCK = 128
LANES = 128
WIDE = 256
HALO = 16
GROUPS = INNER // WIDE
PACK = CONV_CH + LANES
LOG2E = 1.4426950408889634
VMEM_LIMIT = 56 * 1024 * 1024

norm_eps = 1e-05
beta_one = 0.9
beta_two = 0.999
adam_eps = 1e-08
rate_matrix = 0.01
rate_gain = 0.4
rate_conv = 0.1
rate_head = 1.0
weight_decay = 0.1
highest = lax.Precision.HIGHEST
low_type = jnp.bfloat16
full_type = jnp.float32


def dot(left_side, right_side, dims=((1,), (0,)), precision=None):
    return lax.dot_general(
        left_side, right_side, (dims, ((), ())), precision=precision, preferred_element_type=full_type
    )


def dot_nt(left_side, right_side):
    return dot(left_side, right_side, ((1,), (1,)))


def sigmoid(vals):
    return 0.5 * jnp.tanh(0.5 * vals) + 0.5


def lane_ids(shape):
    return lax.broadcasted_iota(jnp.int32, shape, len(shape) - 1)


def widen(vals, first=0):
    left = lane_ids((vals.shape[0], LANES)) < HEAD_DIM
    pairs = [
        jnp.where(left, vals[:, first + i : first + i + 1], vals[:, first + i + 1 : first + i + 2])
        for i in (0, 2)
    ]
    return jnp.concatenate(pairs, axis=1)


def to_front(vals, step):
    return pltpu.roll(vals, lax.rem(LANES - 4 * step, LANES), 1)


def head_rows(ref, step):
    eight = ref[pl.ds(pl.multiple_of(8 * (step // 2), 8), 8), :]
    return pltpu.roll(eight, 4 * lax.rem(step, 2), 0)


def step_terms(raw, head):
    shifted = raw + head[1:2]
    small = jnp.exp(-jnp.abs(shifted))
    log_part = jnp.where(
        small < 0.01, small * (1.0 - small * (0.5 - small * (1.0 / 3.0))), jnp.log(1.0 + small)
    )
    step_sizes = jnp.maximum(shifted, 0.0) + log_part
    slope = jnp.where(shifted >= 0.0, 1.0, small) / (1.0 + small)
    return step_sizes, slope, -jnp.exp(head[0:1])


def convolve(sig, conv, rows):
    total = conv[4:5] + conv[0:1] * sig[HALO - 3 : HALO - 3 + rows, :]
    for k in range(1, CONV_WIDTH):
        total = total + conv[k : k + 1] * sig[HALO - 3 + k : HALO - 3 + k + rows, :]
    return total


def triangle(lower):
    rows = lax.broadcasted_iota(jnp.int32, (BLOCK, BLOCK), 0)
    cols = lax.broadcasted_iota(jnp.int32, (BLOCK, BLOCK), 1)
    return rows >= cols if lower else rows <= cols


def states_kernel(
    sig_ref, maps_ref, raw_ref, conv_ref, conv_maps_ref, head_ref,
    x_ref, bc_ref, run_ref, lag_ref, run_t_ref, lag_t_ref, enter_ref, enter_all_ref, tail_ref, offs_ref,
    states_ref, send_ref,
    sig, in_t,
):
    step = pl.program_id(0)
    rows = x_ref.shape[0]
    blocks = rows // BLOCK

    @pl.when(step == 0)
    def _():
        sig[...] = maps_ref[...].astype(full_type)
        pre = convolve(sig, conv_maps_ref[...], rows)
        maps = pre * sigmoid(pre)
        bc_ref[...] = maps
        in_t[...] = maps[:, :STATE].T.astype(low_type)
        step_sizes, _, rate = step_terms(raw_ref[HALO:, :].astype(full_type), head_ref[...])
        rates = step_sizes * rate * LOG2E
        log_steps = jnp.log2(step_sizes)
        lower = jnp.where(triangle(True), 1.0, 0.0)
        offset = jnp.zeros((1, LANES), full_type)
        offs_ref[...] = jnp.zeros(offs_ref.shape, full_type)
        for c in range(blocks):
            at = slice(c * BLOCK, (c + 1) * BLOCK)
            run = dot(lower, rates[at], precision=highest)
            lag = run - log_steps[at]
            run_ref[at, :] = run
            lag_ref[at, :] = lag
            run_t_ref[:, at] = run.T
            lag_t_ref[:, at] = lag.T
            enter_ref[at, :] = jnp.exp2(run)
            enter_all_ref[at, :] = jnp.exp2(run + offset)
            tail_ref[at, :] = jnp.exp2(run[BLOCK - 1 : BLOCK] - lag)
            offs_ref[c : c + 1, :] = offset
            offset = offset + run[BLOCK - 1 : BLOCK]
        offs_ref[blocks : blocks + 1, :] = offset

    sig[...] = sig_ref[...].astype(full_type)
    pre = convolve(sig, conv_ref[...], rows)
    x = pre * sigmoid(pre)
    x_ref[...] = x
    tail = to_front(tail_ref[...], step)
    last = to_front(offs_ref[...], step)
    state = jnp.zeros((STATE, WIDE), full_type)
    for c in range(blocks):
        at = slice(c * BLOCK, (c + 1) * BLOCK)
        weighted = (x[at] * widen(tail[at])).astype(low_type)
        fade = jnp.exp2(widen(last[c + 1 : c + 2] - last[c : c + 1]))
        state = state * fade + dot(in_t[:, at], weighted)
        states_ref[c] = state.astype(low_type)
    send_ref[:STATE, :] = state.astype(low_type)
    total = widen(last[blocks : blocks + 1])
    high = total.astype(low_type).astype(full_type)
    ids = lax.broadcasted_iota(jnp.int32, (16, WIDE), 0)
    extra = jnp.where(ids == 0, high, jnp.where(ids == 1, total - high, 0.0))
    send_ref[STATE:, :] = extra.astype(low_type)


def outputs_kernel(x_ref, bc_ref, run_ref, lag_t_ref, enter_ref, states_ref, head_ref, y_ref, inter):
    step = pl.program_id(0)
    rows = x_ref.shape[0]
    blocks = rows // BLOCK
    lower = triangle(True)

    @pl.when(step == 0)
    def _():
        for c in range(blocks):
            at = slice(c * BLOCK, (c + 1) * BLOCK)
            maps = bc_ref[at, :].astype(low_type)
            inter[c] = dot_nt(maps[:, STATE:], maps[:, :STATE])

    run = to_front(run_ref[...], step)
    enter = to_front(enter_ref[...], step)
    lag_rows = head_rows(lag_t_ref, step)
    skip = widen(to_front(head_ref[...], step)[2:3])
    left = lane_ids((BLOCK, LANES)) < HEAD_DIM
    for c in range(blocks):
        at = slice(c * BLOCK, (c + 1) * BLOCK)
        x = x_ref[at, :]
        parts = []
        for pair in range(2):
            mixes = []
            for i in range(2):
                h = 2 * pair + i
                lag_row = lag_rows[h : h + 1, at]
                power = jnp.where(lower, run[at, h : h + 1] - lag_row, -1e30)
                mixes.append((jnp.exp2(power) * inter[c]).astype(low_type))
            half = x[:, pair * LANES : (pair + 1) * LANES].astype(low_type)
            zero = jnp.zeros_like(half)
            stacked = jnp.concatenate([jnp.where(left, half, zero), jnp.where(left, zero, half)], axis=0)
            parts.append(dot(jnp.concatenate(mixes, axis=1), stacked))
        y = jnp.concatenate(parts, axis=1) + skip * x
        if c > 0:
            out_map = bc_ref[at, STATE:].astype(low_type)
            y = y + widen(enter[at]) * dot(out_map, states_ref[c - 1])
        y_ref[at, :] = y


def norm_kernel(
    y_ref, gate_ref, back_ref, gain_ref, bc_ref, enter_ref, state_ref,
    normed_ref, grad_y_ref, grad_gate_ref, grad_gain_ref, grad_state_ref,
    gated, low_y,
):
    step = pl.program_id(0)
    rows = y_ref.shape[0]

    @pl.when(step == 0)
    def _():
        grad_gain_ref[...] = jnp.zeros(grad_gain_ref.shape, full_type)
        grad_state_ref[...] = jnp.zeros(grad_state_ref.shape, full_type)

    out_map = bc_ref[:, STATE:]
    out_low = out_map.astype(low_type)
    out_t = out_map.T.astype(low_type)
    squares = jnp.zeros((rows, WIDE), full_type)
    cross = jnp.zeros((rows, WIDE), full_type)
    for j in range(GROUPS):
        at = slice(j * WIDE, (j + 1) * WIDE)
        enter = widen(enter_ref[...], 4 * j)
        y = y_ref[:, at] + enter * dot(out_low, state_ref[:, at])
        y_low = y.astype(low_type)
        low_y[:, at] = y_low
        gate = gate_ref[:, at]
        vals = y_low.astype(full_type) * (gate * sigmoid(gate))
        gated[:, at] = vals
        squares = squares + vals * vals
        cross = cross + vals * (back_ref[:, at] * gain_ref[0:1, at])
    inv = lax.rsqrt(jnp.sum(squares, axis=1, keepdims=True) * (1.0 / INNER) + norm_eps)
    pull = inv * inv * inv * (jnp.sum(cross, axis=1, keepdims=True) * (1.0 / INNER))
    for j in range(GROUPS):
        at = slice(j * WIDE, (j + 1) * WIDE)
        gain = gain_ref[0:1, at]
        back = back_ref[:, at]
        vals = gated[:, at]
        scaled = vals * inv
        normed_ref[:, at] = (scaled * gain).astype(low_type)
        grad_gain_ref[0:1, at] += jnp.sum(back * scaled, axis=0, keepdims=True)
        grad_vals = back * gain * inv - vals * pull
        gate = gate_ref[:, at]
        sig = sigmoid(gate)
        silu = gate * sig
        grad_y = (grad_vals * silu).astype(low_type)
        grad_y_ref[:, at] = grad_y
        slope = sig + silu * (1.0 - sig)
        grad_gate_ref[:, at] = (grad_vals * low_y[:, at].astype(full_type) * slope).astype(low_type)
        enter = widen(enter_ref[...], 4 * j)
        grad_state_ref[:, at] += dot(out_t, (grad_y.astype(full_type) * enter).astype(low_type))


def backward_kernel(
    sig_ref, raw_ref, conv_ref, head_ref, grad_y_ref, bc_ref,
    lag_ref, run_t_ref, enter_ref, tail_ref, offs_ref, states_ref, state_in_ref, grad_in_ref,
    grad_sig_ref, edge_ref, last_ref, grad_conv_ref, grad_skip_ref, grad_head_ref,
    sig, padded, inter, grad_inter, grad_maps, out_t, run_rows, run_cols, run_ends, weighs,
):
    step = pl.program_id(0)
    rows = grad_y_ref.shape[0]
    blocks = rows // BLOCK
    upper = triangle(False)

    @pl.when(step == 0)
    def _():
        for c in range(blocks):
            at = slice(c * BLOCK, (c + 1) * BLOCK)
            maps = bc_ref[at, :].astype(low_type)
            inter[c] = dot_nt(maps[:, :STATE], maps[:, STATE:])
            out_t[:, at] = bc_ref[at, STATE:].T.astype(low_type)
        grad_inter[...] = jnp.zeros(grad_inter.shape, full_type)
        grad_maps[...] = jnp.zeros(grad_maps.shape, full_type)
        run_rows[...] = jnp.zeros(run_rows.shape, full_type)
        run_cols[...] = jnp.zeros(run_cols.shape, full_type)
        run_ends[...] = jnp.zeros(run_ends.shape, full_type)
        weighs[...] = jnp.zeros(weighs.shape, full_type)
        padded[...] = jnp.zeros(padded.shape, full_type)

    def conv_back(grad_pre):
        conv = conv_ref[...]
        grad_sig = conv[3:4] * padded[HALO : HALO + rows, :]
        edge = conv[3:4] * padded[8:HALO, :]
        for k in range(3):
            grad_sig = grad_sig + conv[k : k + 1] * padded[HALO + 3 - k : HALO + 3 - k + rows, :]
            edge = edge + conv[k : k + 1] * padded[11 - k : 19 - k, :]
        grad_sig_ref[...] = grad_sig.astype(low_type)
        edge_ref[...] = edge
        last_ref[...] = grad_sig[rows - 16 :]
        sums = [
            jnp.sum(grad_pre * sig[HALO - 3 + k : HALO - 3 + k + rows, :], axis=0, keepdims=True)
            for k in range(CONV_WIDTH)
        ]
        sums.append(jnp.sum(grad_pre, axis=0, keepdims=True))
        sums.append(jnp.zeros((3, WIDE), full_type))
        grad_conv_ref[...] = jnp.concatenate(sums, axis=0)

    @pl.when(step < GROUPS)
    def _():
        sig[...] = sig_ref[...].astype(full_type)
        lag = to_front(lag_ref[...], step)
        run_all = head_rows(run_t_ref, step)
        enter = to_front(enter_ref[...], step)
        tail = to_front(tail_ref[...], step)
        offs = to_front(offs_ref[...], step)
        skip = widen(to_front(head_ref[...], step)[2:3])
        left = lane_ids((BLOCK, LANES)) < HEAD_DIM
        heads_of = lax.broadcasted_iota(jnp.int32, (WIDE, LANES), 0) // HEAD_DIM + 4 * step
        picks = jnp.where(heads_of == lane_ids((WIDE, LANES)), 1.0, 0.0).astype(low_type)
        state_in = state_in_ref[...].astype(full_type)
        grad_state = grad_in_ref[...].astype(full_type)
        grad_skip = jnp.zeros((1, WIDE), full_type)
        pre_all = convolve(sig, conv_ref[...], rows)

        def head_sums(vals):
            high = vals.astype(low_type)
            rest = (vals - high.astype(full_type)).astype(low_type)
            return dot(high, picks) + dot(rest, picks)

        for c in reversed(range(blocks)):
            at = slice(c * BLOCK, (c + 1) * BLOCK)
            pre = pre_all[at]
            gate = sigmoid(pre)
            x = pre * gate
            x_low = x.astype(low_type)
            x_round = x_low.astype(full_type)
            grad_y = grad_y_ref[at, :]
            grad_y_full = grad_y.astype(full_type)
            in_map = bc_ref[at, :STATE].astype(low_type)
            out_map = bc_ref[at, STATE:].astype(low_type)
            tail_c = widen(tail[at])
            enter_c = widen(enter[at])
            entering = state_in * jnp.exp2(widen(offs[c : c + 1]))
            if c > 0:
                entering = entering + states_ref[c - 1].astype(full_type)
            leaving = states_ref[c].astype(full_type) + state_in * jnp.exp2(widen(offs[c + 1 : c + 2]))
            entering_low = entering.astype(low_type)
            grad_low = grad_state.astype(low_type)
            ends = jnp.sum(grad_state * leaving, axis=0, keepdims=True)
            run_ends[c : c + 1, :] += head_sums(jnp.concatenate([ends, jnp.zeros((7, WIDE), full_type)], axis=0))[0:1]
            grad_x = tail_c * dot(in_map, grad_low)
            grad_maps[at, :STATE] += dot_nt((x * tail_c).astype(low_type), grad_low)
            swept = grad_y_full * enter_c
            swept_low = swept.astype(low_type)
            through = swept * dot(out_map, entering_low)
            grad_maps[at, STATE:] += dot_nt(swept_low, entering_low)
            fade = jnp.exp2(widen(offs[c + 1 : c + 2] - offs[c : c + 1]))
            grad_state = grad_state * fade + dot(out_t[:, at], swept_low)
            parts = []
            sums = []
            for pair in range(2):
                half = slice(pair * LANES, (pair + 1) * LANES)
                grad_half = grad_y[:, half]
                zero = jnp.zeros_like(grad_half)
                stacked = jnp.concatenate(
                    [jnp.where(left, grad_half, zero), jnp.where(left, zero, grad_half)], axis=0
                )
                cross = dot_nt(x_low[:, half], stacked)
                mixes = []
                for i in range(2):
                    h = 2 * pair + i
                    run_row = run_all[h : h + 1, at]
                    power = jnp.where(upper, run_row - lag[at, h : h + 1], -1e30)
                    decay = jnp.exp2(power)
                    mix = (decay * inter[c]).astype(low_type)
                    mixes.append(mix)
                    cross_h = cross[:, i * LANES : (i + 1) * LANES]
                    grad_inter[c] += cross_h * decay
                    sums.append(jnp.sum(cross_h * mix.astype(full_type), axis=0, keepdims=True))
                parts.append(dot(jnp.concatenate(mixes, axis=1), stacked))
            sums.append(jnp.zeros((4, BLOCK), full_type))
            run_rows[pl.ds(pl.multiple_of(8 * step, 8), 8), at] = jnp.concatenate(sums, axis=0)
            grad_x = grad_x + jnp.concatenate(parts, axis=1)
            weigh = head_sums(x_round * grad_x)
            weighs[at, :] += weigh
            run_cols[at, :] += head_sums(through) - weigh
            grad_skip = grad_skip + jnp.sum(grad_y_full * x, axis=0, keepdims=True)
            grad_x = grad_x + skip * grad_y_full
            padded[HALO + c * BLOCK : HALO + (c + 1) * BLOCK, :] = grad_x * (gate + x * (1.0 - gate))
        grad_skip_ref[...] = jnp.broadcast_to(grad_skip, grad_skip_ref.shape)
        conv_back(padded[HALO : HALO + rows, :])

    @pl.when(step == GROUPS)
    def _():
        sig[...] = sig_ref[...].astype(full_type)
        pre_all = convolve(sig, conv_ref[...], rows)
        for c in range(blocks):
            at = slice(c * BLOCK, (c + 1) * BLOCK)
            maps = bc_ref[at, :].astype(low_type)
            grad_block = grad_inter[c]
            grad_bc = grad_maps[at, :] + jnp.concatenate(
                [
                    dot(grad_block.astype(low_type), maps[:, STATE:]),
                    dot(grad_block.T.astype(low_type), maps[:, :STATE]),
                ],
                axis=1,
            )
            pre = pre_all[at]
            gate = sigmoid(pre)
            padded[HALO + c * BLOCK : HALO + (c + 1) * BLOCK, :] = grad_bc * (gate + pre * gate * (1.0 - gate))
        conv_back(padded[HALO : HALO + rows, :])

    @pl.when(step == GROUPS + 1)
    def _():
        head = head_ref[...]
        step_sizes, slope, rate = step_terms(raw_ref[HALO:, :].astype(full_type), head)
        ratio = jnp.where(step_sizes > 1e-30, slope / jnp.maximum(step_sizes, 1e-30), 1.0)
        used = lane_ids((BLOCK, LANES)) < HEADS
        later = jnp.where(upper, 1.0, 0.0)
        rate_sum = jnp.zeros((1, LANES), full_type)
        bias_sum = jnp.zeros((1, LANES), full_type)
        for c in range(blocks):
            at = slice(c * BLOCK, (c + 1) * BLOCK)
            by_head = [run_rows[8 * j : 8 * j + 4, at] for j in range(GROUPS)]
            by_head.append(jnp.zeros((LANES - HEADS, BLOCK), full_type))
            grad_run = jnp.concatenate(by_head, axis=0).T + run_cols[at, :]
            grad_rates = dot(later, grad_run, precision=highest) + run_ends[c : c + 1, :]
            grad_raw = slope[at] * rate * grad_rates + ratio[at] * weighs[at, :]
            grad_raw = jnp.where(used, grad_raw, 0.0)
            grad_sig_ref[at, :LANES] = grad_raw.astype(low_type)
            grad_sig_ref[at, LANES:] = jnp.zeros((BLOCK, LANES), low_type)
            rate_sum = rate_sum + jnp.sum(grad_rates * step_sizes[at], axis=0, keepdims=True)
            bias_sum = bias_sum + jnp.sum(grad_raw, axis=0, keepdims=True)
        grad_head_ref[...] = jnp.concatenate(
            [rate_sum * rate, bias_sum, jnp.zeros((6, LANES), full_type)], axis=0
        )


def run_states(packed, conv, head):
    rows = packed.shape[0] - HALO
    blocks = rows // BLOCK
    whole = lambda shape: pl.BlockSpec(shape, lambda j: (0,) * len(shape))
    small = jax.ShapeDtypeStruct((rows, LANES), full_type)
    small_t = jax.ShapeDtypeStruct((LANES, rows), full_type)
    return pl.pallas_call(
        states_kernel,
        grid=(GROUPS,),
        in_specs=[
            pl.BlockSpec((rows + HALO, WIDE), lambda j: (0, j)),
            pl.BlockSpec((rows + HALO, WIDE), lambda j: (0, GROUPS)),
            pl.BlockSpec((rows + HALO, LANES), lambda j: (0, CONV_CH // LANES)),
            pl.BlockSpec((8, WIDE), lambda j: (0, j)),
            pl.BlockSpec((8, WIDE), lambda j: (0, GROUPS)),
            whole((8, LANES)),
        ],
        out_specs=[
            pl.BlockSpec((rows, WIDE), lambda j: (0, j)),
            whole((rows, WIDE)),
            whole((rows, LANES)),
            whole((rows, LANES)),
            whole((LANES, rows)),
            whole((LANES, rows)),
            whole((rows, LANES)),
            whole((rows, LANES)),
            whole((rows, LANES)),
            whole((16, LANES)),
            pl.BlockSpec((blocks, STATE, WIDE), lambda j: (0, 0, j)),
            pl.BlockSpec((STATE + 16, WIDE), lambda j: (0, j)),
        ],
        out_shape=[
            jax.ShapeDtypeStruct((rows, INNER), full_type),
            jax.ShapeDtypeStruct((rows, WIDE), full_type),
            small, small, small_t, small_t, small, small, small,
            jax.ShapeDtypeStruct((16, LANES), full_type),
            jax.ShapeDtypeStruct((blocks, STATE, INNER), low_type),
            jax.ShapeDtypeStruct((STATE + 16, INNER), low_type),
        ],
        scratch_shapes=[
            pltpu.VMEM((rows + HALO, WIDE), full_type),
            pltpu.VMEM((STATE, rows), low_type),
        ],
        compiler_params=pltpu.CompilerParams(vmem_limit_bytes=VMEM_LIMIT),
        cost_estimate=pl.CostEstimate(flops=10**9, bytes_accessed=15 * 10**6, transcendentals=10**6),
        name="scan_states",
    )(packed, packed, packed, conv, conv, head)


def run_outputs(x, bc, run, lag_t, enter, states, head):
    rows = x.shape[0]
    blocks = rows // BLOCK
    whole = lambda shape: pl.BlockSpec(shape, lambda j: (0,) * len(shape))
    return pl.pallas_call(
        outputs_kernel,
        grid=(GROUPS,),
        in_specs=[
            pl.BlockSpec((rows, WIDE), lambda j: (0, j)),
            whole((rows, WIDE)),
            whole((rows, LANES)),
            whole((LANES, rows)),
            whole((rows, LANES)),
            pl.BlockSpec((blocks, STATE, WIDE), lambda j: (0, 0, j)),
            whole((8, LANES)),
        ],
        out_specs=pl.BlockSpec((rows, WIDE), lambda j: (0, j)),
        out_shape=jax.ShapeDtypeStruct((rows, INNER), full_type),
        scratch_shapes=[pltpu.VMEM((blocks, BLOCK, BLOCK), full_type)],
        compiler_params=pltpu.CompilerParams(vmem_limit_bytes=VMEM_LIMIT),
        cost_estimate=pl.CostEstimate(flops=10**10, bytes_accessed=15 * 10**6, transcendentals=3 * 10**6),
        name="scan_outputs",
    )(x, bc, run, lag_t, enter, states, head)


def run_norm(y, gate, back, gain, bc, enter, state):
    rows = y.shape[0]
    part = BLOCK
    by_rows = lambda cols: pl.BlockSpec((part, cols), lambda i: (i, 0))
    whole = lambda shape: pl.BlockSpec(shape, lambda i: (0,) * len(shape))
    return pl.pallas_call(
        norm_kernel,
        grid=(rows // part,),
        in_specs=[
            by_rows(INNER), by_rows(INNER), by_rows(INNER), whole((8, INNER)),
            by_rows(WIDE), by_rows(LANES), whole((STATE, INNER)),
        ],
        out_specs=[by_rows(INNER), by_rows(INNER), by_rows(INNER), whole((8, INNER)), whole((STATE, INNER))],
        out_shape=[
            jax.ShapeDtypeStruct((rows, INNER), low_type),
            jax.ShapeDtypeStruct((rows, INNER), low_type),
            jax.ShapeDtypeStruct((rows, INNER), low_type),
            jax.ShapeDtypeStruct((8, INNER), full_type),
            jax.ShapeDtypeStruct((STATE, INNER), full_type),
        ],
        scratch_shapes=[pltpu.VMEM((part, INNER), full_type), pltpu.VMEM((part, INNER), low_type)],
        compiler_params=pltpu.CompilerParams(vmem_limit_bytes=VMEM_LIMIT),
        cost_estimate=pl.CostEstimate(flops=10**9, bytes_accessed=30 * 10**6, transcendentals=3 * 10**6),
        name="gated_norm",
    )(y, gate, back, gain, bc, enter, state)


def run_backward(packed, conv, head, grad_y, bc, lag, run_t, enter, tail, offs, states, state_in, grad_in):
    rows = grad_y.shape[0]
    blocks = rows // BLOCK
    whole = lambda shape: pl.BlockSpec(shape, lambda j: (0,) * len(shape))
    most = lambda j, top: jnp.minimum(j, top)
    return pl.pallas_call(
        backward_kernel,
        grid=(GROUPS + 2,),
        in_specs=[
            pl.BlockSpec((rows + HALO, WIDE), lambda j: (0, most(j, GROUPS))),
            pl.BlockSpec((rows + HALO, LANES), lambda j: (0, CONV_CH // LANES)),
            pl.BlockSpec((8, WIDE), lambda j: (0, most(j, GROUPS))),
            whole((8, LANES)),
            pl.BlockSpec((rows, WIDE), lambda j: (0, most(j, GROUPS - 1))),
            whole((rows, WIDE)),
            whole((rows, LANES)),
            whole((LANES, rows)),
            whole((rows, LANES)),
            whole((rows, LANES)),
            whole((16, LANES)),
            pl.BlockSpec((blocks, STATE, WIDE), lambda j: (0, 0, most(j, GROUPS - 1))),
            pl.BlockSpec((STATE, WIDE), lambda j: (0, most(j, GROUPS - 1))),
            pl.BlockSpec((STATE, WIDE), lambda j: (0, most(j, GROUPS - 1))),
        ],
        out_specs=[
            pl.BlockSpec((rows, WIDE), lambda j: (0, j)),
            pl.BlockSpec((8, WIDE), lambda j: (0, most(j, GROUPS))),
            pl.BlockSpec((16, WIDE), lambda j: (0, most(j, GROUPS))),
            pl.BlockSpec((8, WIDE), lambda j: (0, most(j, GROUPS))),
            pl.BlockSpec((8, WIDE), lambda j: (0, most(j, GROUPS - 1))),
            whole((8, LANES)),
        ],
        out_shape=[
            jax.ShapeDtypeStruct((rows, PACK), low_type),
            jax.ShapeDtypeStruct((8, CONV_CH), full_type),
            jax.ShapeDtypeStruct((16, CONV_CH), full_type),
            jax.ShapeDtypeStruct((8, CONV_CH), full_type),
            jax.ShapeDtypeStruct((8, INNER), full_type),
            jax.ShapeDtypeStruct((8, LANES), full_type),
        ],
        scratch_shapes=[
            pltpu.VMEM((rows + HALO, WIDE), full_type),
            pltpu.VMEM((rows + 2 * HALO, WIDE), full_type),
            pltpu.VMEM((blocks, BLOCK, BLOCK), full_type),
            pltpu.VMEM((blocks, BLOCK, BLOCK), full_type),
            pltpu.VMEM((rows, WIDE), full_type),
            pltpu.VMEM((STATE, rows), low_type),
            pltpu.VMEM((LANES, rows), full_type),
            pltpu.VMEM((rows, LANES), full_type),
            pltpu.VMEM((8, LANES), full_type),
            pltpu.VMEM((rows, LANES), full_type),
        ],
        compiler_params=pltpu.CompilerParams(vmem_limit_bytes=VMEM_LIMIT),
        cost_estimate=pl.CostEstimate(flops=2 * 10**10, bytes_accessed=20 * 10**6, transcendentals=5 * 10**6),
        name="scan_backward",
    )(packed, packed, conv, head, grad_y, bc, lag, run_t, enter, tail, offs, states, state_in, grad_in)


def adam_update(weights, gradient, first_moment, second_moment, step_rate, decay_amount):
    next_first = beta_one * first_moment + (1.0 - beta_one) * gradient
    next_second = beta_two * second_moment + (1.0 - beta_two) * gradient * gradient
    corrected = (
        next_first
        / (1.0 - beta_one**STEP)
        / (jnp.sqrt(next_second / (1.0 - beta_two**STEP)) + adam_eps)
    )
    return (weights - step_rate * (corrected + decay_amount * weights), next_first, next_second)


def pad_rows(vals, rows):
    return jnp.pad(vals, ((0, rows - vals.shape[0]), (0, 0)))


def shards(
    inputs, cotangent, w_in, w_dt, w_out, gain_pre, gain_norm, conv_param, head_param,
    first_w_in, second_w_in, first_w_dt, second_w_dt, first_w_out, second_w_out,
    first_gain_pre, second_gain_pre, first_gain_norm, second_gain_norm,
    first_conv, second_conv, first_head, second_head,
):
    wsh_count = lax.axis_size("wsh")
    seq_count = lax.axis_size("seq")
    seq_index = lax.axis_index("seq")
    wsh_index = lax.axis_index("wsh")
    rows_model = D // wsh_count
    rows_inner = INNER // wsh_count
    cols_conv = CONV_CH // wsh_count
    cols_head = HEADS // wsh_count
    flat = jnp.concatenate(
        [gain_pre, gain_norm, conv_param.reshape(-1), head_param.reshape(-1)]
    ).astype(low_type)
    count = flat.shape[0]
    flat = jnp.pad(flat, (0, -count % LANES))
    small = lax.all_gather(flat, "wsh", axis=0)
    part_sig = jnp.concatenate(
        [w_in[:, INNER:].astype(low_type), w_dt.astype(low_type), jnp.zeros((rows_model, LANES - HEADS), low_type)],
        axis=1,
    )
    full_sig = lax.all_gather(part_sig, "wsh", axis=0, tiled=True)
    full_gate = lax.all_gather(w_in[:, :INNER].astype(low_type), "wsh", axis=0, tiled=True)
    full_out = lax.all_gather(w_out.astype(low_type), "wsh", axis=0, tiled=True)
    small = small.astype(full_type)
    ends = [rows_model, rows_model + rows_inner, rows_model + rows_inner + 5 * cols_conv]
    gain_in = small[:, : ends[0]].reshape(-1)
    gain_out = small[:, ends[0] : ends[1]].reshape(1, -1)
    conv = small[:, ends[1] : ends[2]].reshape(wsh_count, 5, cols_conv).transpose(1, 0, 2).reshape(5, CONV_CH)
    head = small[:, ends[2] : ends[2] + 3 * cols_head].reshape(wsh_count, 3, cols_head)
    head = head.transpose(1, 0, 2).reshape(3, HEADS)
    conv = pad_rows(conv, 8)
    head = jnp.pad(head, ((0, 5), (0, LANES - HEADS)))
    tokens_low = inputs[0]
    cot_low = cotangent[0]
    rows = tokens_low.shape[0]
    before = lax.ppermute(tokens_low[rows - HALO :], "seq", [(i, i + 1) for i in range(seq_count - 1)])
    tokens = jnp.concatenate([before, tokens_low], axis=0).astype(full_type)
    inv_rms = lax.rsqrt(jnp.mean(tokens * tokens, axis=-1, keepdims=True) + norm_eps)
    normed_all = (tokens * inv_rms * gain_in).astype(low_type)
    packed = dot(normed_all, full_sig).astype(low_type)
    tokens = tokens[HALO:]
    inv_rms = inv_rms[HALO:]
    normed = normed_all[HALO:]
    x, bc, run, lag, run_t, lag_t, enter, enter_all, tail, offs, states, send = run_states(packed, conv, head)
    gathered = lax.all_gather(send, "seq", axis=0)
    y = run_outputs(x, bc, run, lag_t, enter, states, head)
    gate_vals = dot(normed, full_gate)
    back = dot_nt(cot_low, full_out)
    totals = gathered[:, STATE].astype(full_type) + gathered[:, STATE + 1].astype(full_type)
    state_in = jnp.zeros((STATE, INNER), full_type)
    for z in range(seq_count - 1):
        between = jnp.zeros((INNER,), full_type)
        for other in range(z + 1, seq_count - 1):
            between = between + jnp.where(other < seq_index, totals[other], 0.0)
        state_in = state_in + jnp.where(z < seq_index, jnp.exp2(between), 0.0) * gathered[z, :STATE].astype(full_type)
    state_in = state_in.astype(low_type)
    gain_rows = jnp.broadcast_to(gain_out, (8, INNER))
    normed_out, grad_y, grad_gate, part_gnorm, grad_state = run_norm(
        y, gate_vals, back, gain_rows, bc, enter_all, state_in
    )
    grad_states = lax.all_gather(grad_state.astype(low_type), "seq", axis=0)
    block_out = (tokens + dot(normed_out, full_out)).astype(low_type)[None]
    part_out = lax.psum_scatter(
        dot(normed_out, cot_low, ((0,), (0,))).astype(low_type), "wsh", scatter_dimension=0, tiled=True
    )
    part_gate = lax.psum_scatter(
        dot(normed, grad_gate, ((0,), (0,))).astype(low_type), "wsh", scatter_dimension=0, tiled=True
    )
    grad_normed = dot_nt(grad_gate, full_gate)
    grad_in = jnp.zeros((STATE, INNER), full_type)
    for z in range(1, seq_count):
        between = jnp.zeros((INNER,), full_type)
        for other in range(1, z):
            between = between + jnp.where(other > seq_index, totals[other], 0.0)
        grad_in = grad_in + jnp.where(z > seq_index, jnp.exp2(between), 0.0) * grad_states[z].astype(full_type)
    grad_in = grad_in.astype(low_type)
    grad_pack, edge, last, part_conv, part_skip, part_head = run_backward(
        packed, conv, head, grad_y, bc, lag, run_t, enter, tail, offs, states, state_in, grad_in
    )
    after = lax.ppermute(edge, "seq", [(i, i - 1) for i in range(1, seq_count)])
    fixed = jnp.concatenate([last[:8], last[8:] + after], axis=0).astype(low_type)
    grad_pack = lax.dynamic_update_slice(grad_pack, fixed, (rows - 16, 0))
    part_sig = lax.psum_scatter(
        dot(normed, grad_pack, ((0,), (0,))).astype(low_type), "wsh", scatter_dimension=0, tiled=True
    )
    grad_normed = grad_normed + dot_nt(grad_pack, full_sig)
    scaled = tokens * inv_rms
    part_gpre = jnp.sum(grad_normed * scaled, axis=0)
    pulled = grad_normed * gain_in
    grad_tokens = inv_rms * (pulled - scaled * jnp.mean(pulled * scaled, axis=-1, keepdims=True))
    input_grad = (cot_low.astype(full_type) + grad_tokens)[None]
    skip_sums = part_skip[0].reshape(HEADS, HEAD_DIM).sum(axis=1)
    small_sums = lax.psum(
        jnp.concatenate(
            [part_gpre, part_gnorm[0], part_conv[:5].reshape(-1), part_head[0, :HEADS], part_head[1, :HEADS], skip_sums]
        ),
        ("seq", "wsh"),
    )
    cuts = [D, D + INNER, D + INNER + 5 * CONV_CH]
    grad_gpre = lax.dynamic_slice_in_dim(small_sums[: cuts[0]], wsh_index * rows_model, rows_model, 0)
    grad_gnorm = lax.dynamic_slice_in_dim(small_sums[cuts[0] : cuts[1]], wsh_index * rows_inner, rows_inner, 0)
    grad_conv = lax.dynamic_slice_in_dim(
        small_sums[cuts[1] : cuts[2]].reshape(5, CONV_CH), wsh_index * cols_conv, cols_conv, 1
    )
    grad_head = lax.dynamic_slice_in_dim(
        small_sums[cuts[2] :].reshape(3, HEADS), wsh_index * cols_head, cols_head, 1
    )
    grad_out, sum_gate, sum_sig = (
        lax.psum(part.astype(full_type), "seq") for part in (part_out, part_gate, part_sig)
    )
    grad_in_w = jnp.concatenate([sum_gate, sum_sig[:, :CONV_CH]], axis=1)
    grad_dt = sum_sig[:, CONV_CH : CONV_CH + HEADS]
    params = (w_in, w_dt, w_out, gain_pre, gain_norm, conv_param, head_param)
    gradients = (grad_in_w, grad_dt, grad_out, grad_gpre, grad_gnorm, grad_conv, grad_head)
    firsts = (first_w_in, first_w_dt, first_w_out, first_gain_pre, first_gain_norm, first_conv, first_head)
    seconds = (second_w_in, second_w_dt, second_w_out, second_gain_pre, second_gain_norm, second_conv, second_head)
    step_rates = (rate_matrix, rate_matrix, rate_matrix, rate_gain, rate_gain, rate_conv, rate_head)
    decays = (weight_decay, weight_decay, weight_decay, 0.0, 0.0, 0.0, 0.0)
    updated = [adam_update(*items) for items in zip(params, gradients, firsts, seconds, step_rates, decays)]
    new_params = tuple(entry[0] for entry in updated)
    moments = []
    for entry in updated:
        moments.append(entry[1])
        moments.append(entry[2])
    return (block_out, input_grad) + gradients + new_params + tuple(moments)


def solution(mesh):
    rows, vec, cols = P("wsh", None), P("wsh"), P(None, "wsh")
    tokens = P("wsh", "seq", None)
    params = (rows, rows, rows, vec, vec, cols, cols)
    moments = tuple(spec for spec in params for _ in range(2))
    in_specs = (tokens, tokens) + params + moments
    out_specs = (tokens, tokens) + params + params + moments
    return jax.shard_map(shards, mesh=mesh, in_specs=in_specs, out_specs=out_specs, check_vma=False)
```

```python
import functools

import jax
import jax.numpy as jnp
from jax import lax
from jax.experimental import pallas as pl
from jax.experimental.pallas import tpu as pltpu
from jax.sharding import PartitionSpec as P

D = 1536
HEADS = 48
HEAD_DIM = 64
STATE = 128
CONV_WIDTH = 4
STEP = 2
INNER = 3072
CONV_CH = 3328
BLOCK = 128
LANES = 128
WIDE = 256
HALO = 16
GROUPS = INNER // WIDE
PACK = CONV_CH + LANES
LOG2E = 1.4426950408889634
VMEM_LIMIT = 56 * 1024 * 1024

norm_eps = 1e-05
beta_one = 0.9
beta_two = 0.999
adam_eps = 1e-08
rate_matrix = 0.01
rate_gain = 0.4
rate_conv = 0.1
rate_head = 1.0
weight_decay = 0.1
highest = lax.Precision.HIGHEST
low_type = jnp.bfloat16
full_type = jnp.float32


def dot(left_side, right_side, dims=((1,), (0,)), precision=None):
    return lax.dot_general(
        left_side, right_side, (dims, ((), ())), precision=precision, preferred_element_type=full_type
    )


def dot_nt(left_side, right_side):
    return dot(left_side, right_side, ((1,), (1,)))


def sigmoid(vals):
    return 0.5 * jnp.tanh(0.5 * vals) + 0.5


def lane_ids(shape):
    return lax.broadcasted_iota(jnp.int32, shape, len(shape) - 1)


def widen(vals, first=0):
    left = lane_ids((vals.shape[0], LANES)) < HEAD_DIM
    pairs = [
        jnp.where(left, vals[:, first + i : first + i + 1], vals[:, first + i + 1 : first + i + 2])
        for i in (0, 2)
    ]
    return jnp.concatenate(pairs, axis=1)


def to_front(vals, step):
    return pltpu.roll(vals, lax.rem(LANES - 4 * step, LANES), 1)


def head_rows(ref, step):
    eight = ref[pl.ds(pl.multiple_of(8 * (step // 2), 8), 8), :]
    return pltpu.roll(eight, 4 * lax.rem(step, 2), 0)


def step_terms(raw, head):
    shifted = raw + head[1:2]
    small = jnp.exp(-jnp.abs(shifted))
    log_part = jnp.where(
        small < 0.01, small * (1.0 - small * (0.5 - small * (1.0 / 3.0))), jnp.log(1.0 + small)
    )
    step_sizes = jnp.maximum(shifted, 0.0) + log_part
    slope = jnp.where(shifted >= 0.0, 1.0, small) / (1.0 + small)
    return step_sizes, slope, -jnp.exp(head[0:1])


def convolve(sig, conv, rows):
    total = conv[4:5] + conv[0:1] * sig[HALO - 3 : HALO - 3 + rows, :]
    for k in range(1, CONV_WIDTH):
        total = total + conv[k : k + 1] * sig[HALO - 3 + k : HALO - 3 + k + rows, :]
    return total


def triangle(lower):
    rows = lax.broadcasted_iota(jnp.int32, (BLOCK, BLOCK), 0)
    cols = lax.broadcasted_iota(jnp.int32, (BLOCK, BLOCK), 1)
    return rows >= cols if lower else rows <= cols


def states_kernel(
    sig_ref, maps_ref, raw_ref, conv_ref, conv_maps_ref, head_ref,
    x_ref, bc_ref, run_ref, lag_ref, run_t_ref, lag_t_ref, enter_ref, enter_all_ref, tail_ref, offs_ref,
    states_ref, send_ref,
    sig, in_t,
):
    step = pl.program_id(0)
    rows = x_ref.shape[0]
    blocks = rows // BLOCK

    @pl.when(step == 0)
    def _():
        sig[...] = maps_ref[...].astype(full_type)
        pre = convolve(sig, conv_maps_ref[...], rows)
        maps = pre * sigmoid(pre)
        bc_ref[...] = maps
        in_t[...] = maps[:, :STATE].T.astype(low_type)
        step_sizes, _, rate = step_terms(raw_ref[HALO:, :].astype(full_type), head_ref[...])
        rates = step_sizes * rate * LOG2E
        log_steps = jnp.log2(step_sizes)
        lower = jnp.where(triangle(True), 1.0, 0.0)
        offset = jnp.zeros((1, LANES), full_type)
        offs_ref[...] = jnp.zeros(offs_ref.shape, full_type)
        for c in range(blocks):
            at = slice(c * BLOCK, (c + 1) * BLOCK)
            run = dot(lower, rates[at], precision=highest)
            lag = run - log_steps[at]
            run_ref[at, :] = run
            lag_ref[at, :] = lag
            run_t_ref[:, at] = run.T
            lag_t_ref[:, at] = lag.T
            enter_ref[at, :] = jnp.exp2(run)
            enter_all_ref[at, :] = jnp.exp2(run + offset)
            tail_ref[at, :] = jnp.exp2(run[BLOCK - 1 : BLOCK] - lag)
            offs_ref[c : c + 1, :] = offset
            offset = offset + run[BLOCK - 1 : BLOCK]
        offs_ref[blocks : blocks + 1, :] = offset

    sig[...] = sig_ref[...].astype(full_type)
    pre = convolve(sig, conv_ref[...], rows)
    x = pre * sigmoid(pre)
    x_ref[...] = x
    tail = to_front(tail_ref[...], step)
    last = to_front(offs_ref[...], step)
    state = jnp.zeros((STATE, WIDE), full_type)
    for c in range(blocks):
        at = slice(c * BLOCK, (c + 1) * BLOCK)
        weighted = (x[at] * widen(tail[at])).astype(low_type)
        fade = jnp.exp2(widen(last[c + 1 : c + 2] - last[c : c + 1]))
        state = state * fade + dot(in_t[:, at], weighted)
        states_ref[c] = state.astype(low_type)
    send_ref[:STATE, :] = state.astype(low_type)
    total = widen(last[blocks : blocks + 1])
    high = total.astype(low_type).astype(full_type)
    ids = lax.broadcasted_iota(jnp.int32, (16, WIDE), 0)
    extra = jnp.where(ids == 0, high, jnp.where(ids == 1, total - high, 0.0))
    send_ref[STATE:, :] = extra.astype(low_type)


def outputs_kernel(x_ref, bc_ref, run_ref, lag_t_ref, enter_ref, states_ref, head_ref, y_ref, inter):
    step = pl.program_id(0)
    rows = x_ref.shape[0]
    blocks = rows // BLOCK
    lower = triangle(True)

    @pl.when(step == 0)
    def _():
        for c in range(blocks):
            at = slice(c * BLOCK, (c + 1) * BLOCK)
            maps = bc_ref[at, :].astype(low_type)
            inter[c] = dot_nt(maps[:, STATE:], maps[:, :STATE])

    run = to_front(run_ref[...], step)
    enter = to_front(enter_ref[...], step)
    lag_rows = head_rows(lag_t_ref, step)
    skip = widen(to_front(head_ref[...], step)[2:3])
    left = lane_ids((BLOCK, LANES)) < HEAD_DIM
    for c in range(blocks):
        at = slice(c * BLOCK, (c + 1) * BLOCK)
        x = x_ref[at, :]
        parts = []
        for pair in range(2):
            mixes = []
            for i in range(2):
                h = 2 * pair + i
                lag_row = lag_rows[h : h + 1, at]
                power = jnp.where(lower, run[at, h : h + 1] - lag_row, -1e30)
                mixes.append((jnp.exp2(power) * inter[c]).astype(low_type))
            half = x[:, pair * LANES : (pair + 1) * LANES].astype(low_type)
            zero = jnp.zeros_like(half)
            stacked = jnp.concatenate([jnp.where(left, half, zero), jnp.where(left, zero, half)], axis=0)
            parts.append(dot(jnp.concatenate(mixes, axis=1), stacked))
        y = jnp.concatenate(parts, axis=1) + skip * x
        if c > 0:
            out_map = bc_ref[at, STATE:].astype(low_type)
            y = y + widen(enter[at]) * dot(out_map, states_ref[c - 1])
        y_ref[at, :] = y


def norm_kernel(
    y_ref, gate_ref, back_ref, gain_ref, bc_ref, enter_ref, state_ref,
    normed_ref, grad_y_ref, grad_gate_ref, grad_gain_ref, grad_state_ref,
    gated, low_y,
):
    step = pl.program_id(0)
    rows = y_ref.shape[0]

    @pl.when(step == 0)
    def _():
        grad_gain_ref[...] = jnp.zeros(grad_gain_ref.shape, full_type)
        grad_state_ref[...] = jnp.zeros(grad_state_ref.shape, full_type)

    out_map = bc_ref[:, STATE:]
    out_low = out_map.astype(low_type)
    out_t = out_map.T.astype(low_type)
    squares = jnp.zeros((rows, WIDE), full_type)
    cross = jnp.zeros((rows, WIDE), full_type)
    for j in range(GROUPS):
        at = slice(j * WIDE, (j + 1) * WIDE)
        enter = widen(enter_ref[...], 4 * j)
        y = y_ref[:, at] + enter * dot(out_low, state_ref[:, at])
        y_low = y.astype(low_type)
        low_y[:, at] = y_low
        gate = gate_ref[:, at]
        vals = y_low.astype(full_type) * (gate * sigmoid(gate))
        gated[:, at] = vals
        squares = squares + vals * vals
        cross = cross + vals * (back_ref[:, at] * gain_ref[0:1, at])
    inv = lax.rsqrt(jnp.sum(squares, axis=1, keepdims=True) * (1.0 / INNER) + norm_eps)
    pull = inv * inv * inv * (jnp.sum(cross, axis=1, keepdims=True) * (1.0 / INNER))
    for j in range(GROUPS):
        at = slice(j * WIDE, (j + 1) * WIDE)
        gain = gain_ref[0:1, at]
        back = back_ref[:, at]
        vals = gated[:, at]
        scaled = vals * inv
        normed_ref[:, at] = (scaled * gain).astype(low_type)
        grad_gain_ref[0:1, at] += jnp.sum(back * scaled, axis=0, keepdims=True)
        grad_vals = back * gain * inv - vals * pull
        gate = gate_ref[:, at]
        sig = sigmoid(gate)
        silu = gate * sig
        grad_y = (grad_vals * silu).astype(low_type)
        grad_y_ref[:, at] = grad_y
        slope = sig + silu * (1.0 - sig)
        grad_gate_ref[:, at] = (grad_vals * low_y[:, at].astype(full_type) * slope).astype(low_type)
        enter = widen(enter_ref[...], 4 * j)
        grad_state_ref[:, at] += dot(out_t, (grad_y.astype(full_type) * enter).astype(low_type))


def backward_kernel(
    sig_ref, raw_ref, conv_ref, head_ref, grad_y_ref, bc_ref,
    lag_ref, run_t_ref, enter_ref, tail_ref, offs_ref, states_ref, state_in_ref, grad_in_ref,
    grad_sig_ref, edge_ref, last_ref, grad_conv_ref, grad_skip_ref, grad_head_ref,
    sig, padded, inter, grad_inter, grad_maps, out_t, run_rows, run_cols, run_ends, weighs,
):
    step = pl.program_id(0)
    rows = grad_y_ref.shape[0]
    blocks = rows // BLOCK
    upper = triangle(False)

    @pl.when(step == 0)
    def _():
        for c in range(blocks):
            at = slice(c * BLOCK, (c + 1) * BLOCK)
            maps = bc_ref[at, :].astype(low_type)
            inter[c] = dot_nt(maps[:, :STATE], maps[:, STATE:])
            out_t[:, at] = bc_ref[at, STATE:].T.astype(low_type)
        grad_inter[...] = jnp.zeros(grad_inter.shape, full_type)
        grad_maps[...] = jnp.zeros(grad_maps.shape, full_type)
        run_rows[...] = jnp.zeros(run_rows.shape, full_type)
        run_cols[...] = jnp.zeros(run_cols.shape, full_type)
        run_ends[...] = jnp.zeros(run_ends.shape, full_type)
        weighs[...] = jnp.zeros(weighs.shape, full_type)
        padded[...] = jnp.zeros(padded.shape, full_type)

    def conv_back(grad_pre):
        conv = conv_ref[...]
        grad_sig = conv[3:4] * padded[HALO : HALO + rows, :]
        edge = conv[3:4] * padded[8:HALO, :]
        for k in range(3):
            grad_sig = grad_sig + conv[k : k + 1] * padded[HALO + 3 - k : HALO + 3 - k + rows, :]
            edge = edge + conv[k : k + 1] * padded[11 - k : 19 - k, :]
        grad_sig_ref[...] = grad_sig.astype(low_type)
        edge_ref[...] = edge
        last_ref[...] = grad_sig[rows - 16 :]
        sums = [
            jnp.sum(grad_pre * sig[HALO - 3 + k : HALO - 3 + k + rows, :], axis=0, keepdims=True)
            for k in range(CONV_WIDTH)
        ]
        sums.append(jnp.sum(grad_pre, axis=0, keepdims=True))
        sums.append(jnp.zeros((3, WIDE), full_type))
        grad_conv_ref[...] = jnp.concatenate(sums, axis=0)

    @pl.when(step < GROUPS)
    def _():
        sig[...] = sig_ref[...].astype(full_type)
        lag = to_front(lag_ref[...], step)
        run_all = head_rows(run_t_ref, step)
        enter = to_front(enter_ref[...], step)
        tail = to_front(tail_ref[...], step)
        offs = to_front(offs_ref[...], step)
        skip = widen(to_front(head_ref[...], step)[2:3])
        left = lane_ids((BLOCK, LANES)) < HEAD_DIM
        heads_of = lax.broadcasted_iota(jnp.int32, (WIDE, LANES), 0) // HEAD_DIM + 4 * step
        picks = jnp.where(heads_of == lane_ids((WIDE, LANES)), 1.0, 0.0).astype(low_type)
        state_in = state_in_ref[...].astype(full_type)
        grad_state = grad_in_ref[...].astype(full_type)
        grad_skip = jnp.zeros((1, WIDE), full_type)
        pre_all = convolve(sig, conv_ref[...], rows)

        def head_sums(vals):
            high = vals.astype(low_type)
            rest = (vals - high.astype(full_type)).astype(low_type)
            return dot(high, picks) + dot(rest, picks)

        for c in reversed(range(blocks)):
            at = slice(c * BLOCK, (c + 1) * BLOCK)
            pre = pre_all[at]
            gate = sigmoid(pre)
            x = pre * gate
            x_low = x.astype(low_type)
            x_round = x_low.astype(full_type)
            grad_y = grad_y_ref[at, :]
            grad_y_full = grad_y.astype(full_type)
            in_map = bc_ref[at, :STATE].astype(low_type)
            out_map = bc_ref[at, STATE:].astype(low_type)
            tail_c = widen(tail[at])
            enter_c = widen(enter[at])
            entering = state_in * jnp.exp2(widen(offs[c : c + 1]))
            if c > 0:
                entering = entering + states_ref[c - 1].astype(full_type)
            leaving = states_ref[c].astype(full_type) + state_in * jnp.exp2(widen(offs[c + 1 : c + 2]))
            entering_low = entering.astype(low_type)
            grad_low = grad_state.astype(low_type)
            ends = jnp.sum(grad_state * leaving, axis=0, keepdims=True)
            run_ends[c : c + 1, :] += head_sums(jnp.concatenate([ends, jnp.zeros((7, WIDE), full_type)], axis=0))[0:1]
            grad_x = tail_c * dot(in_map, grad_low)
            grad_maps[at, :STATE] += dot_nt((x * tail_c).astype(low_type), grad_low)
            swept = grad_y_full * enter_c
            swept_low = swept.astype(low_type)
            through = swept * dot(out_map, entering_low)
            grad_maps[at, STATE:] += dot_nt(swept_low, entering_low)
            fade = jnp.exp2(widen(offs[c + 1 : c + 2] - offs[c : c + 1]))
            grad_state = grad_state * fade + dot(out_t[:, at], swept_low)
            parts = []
            sums = []
            for pair in range(2):
                half = slice(pair * LANES, (pair + 1) * LANES)
                grad_half = grad_y[:, half]
                zero = jnp.zeros_like(grad_half)
                stacked = jnp.concatenate(
                    [jnp.where(left, grad_half, zero), jnp.where(left, zero, grad_half)], axis=0
                )
                cross = dot_nt(x_low[:, half], stacked)
                mixes = []
                for i in range(2):
                    h = 2 * pair + i
                    run_row = run_all[h : h + 1, at]
                    power = jnp.where(upper, run_row - lag[at, h : h + 1], -1e30)
                    decay = jnp.exp2(power)
                    mix = (decay * inter[c]).astype(low_type)
                    mixes.append(mix)
                    cross_h = cross[:, i * LANES : (i + 1) * LANES]
                    grad_inter[c] += cross_h * decay
                    sums.append(jnp.sum(cross_h * mix.astype(full_type), axis=0, keepdims=True))
                parts.append(dot(jnp.concatenate(mixes, axis=1), stacked))
            sums.append(jnp.zeros((4, BLOCK), full_type))
            run_rows[pl.ds(pl.multiple_of(8 * step, 8), 8), at] = jnp.concatenate(sums, axis=0)
            grad_x = grad_x + jnp.concatenate(parts, axis=1)
            weigh = head_sums(x_round * grad_x)
            weighs[at, :] += weigh
            run_cols[at, :] += head_sums(through) - weigh
            grad_skip = grad_skip + jnp.sum(grad_y_full * x, axis=0, keepdims=True)
            grad_x = grad_x + skip * grad_y_full
            padded[HALO + c * BLOCK : HALO + (c + 1) * BLOCK, :] = grad_x * (gate + x * (1.0 - gate))
        grad_skip_ref[...] = jnp.broadcast_to(grad_skip, grad_skip_ref.shape)
        conv_back(padded[HALO : HALO + rows, :])

    @pl.when(step == GROUPS)
    def _():
        sig[...] = sig_ref[...].astype(full_type)
        pre_all = convolve(sig, conv_ref[...], rows)
        for c in range(blocks):
            at = slice(c * BLOCK, (c + 1) * BLOCK)
            maps = bc_ref[at, :].astype(low_type)
            grad_block = grad_inter[c]
            grad_bc = grad_maps[at, :] + jnp.concatenate(
                [
                    dot(grad_block.astype(low_type), maps[:, STATE:]),
                    dot(grad_block.T.astype(low_type), maps[:, :STATE]),
                ],
                axis=1,
            )
            pre = pre_all[at]
            gate = sigmoid(pre)
            padded[HALO + c * BLOCK : HALO + (c + 1) * BLOCK, :] = grad_bc * (gate + pre * gate * (1.0 - gate))
        conv_back(padded[HALO : HALO + rows, :])

    @pl.when(step == GROUPS + 1)
    def _():
        head = head_ref[...]
        step_sizes, slope, rate = step_terms(raw_ref[HALO:, :].astype(full_type), head)
        ratio = jnp.where(step_sizes > 1e-30, slope / jnp.maximum(step_sizes, 1e-30), 1.0)
        used = lane_ids((BLOCK, LANES)) < HEADS
        later = jnp.where(upper, 1.0, 0.0)
        rate_sum = jnp.zeros((1, LANES), full_type)
        bias_sum = jnp.zeros((1, LANES), full_type)
        for c in range(blocks):
            at = slice(c * BLOCK, (c + 1) * BLOCK)
            by_head = [run_rows[8 * j : 8 * j + 4, at] for j in range(GROUPS)]
            by_head.append(jnp.zeros((LANES - HEADS, BLOCK), full_type))
            grad_run = jnp.concatenate(by_head, axis=0).T + run_cols[at, :]
            grad_rates = dot(later, grad_run, precision=highest) + run_ends[c : c + 1, :]
            grad_raw = slope[at] * rate * grad_rates + ratio[at] * weighs[at, :]
            grad_raw = jnp.where(used, grad_raw, 0.0)
            grad_sig_ref[at, :LANES] = grad_raw.astype(low_type)
            grad_sig_ref[at, LANES:] = jnp.zeros((BLOCK, LANES), low_type)
            rate_sum = rate_sum + jnp.sum(grad_rates * step_sizes[at], axis=0, keepdims=True)
            bias_sum = bias_sum + jnp.sum(grad_raw, axis=0, keepdims=True)
        grad_head_ref[...] = jnp.concatenate(
            [rate_sum * rate, bias_sum, jnp.zeros((6, LANES), full_type)], axis=0
        )


def run_states(packed, conv, head):
    rows = packed.shape[0] - HALO
    blocks = rows // BLOCK
    whole = lambda shape: pl.BlockSpec(shape, lambda j: (0,) * len(shape))
    small = jax.ShapeDtypeStruct((rows, LANES), full_type)
    small_t = jax.ShapeDtypeStruct((LANES, rows), full_type)
    return pl.pallas_call(
        states_kernel,
        grid=(GROUPS,),
        in_specs=[
            pl.BlockSpec((rows + HALO, WIDE), lambda j: (0, j)),
            pl.BlockSpec((rows + HALO, WIDE), lambda j: (0, GROUPS)),
            pl.BlockSpec((rows + HALO, LANES), lambda j: (0, CONV_CH // LANES)),
            pl.BlockSpec((8, WIDE), lambda j: (0, j)),
            pl.BlockSpec((8, WIDE), lambda j: (0, GROUPS)),
            whole((8, LANES)),
        ],
        out_specs=[
            pl.BlockSpec((rows, WIDE), lambda j: (0, j)),
            whole((rows, WIDE)),
            whole((rows, LANES)),
            whole((rows, LANES)),
            whole((LANES, rows)),
            whole((LANES, rows)),
            whole((rows, LANES)),
            whole((rows, LANES)),
            whole((rows, LANES)),
            whole((16, LANES)),
            pl.BlockSpec((blocks, STATE, WIDE), lambda j: (0, 0, j)),
            pl.BlockSpec((STATE + 16, WIDE), lambda j: (0, j)),
        ],
        out_shape=[
            jax.ShapeDtypeStruct((rows, INNER), full_type),
            jax.ShapeDtypeStruct((rows, WIDE), full_type),
            small, small, small_t, small_t, small, small, small,
            jax.ShapeDtypeStruct((16, LANES), full_type),
            jax.ShapeDtypeStruct((blocks, STATE, INNER), low_type),
            jax.ShapeDtypeStruct((STATE + 16, INNER), low_type),
        ],
        scratch_shapes=[
            pltpu.VMEM((rows + HALO, WIDE), full_type),
            pltpu.VMEM((STATE, rows), low_type),
        ],
        compiler_params=pltpu.CompilerParams(vmem_limit_bytes=VMEM_LIMIT),
        cost_estimate=pl.CostEstimate(flops=10**9, bytes_accessed=15 * 10**6, transcendentals=10**6),
        name="scan_states",
    )(packed, packed, packed, conv, conv, head)


def run_outputs(x, bc, run, lag_t, enter, states, head):
    rows = x.shape[0]
    blocks = rows // BLOCK
    whole = lambda shape: pl.BlockSpec(shape, lambda j: (0,) * len(shape))
    return pl.pallas_call(
        outputs_kernel,
        grid=(GROUPS,),
        in_specs=[
            pl.BlockSpec((rows, WIDE), lambda j: (0, j)),
            whole((rows, WIDE)),
            whole((rows, LANES)),
            whole((LANES, rows)),
            whole((rows, LANES)),
            pl.BlockSpec((blocks, STATE, WIDE), lambda j: (0, 0, j)),
            whole((8, LANES)),
        ],
        out_specs=pl.BlockSpec((rows, WIDE), lambda j: (0, j)),
        out_shape=jax.ShapeDtypeStruct((rows, INNER), full_type),
        scratch_shapes=[pltpu.VMEM((blocks, BLOCK, BLOCK), full_type)],
        compiler_params=pltpu.CompilerParams(vmem_limit_bytes=VMEM_LIMIT),
        cost_estimate=pl.CostEstimate(flops=10**10, bytes_accessed=15 * 10**6, transcendentals=3 * 10**6),
        name="scan_outputs",
    )(x, bc, run, lag_t, enter, states, head)


def run_norm(y, gate, back, gain, bc, enter, state):
    rows = y.shape[0]
    part = BLOCK
    by_rows = lambda cols: pl.BlockSpec((part, cols), lambda i: (i, 0))
    whole = lambda shape: pl.BlockSpec(shape, lambda i: (0,) * len(shape))
    return pl.pallas_call(
        norm_kernel,
        grid=(rows // part,),
        in_specs=[
            by_rows(INNER), by_rows(INNER), by_rows(INNER), whole((8, INNER)),
            by_rows(WIDE), by_rows(LANES), whole((STATE, INNER)),
        ],
        out_specs=[by_rows(INNER), by_rows(INNER), by_rows(INNER), whole((8, INNER)), whole((STATE, INNER))],
        out_shape=[
            jax.ShapeDtypeStruct((rows, INNER), low_type),
            jax.ShapeDtypeStruct((rows, INNER), low_type),
            jax.ShapeDtypeStruct((rows, INNER), low_type),
            jax.ShapeDtypeStruct((8, INNER), full_type),
            jax.ShapeDtypeStruct((STATE, INNER), full_type),
        ],
        scratch_shapes=[pltpu.VMEM((part, INNER), full_type), pltpu.VMEM((part, INNER), low_type)],
        compiler_params=pltpu.CompilerParams(vmem_limit_bytes=VMEM_LIMIT),
        cost_estimate=pl.CostEstimate(flops=10**9, bytes_accessed=30 * 10**6, transcendentals=3 * 10**6),
        name="gated_norm",
    )(y, gate, back, gain, bc, enter, state)


def run_backward(packed, conv, head, grad_y, bc, lag, run_t, enter, tail, offs, states, state_in, grad_in):
    rows = grad_y.shape[0]
    blocks = rows // BLOCK
    whole = lambda shape: pl.BlockSpec(shape, lambda j: (0,) * len(shape))
    most = lambda j, top: jnp.minimum(j, top)
    return pl.pallas_call(
        backward_kernel,
        grid=(GROUPS + 2,),
        in_specs=[
            pl.BlockSpec((rows + HALO, WIDE), lambda j: (0, most(j, GROUPS))),
            pl.BlockSpec((rows + HALO, LANES), lambda j: (0, CONV_CH // LANES)),
            pl.BlockSpec((8, WIDE), lambda j: (0, most(j, GROUPS))),
            whole((8, LANES)),
            pl.BlockSpec((rows, WIDE), lambda j: (0, most(j, GROUPS - 1))),
            whole((rows, WIDE)),
            whole((rows, LANES)),
            whole((LANES, rows)),
            whole((rows, LANES)),
            whole((rows, LANES)),
            whole((16, LANES)),
            pl.BlockSpec((blocks, STATE, WIDE), lambda j: (0, 0, most(j, GROUPS - 1))),
            pl.BlockSpec((STATE, WIDE), lambda j: (0, most(j, GROUPS - 1))),
            pl.BlockSpec((STATE, WIDE), lambda j: (0, most(j, GROUPS - 1))),
        ],
        out_specs=[
            pl.BlockSpec((rows, WIDE), lambda j: (0, j)),
            pl.BlockSpec((8, WIDE), lambda j: (0, most(j, GROUPS))),
            pl.BlockSpec((16, WIDE), lambda j: (0, most(j, GROUPS))),
            pl.BlockSpec((8, WIDE), lambda j: (0, most(j, GROUPS))),
            pl.BlockSpec((8, WIDE), lambda j: (0, most(j, GROUPS - 1))),
            whole((8, LANES)),
        ],
        out_shape=[
            jax.ShapeDtypeStruct((rows, PACK), low_type),
            jax.ShapeDtypeStruct((8, CONV_CH), full_type),
            jax.ShapeDtypeStruct((16, CONV_CH), full_type),
            jax.ShapeDtypeStruct((8, CONV_CH), full_type),
            jax.ShapeDtypeStruct((8, INNER), full_type),
            jax.ShapeDtypeStruct((8, LANES), full_type),
        ],
        scratch_shapes=[
            pltpu.VMEM((rows + HALO, WIDE), full_type),
            pltpu.VMEM((rows + 2 * HALO, WIDE), full_type),
            pltpu.VMEM((blocks, BLOCK, BLOCK), full_type),
            pltpu.VMEM((blocks, BLOCK, BLOCK), full_type),
            pltpu.VMEM((rows, WIDE), full_type),
            pltpu.VMEM((STATE, rows), low_type),
            pltpu.VMEM((LANES, rows), full_type),
            pltpu.VMEM((rows, LANES), full_type),
            pltpu.VMEM((8, LANES), full_type),
            pltpu.VMEM((rows, LANES), full_type),
        ],
        compiler_params=pltpu.CompilerParams(vmem_limit_bytes=VMEM_LIMIT),
        cost_estimate=pl.CostEstimate(flops=2 * 10**10, bytes_accessed=20 * 10**6, transcendentals=5 * 10**6),
        name="scan_backward",
    )(packed, packed, conv, head, grad_y, bc, lag, run_t, enter, tail, offs, states, state_in, grad_in)


def adam_update(weights, gradient, first_moment, second_moment, step_rate, decay_amount):
    next_first = beta_one * first_moment + (1.0 - beta_one) * gradient
    next_second = beta_two * second_moment + (1.0 - beta_two) * gradient * gradient
    corrected = (
        next_first
        / (1.0 - beta_one**STEP)
        / (jnp.sqrt(next_second / (1.0 - beta_two**STEP)) + adam_eps)
    )
    return (weights - step_rate * (corrected + decay_amount * weights), next_first, next_second)


def pad_rows(vals, rows):
    return jnp.pad(vals, ((0, rows - vals.shape[0]), (0, 0)))


def swap(vals, bit, axis="wsh"):
    return lax.ppermute(vals, axis, [(i, i ^ bit) for i in range(lax.axis_size(axis))])


def gather_pieces(own, count, also=None):
    rows = own.shape[0]
    far = [1 << b for b in range(1, count.bit_length() - 1)]
    pieces = [(0, 0, own)]
    if len(far) == 2:
        one, two = far
        half = rows // 2
        by_one = swap(own, one)
        by_two = swap(own, two)
        pieces += [(one, 0, by_one), (two, 0, by_two)]
        pieces += [(one | two, 0, swap(by_two[:half], one)), (one | two, half, swap(by_one[half:], two))]
    else:
        for bit in far:
            pieces += [(r ^ bit, first, swap(piece, bit)) for r, first, piece in pieces]
    marks = [piece for _, _, piece in pieces[-2:]]
    return pieces + [(r ^ 1, first, swap(piece, 1)) for r, first, piece in pieces], marks


def piece_kernel(spots, rows, me_ref, left_ref, *refs):
    sources, out_ref, whole_ref = refs[: len(spots)], refs[len(spots)], refs[len(spots) + 1]
    for source, (r, first) in zip(sources, spots):
        start = lax.bitwise_xor(me_ref[0], r) * rows + first
        whole_ref[pl.ds(pl.multiple_of(start, 16), source.shape[0]), :] = source[...]
    out_ref[...] = dot(left_ref[...], whole_ref[...]).astype(out_ref.dtype)


def multiply_pieces(left, pieces, count, out_type, name):
    rows, cols = pieces[0][2].shape
    tile = 512
    me = jnp.reshape(lax.axis_index("wsh"), (1,)).astype(jnp.int32)
    spots = [(r, first) for r, first, _ in pieces]
    return pl.pallas_call(
        functools.partial(piece_kernel, spots, rows),
        grid=(pl.cdiv(cols, tile),),
        in_specs=[pl.BlockSpec(memory_space=pltpu.SMEM), pl.BlockSpec(left.shape, lambda j: (0, 0))]
        + [pl.BlockSpec((piece.shape[0], tile), lambda j: (0, j)) for _, _, piece in pieces],
        out_specs=[
            pl.BlockSpec((left.shape[0], tile), lambda j: (0, j)),
            pl.BlockSpec((rows * count, tile), lambda j: (0, j)),
        ],
        out_shape=[
            jax.ShapeDtypeStruct((left.shape[0], cols), out_type),
            jax.ShapeDtypeStruct((rows * count, cols), low_type),
        ],
        compiler_params=pltpu.CompilerParams(vmem_limit_bytes=VMEM_LIMIT),
        cost_estimate=pl.CostEstimate(
            flops=2 * left.shape[0] * rows * count * cols, bytes_accessed=4 * rows * count * cols, transcendentals=0
        ),
        name=name,
    )(me, left, *[piece for _, _, piece in pieces])


def back_kernel(spots, me_ref, left_ref, *refs):
    sources, out_ref, whole_ref = refs[: len(spots)], refs[len(spots)], refs[len(spots) + 1]
    step = pl.program_id(0)
    for r in sorted({r for r, _ in spots}):

        @pl.when(step == r)
        def _():
            for source, (other, first) in zip(sources, spots):
                if other == r:
                    whole_ref[first : first + source.shape[0], :] = source[...]
            out_ref[...] = dot_nt(left_ref[...], whole_ref[...])


def multiply_back(left, pieces, count, name):
    rows, cols = pieces[0][2].shape
    if rows % LANES:
        whole = jnp.zeros((rows * count, cols), low_type)
        for r, first, piece in pieces:
            start = lax.bitwise_xor(lax.axis_index("wsh"), r) * rows + first
            whole = lax.dynamic_update_slice_in_dim(whole, piece, start, 0)
        return dot_nt(left, whole), whole
    me = jnp.reshape(lax.axis_index("wsh"), (1,)).astype(jnp.int32)
    spots = [(r, first) for r, first, _ in pieces]
    once = pl.Buffered(1)
    grid_spec = pltpu.PrefetchScalarGridSpec(
        num_scalar_prefetch=1,
        grid=(count,),
        in_specs=[pl.BlockSpec(left.shape, lambda j, me: (0, 0), pipeline_mode=once)]
        + [pl.BlockSpec(piece.shape, lambda j, me: (0, 0), pipeline_mode=once) for _, _, piece in pieces],
        out_specs=[
            pl.BlockSpec((left.shape[0], rows), lambda j, me: (0, lax.bitwise_xor(me[0], j))),
            pl.BlockSpec((rows, cols), lambda j, me: (lax.bitwise_xor(me[0], j), 0)),
        ],
    )
    return pl.pallas_call(
        functools.partial(back_kernel, spots),
        grid_spec=grid_spec,
        out_shape=[
            jax.ShapeDtypeStruct((left.shape[0], rows * count), full_type),
            jax.ShapeDtypeStruct((rows * count, cols), low_type),
        ],
        compiler_params=pltpu.CompilerParams(vmem_limit_bytes=VMEM_LIMIT),
        cost_estimate=pl.CostEstimate(
            flops=2 * left.shape[0] * rows * count * cols, bytes_accessed=4 * rows * count * cols, transcendentals=0
        ),
        name=name,
    )(me, left, *[piece for _, _, piece in pieces])


def sum_small(vals):
    for axis in ("wsh", "seq"):
        bit = 1
        while bit < lax.axis_size(axis):
            vals = vals + swap(vals, bit, axis)
            bit = 2 * bit
    return vals


TILE = 384
SLACK = 1


def part_orders(count):
    far = [b for b in range(count.bit_length() - 2)]
    return [far[p:] + far[:p] for p in range(len(far))]


def held(order, phase, bits):
    done = sum(1 << b for b in order[:phase])
    left = [m for m in range(1 << bits) if m & done == 0]
    bit = 1 << order[phase]
    return [m for m in left if m & bit == 0], [m for m in left if m & bit]


def reduce_kernel(counts, rights_at, lefts_ref, *refs):
    wsh_count, seq_count, starts = counts
    n_rights = len(starts)
    right_refs, out_ref = refs[:n_rights], refs[n_rights]
    (tile, stage, pair, *rest) = refs[n_rights + 1 :]
    orders = part_orders(wsh_count)
    bits = len(orders)
    lands, rest = rest[:bits], rest[bits:]
    from_left, from_right, pair_sems, far_sems, seq_sems, out_sems = rest
    chunks, blocks, rows, _ = pair.shape
    part = rows // bits
    me = lax.axis_index("wsh")
    z = lax.axis_index("seq")
    root = seq_count // 2
    MESH = pl.DeviceIdType.MESH

    barrier = pltpu.get_barrier_semaphore()
    for b in range(bits + 1):
        pl.semaphore_signal(barrier, inc=1, device_id={"wsh": lax.bitwise_xor(me, 1 << b)}, device_id_type=MESH)

    @pl.when(z > 0)
    def _():
        pl.semaphore_signal(barrier, inc=1, device_id={"seq": z - 1}, device_id_type=MESH)

    @pl.when(z < seq_count - 1)
    def _():
        pl.semaphore_signal(barrier, inc=1, device_id={"seq": z + 1}, device_id_type=MESH)

    along = jnp.where(z > 0, 1, 0) + jnp.where(z < seq_count - 1, 1, 0)
    pl.semaphore_wait(barrier, bits + 1 + along)

    def pair_copy(k):
        return pltpu.make_async_remote_copy(
            src_ref=stage.at[lax.rem(k, 2)], dst_ref=pair.at[k],
            send_sem=pair_sems.at[0, k], recv_sem=pair_sems.at[1, k],
            device_id={"wsh": lax.bitwise_xor(me, 1)}, device_id_type=MESH,
        )

    spots = []
    for q in range(bits):
        for p, order in enumerate(orders):
            for i, m in enumerate(held(order, q, bits)[1]):
                spots.append((q, p, i, m, 2 << order[q]))

    def far_copies(k, phase):
        return [
            pltpu.make_async_remote_copy(
                src_ref=pair.at[k, m, pl.ds(p * part, part)], dst_ref=lands[q].at[k, p, i],
                send_sem=far_sems.at[0, n, k], recv_sem=far_sems.at[1, n, k],
                device_id={"wsh": lax.bitwise_xor(me, bit)}, device_id_type=MESH,
            )
            for n, (q, p, i, m, bit) in enumerate(spots)
            if q == phase
        ]

    def to_right(k, source):
        return pltpu.make_async_remote_copy(
            src_ref=source, dst_ref=from_left.at[k],
            send_sem=seq_sems.at[0, k], recv_sem=seq_sems.at[1, k],
            device_id={"seq": z + 1}, device_id_type=MESH,
        )

    def to_left(k, source):
        return pltpu.make_async_remote_copy(
            src_ref=source, dst_ref=from_right.at[k],
            send_sem=seq_sems.at[2, k], recv_sem=seq_sems.at[3, k],
            device_id={"seq": z - 1}, device_id_type=MESH,
        )

    def out_copy(k, source):
        return pltpu.make_async_copy(source, out_ref.at[k], out_sems.at[k])

    def product(k, first):
        for n, (start, stop, spans) in enumerate(rights_at):
            @pl.when((k >= start) & (k < stop))
            def _():
                col = lax.rem(k - start, spans) * TILE
                tile[...] = right_refs[n][:, pl.ds(pl.multiple_of(col, LANES), TILE)]
        left_at = jnp.where(k < rights_at[0][1], 1 + k // rights_at[0][2], 0)
        half = blocks * rows
        return dot(lefts_ref[left_at, pl.ds(first * half, half), :], tile[...])

    def begin(k):
        @pl.when(k >= 2)
        def _():
            pair_copy(k - 2).wait_send()
        vals = product(k, 1)
        for b in range(blocks):
            stage[lax.rem(k, 2), b] = vals[b * rows : (b + 1) * rows].astype(low_type)
        pair_copy(k).start()

    def add_pair(k):
        vals = product(k, 0)
        pair_copy(k).wait_recv()
        for b in range(blocks):
            total = vals[b * rows : (b + 1) * rows] + pair[k, b].astype(full_type)
            pair[k, b] = total.astype(low_type)
        for copy in far_copies(k, 0):
            copy.start()

    def add_far(k, phase):
        for copy in far_copies(k, phase):
            copy.wait_recv()
        for p, order in enumerate(orders):
            at = pl.ds(p * part, part)
            for i, m in enumerate(held(order, phase, bits)[0]):
                total = pair[k, m, at].astype(full_type) + lands[phase][k, p, i].astype(full_type)
                pair[k, m, at] = total.astype(low_type)
        if phase < bits - 1:
            for copy in far_copies(k, phase + 1):
                copy.start()

    def add_to(k, land):
        pair[k, 0] = (pair[k, 0].astype(full_type) + land[k].astype(full_type)).astype(low_type)

    def seq_up(k):
        mine = pair.at[k, 0]

        @pl.when((z > 0) & (z <= root))
        def _():
            to_right(k, mine).wait_recv()
            add_to(k, from_left)

        @pl.when((z < seq_count - 1) & (z >= root))
        def _():
            to_left(k, mine).wait_recv()
            add_to(k, from_right)

        @pl.when((z < seq_count - 1) & (z <= root))
        def _():
            to_right(k, mine).start()

        @pl.when((z > 0) & (z >= root))
        def _():
            to_left(k, mine).start()

    def seq_down(k):
        @pl.when(z == root)
        def _():
            out_copy(k, pair.at[k, 0]).start()

        @pl.when(z < root)
        def _():
            to_left(k, from_right.at[k]).wait_recv()
            out_copy(k, from_right.at[k]).start()
            pl.when(z > 0)(lambda: to_left(k, from_right.at[k]).start())

        @pl.when(z > root)
        def _():
            to_right(k, from_left.at[k]).wait_recv()
            out_copy(k, from_left.at[k]).start()
            pl.when(z < seq_count - 1)(lambda: to_right(k, from_left.at[k]).start())

    far = jnp.abs(z - root)
    farthest = max(root, seq_count - 1 - root)
    stages = [(0, begin), (1, add_pair)] + [(2 + q, functools.partial(add_far, phase=q)) for q in range(bits)]
    stages += [
        (2 + bits + SLACK * (farthest - far), seq_up),
        (3 + bits + SLACK * (farthest + far), seq_down),
    ]
    depth = 4 + bits + SLACK * 2 * farthest

    def turn(s, carry):
        for offset, run in stages:
            pl.when((s >= offset) & (s < chunks + offset))(lambda run=run, offset=offset: run(s - offset))
        return carry

    lax.fori_loop(0, chunks + depth, turn, 0)

    def finish(k, carry):
        for q in range(bits):
            for copy in far_copies(k, q):
                copy.wait_send()
        pl.when(z < seq_count - 1)(lambda: to_right(k, pair.at[k, 0]).wait_send())
        pl.when(z > 0)(lambda: to_left(k, pair.at[k, 0]).wait_send())
        out_copy(k, pair.at[k, 0]).wait()
        return carry

    lax.fori_loop(0, chunks, finish, 0)
    for k in (chunks - 2, chunks - 1):
        pair_copy(k).wait_send()


def reduce_rows(lefts, out_right, gate_right, sig_right):
    wsh_count, seq_count = lax.axis_size("wsh"), lax.axis_size("seq")
    rows = D // wsh_count
    orders = part_orders(wsh_count)
    bits = len(orders)
    n_out, n_gate, n_sig = (right.shape[1] // TILE for right in (out_right, gate_right, sig_right))
    groups = lefts.shape[0] - 1
    starts = [0, groups * n_out, groups * n_out + n_gate]
    chunks = starts[2] + n_sig
    rights_at = [(0, starts[1], n_out), (starts[1], starts[2], n_gate), (starts[2], chunks, n_sig)]
    low = lambda *shape: pltpu.VMEM(shape, low_type)
    dma = pltpu.SemaphoreType.DMA
    copies = bits * ((1 << bits) - 1)
    vmem = pl.BlockSpec(memory_space=pltpu.VMEM)
    return pl.pallas_call(
        functools.partial(reduce_kernel, (wsh_count, seq_count, starts), rights_at),
        in_specs=[vmem] * 4,
        out_specs=pl.BlockSpec(memory_space=pl.ANY),
        out_shape=jax.ShapeDtypeStruct((chunks, rows, TILE), low_type),
        scratch_shapes=[
            low(out_right.shape[0], TILE),
            low(2, 1 << bits, rows, TILE),
            low(chunks, 1 << bits, rows, TILE),
            *[low(chunks, bits, 1 << (bits - 1 - q), rows // bits, TILE) for q in range(bits)],
            low(chunks, rows, TILE),
            low(chunks, rows, TILE),
            dma((2, chunks)),
            dma((2, copies, chunks)),
            dma((4, chunks)),
            dma((chunks,)),
        ],
        compiler_params=pltpu.CompilerParams(
            collective_id=0, has_side_effects=True, vmem_limit_bytes=60 * 1024 * 1024
        ),
        cost_estimate=pl.CostEstimate(flops=10**11, bytes_accessed=20 * 10**6, transcendentals=0),
        name="reduce_gradients",
    )(lefts, out_right, gate_right, sig_right)


def adam_kernel(start, rate, decay, *refs):
    share_ref, weight_ref, first_ref, second_ref, grad_ref, next_ref, next_first_ref, next_second_ref = refs
    grad = share_ref[0].astype(full_type)
    grad_ref[...] = grad
    next_ref[...], next_first_ref[...], next_second_ref[...] = adam_update(
        weight_ref[...], grad, first_ref[...], second_ref[...], rate, decay
    )


def adam_chunks(sums, start, weights, first_moment, second_moment, rate, decay, name):
    all_rows, cols = weights.shape
    rows = sums.shape[1]
    tiles = pl.cdiv(cols, TILE)
    block = pl.BlockSpec((rows, TILE), lambda i, j: (i, j))
    return pl.pallas_call(
        functools.partial(adam_kernel, start, rate, decay),
        grid=(all_rows // rows, tiles),
        in_specs=[pl.BlockSpec((1, rows, TILE), lambda i, j: (start + i * tiles + j, 0, 0))] + [block] * 3,
        out_specs=[block] * 4,
        out_shape=[jax.ShapeDtypeStruct(weights.shape, full_type)] * 4,
        compiler_params=pltpu.CompilerParams(vmem_limit_bytes=VMEM_LIMIT),
        cost_estimate=pl.CostEstimate(
            flops=20 * weights.size, bytes_accessed=30 * weights.size, transcendentals=weights.size
        ),
        name=name,
    )(sums, weights, first_moment, second_moment)


def relative_rows(vals, count, groups):
    size = vals.shape[1] // (count * groups)
    me = lax.axis_index("wsh")
    order = [r for r in range(count) if r % 2 == 0] + [r for r in range(count) if r % 2 == 1]
    turned = vals.T
    parts = [
        lax.dynamic_slice_in_dim(turned, (lax.bitwise_xor(me, r) * groups + g) * size, size, 0)
        for g in range(groups)
        for r in order
    ]
    return jnp.concatenate(parts, axis=0).reshape(groups, count * size, vals.shape[0])


def after(vals, *others):
    return lax.optimization_barrier((vals,) + others)[0]


def shift(vals, by):
    count = lax.axis_size("seq")
    pairs = [(i, i + by) for i in range(count) if 0 <= i + by < count]
    return lax.ppermute(vals, "seq", pairs)


def carry_states(own, fades, sign):
    count = lax.axis_size("seq")
    span, span_fade = own, fades
    result, fade = None, jnp.zeros_like(fades)
    reach = 1
    while reach < count:
        got, got_fade = shift(span, sign * reach), shift(span_fade, sign * reach)
        if result is None:
            result = got
        else:
            result = (result.astype(full_type) + jnp.exp2(fade)[None, :] * got.astype(full_type)).astype(low_type)
        span = (span.astype(full_type) + jnp.exp2(span_fade)[None, :] * got.astype(full_type)).astype(low_type)
        fade, span_fade = fade + got_fade, span_fade + got_fade
        reach = 2 * reach
    return result


def shards(
    inputs, cotangent, w_in, w_dt, w_out, gain_pre, gain_norm, conv_param, head_param,
    first_w_in, second_w_in, first_w_dt, second_w_dt, first_w_out, second_w_out,
    first_gain_pre, second_gain_pre, first_gain_norm, second_gain_norm,
    first_conv, second_conv, first_head, second_head,
):
    wsh_count = lax.axis_size("wsh")
    seq_count = lax.axis_size("seq")
    seq_index = lax.axis_index("seq")
    wsh_index = lax.axis_index("wsh")
    rows_model = D // wsh_count
    rows_inner = INNER // wsh_count
    cols_conv = CONV_CH // wsh_count
    cols_head = HEADS // wsh_count
    flat = jnp.concatenate(
        [gain_pre, gain_norm, conv_param.reshape(-1), head_param.reshape(-1)]
    ).astype(low_type)
    count = flat.shape[0]
    flat = jnp.pad(flat, (0, -count % LANES))
    part_sig = jnp.concatenate(
        [w_in[:, INNER:].astype(low_type), w_dt.astype(low_type), jnp.zeros((rows_model, LANES - HEADS), low_type)],
        axis=1,
    )
    small = lax.all_gather(flat, "wsh", axis=0)
    part_sig = after(part_sig, small)
    sig_pieces, marks = gather_pieces(part_sig, wsh_count)
    gate_pieces, marks = gather_pieces(after(w_in[:, :INNER].astype(low_type), *marks), wsh_count)
    out_pieces, marks = gather_pieces(after(w_out.astype(low_type), *marks), wsh_count)
    small = small.astype(full_type)
    ends = [rows_model, rows_model + rows_inner, rows_model + rows_inner + 5 * cols_conv]
    gain_in = small[:, : ends[0]].reshape(-1)
    gain_out = small[:, ends[0] : ends[1]].reshape(1, -1)
    conv = small[:, ends[1] : ends[2]].reshape(wsh_count, 5, cols_conv).transpose(1, 0, 2).reshape(5, CONV_CH)
    head = small[:, ends[2] : ends[2] + 3 * cols_head].reshape(wsh_count, 3, cols_head)
    head = head.transpose(1, 0, 2).reshape(3, HEADS)
    conv = pad_rows(conv, 8)
    head = jnp.pad(head, ((0, 5), (0, LANES - HEADS)))
    tokens_low = inputs[0]
    cot_low = cotangent[0]
    rows = tokens_low.shape[0]
    before = lax.ppermute(tokens_low[rows - HALO :], "seq", [(i, i + 1) for i in range(seq_count - 1)])
    tokens = jnp.concatenate([before, tokens_low], axis=0).astype(full_type)
    inv_rms = lax.rsqrt(jnp.mean(tokens * tokens, axis=-1, keepdims=True) + norm_eps)
    normed_all = (tokens * inv_rms * gain_in).astype(low_type)
    packed, full_sig = multiply_pieces(normed_all, sig_pieces, wsh_count, low_type, "project_signal")
    tokens = tokens[HALO:]
    inv_rms = inv_rms[HALO:]
    normed = normed_all[HALO:]
    x, bc, run, lag, run_t, lag_t, enter, enter_all, tail, offs, states, send = run_states(packed, conv, head)
    fades = send[STATE].astype(full_type) + send[STATE + 1].astype(full_type)
    state_in = carry_states(send[:STATE], fades, 1)
    y = run_outputs(x, bc, run, lag_t, enter, states, head)
    gate_vals, full_gate = multiply_pieces(normed, gate_pieces, wsh_count, full_type, "project_gate")
    back, full_out = multiply_back(cot_low, out_pieces, wsh_count, "project_back")
    gain_rows = jnp.broadcast_to(gain_out, (8, INNER))
    normed_out, grad_y, grad_gate, part_gnorm, grad_state = run_norm(
        y, gate_vals, back, gain_rows, bc, enter_all, state_in
    )
    grad_in = carry_states(grad_state.astype(low_type), fades, -1)
    block_out = (tokens + dot(normed_out, full_out)).astype(low_type)[None]
    grad_normed = dot_nt(grad_gate, full_gate)
    grad_pack, edge, last, part_conv, part_skip, part_head = run_backward(
        packed, conv, head, grad_y, bc, lag, run_t, enter, tail, offs, states, state_in, grad_in
    )
    edge_next = lax.ppermute(edge, "seq", [(i, i - 1) for i in range(1, seq_count)])
    fixed = jnp.concatenate([last[:8], last[8:] + edge_next], axis=0).astype(low_type)
    grad_pack = lax.dynamic_update_slice(grad_pack, fixed, (rows - 16, 0))
    grad_normed = grad_normed + dot_nt(grad_pack, full_sig)
    scaled = tokens * inv_rms
    part_gpre = jnp.sum(grad_normed * scaled, axis=0)
    pulled = grad_normed * gain_in
    grad_tokens = inv_rms * (pulled - scaled * jnp.mean(pulled * scaled, axis=-1, keepdims=True))
    input_grad = (cot_low.astype(full_type) + grad_tokens)[None]
    skip_sums = part_skip[0].reshape(HEADS, HEAD_DIM).sum(axis=1)
    small_parts = [
        part_gpre, part_gnorm[0], part_conv[:5].reshape(-1), part_head[0, :HEADS], part_head[1, :HEADS], skip_sums
    ]
    small_sums = sum_small(jnp.concatenate(small_parts))
    cuts = [D, D + INNER, D + INNER + 5 * CONV_CH]
    grad_gpre = lax.dynamic_slice_in_dim(small_sums[: cuts[0]], wsh_index * rows_model, rows_model, 0)
    grad_gnorm = lax.dynamic_slice_in_dim(small_sums[cuts[0] : cuts[1]], wsh_index * rows_inner, rows_inner, 0)
    grad_conv = lax.dynamic_slice_in_dim(
        small_sums[cuts[1] : cuts[2]].reshape(5, CONV_CH), wsh_index * cols_conv, cols_conv, 1
    )
    grad_head = lax.dynamic_slice_in_dim(
        small_sums[cuts[2] :].reshape(3, HEADS), wsh_index * cols_head, cols_head, 1
    )
    lefts = jnp.concatenate(
        [relative_rows(normed, wsh_count, 1), relative_rows(normed_out, wsh_count, INNER // D)], axis=0
    )
    sums = reduce_rows(lefts, cot_low, grad_gate, grad_pack)
    tiles_out = (INNER // D) * (D // TILE)
    grad_out, *new_out = adam_chunks(sums, 0, w_out, first_w_out, second_w_out, rate_matrix, weight_decay, "adam_w_out")
    grad_in_w, *new_in = adam_chunks(
        sums, tiles_out, w_in, first_w_in, second_w_in, rate_matrix, weight_decay, "adam_w_in"
    )
    at_dt = CONV_CH % TILE
    grad_dt = sums[-1, :, at_dt : at_dt + HEADS].astype(full_type)
    params = (w_in, w_dt, w_out, gain_pre, gain_norm, conv_param, head_param)
    gradients = (grad_in_w, grad_dt, grad_out, grad_gpre, grad_gnorm, grad_conv, grad_head)
    firsts = (first_w_in, first_w_dt, first_w_out, first_gain_pre, first_gain_norm, first_conv, first_head)
    seconds = (second_w_in, second_w_dt, second_w_out, second_gain_pre, second_gain_norm, second_conv, second_head)
    step_rates = (rate_matrix, rate_matrix, rate_matrix, rate_gain, rate_gain, rate_conv, rate_head)
    decays = (weight_decay, weight_decay, weight_decay, 0.0, 0.0, 0.0, 0.0)
    updated = [
        None if i in (0, 2) else adam_update(*items)
        for i, items in enumerate(zip(params, gradients, firsts, seconds, step_rates, decays))
    ]
    updated[0], updated[2] = new_in, new_out
    new_params = tuple(entry[0] for entry in updated)
    moments = []
    for entry in updated:
        moments.append(entry[1])
        moments.append(entry[2])
    return (block_out, input_grad) + gradients + new_params + tuple(moments)


def solution(mesh):
    rows, vec, cols = P("wsh", None), P("wsh"), P(None, "wsh")
    tokens = P("wsh", "seq", None)
    params = (rows, rows, rows, vec, vec, cols, cols)
    moments = tuple(spec for spec in params for _ in range(2))
    in_specs = (tokens, tokens) + params + moments
    out_specs = (tokens, tokens) + params + params + moments
    return jax.shard_map(shards, mesh=mesh, in_specs=in_specs, out_specs=out_specs, check_vma=False)
```

```python
import functools

import jax
import jax.numpy as jnp
from jax import lax
from jax.experimental import pallas as pl
from jax.experimental.pallas import tpu as pltpu
from jax.sharding import PartitionSpec as P

D = 1536
HEADS = 48
HEAD_DIM = 64
STATE = 128
CONV_WIDTH = 4
STEP = 2
INNER = 3072
CONV_CH = 3328
BLOCK = 128
LANES = 128
WIDE = 256
HALO = 16
GROUPS = INNER // WIDE
CHAIN_LAG = 2
AHEAD = 6
PACK = CONV_CH + LANES
LOG2E = 1.4426950408889634
VMEM_LIMIT = 56 * 1024 * 1024

norm_eps = 1e-05
beta_one = 0.9
beta_two = 0.999
adam_eps = 1e-08
rate_matrix = 0.01
rate_gain = 0.4
rate_conv = 0.1
rate_head = 1.0
weight_decay = 0.1
highest = lax.Precision.HIGHEST
low_type = jnp.bfloat16
full_type = jnp.float32


def dot(left_side, right_side, dims=((1,), (0,)), precision=None):
    return lax.dot_general(
        left_side, right_side, (dims, ((), ())), precision=precision, preferred_element_type=full_type
    )


def dot_nt(left_side, right_side):
    return dot(left_side, right_side, ((1,), (1,)))


def sigmoid(vals):
    return 0.5 * jnp.tanh(0.5 * vals) + 0.5


def lane_ids(shape):
    return lax.broadcasted_iota(jnp.int32, shape, len(shape) - 1)


def widen(vals, first=0):
    left = lane_ids((vals.shape[0], LANES)) < HEAD_DIM
    pairs = [
        jnp.where(left, vals[:, first + i : first + i + 1], vals[:, first + i + 1 : first + i + 2])
        for i in (0, 2)
    ]
    return jnp.concatenate(pairs, axis=1)


def to_front(vals, step):
    return pltpu.roll(vals, lax.rem(LANES - 4 * step, LANES), 1)


def head_rows(ref, step):
    eight = ref[pl.ds(pl.multiple_of(8 * (step // 2), 8), 8), :]
    return pltpu.roll(eight, 4 * lax.rem(step, 2), 0)


def step_terms(raw, head):
    shifted = raw + head[1:2]
    small = jnp.exp(-jnp.abs(shifted))
    log_part = jnp.where(
        small < 0.01, small * (1.0 - small * (0.5 - small * (1.0 / 3.0))), jnp.log(1.0 + small)
    )
    step_sizes = jnp.maximum(shifted, 0.0) + log_part
    slope = jnp.where(shifted >= 0.0, 1.0, small) / (1.0 + small)
    return step_sizes, slope, -jnp.exp(head[0:1])


def convolve(sig, conv, rows):
    total = conv[4:5] + conv[0:1] * sig[HALO - 3 : HALO - 3 + rows, :]
    for k in range(1, CONV_WIDTH):
        total = total + conv[k : k + 1] * sig[HALO - 3 + k : HALO - 3 + k + rows, :]
    return total


def triangle(lower):
    rows = lax.broadcasted_iota(jnp.int32, (BLOCK, BLOCK), 0)
    cols = lax.broadcasted_iota(jnp.int32, (BLOCK, BLOCK), 1)
    return rows >= cols if lower else rows <= cols


def greet_along():
    z = lax.axis_index("seq")
    seq_count = lax.axis_size("seq")
    barrier = pltpu.get_barrier_semaphore()

    @pl.when(z > 0)
    def _():
        pl.semaphore_signal(barrier, inc=1, device_id={"seq": z - 1}, device_id_type=pl.DeviceIdType.MESH)

    @pl.when(z < seq_count - 1)
    def _():
        pl.semaphore_signal(barrier, inc=1, device_id={"seq": z + 1}, device_id_type=pl.DeviceIdType.MESH)

    pl.semaphore_wait(barrier, jnp.where(z > 0, 1, 0) + jnp.where(z < seq_count - 1, 1, 0))


def states_kernel(
    sig_ref, maps_ref, raw_ref, conv_ref, conv_maps_ref, head_ref,
    x_ref, bc_ref, run_ref, lag_ref, run_t_ref, lag_t_ref, enter_ref, enter_all_ref, tail_ref, offs_ref,
    states_ref, before_ref,
    sig, in_t, ends, stage, land, sems,
):
    step = pl.program_id(0)
    rows = x_ref.shape[0]
    blocks = rows // BLOCK
    z = lax.axis_index("seq")
    seq_count = lax.axis_size("seq")

    def to_next(k):
        return pltpu.make_async_remote_copy(
            src_ref=stage.at[k], dst_ref=land.at[k], send_sem=sems.at[0, k], recv_sem=sems.at[1, k],
            device_id={"seq": z + 1}, device_id_type=pl.DeviceIdType.MESH,
        )

    @pl.when(step == 0)
    def _():
        greet_along()
        sig[...] = maps_ref[...].astype(full_type)
        pre = convolve(sig, conv_maps_ref[...], rows)
        maps = pre * sigmoid(pre)
        bc_ref[...] = maps
        in_t[...] = maps[:, :STATE].T.astype(low_type)
        step_sizes, _, rate = step_terms(raw_ref[HALO:, :].astype(full_type), head_ref[...])
        rates = step_sizes * rate * LOG2E
        log_steps = jnp.log2(step_sizes)
        lower = jnp.where(triangle(True), 1.0, 0.0)
        offset = jnp.zeros((1, LANES), full_type)
        offs_ref[...] = jnp.zeros(offs_ref.shape, full_type)
        for c in range(blocks):
            at = slice(c * BLOCK, (c + 1) * BLOCK)
            run = dot(lower, rates[at], precision=highest)
            lag = run - log_steps[at]
            run_ref[at, :] = run
            lag_ref[at, :] = lag
            run_t_ref[:, at] = run.T
            lag_t_ref[:, at] = lag.T
            enter_ref[at, :] = jnp.exp2(run)
            enter_all_ref[at, :] = jnp.exp2(run + offset)
            tail_ref[at, :] = jnp.exp2(run[BLOCK - 1 : BLOCK] - lag)
            offs_ref[c : c + 1, :] = offset
            offset = offset + run[BLOCK - 1 : BLOCK]
        offs_ref[blocks : blocks + 1, :] = offset

    @pl.when(step < GROUPS)
    def _():
        sig[...] = sig_ref[...].astype(full_type)
        pre = convolve(sig, conv_ref[...], rows)
        x = pre * sigmoid(pre)
        x_ref[...] = x
        tail = to_front(tail_ref[...], step)
        last = to_front(offs_ref[...], step)
        state = jnp.zeros((STATE, WIDE), full_type)
        for c in range(blocks):
            at = slice(c * BLOCK, (c + 1) * BLOCK)
            weighted = (x[at] * widen(tail[at])).astype(low_type)
            fade = jnp.exp2(widen(last[c + 1 : c + 2] - last[c : c + 1]))
            state = state * fade + dot(in_t[:, at], weighted)
            states_ref[c] = state.astype(low_type)
        ends[step] = state

    @pl.when(step >= CHAIN_LAG)
    def _():
        k = step - CHAIN_LAG

        @pl.when(z == 0)
        def _():
            land[k] = jnp.zeros((STATE, WIDE), low_type)

        @pl.when(z > 0)
        def _():
            to_next(k).wait_recv()

        before_ref[...] = land[k]

        @pl.when(z < seq_count - 1)
        def _():
            fade = jnp.exp2(widen(to_front(offs_ref[...], k)[blocks : blocks + 1]))
            stage[k] = (ends[k] + fade * land[k].astype(full_type)).astype(low_type)
            to_next(k).start()

    @pl.when((step == GROUPS + CHAIN_LAG - 1) & (z < seq_count - 1))
    def _():
        for k in range(GROUPS):
            to_next(k).wait_send()


def outputs_kernel(x_ref, bc_ref, run_ref, lag_t_ref, enter_ref, states_ref, head_ref, y_ref, inter):
    step = pl.program_id(0)
    rows = x_ref.shape[0]
    blocks = rows // BLOCK
    lower = triangle(True)

    @pl.when(step == 0)
    def _():
        for c in range(blocks):
            at = slice(c * BLOCK, (c + 1) * BLOCK)
            maps = bc_ref[at, :].astype(low_type)
            inter[c] = dot_nt(maps[:, STATE:], maps[:, :STATE])

    run = to_front(run_ref[...], step)
    enter = to_front(enter_ref[...], step)
    lag_rows = head_rows(lag_t_ref, step)
    skip = widen(to_front(head_ref[...], step)[2:3])
    left = lane_ids((BLOCK, LANES)) < HEAD_DIM
    for c in range(blocks):
        at = slice(c * BLOCK, (c + 1) * BLOCK)
        x = x_ref[at, :]
        parts = []
        for pair in range(2):
            mixes = []
            for i in range(2):
                h = 2 * pair + i
                lag_row = lag_rows[h : h + 1, at]
                power = jnp.where(lower, run[at, h : h + 1] - lag_row, -1e30)
                mixes.append((jnp.exp2(power) * inter[c]).astype(low_type))
            half = x[:, pair * LANES : (pair + 1) * LANES].astype(low_type)
            zero = jnp.zeros_like(half)
            stacked = jnp.concatenate([jnp.where(left, half, zero), jnp.where(left, zero, half)], axis=0)
            parts.append(dot(jnp.concatenate(mixes, axis=1), stacked))
        y = jnp.concatenate(parts, axis=1) + skip * x
        if c > 0:
            out_map = bc_ref[at, STATE:].astype(low_type)
            y = y + widen(enter[at]) * dot(out_map, states_ref[c - 1])
        y_ref[at, :] = y


def norm_kernel(
    y_ref, gate_ref, back_ref, gain_ref, bc_ref, enter_ref, state_ref,
    normed_ref, normed_t_ref, grad_y_ref, grad_gate_ref, grad_gain_ref, grad_state_ref,
    gated, low_y,
):
    step = pl.program_id(0)
    rows = y_ref.shape[0]

    @pl.when(step == 0)
    def _():
        grad_gain_ref[...] = jnp.zeros(grad_gain_ref.shape, full_type)
        grad_state_ref[...] = jnp.zeros(grad_state_ref.shape, full_type)

    out_map = bc_ref[:, STATE:]
    out_low = out_map.astype(low_type)
    out_t = out_map.T.astype(low_type)
    squares = jnp.zeros((rows, WIDE), full_type)
    cross = jnp.zeros((rows, WIDE), full_type)
    for j in range(GROUPS):
        at = slice(j * WIDE, (j + 1) * WIDE)
        enter = widen(enter_ref[...], 4 * j)
        y = y_ref[:, at] + enter * dot(out_low, state_ref[:, at])
        y_low = y.astype(low_type)
        low_y[:, at] = y_low
        gate = gate_ref[:, at]
        vals = y_low.astype(full_type) * (gate * sigmoid(gate))
        gated[:, at] = vals
        squares = squares + vals * vals
        cross = cross + vals * (back_ref[:, at] * gain_ref[0:1, at])
    inv = lax.rsqrt(jnp.sum(squares, axis=1, keepdims=True) * (1.0 / INNER) + norm_eps)
    pull = inv * inv * inv * (jnp.sum(cross, axis=1, keepdims=True) * (1.0 / INNER))
    for j in range(GROUPS):
        at = slice(j * WIDE, (j + 1) * WIDE)
        gain = gain_ref[0:1, at]
        back = back_ref[:, at]
        vals = gated[:, at]
        scaled = vals * inv
        normed = (scaled * gain).astype(low_type)
        normed_ref[:, at] = normed
        normed_t_ref[at, :] = normed.T
        grad_gain_ref[0:1, at] += jnp.sum(back * scaled, axis=0, keepdims=True)
        grad_vals = back * gain * inv - vals * pull
        gate = gate_ref[:, at]
        sig = sigmoid(gate)
        silu = gate * sig
        grad_y = (grad_vals * silu).astype(low_type)
        grad_y_ref[:, at] = grad_y
        slope = sig + silu * (1.0 - sig)
        grad_gate_ref[:, at] = (grad_vals * low_y[:, at].astype(full_type) * slope).astype(low_type)
        enter = widen(enter_ref[...], 4 * j)
        grad_state_ref[:, at] += dot(out_t, (grad_y.astype(full_type) * enter).astype(low_type))


def backward_kernel(
    counts, spans, left_rows,
    sig_ref, raw_ref, conv_ref, head_ref, grad_y_ref, bc_ref,
    lag_ref, run_t_ref, enter_ref, tail_ref, offs_ref, states_ref, state_in_ref, grad_state_ref,
    lefts_ref, cot_ref, grad_gate_ref,
    grad_sig_ref, edge_ref, last_ref, grad_conv_ref, grad_skip_ref, grad_head_ref, sums_ref,
    sig, padded, inter, grad_inter, grad_maps, out_t, run_rows, run_cols, run_ends, weighs,
    stage, land, chain_sems, *scratch,
):
    step = pl.program_id(0) - AHEAD
    rows = grad_y_ref.shape[0]
    blocks = rows // BLOCK
    z = lax.axis_index("seq")
    seq_count = counts[1]
    turns, turn, finish = reduce_turns(
        *counts, spans, [lefts_ref, *left_rows], [cot_ref, grad_gate_ref], sums_ref, scratch
    )
    place = step + AHEAD
    steps = GROUPS + 2 + AHEAD

    def to_previous(k):
        return pltpu.make_async_remote_copy(
            src_ref=stage.at[k], dst_ref=land.at[k], send_sem=chain_sems.at[0, k], recv_sem=chain_sems.at[1, k],
            device_id={"seq": z - 1}, device_id_type=pl.DeviceIdType.MESH,
        )

    def chain(k):
        @pl.when(z == seq_count - 1)
        def _():
            land[k] = jnp.zeros((STATE, WIDE), low_type)

        @pl.when(z < seq_count - 1)
        def _():
            to_previous(k).wait_recv()

        @pl.when(z > 0)
        def _():
            fade = jnp.exp2(widen(to_front(offs_ref[...], k)[blocks : blocks + 1]))
            own = grad_state_ref[:, pl.ds(pl.multiple_of(k * WIDE, WIDE), WIDE)]
            stage[k] = (own + fade * land[k].astype(full_type)).astype(low_type)
            to_previous(k).start()

    @pl.when(place == 0)
    def _():
        greet()

    lax.fori_loop(place * turns // steps, (place + 1) * turns // steps, turn, 0)
    upper = triangle(False)

    @pl.when(place < AHEAD)
    def _():
        for i in range(GROUPS // AHEAD):
            chain(place * (GROUPS // AHEAD) + i)

    @pl.when(place == steps - 1)
    def _():
        finish()

        @pl.when(z > 0)
        def _():
            for k in range(GROUPS):
                to_previous(k).wait_send()

    @pl.when(step == 0)
    def _():
        for c in range(blocks):
            at = slice(c * BLOCK, (c + 1) * BLOCK)
            maps = bc_ref[at, :].astype(low_type)
            inter[c] = dot_nt(maps[:, :STATE], maps[:, STATE:])
            out_t[:, at] = bc_ref[at, STATE:].T.astype(low_type)
        grad_inter[...] = jnp.zeros(grad_inter.shape, full_type)
        grad_maps[...] = jnp.zeros(grad_maps.shape, full_type)
        run_rows[...] = jnp.zeros(run_rows.shape, full_type)
        run_cols[...] = jnp.zeros(run_cols.shape, full_type)
        run_ends[...] = jnp.zeros(run_ends.shape, full_type)
        weighs[...] = jnp.zeros(weighs.shape, full_type)
        padded[...] = jnp.zeros(padded.shape, full_type)

    def conv_back(grad_pre):
        conv = conv_ref[...]
        grad_sig = conv[3:4] * padded[HALO : HALO + rows, :]
        edge = conv[3:4] * padded[8:HALO, :]
        for k in range(3):
            grad_sig = grad_sig + conv[k : k + 1] * padded[HALO + 3 - k : HALO + 3 - k + rows, :]
            edge = edge + conv[k : k + 1] * padded[11 - k : 19 - k, :]
        grad_sig_ref[...] = grad_sig.astype(low_type)
        edge_ref[...] = edge
        last_ref[...] = grad_sig[rows - 16 :]
        sums = [
            jnp.sum(grad_pre * sig[HALO - 3 + k : HALO - 3 + k + rows, :], axis=0, keepdims=True)
            for k in range(CONV_WIDTH)
        ]
        sums.append(jnp.sum(grad_pre, axis=0, keepdims=True))
        sums.append(jnp.zeros((3, WIDE), full_type))
        grad_conv_ref[...] = jnp.concatenate(sums, axis=0)

    @pl.when((step >= 0) & (step < GROUPS))
    def _():
        sig[...] = sig_ref[...].astype(full_type)
        lag = to_front(lag_ref[...], step)
        run_all = head_rows(run_t_ref, step)
        enter = to_front(enter_ref[...], step)
        tail = to_front(tail_ref[...], step)
        offs = to_front(offs_ref[...], step)
        skip = widen(to_front(head_ref[...], step)[2:3])
        left = lane_ids((BLOCK, LANES)) < HEAD_DIM
        heads_of = lax.broadcasted_iota(jnp.int32, (WIDE, LANES), 0) // HEAD_DIM + 4 * step
        picks = jnp.where(heads_of == lane_ids((WIDE, LANES)), 1.0, 0.0).astype(low_type)
        state_in = state_in_ref[...].astype(full_type)
        grad_state = land[step].astype(full_type)
        grad_skip = jnp.zeros((1, WIDE), full_type)
        pre_all = convolve(sig, conv_ref[...], rows)

        def head_sums(vals):
            high = vals.astype(low_type)
            rest = (vals - high.astype(full_type)).astype(low_type)
            return dot(high, picks) + dot(rest, picks)

        for c in reversed(range(blocks)):
            at = slice(c * BLOCK, (c + 1) * BLOCK)
            pre = pre_all[at]
            gate = sigmoid(pre)
            x = pre * gate
            x_low = x.astype(low_type)
            x_round = x_low.astype(full_type)
            grad_y = grad_y_ref[at, :]
            grad_y_full = grad_y.astype(full_type)
            in_map = bc_ref[at, :STATE].astype(low_type)
            out_map = bc_ref[at, STATE:].astype(low_type)
            tail_c = widen(tail[at])
            enter_c = widen(enter[at])
            entering = state_in * jnp.exp2(widen(offs[c : c + 1]))
            if c > 0:
                entering = entering + states_ref[c - 1].astype(full_type)
            leaving = states_ref[c].astype(full_type) + state_in * jnp.exp2(widen(offs[c + 1 : c + 2]))
            entering_low = entering.astype(low_type)
            grad_low = grad_state.astype(low_type)
            ends = jnp.sum(grad_state * leaving, axis=0, keepdims=True)
            run_ends[c : c + 1, :] += head_sums(jnp.concatenate([ends, jnp.zeros((7, WIDE), full_type)], axis=0))[0:1]
            grad_x = tail_c * dot(in_map, grad_low)
            grad_maps[at, :STATE] += dot_nt((x * tail_c).astype(low_type), grad_low)
            swept = grad_y_full * enter_c
            swept_low = swept.astype(low_type)
            through = swept * dot(out_map, entering_low)
            grad_maps[at, STATE:] += dot_nt(swept_low, entering_low)
            fade = jnp.exp2(widen(offs[c + 1 : c + 2] - offs[c : c + 1]))
            grad_state = grad_state * fade + dot(out_t[:, at], swept_low)
            parts = []
            sums = []
            for pair in range(2):
                half = slice(pair * LANES, (pair + 1) * LANES)
                grad_half = grad_y[:, half]
                zero = jnp.zeros_like(grad_half)
                stacked = jnp.concatenate(
                    [jnp.where(left, grad_half, zero), jnp.where(left, zero, grad_half)], axis=0
                )
                cross = dot_nt(x_low[:, half], stacked)
                mixes = []
                for i in range(2):
                    h = 2 * pair + i
                    run_row = run_all[h : h + 1, at]
                    power = jnp.where(upper, run_row - lag[at, h : h + 1], -1e30)
                    decay = jnp.exp2(power)
                    mix = (decay * inter[c]).astype(low_type)
                    mixes.append(mix)
                    cross_h = cross[:, i * LANES : (i + 1) * LANES]
                    grad_inter[c] += cross_h * decay
                    sums.append(jnp.sum(cross_h * mix.astype(full_type), axis=0, keepdims=True))
                parts.append(dot(jnp.concatenate(mixes, axis=1), stacked))
            sums.append(jnp.zeros((4, BLOCK), full_type))
            run_rows[pl.ds(pl.multiple_of(8 * step, 8), 8), at] = jnp.concatenate(sums, axis=0)
            grad_x = grad_x + jnp.concatenate(parts, axis=1)
            weigh = head_sums(x_round * grad_x)
            weighs[at, :] += weigh
            run_cols[at, :] += head_sums(through) - weigh
            grad_skip = grad_skip + jnp.sum(grad_y_full * x, axis=0, keepdims=True)
            grad_x = grad_x + skip * grad_y_full
            padded[HALO + c * BLOCK : HALO + (c + 1) * BLOCK, :] = grad_x * (gate + x * (1.0 - gate))
        grad_skip_ref[...] = jnp.broadcast_to(grad_skip, grad_skip_ref.shape)
        conv_back(padded[HALO : HALO + rows, :])

    @pl.when(step == GROUPS)
    def _():
        sig[...] = sig_ref[...].astype(full_type)
        pre_all = convolve(sig, conv_ref[...], rows)
        for c in range(blocks):
            at = slice(c * BLOCK, (c + 1) * BLOCK)
            maps = bc_ref[at, :].astype(low_type)
            grad_block = grad_inter[c]
            grad_bc = grad_maps[at, :] + jnp.concatenate(
                [
                    dot(grad_block.astype(low_type), maps[:, STATE:]),
                    dot(grad_block.T.astype(low_type), maps[:, :STATE]),
                ],
                axis=1,
            )
            pre = pre_all[at]
            gate = sigmoid(pre)
            padded[HALO + c * BLOCK : HALO + (c + 1) * BLOCK, :] = grad_bc * (gate + pre * gate * (1.0 - gate))
        conv_back(padded[HALO : HALO + rows, :])

    @pl.when(step == GROUPS + 1)
    def _():
        head = head_ref[...]
        step_sizes, slope, rate = step_terms(raw_ref[HALO:, :].astype(full_type), head)
        ratio = jnp.where(step_sizes > 1e-30, slope / jnp.maximum(step_sizes, 1e-30), 1.0)
        used = lane_ids((BLOCK, LANES)) < HEADS
        later = jnp.where(upper, 1.0, 0.0)
        rate_sum = jnp.zeros((1, LANES), full_type)
        bias_sum = jnp.zeros((1, LANES), full_type)
        for c in range(blocks):
            at = slice(c * BLOCK, (c + 1) * BLOCK)
            by_head = [run_rows[8 * j : 8 * j + 4, at] for j in range(GROUPS)]
            by_head.append(jnp.zeros((LANES - HEADS, BLOCK), full_type))
            grad_run = jnp.concatenate(by_head, axis=0).T + run_cols[at, :]
            grad_rates = dot(later, grad_run, precision=highest) + run_ends[c : c + 1, :]
            grad_raw = slope[at] * rate * grad_rates + ratio[at] * weighs[at, :]
            grad_raw = jnp.where(used, grad_raw, 0.0)
            grad_sig_ref[at, :LANES] = grad_raw.astype(low_type)
            grad_sig_ref[at, LANES:] = jnp.zeros((BLOCK, LANES), low_type)
            rate_sum = rate_sum + jnp.sum(grad_rates * step_sizes[at], axis=0, keepdims=True)
            bias_sum = bias_sum + jnp.sum(grad_raw, axis=0, keepdims=True)
        grad_head_ref[...] = jnp.concatenate(
            [rate_sum * rate, bias_sum, jnp.zeros((6, LANES), full_type)], axis=0
        )


def run_states(packed, conv, head):
    rows = packed.shape[0] - HALO
    blocks = rows // BLOCK
    last = lambda j: jnp.minimum(j, GROUPS - 1)
    whole = lambda shape: pl.BlockSpec(shape, lambda j: (0,) * len(shape))
    small = jax.ShapeDtypeStruct((rows, LANES), full_type)
    small_t = jax.ShapeDtypeStruct((LANES, rows), full_type)
    return pl.pallas_call(
        states_kernel,
        grid=(GROUPS + CHAIN_LAG,),
        in_specs=[
            pl.BlockSpec((rows + HALO, WIDE), lambda j: (0, last(j))),
            pl.BlockSpec((rows + HALO, WIDE), lambda j: (0, GROUPS)),
            pl.BlockSpec((rows + HALO, LANES), lambda j: (0, CONV_CH // LANES)),
            pl.BlockSpec((8, WIDE), lambda j: (0, last(j))),
            pl.BlockSpec((8, WIDE), lambda j: (0, GROUPS)),
            whole((8, LANES)),
        ],
        out_specs=[
            pl.BlockSpec((rows, WIDE), lambda j: (0, last(j))),
            whole((rows, WIDE)),
            whole((rows, LANES)),
            whole((rows, LANES)),
            whole((LANES, rows)),
            whole((LANES, rows)),
            whole((rows, LANES)),
            whole((rows, LANES)),
            whole((rows, LANES)),
            whole((16, LANES)),
            pl.BlockSpec((blocks, STATE, WIDE), lambda j: (0, 0, last(j))),
            pl.BlockSpec((STATE, WIDE), lambda j: (0, jnp.maximum(j - CHAIN_LAG, 0))),
        ],
        out_shape=[
            jax.ShapeDtypeStruct((rows, INNER), full_type),
            jax.ShapeDtypeStruct((rows, WIDE), full_type),
            small, small, small_t, small_t, small, small, small,
            jax.ShapeDtypeStruct((16, LANES), full_type),
            jax.ShapeDtypeStruct((blocks, STATE, INNER), low_type),
            jax.ShapeDtypeStruct((STATE, INNER), low_type),
        ],
        scratch_shapes=[
            pltpu.VMEM((rows + HALO, WIDE), full_type),
            pltpu.VMEM((STATE, rows), low_type),
            pltpu.VMEM((GROUPS, STATE, WIDE), full_type),
            pltpu.VMEM((GROUPS, STATE, WIDE), low_type),
            pltpu.VMEM((GROUPS, STATE, WIDE), low_type),
            pltpu.SemaphoreType.DMA((2, GROUPS)),
        ],
        compiler_params=pltpu.CompilerParams(collective_id=1, has_side_effects=True, vmem_limit_bytes=VMEM_LIMIT),
        cost_estimate=pl.CostEstimate(flops=10**9, bytes_accessed=15 * 10**6, transcendentals=10**6),
        name="scan_states",
    )(packed, packed, packed, conv, conv, head)


def run_outputs(x, bc, run, lag_t, enter, states, head):
    rows = x.shape[0]
    blocks = rows // BLOCK
    whole = lambda shape: pl.BlockSpec(shape, lambda j: (0,) * len(shape))
    return pl.pallas_call(
        outputs_kernel,
        grid=(GROUPS,),
        in_specs=[
            pl.BlockSpec((rows, WIDE), lambda j: (0, j)),
            whole((rows, WIDE)),
            whole((rows, LANES)),
            whole((LANES, rows)),
            whole((rows, LANES)),
            pl.BlockSpec((blocks, STATE, WIDE), lambda j: (0, 0, j)),
            whole((8, LANES)),
        ],
        out_specs=pl.BlockSpec((rows, WIDE), lambda j: (0, j)),
        out_shape=jax.ShapeDtypeStruct((rows, INNER), full_type),
        scratch_shapes=[pltpu.VMEM((blocks, BLOCK, BLOCK), full_type)],
        compiler_params=pltpu.CompilerParams(vmem_limit_bytes=VMEM_LIMIT),
        cost_estimate=pl.CostEstimate(flops=10**10, bytes_accessed=15 * 10**6, transcendentals=3 * 10**6),
        name="scan_outputs",
    )(x, bc, run, lag_t, enter, states, head)


def run_norm(y, gate, back, gain, bc, enter, state):
    rows = y.shape[0]
    part = BLOCK
    by_rows = lambda cols: pl.BlockSpec((part, cols), lambda i: (i, 0))
    whole = lambda shape: pl.BlockSpec(shape, lambda i: (0,) * len(shape))
    return pl.pallas_call(
        norm_kernel,
        grid=(rows // part,),
        in_specs=[
            by_rows(INNER), by_rows(INNER), by_rows(INNER), whole((8, INNER)),
            by_rows(WIDE), by_rows(LANES), whole((STATE, INNER)),
        ],
        out_specs=[
            by_rows(INNER), pl.BlockSpec((INNER, part), lambda i: (0, i)), by_rows(INNER), by_rows(INNER),
            whole((8, INNER)), whole((STATE, INNER)),
        ],
        out_shape=[
            jax.ShapeDtypeStruct((rows, INNER), low_type),
            jax.ShapeDtypeStruct((INNER, rows), low_type),
            jax.ShapeDtypeStruct((rows, INNER), low_type),
            jax.ShapeDtypeStruct((rows, INNER), low_type),
            jax.ShapeDtypeStruct((8, INNER), full_type),
            jax.ShapeDtypeStruct((STATE, INNER), full_type),
        ],
        scratch_shapes=[pltpu.VMEM((part, INNER), full_type), pltpu.VMEM((part, INNER), low_type)],
        compiler_params=pltpu.CompilerParams(vmem_limit_bytes=VMEM_LIMIT),
        cost_estimate=pl.CostEstimate(flops=10**9, bytes_accessed=30 * 10**6, transcendentals=3 * 10**6),
        name="gated_norm",
    )(y, gate, back, gain, bc, enter, state)


def run_backward(
    packed, conv, head, grad_y, bc, lag, run_t, enter, tail, offs, states, state_in, grad_state, lefts, cot, grad_gate
):
    rows = grad_y.shape[0]
    blocks = rows // BLOCK
    wsh_count, seq_count = lax.axis_size("wsh"), lax.axis_size("seq")
    groups = INNER // D
    n_out, n_gate = cot.shape[1] // TILE, grad_gate.shape[1] // TILE
    spans = [(0, n_out, groups), (n_out * groups, n_gate, 1)]
    chunks = n_out * groups + n_gate
    low_at = lambda j, top: jnp.clip(j - AHEAD, 0, top)
    once = pl.Buffered(1)
    whole = lambda shape: pl.BlockSpec(shape, lambda j: (0,) * len(shape), pipeline_mode=once)
    kept = lambda shape: pl.BlockSpec(shape, lambda j: (0,) * len(shape))
    return pl.pallas_call(
        functools.partial(backward_kernel, (wsh_count, seq_count), spans, [INNER, D]),
        grid=(GROUPS + 2 + AHEAD,),
        in_specs=[
            pl.BlockSpec((rows + HALO, WIDE), lambda j: (0, low_at(j, GROUPS))),
            pl.BlockSpec((rows + HALO, LANES), lambda j: (0, CONV_CH // LANES), pipeline_mode=once),
            pl.BlockSpec((8, WIDE), lambda j: (0, low_at(j, GROUPS))),
            whole((8, LANES)),
            pl.BlockSpec((rows, WIDE), lambda j: (0, low_at(j, GROUPS - 1))),
            whole((rows, WIDE)),
            whole((rows, LANES)),
            whole((LANES, rows)),
            whole((rows, LANES)),
            whole((rows, LANES)),
            whole((16, LANES)),
            pl.BlockSpec((blocks, STATE, WIDE), lambda j: (0, 0, low_at(j, GROUPS - 1))),
            pl.BlockSpec((STATE, WIDE), lambda j: (0, low_at(j, GROUPS - 1))),
            whole((STATE, INNER)),
            whole(lefts.shape),
            whole(cot.shape),
            whole(grad_gate.shape),
        ],
        out_specs=[
            pl.BlockSpec((rows, WIDE), lambda j: (0, low_at(j, GROUPS + 1))),
            pl.BlockSpec((8, WIDE), lambda j: (0, low_at(j, GROUPS))),
            pl.BlockSpec((16, WIDE), lambda j: (0, low_at(j, GROUPS))),
            pl.BlockSpec((8, WIDE), lambda j: (0, low_at(j, GROUPS))),
            pl.BlockSpec((8, WIDE), lambda j: (0, low_at(j, GROUPS - 1))),
            kept((8, LANES)),
            pl.BlockSpec(memory_space=pl.ANY),
        ],
        out_shape=[
            jax.ShapeDtypeStruct((rows, PACK), low_type),
            jax.ShapeDtypeStruct((8, CONV_CH), full_type),
            jax.ShapeDtypeStruct((16, CONV_CH), full_type),
            jax.ShapeDtypeStruct((8, CONV_CH), full_type),
            jax.ShapeDtypeStruct((8, INNER), full_type),
            jax.ShapeDtypeStruct((8, LANES), full_type),
            jax.ShapeDtypeStruct((chunks, D // wsh_count, TILE), low_type),
        ],
        scratch_shapes=[
            pltpu.VMEM((rows + HALO, WIDE), full_type),
            pltpu.VMEM((rows + 2 * HALO, WIDE), full_type),
            pltpu.VMEM((blocks, BLOCK, BLOCK), full_type),
            pltpu.VMEM((blocks, BLOCK, BLOCK), full_type),
            pltpu.VMEM((rows, WIDE), full_type),
            pltpu.VMEM((STATE, rows), low_type),
            pltpu.VMEM((LANES, rows), full_type),
            pltpu.VMEM((rows, LANES), full_type),
            pltpu.VMEM((8, LANES), full_type),
            pltpu.VMEM((rows, LANES), full_type),
            pltpu.VMEM((GROUPS, STATE, WIDE), low_type),
            pltpu.VMEM((GROUPS, STATE, WIDE), low_type),
            pltpu.SemaphoreType.DMA((2, GROUPS)),
            *reduce_scratch(chunks, rows, wsh_count),
        ],
        compiler_params=pltpu.CompilerParams(collective_id=2, has_side_effects=True, vmem_limit_bytes=VMEM_LIMIT),
        cost_estimate=pl.CostEstimate(flops=10**11, bytes_accessed=20 * 10**6, transcendentals=5 * 10**6),
        name="scan_backward",
    )(
        packed, packed, conv, head, grad_y, bc, lag, run_t, enter, tail, offs, states, state_in, grad_state,
        lefts, cot, grad_gate,
    )


def adam_update(weights, gradient, first_moment, second_moment, step_rate, decay_amount):
    next_first = beta_one * first_moment + (1.0 - beta_one) * gradient
    next_second = beta_two * second_moment + (1.0 - beta_two) * gradient * gradient
    corrected = (
        next_first
        / (1.0 - beta_one**STEP)
        / (jnp.sqrt(next_second / (1.0 - beta_two**STEP)) + adam_eps)
    )
    return (weights - step_rate * (corrected + decay_amount * weights), next_first, next_second)


def pad_rows(vals, rows):
    return jnp.pad(vals, ((0, rows - vals.shape[0]), (0, 0)))


def swap(vals, bit, axis="wsh"):
    return lax.ppermute(vals, axis, [(i, i ^ bit) for i in range(lax.axis_size(axis))])


def gather_pieces(own, count, also=None):
    rows = own.shape[0]
    far = [1 << b for b in range(1, count.bit_length() - 1)]
    pieces = [(0, 0, own)]
    if len(far) == 2:
        one, two = far
        half = rows // 2
        by_one = swap(own, one)
        by_two = swap(own, two)
        pieces += [(one, 0, by_one), (two, 0, by_two)]
        pieces += [(one | two, 0, swap(by_two[:half], one)), (one | two, half, swap(by_one[half:], two))]
    else:
        for bit in far:
            pieces += [(r ^ bit, first, swap(piece, bit)) for r, first, piece in pieces]
    marks = [piece for _, _, piece in pieces[-2:]]
    return pieces + [(r ^ 1, first, swap(piece, 1)) for r, first, piece in pieces], marks


def piece_kernel(spots, rows, me_ref, left_ref, *refs):
    sources, out_ref, whole_ref = refs[: len(spots)], refs[len(spots)], refs[len(spots) + 1]
    for source, (r, first) in zip(sources, spots):
        start = lax.bitwise_xor(me_ref[0], r) * rows + first
        whole_ref[pl.ds(pl.multiple_of(start, 16), source.shape[0]), :] = source[...]
    out_ref[...] = dot(left_ref[...], whole_ref[...]).astype(out_ref.dtype)


def multiply_pieces(left, pieces, count, out_type, name):
    rows, cols = pieces[0][2].shape
    tile = 512
    me = jnp.reshape(lax.axis_index("wsh"), (1,)).astype(jnp.int32)
    spots = [(r, first) for r, first, _ in pieces]
    return pl.pallas_call(
        functools.partial(piece_kernel, spots, rows),
        grid=(pl.cdiv(cols, tile),),
        in_specs=[pl.BlockSpec(memory_space=pltpu.SMEM), pl.BlockSpec(left.shape, lambda j: (0, 0))]
        + [pl.BlockSpec((piece.shape[0], tile), lambda j: (0, j)) for _, _, piece in pieces],
        out_specs=[
            pl.BlockSpec((left.shape[0], tile), lambda j: (0, j)),
            pl.BlockSpec((rows * count, tile), lambda j: (0, j)),
        ],
        out_shape=[
            jax.ShapeDtypeStruct((left.shape[0], cols), out_type),
            jax.ShapeDtypeStruct((rows * count, cols), low_type),
        ],
        compiler_params=pltpu.CompilerParams(vmem_limit_bytes=VMEM_LIMIT),
        cost_estimate=pl.CostEstimate(
            flops=2 * left.shape[0] * rows * count * cols, bytes_accessed=4 * rows * count * cols, transcendentals=0
        ),
        name=name,
    )(me, left, *[piece for _, _, piece in pieces])


def back_kernel(spots, me_ref, left_ref, *refs):
    sources, out_ref, whole_ref = refs[: len(spots)], refs[len(spots)], refs[len(spots) + 1]
    step = pl.program_id(0)
    for r in sorted({r for r, _ in spots}):

        @pl.when(step == r)
        def _():
            for source, (other, first) in zip(sources, spots):
                if other == r:
                    whole_ref[first : first + source.shape[0], :] = source[...]
            out_ref[...] = dot_nt(left_ref[...], whole_ref[...])


def multiply_back(left, pieces, count, name):
    rows, cols = pieces[0][2].shape
    if rows % LANES:
        whole = jnp.zeros((rows * count, cols), low_type)
        for r, first, piece in pieces:
            start = lax.bitwise_xor(lax.axis_index("wsh"), r) * rows + first
            whole = lax.dynamic_update_slice_in_dim(whole, piece, start, 0)
        return dot_nt(left, whole), whole
    me = jnp.reshape(lax.axis_index("wsh"), (1,)).astype(jnp.int32)
    spots = [(r, first) for r, first, _ in pieces]
    once = pl.Buffered(1)
    grid_spec = pltpu.PrefetchScalarGridSpec(
        num_scalar_prefetch=1,
        grid=(count,),
        in_specs=[pl.BlockSpec(left.shape, lambda j, me: (0, 0), pipeline_mode=once)]
        + [pl.BlockSpec(piece.shape, lambda j, me: (0, 0), pipeline_mode=once) for _, _, piece in pieces],
        out_specs=[
            pl.BlockSpec((left.shape[0], rows), lambda j, me: (0, lax.bitwise_xor(me[0], j))),
            pl.BlockSpec((rows, cols), lambda j, me: (lax.bitwise_xor(me[0], j), 0)),
        ],
    )
    return pl.pallas_call(
        functools.partial(back_kernel, spots),
        grid_spec=grid_spec,
        out_shape=[
            jax.ShapeDtypeStruct((left.shape[0], rows * count), full_type),
            jax.ShapeDtypeStruct((rows * count, cols), low_type),
        ],
        compiler_params=pltpu.CompilerParams(vmem_limit_bytes=VMEM_LIMIT),
        cost_estimate=pl.CostEstimate(
            flops=2 * left.shape[0] * rows * count * cols, bytes_accessed=4 * rows * count * cols, transcendentals=0
        ),
        name=name,
    )(me, left, *[piece for _, _, piece in pieces])


def sum_small(vals):
    for axis in ("wsh", "seq"):
        bit = 1
        while bit < lax.axis_size(axis):
            vals = vals + swap(vals, bit, axis)
            bit = 2 * bit
    return vals


TILE = 384
SLACK = 1


def part_orders(count):
    far = [b for b in range(count.bit_length() - 2)]
    return [far[p:] + far[:p] for p in range(len(far))]


def held(order, phase, bits):
    done = sum(1 << b for b in order[:phase])
    left = [m for m in range(1 << bits) if m & done == 0]
    bit = 1 << order[phase]
    return [m for m in left if m & bit == 0], [m for m in left if m & bit]


def greet():
    me, z = lax.axis_index("wsh"), lax.axis_index("seq")
    seq_count = lax.axis_size("seq")
    barrier = pltpu.get_barrier_semaphore()
    mesh_id = pl.DeviceIdType.MESH
    bits = lax.axis_size("wsh").bit_length() - 1
    for b in range(bits):
        pl.semaphore_signal(barrier, inc=1, device_id={"wsh": lax.bitwise_xor(me, 1 << b)}, device_id_type=mesh_id)

    @pl.when(z > 0)
    def _():
        pl.semaphore_signal(barrier, inc=1, device_id={"seq": z - 1}, device_id_type=mesh_id)

    @pl.when(z < seq_count - 1)
    def _():
        pl.semaphore_signal(barrier, inc=1, device_id={"seq": z + 1}, device_id_type=mesh_id)

    along = jnp.where(z > 0, 1, 0) + jnp.where(z < seq_count - 1, 1, 0)
    pl.semaphore_wait(barrier, bits + along)


def reduce_turns(wsh_count, seq_count, spans, left_refs, right_refs, out_ref, scratch):
    orders = part_orders(wsh_count)
    bits = len(orders)
    tile, stage, pair, *rest = scratch
    lands, rest = rest[:bits], rest[bits:]
    from_left, from_right, pair_sems, far_sems, seq_sems, out_sems = rest
    chunks, blocks, rows, _ = pair.shape
    part = rows // bits
    me = lax.axis_index("wsh")
    z = lax.axis_index("seq")
    root = seq_count // 2
    mesh_id = pl.DeviceIdType.MESH

    def pair_copy(k):
        return pltpu.make_async_remote_copy(
            src_ref=stage.at[lax.rem(k, 2)], dst_ref=pair.at[k],
            send_sem=pair_sems.at[0, k], recv_sem=pair_sems.at[1, k],
            device_id={"wsh": lax.bitwise_xor(me, 1)}, device_id_type=mesh_id,
        )

    spots = []
    for q in range(bits):
        for p, order in enumerate(orders):
            for i, m in enumerate(held(order, q, bits)[1]):
                spots.append((q, p, i, m, 2 << order[q]))

    def far_copies(k, phase):
        return [
            pltpu.make_async_remote_copy(
                src_ref=pair.at[k, m, pl.ds(p * part, part)], dst_ref=lands[q].at[k, p, i],
                send_sem=far_sems.at[0, n, k], recv_sem=far_sems.at[1, n, k],
                device_id={"wsh": lax.bitwise_xor(me, bit)}, device_id_type=mesh_id,
            )
            for n, (q, p, i, m, bit) in enumerate(spots)
            if q == phase
        ]

    def to_right(k, source):
        return pltpu.make_async_remote_copy(
            src_ref=source, dst_ref=from_left.at[k],
            send_sem=seq_sems.at[0, k], recv_sem=seq_sems.at[1, k],
            device_id={"seq": z + 1}, device_id_type=mesh_id,
        )

    def to_left(k, source):
        return pltpu.make_async_remote_copy(
            src_ref=source, dst_ref=from_right.at[k],
            send_sem=seq_sems.at[2, k], recv_sem=seq_sems.at[3, k],
            device_id={"seq": z - 1}, device_id_type=mesh_id,
        )

    def out_copy(k, source):
        return pltpu.make_async_copy(source, out_ref.at[k], out_sems.at[k])

    def take_tile(k):
        for (start, tiles, groups), right_ref in zip(spans, right_refs):

            @pl.when((k >= start) & (k < start + tiles * groups))
            def _():
                col = lax.rem(k - start, tiles) * TILE
                tile[...] = right_ref[:, pl.ds(pl.multiple_of(col, LANES), TILE)]

    def product(k, b, core):
        owner = lax.bitwise_xor(me, 2 * b + core)
        if len(left_refs) == 1:
            group, groups, left_ref = 0, 1, left_refs[0]
            first = owner * rows
            return dot(left_ref[pl.ds(pl.multiple_of(first, 16), rows), :], tile[...])
        first = jnp.zeros((), jnp.int32)
        base = 0
        for (start, tiles, groups), left_rows in zip(spans, left_refs[1:]):
            at = base + (owner * groups + (k - start) // tiles) * rows
            first = jnp.where((k >= start) & (k < start + tiles * groups), at, first)
            base += left_rows
        return dot(left_refs[0][pl.ds(pl.multiple_of(first, 16), rows), :], tile[...])

    def begin(k):
        @pl.when(k >= 2)
        def _():
            pair_copy(k - 2).wait_send()

        take_tile(k)
        for b in range(blocks):
            stage[lax.rem(k, 2), b] = product(k, b, 1).astype(low_type)
        pair_copy(k).start()

    def add_pair(k):
        take_tile(k)
        pair_copy(k).wait_recv()
        for b in range(blocks):
            pair[k, b] = (product(k, b, 0) + pair[k, b].astype(full_type)).astype(low_type)
        for copy in far_copies(k, 0):
            copy.start()

    def add_far(k, phase):
        for copy in far_copies(k, phase):
            copy.wait_recv()
        for p, order in enumerate(orders):
            at = pl.ds(p * part, part)
            for i, m in enumerate(held(order, phase, bits)[0]):
                total = pair[k, m, at].astype(full_type) + lands[phase][k, p, i].astype(full_type)
                pair[k, m, at] = total.astype(low_type)
        if phase < bits - 1:
            for copy in far_copies(k, phase + 1):
                copy.start()

    def add_to(k, land):
        pair[k, 0] = (pair[k, 0].astype(full_type) + land[k].astype(full_type)).astype(low_type)

    def seq_up(k):
        mine = pair.at[k, 0]

        @pl.when((z > 0) & (z <= root))
        def _():
            to_right(k, mine).wait_recv()
            add_to(k, from_left)

        @pl.when((z < seq_count - 1) & (z >= root))
        def _():
            to_left(k, mine).wait_recv()
            add_to(k, from_right)

        @pl.when((z < seq_count - 1) & (z <= root))
        def _():
            to_right(k, mine).start()

        @pl.when((z > 0) & (z >= root))
        def _():
            to_left(k, mine).start()

    def seq_down(k):
        @pl.when(z == root)
        def _():
            out_copy(k, pair.at[k, 0]).start()

        @pl.when(z < root)
        def _():
            to_left(k, from_right.at[k]).wait_recv()
            out_copy(k, from_right.at[k]).start()
            pl.when(z > 0)(lambda: to_left(k, from_right.at[k]).start())

        @pl.when(z > root)
        def _():
            to_right(k, from_left.at[k]).wait_recv()
            out_copy(k, from_left.at[k]).start()
            pl.when(z < seq_count - 1)(lambda: to_right(k, from_left.at[k]).start())

    far = jnp.abs(z - root)
    farthest = max(root, seq_count - 1 - root)
    stages = [(0, begin), (1, add_pair)] + [(2 + q, functools.partial(add_far, phase=q)) for q in range(bits)]
    stages += [
        (2 + bits + SLACK * (farthest - far), seq_up),
        (3 + bits + SLACK * (farthest + far), seq_down),
    ]
    turns = chunks + 4 + bits + SLACK * 2 * farthest

    def turn(s, carry):
        for offset, run in stages:
            pl.when((s >= offset) & (s < chunks + offset))(lambda run=run, offset=offset: run(s - offset))
        return carry

    def finish():
        def wait_all(k, carry):
            for q in range(bits):
                for copy in far_copies(k, q):
                    copy.wait_send()
            pl.when(z < seq_count - 1)(lambda: to_right(k, pair.at[k, 0]).wait_send())
            pl.when(z > 0)(lambda: to_left(k, pair.at[k, 0]).wait_send())
            out_copy(k, pair.at[k, 0]).wait()
            return carry

        lax.fori_loop(0, chunks, wait_all, 0)
        for k in (chunks - 2, chunks - 1):
            pair_copy(k).wait_send()

    return turns, turn, finish


def reduce_scratch(chunks, depth, wsh_count):
    rows = D // wsh_count
    bits = len(part_orders(wsh_count))
    low = lambda *shape: pltpu.VMEM(shape, low_type)
    dma = pltpu.SemaphoreType.DMA
    return [
        low(depth, TILE),
        low(2, 1 << bits, rows, TILE),
        low(chunks, 1 << bits, rows, TILE),
        *[low(chunks, bits, 1 << (bits - 1 - q), rows // bits, TILE) for q in range(bits)],
        low(chunks, rows, TILE),
        low(chunks, rows, TILE),
        dma((2, chunks)),
        dma((2, bits * ((1 << bits) - 1), chunks)),
        dma((4, chunks)),
        dma((chunks,)),
    ]


def reduce_kernel(counts, spans, left_ref, right_ref, out_ref, *scratch):
    greet()
    turns, turn, finish = reduce_turns(*counts, spans, [left_ref], [right_ref], out_ref, scratch)
    lax.fori_loop(0, turns, turn, 0)
    finish()


def reduce_rows(left, right):
    wsh_count, seq_count = lax.axis_size("wsh"), lax.axis_size("seq")
    chunks = right.shape[1] // TILE
    vmem = pl.BlockSpec(memory_space=pltpu.VMEM)
    return pl.pallas_call(
        functools.partial(reduce_kernel, (wsh_count, seq_count), [(0, chunks, 1)]),
        in_specs=[vmem] * 2,
        out_specs=pl.BlockSpec(memory_space=pl.ANY),
        out_shape=jax.ShapeDtypeStruct((chunks, D // wsh_count, TILE), low_type),
        scratch_shapes=reduce_scratch(chunks, right.shape[0], wsh_count),
        compiler_params=pltpu.CompilerParams(collective_id=0, has_side_effects=True, vmem_limit_bytes=VMEM_LIMIT),
        cost_estimate=pl.CostEstimate(flops=5 * 10**10, bytes_accessed=20 * 10**6, transcendentals=0),
        name="reduce_gradients",
    )(left, right)


def adam_kernel(start, rate, decay, *refs):
    share_ref, weight_ref, first_ref, second_ref, grad_ref, next_ref, next_first_ref, next_second_ref = refs
    grad = share_ref[0].astype(full_type)
    grad_ref[...] = grad
    next_ref[...], next_first_ref[...], next_second_ref[...] = adam_update(
        weight_ref[...], grad, first_ref[...], second_ref[...], rate, decay
    )


def adam_chunks(sums, start, weights, first_moment, second_moment, rate, decay, name):
    all_rows, cols = weights.shape
    rows = sums.shape[1]
    tiles = pl.cdiv(cols, TILE)
    block = pl.BlockSpec((rows, TILE), lambda i, j: (i, j))
    return pl.pallas_call(
        functools.partial(adam_kernel, start, rate, decay),
        grid=(all_rows // rows, tiles),
        in_specs=[pl.BlockSpec((1, rows, TILE), lambda i, j: (start + i * tiles + j, 0, 0))] + [block] * 3,
        out_specs=[block] * 4,
        out_shape=[jax.ShapeDtypeStruct(weights.shape, full_type)] * 4,
        compiler_params=pltpu.CompilerParams(vmem_limit_bytes=VMEM_LIMIT),
        cost_estimate=pl.CostEstimate(
            flops=20 * weights.size, bytes_accessed=30 * weights.size, transcendentals=weights.size
        ),
        name=name,
    )(sums, weights, first_moment, second_moment)


def after(vals, *others):
    return lax.optimization_barrier((vals,) + others)[0]


TILE = 384
SLACK = 1


def part_orders(count):
    far = [b for b in range(count.bit_length() - 2)]
    return [far[p:] + far[:p] for p in range(len(far))]


def held(order, phase, bits):
    done = sum(1 << b for b in order[:phase])
    left = [m for m in range(1 << bits) if m & done == 0]
    bit = 1 << order[phase]
    return [m for m in left if m & bit == 0], [m for m in left if m & bit]


def greet():
    me, z = lax.axis_index("wsh"), lax.axis_index("seq")
    seq_count = lax.axis_size("seq")
    barrier = pltpu.get_barrier_semaphore()
    mesh_id = pl.DeviceIdType.MESH
    bits = lax.axis_size("wsh").bit_length() - 1
    for b in range(bits):
        pl.semaphore_signal(barrier, inc=1, device_id={"wsh": lax.bitwise_xor(me, 1 << b)}, device_id_type=mesh_id)

    @pl.when(z > 0)
    def _():
        pl.semaphore_signal(barrier, inc=1, device_id={"seq": z - 1}, device_id_type=mesh_id)

    @pl.when(z < seq_count - 1)
    def _():
        pl.semaphore_signal(barrier, inc=1, device_id={"seq": z + 1}, device_id_type=mesh_id)

    along = jnp.where(z > 0, 1, 0) + jnp.where(z < seq_count - 1, 1, 0)
    pl.semaphore_wait(barrier, bits + along)


def reduce_turns(wsh_count, seq_count, spans, left_refs, right_refs, out_ref, scratch):
    orders = part_orders(wsh_count)
    bits = len(orders)
    tile, stage, pair, *rest = scratch
    lands, rest = rest[:bits], rest[bits:]
    from_left, from_right, pair_sems, far_sems, seq_sems, out_sems = rest
    chunks, blocks, rows, _ = pair.shape
    part = rows // bits
    me = lax.axis_index("wsh")
    z = lax.axis_index("seq")
    root = seq_count // 2
    mesh_id = pl.DeviceIdType.MESH

    def pair_copy(k):
        return pltpu.make_async_remote_copy(
            src_ref=stage.at[lax.rem(k, 2)], dst_ref=pair.at[k],
            send_sem=pair_sems.at[0, k], recv_sem=pair_sems.at[1, k],
            device_id={"wsh": lax.bitwise_xor(me, 1)}, device_id_type=mesh_id,
        )

    spots = []
    for q in range(bits):
        for p, order in enumerate(orders):
            for i, m in enumerate(held(order, q, bits)[1]):
                spots.append((q, p, i, m, 2 << order[q]))

    def far_copies(k, phase):
        return [
            pltpu.make_async_remote_copy(
                src_ref=pair.at[k, m, pl.ds(p * part, part)], dst_ref=lands[q].at[k, p, i],
                send_sem=far_sems.at[0, n, k], recv_sem=far_sems.at[1, n, k],
                device_id={"wsh": lax.bitwise_xor(me, bit)}, device_id_type=mesh_id,
            )
            for n, (q, p, i, m, bit) in enumerate(spots)
            if q == phase
        ]

    def to_right(k, source):
        return pltpu.make_async_remote_copy(
            src_ref=source, dst_ref=from_left.at[k],
            send_sem=seq_sems.at[0, k], recv_sem=seq_sems.at[1, k],
            device_id={"seq": z + 1}, device_id_type=mesh_id,
        )

    def to_left(k, source):
        return pltpu.make_async_remote_copy(
            src_ref=source, dst_ref=from_right.at[k],
            send_sem=seq_sems.at[2, k], recv_sem=seq_sems.at[3, k],
            device_id={"seq": z - 1}, device_id_type=mesh_id,
        )

    def out_copy(k, source):
        return pltpu.make_async_copy(source, out_ref.at[k], out_sems.at[k])

    def take_tile(k):
        for (start, tiles, groups), right_ref in zip(spans, right_refs):

            @pl.when((k >= start) & (k < start + tiles * groups))
            def _():
                col = lax.rem(k - start, tiles) * TILE
                tile[...] = right_ref[:, pl.ds(pl.multiple_of(col, LANES), TILE)]

    def product(k, b, core):
        owner = lax.bitwise_xor(me, 2 * b + core)
        if len(left_refs) == 1:
            group, groups, left_ref = 0, 1, left_refs[0]
            first = owner * rows
            return dot(left_ref[pl.ds(pl.multiple_of(first, 16), rows), :], tile[...])
        first = jnp.zeros((), jnp.int32)
        base = 0
        for (start, tiles, groups), left_rows in zip(spans, left_refs[1:]):
            at = base + (owner * groups + (k - start) // tiles) * rows
            first = jnp.where((k >= start) & (k < start + tiles * groups), at, first)
            base += left_rows
        return dot(left_refs[0][pl.ds(pl.multiple_of(first, 16), rows), :], tile[...])

    def begin(k):
        @pl.when(k >= 2)
        def _():
            pair_copy(k - 2).wait_send()

        take_tile(k)
        for b in range(blocks):
            stage[lax.rem(k, 2), b] = product(k, b, 1).astype(low_type)
        pair_copy(k).start()

    def add_pair(k):
        take_tile(k)
        pair_copy(k).wait_recv()
        for b in range(blocks):
            pair[k, b] = (product(k, b, 0) + pair[k, b].astype(full_type)).astype(low_type)
        for copy in far_copies(k, 0):
            copy.start()

    def add_far(k, phase):
        for copy in far_copies(k, phase):
            copy.wait_recv()
        for p, order in enumerate(orders):
            at = pl.ds(p * part, part)
            for i, m in enumerate(held(order, phase, bits)[0]):
                total = pair[k, m, at].astype(full_type) + lands[phase][k, p, i].astype(full_type)
                pair[k, m, at] = total.astype(low_type)
        if phase < bits - 1:
            for copy in far_copies(k, phase + 1):
                copy.start()

    def add_to(k, land):
        pair[k, 0] = (pair[k, 0].astype(full_type) + land[k].astype(full_type)).astype(low_type)

    def seq_up(k):
        mine = pair.at[k, 0]

        @pl.when((z > 0) & (z <= root))
        def _():
            to_right(k, mine).wait_recv()
            add_to(k, from_left)

        @pl.when((z < seq_count - 1) & (z >= root))
        def _():
            to_left(k, mine).wait_recv()
            add_to(k, from_right)

        @pl.when((z < seq_count - 1) & (z <= root))
        def _():
            to_right(k, mine).start()

        @pl.when((z > 0) & (z >= root))
        def _():
            to_left(k, mine).start()

    def seq_down(k):
        @pl.when(z == root)
        def _():
            out_copy(k, pair.at[k, 0]).start()

        @pl.when(z < root)
        def _():
            to_left(k, from_right.at[k]).wait_recv()
            out_copy(k, from_right.at[k]).start()
            pl.when(z > 0)(lambda: to_left(k, from_right.at[k]).start())

        @pl.when(z > root)
        def _():
            to_right(k, from_left.at[k]).wait_recv()
            out_copy(k, from_left.at[k]).start()
            pl.when(z < seq_count - 1)(lambda: to_right(k, from_left.at[k]).start())

    far = jnp.abs(z - root)
    farthest = max(root, seq_count - 1 - root)
    stages = [(0, begin), (1, add_pair)] + [(2 + q, functools.partial(add_far, phase=q)) for q in range(bits)]
    stages += [
        (2 + bits + SLACK * (farthest - far), seq_up),
        (3 + bits + SLACK * (farthest + far), seq_down),
    ]
    turns = chunks + 4 + bits + SLACK * 2 * farthest

    def turn(s, carry):
        for offset, run in stages:
            pl.when((s >= offset) & (s < chunks + offset))(lambda run=run, offset=offset: run(s - offset))
        return carry

    def finish():
        def wait_all(k, carry):
            for q in range(bits):
                for copy in far_copies(k, q):
                    copy.wait_send()
            pl.when(z < seq_count - 1)(lambda: to_right(k, pair.at[k, 0]).wait_send())
            pl.when(z > 0)(lambda: to_left(k, pair.at[k, 0]).wait_send())
            out_copy(k, pair.at[k, 0]).wait()
            return carry

        lax.fori_loop(0, chunks, wait_all, 0)
        for k in (chunks - 2, chunks - 1):
            pair_copy(k).wait_send()

    return turns, turn, finish


def reduce_scratch(chunks, depth, wsh_count):
    rows = D // wsh_count
    bits = len(part_orders(wsh_count))
    low = lambda *shape: pltpu.VMEM(shape, low_type)
    dma = pltpu.SemaphoreType.DMA
    return [
        low(depth, TILE),
        low(2, 1 << bits, rows, TILE),
        low(chunks, 1 << bits, rows, TILE),
        *[low(chunks, bits, 1 << (bits - 1 - q), rows // bits, TILE) for q in range(bits)],
        low(chunks, rows, TILE),
        low(chunks, rows, TILE),
        dma((2, chunks)),
        dma((2, bits * ((1 << bits) - 1), chunks)),
        dma((4, chunks)),
        dma((chunks,)),
    ]


def reduce_kernel(counts, spans, left_ref, right_ref, out_ref, *scratch):
    greet()
    turns, turn, finish = reduce_turns(*counts, spans, [left_ref], [right_ref], out_ref, scratch)
    lax.fori_loop(0, turns, turn, 0)
    finish()


def reduce_rows(left, right):
    wsh_count, seq_count = lax.axis_size("wsh"), lax.axis_size("seq")
    chunks = right.shape[1] // TILE
    vmem = pl.BlockSpec(memory_space=pltpu.VMEM)
    return pl.pallas_call(
        functools.partial(reduce_kernel, (wsh_count, seq_count), [(0, chunks, 1)]),
        in_specs=[vmem] * 2,
        out_specs=pl.BlockSpec(memory_space=pl.ANY),
        out_shape=jax.ShapeDtypeStruct((chunks, D // wsh_count, TILE), low_type),
        scratch_shapes=reduce_scratch(chunks, right.shape[0], wsh_count),
        compiler_params=pltpu.CompilerParams(collective_id=0, has_side_effects=True, vmem_limit_bytes=VMEM_LIMIT),
        cost_estimate=pl.CostEstimate(flops=5 * 10**10, bytes_accessed=20 * 10**6, transcendentals=0),
        name="reduce_gradients",
    )(left, right)


def adam_kernel(start, rate, decay, *refs):
    share_ref, weight_ref, first_ref, second_ref, grad_ref, next_ref, next_first_ref, next_second_ref = refs
    grad = share_ref[0].astype(full_type)
    grad_ref[...] = grad
    next_ref[...], next_first_ref[...], next_second_ref[...] = adam_update(
        weight_ref[...], grad, first_ref[...], second_ref[...], rate, decay
    )


def adam_chunks(sums, start, weights, first_moment, second_moment, rate, decay, name):
    all_rows, cols = weights.shape
    rows = sums.shape[1]
    tiles = pl.cdiv(cols, TILE)
    block = pl.BlockSpec((rows, TILE), lambda i, j: (i, j))
    return pl.pallas_call(
        functools.partial(adam_kernel, start, rate, decay),
        grid=(all_rows // rows, tiles),
        in_specs=[pl.BlockSpec((1, rows, TILE), lambda i, j: (start + i * tiles + j, 0, 0))] + [block] * 3,
        out_specs=[block] * 4,
        out_shape=[jax.ShapeDtypeStruct(weights.shape, full_type)] * 4,
        compiler_params=pltpu.CompilerParams(vmem_limit_bytes=VMEM_LIMIT),
        cost_estimate=pl.CostEstimate(
            flops=20 * weights.size, bytes_accessed=30 * weights.size, transcendentals=weights.size
        ),
        name=name,
    )(sums, weights, first_moment, second_moment)


def after(vals, *others):
    return lax.optimization_barrier((vals,) + others)[0]


def shift(vals, by):
    count = lax.axis_size("seq")
    pairs = [(i, i + by) for i in range(count) if 0 <= i + by < count]
    return lax.ppermute(vals, "seq", pairs)


TILE = 384
SLACK = 1


def part_orders(count):
    far = [b for b in range(count.bit_length() - 2)]
    return [far[p:] + far[:p] for p in range(len(far))]


def held(order, phase, bits):
    done = sum(1 << b for b in order[:phase])
    left = [m for m in range(1 << bits) if m & done == 0]
    bit = 1 << order[phase]
    return [m for m in left if m & bit == 0], [m for m in left if m & bit]


def greet():
    me, z = lax.axis_index("wsh"), lax.axis_index("seq")
    seq_count = lax.axis_size("seq")
    barrier = pltpu.get_barrier_semaphore()
    mesh_id = pl.DeviceIdType.MESH
    bits = lax.axis_size("wsh").bit_length() - 1
    for b in range(bits):
        pl.semaphore_signal(barrier, inc=1, device_id={"wsh": lax.bitwise_xor(me, 1 << b)}, device_id_type=mesh_id)

    @pl.when(z > 0)
    def _():
        pl.semaphore_signal(barrier, inc=1, device_id={"seq": z - 1}, device_id_type=mesh_id)

    @pl.when(z < seq_count - 1)
    def _():
        pl.semaphore_signal(barrier, inc=1, device_id={"seq": z + 1}, device_id_type=mesh_id)

    along = jnp.where(z > 0, 1, 0) + jnp.where(z < seq_count - 1, 1, 0)
    pl.semaphore_wait(barrier, bits + along)


def reduce_turns(wsh_count, seq_count, spans, left_refs, right_refs, out_ref, scratch):
    orders = part_orders(wsh_count)
    bits = len(orders)
    tile, stage, pair, *rest = scratch
    lands, rest = rest[:bits], rest[bits:]
    from_left, from_right, pair_sems, far_sems, seq_sems, out_sems = rest
    chunks, blocks, rows, _ = pair.shape
    part = rows // bits
    me = lax.axis_index("wsh")
    z = lax.axis_index("seq")
    root = seq_count // 2
    mesh_id = pl.DeviceIdType.MESH

    def pair_copy(k):
        return pltpu.make_async_remote_copy(
            src_ref=stage.at[lax.rem(k, 2)], dst_ref=pair.at[k],
            send_sem=pair_sems.at[0, k], recv_sem=pair_sems.at[1, k],
            device_id={"wsh": lax.bitwise_xor(me, 1)}, device_id_type=mesh_id,
        )

    spots = []
    for q in range(bits):
        for p, order in enumerate(orders):
            for i, m in enumerate(held(order, q, bits)[1]):
                spots.append((q, p, i, m, 2 << order[q]))

    def far_copies(k, phase):
        return [
            pltpu.make_async_remote_copy(
                src_ref=pair.at[k, m, pl.ds(p * part, part)], dst_ref=lands[q].at[k, p, i],
                send_sem=far_sems.at[0, n, k], recv_sem=far_sems.at[1, n, k],
                device_id={"wsh": lax.bitwise_xor(me, bit)}, device_id_type=mesh_id,
            )
            for n, (q, p, i, m, bit) in enumerate(spots)
            if q == phase
        ]

    def to_right(k, source):
        return pltpu.make_async_remote_copy(
            src_ref=source, dst_ref=from_left.at[k],
            send_sem=seq_sems.at[0, k], recv_sem=seq_sems.at[1, k],
            device_id={"seq": z + 1}, device_id_type=mesh_id,
        )

    def to_left(k, source):
        return pltpu.make_async_remote_copy(
            src_ref=source, dst_ref=from_right.at[k],
            send_sem=seq_sems.at[2, k], recv_sem=seq_sems.at[3, k],
            device_id={"seq": z - 1}, device_id_type=mesh_id,
        )

    def out_copy(k, source):
        return pltpu.make_async_copy(source, out_ref.at[k], out_sems.at[k])

    def take_tile(k):
        for (start, tiles, groups), right_ref in zip(spans, right_refs):

            @pl.when((k >= start) & (k < start + tiles * groups))
            def _():
                col = lax.rem(k - start, tiles) * TILE
                tile[...] = right_ref[:, pl.ds(pl.multiple_of(col, LANES), TILE)]

    def product(k, b, core):
        owner = lax.bitwise_xor(me, 2 * b + core)
        if len(left_refs) == 1:
            group, groups, left_ref = 0, 1, left_refs[0]
            first = owner * rows
            return dot(left_ref[pl.ds(pl.multiple_of(first, 16), rows), :], tile[...])
        first = jnp.zeros((), jnp.int32)
        base = 0
        for (start, tiles, groups), left_rows in zip(spans, left_refs[1:]):
            at = base + (owner * groups + (k - start) // tiles) * rows
            first = jnp.where((k >= start) & (k < start + tiles * groups), at, first)
            base += left_rows
        return dot(left_refs[0][pl.ds(pl.multiple_of(first, 16), rows), :], tile[...])

    def begin(k):
        @pl.when(k >= 2)
        def _():
            pair_copy(k - 2).wait_send()

        take_tile(k)
        for b in range(blocks):
            stage[lax.rem(k, 2), b] = product(k, b, 1).astype(low_type)
        pair_copy(k).start()

    def add_pair(k):
        take_tile(k)
        pair_copy(k).wait_recv()
        for b in range(blocks):
            pair[k, b] = (product(k, b, 0) + pair[k, b].astype(full_type)).astype(low_type)
        for copy in far_copies(k, 0):
            copy.start()

    def add_far(k, phase):
        for copy in far_copies(k, phase):
            copy.wait_recv()
        for p, order in enumerate(orders):
            at = pl.ds(p * part, part)
            for i, m in enumerate(held(order, phase, bits)[0]):
                total = pair[k, m, at].astype(full_type) + lands[phase][k, p, i].astype(full_type)
                pair[k, m, at] = total.astype(low_type)
        if phase < bits - 1:
            for copy in far_copies(k, phase + 1):
                copy.start()

    def add_to(k, land):
        pair[k, 0] = (pair[k, 0].astype(full_type) + land[k].astype(full_type)).astype(low_type)

    def seq_up(k):
        mine = pair.at[k, 0]

        @pl.when((z > 0) & (z <= root))
        def _():
            to_right(k, mine).wait_recv()
            add_to(k, from_left)

        @pl.when((z < seq_count - 1) & (z >= root))
        def _():
            to_left(k, mine).wait_recv()
            add_to(k, from_right)

        @pl.when((z < seq_count - 1) & (z <= root))
        def _():
            to_right(k, mine).start()

        @pl.when((z > 0) & (z >= root))
        def _():
            to_left(k, mine).start()

    def seq_down(k):
        @pl.when(z == root)
        def _():
            out_copy(k, pair.at[k, 0]).start()

        @pl.when(z < root)
        def _():
            to_left(k, from_right.at[k]).wait_recv()
            out_copy(k, from_right.at[k]).start()
            pl.when(z > 0)(lambda: to_left(k, from_right.at[k]).start())

        @pl.when(z > root)
        def _():
            to_right(k, from_left.at[k]).wait_recv()
            out_copy(k, from_left.at[k]).start()
            pl.when(z < seq_count - 1)(lambda: to_right(k, from_left.at[k]).start())

    far = jnp.abs(z - root)
    farthest = max(root, seq_count - 1 - root)
    stages = [(0, begin), (1, add_pair)] + [(2 + q, functools.partial(add_far, phase=q)) for q in range(bits)]
    stages += [
        (2 + bits + SLACK * (farthest - far), seq_up),
        (3 + bits + SLACK * (farthest + far), seq_down),
    ]
    turns = chunks + 4 + bits + SLACK * 2 * farthest

    def turn(s, carry):
        for offset, run in stages:
            pl.when((s >= offset) & (s < chunks + offset))(lambda run=run, offset=offset: run(s - offset))
        return carry

    def finish():
        def wait_all(k, carry):
            for q in range(bits):
                for copy in far_copies(k, q):
                    copy.wait_send()
            pl.when(z < seq_count - 1)(lambda: to_right(k, pair.at[k, 0]).wait_send())
            pl.when(z > 0)(lambda: to_left(k, pair.at[k, 0]).wait_send())
            out_copy(k, pair.at[k, 0]).wait()
            return carry

        lax.fori_loop(0, chunks, wait_all, 0)
        for k in (chunks - 2, chunks - 1):
            pair_copy(k).wait_send()

    return turns, turn, finish


def reduce_scratch(chunks, depth, wsh_count):
    rows = D // wsh_count
    bits = len(part_orders(wsh_count))
    low = lambda *shape: pltpu.VMEM(shape, low_type)
    dma = pltpu.SemaphoreType.DMA
    return [
        low(depth, TILE),
        low(2, 1 << bits, rows, TILE),
        low(chunks, 1 << bits, rows, TILE),
        *[low(chunks, bits, 1 << (bits - 1 - q), rows // bits, TILE) for q in range(bits)],
        low(chunks, rows, TILE),
        low(chunks, rows, TILE),
        dma((2, chunks)),
        dma((2, bits * ((1 << bits) - 1), chunks)),
        dma((4, chunks)),
        dma((chunks,)),
    ]


def reduce_kernel(counts, spans, left_ref, right_ref, out_ref, *scratch):
    greet()
    turns, turn, finish = reduce_turns(*counts, spans, [left_ref], [right_ref], out_ref, scratch)
    lax.fori_loop(0, turns, turn, 0)
    finish()


def reduce_rows(left, right):
    wsh_count, seq_count = lax.axis_size("wsh"), lax.axis_size("seq")
    chunks = right.shape[1] // TILE
    vmem = pl.BlockSpec(memory_space=pltpu.VMEM)
    return pl.pallas_call(
        functools.partial(reduce_kernel, (wsh_count, seq_count), [(0, chunks, 1)]),
        in_specs=[vmem] * 2,
        out_specs=pl.BlockSpec(memory_space=pl.ANY),
        out_shape=jax.ShapeDtypeStruct((chunks, D // wsh_count, TILE), low_type),
        scratch_shapes=reduce_scratch(chunks, right.shape[0], wsh_count),
        compiler_params=pltpu.CompilerParams(collective_id=0, has_side_effects=True, vmem_limit_bytes=VMEM_LIMIT),
        cost_estimate=pl.CostEstimate(flops=5 * 10**10, bytes_accessed=20 * 10**6, transcendentals=0),
        name="reduce_gradients",
    )(left, right)


def adam_kernel(start, rate, decay, *refs):
    share_ref, weight_ref, first_ref, second_ref, grad_ref, next_ref, next_first_ref, next_second_ref = refs
    grad = share_ref[0].astype(full_type)
    grad_ref[...] = grad
    next_ref[...], next_first_ref[...], next_second_ref[...] = adam_update(
        weight_ref[...], grad, first_ref[...], second_ref[...], rate, decay
    )


def adam_chunks(sums, start, weights, first_moment, second_moment, rate, decay, name):
    all_rows, cols = weights.shape
    rows = sums.shape[1]
    tiles = pl.cdiv(cols, TILE)
    block = pl.BlockSpec((rows, TILE), lambda i, j: (i, j))
    return pl.pallas_call(
        functools.partial(adam_kernel, start, rate, decay),
        grid=(all_rows // rows, tiles),
        in_specs=[pl.BlockSpec((1, rows, TILE), lambda i, j: (start + i * tiles + j, 0, 0))] + [block] * 3,
        out_specs=[block] * 4,
        out_shape=[jax.ShapeDtypeStruct(weights.shape, full_type)] * 4,
        compiler_params=pltpu.CompilerParams(vmem_limit_bytes=VMEM_LIMIT),
        cost_estimate=pl.CostEstimate(
            flops=20 * weights.size, bytes_accessed=30 * weights.size, transcendentals=weights.size
        ),
        name=name,
    )(sums, weights, first_moment, second_moment)


def after(vals, *others):
    return lax.optimization_barrier((vals,) + others)[0]


def shift(vals, by):
    count = lax.axis_size("seq")
    pairs = [(i, i + by) for i in range(count) if 0 <= i + by < count]
    return lax.ppermute(vals, "seq", pairs)


def carry_states(own, fades, sign):
    count = lax.axis_size("seq")
    span, span_fade = own, fades
    result, fade = None, jnp.zeros_like(fades)
    reach = 1
    while reach < count:
        got, got_fade = shift(span, sign * reach), shift(span_fade, sign * reach)
        if result is None:
            result = got
        else:
            result = (result.astype(full_type) + jnp.exp2(fade)[None, :] * got.astype(full_type)).astype(low_type)
        span = (span.astype(full_type) + jnp.exp2(span_fade)[None, :] * got.astype(full_type)).astype(low_type)
        fade, span_fade = fade + got_fade, span_fade + got_fade
        reach = 2 * reach
    return result


def shards(
    inputs, cotangent, w_in, w_dt, w_out, gain_pre, gain_norm, conv_param, head_param,
    first_w_in, second_w_in, first_w_dt, second_w_dt, first_w_out, second_w_out,
    first_gain_pre, second_gain_pre, first_gain_norm, second_gain_norm,
    first_conv, second_conv, first_head, second_head,
):
    wsh_count = lax.axis_size("wsh")
    seq_count = lax.axis_size("seq")
    seq_index = lax.axis_index("seq")
    wsh_index = lax.axis_index("wsh")
    rows_model = D // wsh_count
    rows_inner = INNER // wsh_count
    cols_conv = CONV_CH // wsh_count
    cols_head = HEADS // wsh_count
    flat = jnp.concatenate(
        [gain_pre, gain_norm, conv_param.reshape(-1), head_param.reshape(-1)]
    ).astype(low_type)
    count = flat.shape[0]
    flat = jnp.pad(flat, (0, -count % LANES))
    part_sig = jnp.concatenate(
        [w_in[:, INNER:].astype(low_type), w_dt.astype(low_type), jnp.zeros((rows_model, LANES - HEADS), low_type)],
        axis=1,
    )
    small = lax.all_gather(flat, "wsh", axis=0)
    part_sig = after(part_sig, small)
    sig_pieces, marks = gather_pieces(part_sig, wsh_count)
    gate_pieces, marks = gather_pieces(after(w_in[:, :INNER].astype(low_type), *marks), wsh_count)
    out_pieces, marks = gather_pieces(after(w_out.astype(low_type), *marks), wsh_count)
    small = small.astype(full_type)
    ends = [rows_model, rows_model + rows_inner, rows_model + rows_inner + 5 * cols_conv]
    gain_in = small[:, : ends[0]].reshape(-1)
    gain_out = small[:, ends[0] : ends[1]].reshape(1, -1)
    conv = small[:, ends[1] : ends[2]].reshape(wsh_count, 5, cols_conv).transpose(1, 0, 2).reshape(5, CONV_CH)
    head = small[:, ends[2] : ends[2] + 3 * cols_head].reshape(wsh_count, 3, cols_head)
    head = head.transpose(1, 0, 2).reshape(3, HEADS)
    conv = pad_rows(conv, 8)
    head = jnp.pad(head, ((0, 5), (0, LANES - HEADS)))
    tokens_low = inputs[0]
    cot_low = cotangent[0]
    rows = tokens_low.shape[0]
    before = lax.ppermute(tokens_low[rows - HALO :], "seq", [(i, i + 1) for i in range(seq_count - 1)])
    tokens = jnp.concatenate([before, tokens_low], axis=0).astype(full_type)
    inv_rms = lax.rsqrt(jnp.mean(tokens * tokens, axis=-1, keepdims=True) + norm_eps)
    normed_all = (tokens * inv_rms * gain_in).astype(low_type)
    packed, full_sig = multiply_pieces(normed_all, sig_pieces, wsh_count, low_type, "project_signal")
    tokens = tokens[HALO:]
    inv_rms = inv_rms[HALO:]
    normed = normed_all[HALO:]
    normed_t = normed.T
    x, bc, run, lag, run_t, lag_t, enter, enter_all, tail, offs, states, state_in = run_states(packed, conv, head)
    y = run_outputs(x, bc, run, lag_t, enter, states, head)
    gate_vals, full_gate = multiply_pieces(normed, gate_pieces, wsh_count, full_type, "project_gate")
    back, full_out = multiply_back(cot_low, out_pieces, wsh_count, "project_back")
    gain_rows = jnp.broadcast_to(gain_out, (8, INNER))
    normed_out, normed_out_t, grad_y, grad_gate, part_gnorm, grad_state = run_norm(
        y, gate_vals, back, gain_rows, bc, enter_all, state_in
    )
    block_out = (tokens + dot(normed_out, full_out)).astype(low_type)[None]
    grad_normed = dot_nt(grad_gate, full_gate)
    lefts = jnp.concatenate([normed_out_t, normed_t], axis=0)
    grad_pack, edge, last, part_conv, part_skip, part_head, sums_early = run_backward(
        packed, conv, head, grad_y, bc, lag, run_t, enter, tail, offs, states, state_in, grad_state,
        lefts, cot_low, grad_gate,
    )
    edge_next = lax.ppermute(edge, "seq", [(i, i - 1) for i in range(1, seq_count)])
    fixed = jnp.concatenate([last[:8], last[8:] + edge_next], axis=0).astype(low_type)
    grad_pack = lax.dynamic_update_slice(grad_pack, fixed, (rows - 16, 0))
    grad_normed = grad_normed + dot_nt(grad_pack, full_sig)
    scaled = tokens * inv_rms
    part_gpre = jnp.sum(grad_normed * scaled, axis=0)
    pulled = grad_normed * gain_in
    grad_tokens = inv_rms * (pulled - scaled * jnp.mean(pulled * scaled, axis=-1, keepdims=True))
    input_grad = (cot_low.astype(full_type) + grad_tokens)[None]
    skip_sums = part_skip[0].reshape(HEADS, HEAD_DIM).sum(axis=1)
    small_parts = [
        part_gpre, part_gnorm[0], part_conv[:5].reshape(-1), part_head[0, :HEADS], part_head[1, :HEADS], skip_sums
    ]
    small_sums = sum_small(jnp.concatenate(small_parts))
    cuts = [D, D + INNER, D + INNER + 5 * CONV_CH]
    grad_gpre = lax.dynamic_slice_in_dim(small_sums[: cuts[0]], wsh_index * rows_model, rows_model, 0)
    grad_gnorm = lax.dynamic_slice_in_dim(small_sums[cuts[0] : cuts[1]], wsh_index * rows_inner, rows_inner, 0)
    grad_conv = lax.dynamic_slice_in_dim(
        small_sums[cuts[1] : cuts[2]].reshape(5, CONV_CH), wsh_index * cols_conv, cols_conv, 1
    )
    grad_head = lax.dynamic_slice_in_dim(
        small_sums[cuts[2] :].reshape(3, HEADS), wsh_index * cols_head, cols_head, 1
    )
    sums_sig = reduce_rows(normed_t, grad_pack)
    tiles_out = (INNER // D) * (D // TILE)
    sums = jnp.concatenate([sums_early[tiles_out:], sums_sig], axis=0)
    grad_out, *new_out = adam_chunks(
        sums_early, 0, w_out, first_w_out, second_w_out, rate_matrix, weight_decay, "adam_w_out"
    )
    grad_in_w, *new_in = adam_chunks(sums, 0, w_in, first_w_in, second_w_in, rate_matrix, weight_decay, "adam_w_in")
    at_dt = CONV_CH % TILE
    grad_dt = sums_sig[-1, :, at_dt : at_dt + HEADS].astype(full_type)
    params = (w_in, w_dt, w_out, gain_pre, gain_norm, conv_param, head_param)
    gradients = (grad_in_w, grad_dt, grad_out, grad_gpre, grad_gnorm, grad_conv, grad_head)
    firsts = (first_w_in, first_w_dt, first_w_out, first_gain_pre, first_gain_norm, first_conv, first_head)
    seconds = (second_w_in, second_w_dt, second_w_out, second_gain_pre, second_gain_norm, second_conv, second_head)
    step_rates = (rate_matrix, rate_matrix, rate_matrix, rate_gain, rate_gain, rate_conv, rate_head)
    decays = (weight_decay, weight_decay, weight_decay, 0.0, 0.0, 0.0, 0.0)
    updated = [
        None if i in (0, 2) else adam_update(*items)
        for i, items in enumerate(zip(params, gradients, firsts, seconds, step_rates, decays))
    ]
    updated[0], updated[2] = new_in, new_out
    new_params = tuple(entry[0] for entry in updated)
    moments = []
    for entry in updated:
        moments.append(entry[1])
        moments.append(entry[2])
    return (block_out, input_grad) + gradients + new_params + tuple(moments)


def solution(mesh):
    rows, vec, cols = P("wsh", None), P("wsh"), P(None, "wsh")
    tokens = P("wsh", "seq", None)
    params = (rows, rows, rows, vec, vec, cols, cols)
    moments = tuple(spec for spec in params for _ in range(2))
    in_specs = (tokens, tokens) + params + moments
    out_specs = (tokens, tokens) + params + params + moments
    return jax.shard_map(shards, mesh=mesh, in_specs=in_specs, out_specs=out_specs, check_vma=False)
```

```python
import functools

import jax
import jax.numpy as jnp
from jax import lax
from jax.experimental import pallas as pl
from jax.experimental.pallas import tpu as pltpu
from jax.sharding import PartitionSpec as P

D = 1536
HEADS = 48
HEAD_DIM = 64
STATE = 128
CONV_WIDTH = 4
STEP = 2
INNER = 3072
CONV_CH = 3328
BLOCK = 128
LANES = 128
WIDE = 256
HALO = 16
GROUPS = INNER // WIDE
CHAIN_LAG = 2
AHEAD = 6
PACK = CONV_CH + LANES
LOG2E = 1.4426950408889634
VMEM_LIMIT = 56 * 1024 * 1024

norm_eps = 1e-05
beta_one = 0.9
beta_two = 0.999
adam_eps = 1e-08
rate_matrix = 0.01
rate_gain = 0.4
rate_conv = 0.1
rate_head = 1.0
weight_decay = 0.1
highest = lax.Precision.HIGHEST
low_type = jnp.bfloat16
full_type = jnp.float32


def dot(left_side, right_side, dims=((1,), (0,)), precision=None):
    return lax.dot_general(
        left_side, right_side, (dims, ((), ())), precision=precision, preferred_element_type=full_type
    )


def dot_nt(left_side, right_side):
    return dot(left_side, right_side, ((1,), (1,)))


def sigmoid(vals):
    return 0.5 * jnp.tanh(0.5 * vals) + 0.5


def lane_ids(shape):
    return lax.broadcasted_iota(jnp.int32, shape, len(shape) - 1)


def widen(vals, first=0):
    left = lane_ids((vals.shape[0], LANES)) < HEAD_DIM
    pairs = [
        jnp.where(left, vals[:, first + i : first + i + 1], vals[:, first + i + 1 : first + i + 2])
        for i in (0, 2)
    ]
    return jnp.concatenate(pairs, axis=1)


def to_front(vals, step):
    return pltpu.roll(vals, lax.rem(LANES - 4 * step, LANES), 1)


def head_rows(ref, step):
    eight = ref[pl.ds(pl.multiple_of(8 * (step // 2), 8), 8), :]
    return pltpu.roll(eight, 4 * lax.rem(step, 2), 0)


def step_terms(raw, head):
    shifted = raw + head[1:2]
    small = jnp.exp(-jnp.abs(shifted))
    log_part = jnp.where(
        small < 0.01, small * (1.0 - small * (0.5 - small * (1.0 / 3.0))), jnp.log(1.0 + small)
    )
    step_sizes = jnp.maximum(shifted, 0.0) + log_part
    slope = jnp.where(shifted >= 0.0, 1.0, small) / (1.0 + small)
    return step_sizes, slope, -jnp.exp(head[0:1])


def convolve(sig, conv, rows):
    total = conv[4:5] + conv[0:1] * sig[HALO - 3 : HALO - 3 + rows, :]
    for k in range(1, CONV_WIDTH):
        total = total + conv[k : k + 1] * sig[HALO - 3 + k : HALO - 3 + k + rows, :]
    return total


def triangle(lower):
    rows = lax.broadcasted_iota(jnp.int32, (BLOCK, BLOCK), 0)
    cols = lax.broadcasted_iota(jnp.int32, (BLOCK, BLOCK), 1)
    return rows >= cols if lower else rows <= cols


def greet_along():
    z = lax.axis_index("seq")
    seq_count = lax.axis_size("seq")
    barrier = pltpu.get_barrier_semaphore()

    @pl.when(z > 0)
    def _():
        pl.semaphore_signal(barrier, inc=1, device_id={"seq": z - 1}, device_id_type=pl.DeviceIdType.MESH)

    @pl.when(z < seq_count - 1)
    def _():
        pl.semaphore_signal(barrier, inc=1, device_id={"seq": z + 1}, device_id_type=pl.DeviceIdType.MESH)

    pl.semaphore_wait(barrier, jnp.where(z > 0, 1, 0) + jnp.where(z < seq_count - 1, 1, 0))


def states_kernel(
    sig_ref, maps_ref, raw_ref, conv_ref, conv_maps_ref, head_ref,
    x_ref, bc_ref, run_ref, lag_ref, run_t_ref, lag_t_ref, enter_ref, enter_all_ref, tail_ref, offs_ref,
    states_ref, before_ref,
    sig, in_t, ends, stage, land, sems,
):
    step = pl.program_id(0)
    rows = x_ref.shape[0]
    blocks = rows // BLOCK
    z = lax.axis_index("seq")
    seq_count = lax.axis_size("seq")

    def to_next(k):
        return pltpu.make_async_remote_copy(
            src_ref=stage.at[k], dst_ref=land.at[k], send_sem=sems.at[0, k], recv_sem=sems.at[1, k],
            device_id={"seq": z + 1}, device_id_type=pl.DeviceIdType.MESH,
        )

    @pl.when(step == 0)
    def _():
        greet_along()
        sig[...] = maps_ref[...].astype(full_type)
        pre = convolve(sig, conv_maps_ref[...], rows)
        maps = pre * sigmoid(pre)
        bc_ref[...] = maps
        in_t[...] = maps[:, :STATE].T.astype(low_type)
        step_sizes, _, rate = step_terms(raw_ref[HALO:, :].astype(full_type), head_ref[...])
        rates = step_sizes * rate * LOG2E
        log_steps = jnp.log2(step_sizes)
        lower = jnp.where(triangle(True), 1.0, 0.0)
        offset = jnp.zeros((1, LANES), full_type)
        offs_ref[...] = jnp.zeros(offs_ref.shape, full_type)
        for c in range(blocks):
            at = slice(c * BLOCK, (c + 1) * BLOCK)
            run = dot(lower, rates[at], precision=highest)
            lag = run - log_steps[at]
            run_ref[at, :] = run
            lag_ref[at, :] = lag
            run_t_ref[:, at] = run.T
            lag_t_ref[:, at] = lag.T
            enter_ref[at, :] = jnp.exp2(run)
            enter_all_ref[at, :] = jnp.exp2(run + offset)
            tail_ref[at, :] = jnp.exp2(run[BLOCK - 1 : BLOCK] - lag)
            offs_ref[c : c + 1, :] = offset
            offset = offset + run[BLOCK - 1 : BLOCK]
        offs_ref[blocks : blocks + 1, :] = offset

    @pl.when(step < GROUPS)
    def _():
        sig[...] = sig_ref[...].astype(full_type)
        pre = convolve(sig, conv_ref[...], rows)
        x = pre * sigmoid(pre)
        x_ref[...] = x
        tail = to_front(tail_ref[...], step)
        last = to_front(offs_ref[...], step)
        state = jnp.zeros((STATE, WIDE), full_type)
        for c in range(blocks):
            at = slice(c * BLOCK, (c + 1) * BLOCK)
            weighted = (x[at] * widen(tail[at])).astype(low_type)
            fade = jnp.exp2(widen(last[c + 1 : c + 2] - last[c : c + 1]))
            state = state * fade + dot(in_t[:, at], weighted)
            states_ref[c] = state.astype(low_type)
        ends[step] = state

    @pl.when(step >= CHAIN_LAG)
    def _():
        k = step - CHAIN_LAG

        @pl.when(z == 0)
        def _():
            land[k] = jnp.zeros((STATE, WIDE), low_type)

        @pl.when(z > 0)
        def _():
            to_next(k).wait_recv()

        before_ref[...] = land[k]

        @pl.when(z < seq_count - 1)
        def _():
            fade = jnp.exp2(widen(to_front(offs_ref[...], k)[blocks : blocks + 1]))
            stage[k] = (ends[k] + fade * land[k].astype(full_type)).astype(low_type)
            to_next(k).start()

    @pl.when((step == GROUPS + CHAIN_LAG - 1) & (z < seq_count - 1))
    def _():
        for k in range(GROUPS):
            to_next(k).wait_send()


def outputs_kernel(x_ref, bc_ref, run_ref, lag_t_ref, enter_ref, states_ref, head_ref, y_ref, inter):
    step = pl.program_id(0)
    rows = x_ref.shape[0]
    blocks = rows // BLOCK
    lower = triangle(True)

    @pl.when(step == 0)
    def _():
        for c in range(blocks):
            at = slice(c * BLOCK, (c + 1) * BLOCK)
            maps = bc_ref[at, :].astype(low_type)
            inter[c] = dot_nt(maps[:, STATE:], maps[:, :STATE])

    run = to_front(run_ref[...], step)
    enter = to_front(enter_ref[...], step)
    lag_rows = head_rows(lag_t_ref, step)
    skip = widen(to_front(head_ref[...], step)[2:3])
    left = lane_ids((BLOCK, LANES)) < HEAD_DIM
    for c in range(blocks):
        at = slice(c * BLOCK, (c + 1) * BLOCK)
        x = x_ref[at, :]
        parts = []
        for pair in range(2):
            mixes = []
            for i in range(2):
                h = 2 * pair + i
                lag_row = lag_rows[h : h + 1, at]
                power = jnp.where(lower, run[at, h : h + 1] - lag_row, -1e30)
                mixes.append((jnp.exp2(power) * inter[c]).astype(low_type))
            half = x[:, pair * LANES : (pair + 1) * LANES].astype(low_type)
            zero = jnp.zeros_like(half)
            stacked = jnp.concatenate([jnp.where(left, half, zero), jnp.where(left, zero, half)], axis=0)
            parts.append(dot(jnp.concatenate(mixes, axis=1), stacked))
        y = jnp.concatenate(parts, axis=1) + skip * x
        if c > 0:
            out_map = bc_ref[at, STATE:].astype(low_type)
            y = y + widen(enter[at]) * dot(out_map, states_ref[c - 1])
        y_ref[at, :] = y


def norm_kernel(
    y_ref, gate_ref, back_ref, gain_ref, bc_ref, enter_ref, state_ref,
    normed_ref, normed_t_ref, grad_y_ref, grad_gate_ref, grad_gain_ref, grad_state_ref,
    gated, low_y,
):
    step = pl.program_id(0)
    rows = y_ref.shape[0]

    @pl.when(step == 0)
    def _():
        grad_gain_ref[...] = jnp.zeros(grad_gain_ref.shape, full_type)
        grad_state_ref[...] = jnp.zeros(grad_state_ref.shape, full_type)

    out_map = bc_ref[:, STATE:]
    out_low = out_map.astype(low_type)
    out_t = out_map.T.astype(low_type)
    squares = jnp.zeros((rows, WIDE), full_type)
    cross = jnp.zeros((rows, WIDE), full_type)
    for j in range(GROUPS):
        at = slice(j * WIDE, (j + 1) * WIDE)
        enter = widen(enter_ref[...], 4 * j)
        y = y_ref[:, at] + enter * dot(out_low, state_ref[:, at])
        y_low = y.astype(low_type)
        low_y[:, at] = y_low
        gate = gate_ref[:, at]
        vals = y_low.astype(full_type) * (gate * sigmoid(gate))
        gated[:, at] = vals
        squares = squares + vals * vals
        cross = cross + vals * (back_ref[:, at] * gain_ref[0:1, at])
    inv = lax.rsqrt(jnp.sum(squares, axis=1, keepdims=True) * (1.0 / INNER) + norm_eps)
    pull = inv * inv * inv * (jnp.sum(cross, axis=1, keepdims=True) * (1.0 / INNER))
    for j in range(GROUPS):
        at = slice(j * WIDE, (j + 1) * WIDE)
        gain = gain_ref[0:1, at]
        back = back_ref[:, at]
        vals = gated[:, at]
        scaled = vals * inv
        normed = (scaled * gain).astype(low_type)
        normed_ref[:, at] = normed
        normed_t_ref[at, :] = normed.T
        grad_gain_ref[0:1, at] += jnp.sum(back * scaled, axis=0, keepdims=True)
        grad_vals = back * gain * inv - vals * pull
        gate = gate_ref[:, at]
        sig = sigmoid(gate)
        silu = gate * sig
        grad_y = (grad_vals * silu).astype(low_type)
        grad_y_ref[:, at] = grad_y
        slope = sig + silu * (1.0 - sig)
        grad_gate_ref[:, at] = (grad_vals * low_y[:, at].astype(full_type) * slope).astype(low_type)
        enter = widen(enter_ref[...], 4 * j)
        grad_state_ref[:, at] += dot(out_t, (grad_y.astype(full_type) * enter).astype(low_type))


def backward_kernel(
    counts, spans,
    sig_ref, raw_ref, conv_ref, head_ref, grad_y_ref, bc_ref,
    lag_ref, run_t_ref, enter_ref, tail_ref, offs_ref, states_ref, state_in_ref, grad_state_ref,
    lefts_ref, cot_ref, grad_gate_ref, full_gate_ref, full_sig_ref,
    grad_normed_ref, grad_conv_ref, grad_skip_ref, grad_head_ref, sums_ref,
    sig, padded, inter, grad_inter, grad_maps, out_t, run_rows, run_cols, run_ends, weighs,
    stage, land, chain_sems, grad_pack, lasts, edges, edge_land, edge_sems, grad_normed, weights, weight_sems, done_sems,
    *scratch,
):
    place = pl.program_id(0)
    step = place - AHEAD
    steps = GROUPS + 2 + AHEAD
    rows = grad_y_ref.shape[0]
    blocks = rows // BLOCK
    z = lax.axis_index("seq")
    seq_count = counts[1]
    mesh_id = pl.DeviceIdType.MESH
    first_gate, first_sig = spans[1][0], spans[2][0]
    chunks = first_sig + spans[2][1]

    def weight_copies(k):
        slot = lax.rem(k, 2)
        for ref, first, last in ((full_gate_ref, first_gate, first_sig), (full_sig_ref, first_sig, chunks)):
            col = pl.multiple_of(jnp.clip(k - first, 0, last - first - 1) * TILE, LANES)
            copy = pltpu.make_async_copy(ref.at[:, pl.ds(col, TILE)], weights.at[slot], weight_sems.at[slot])
            yield (k >= first) & (k < last), copy

    def beside(k, tile):
        for right, copy in weight_copies(k):
            pl.when(right)(copy.wait)
        for right, copy in weight_copies(k + 1):
            pl.when(right)(copy.start)

        @pl.when(k == first_gate)
        def _():
            grad_normed[...] = dot_nt(tile[...], weights[lax.rem(k, 2)])

        @pl.when(k > first_gate)
        def _():
            grad_normed[...] += dot_nt(tile[...], weights[lax.rem(k, 2)])

    turns, turn, finish = reduce_turns(
        *counts, spans, lefts_ref, [cot_ref, grad_gate_ref, grad_pack], sums_ref, scratch, beside
    )

    def to_previous(k):
        return pltpu.make_async_remote_copy(
            src_ref=stage.at[k], dst_ref=land.at[k], send_sem=chain_sems.at[0, k], recv_sem=chain_sems.at[1, k],
            device_id={"seq": z - 1}, device_id_type=mesh_id,
        )

    def edge_copy(k):
        return pltpu.make_async_remote_copy(
            src_ref=edges.at[k], dst_ref=edge_land.at[k], send_sem=edge_sems.at[0, k], recv_sem=edge_sems.at[1, k],
            device_id={"seq": z - 1}, device_id_type=mesh_id,
        )

    def chain(k):
        @pl.when(z == seq_count - 1)
        def _():
            land[k] = jnp.zeros((STATE, WIDE), low_type)

        @pl.when(z < seq_count - 1)
        def _():
            to_previous(k).wait_recv()

        @pl.when(z > 0)
        def _():
            fade = jnp.exp2(widen(to_front(offs_ref[...], k)[blocks : blocks + 1]))
            own = grad_state_ref[:, pl.ds(pl.multiple_of(k * WIDE, WIDE), WIDE)]
            stage[k] = (own + fade * land[k].astype(full_type)).astype(low_type)
            to_previous(k).start()

    def mend(k):
        @pl.when(z == seq_count - 1)
        def _():
            edge_land[k] = jnp.zeros((8, WIDE), full_type)

        @pl.when(z < seq_count - 1)
        def _():
            edge_copy(k).wait_recv()

        whole = lasts[k] + jnp.concatenate([jnp.zeros((8, WIDE), full_type), edge_land[k]], axis=0)
        grad_pack[rows - 16 :, pl.ds(pl.multiple_of(k * WIDE, WIDE), WIDE)] = whole.astype(low_type)

    @pl.when(place == 0)
    def _():
        greet()

    @pl.when((step >= 1) & (step <= GROUPS + 1))
    def _():
        mend(step - 1)

    early = chunks - 1
    for i in range(spans[2][1] - 1):
        at = next(p for p in range(steps) if (p + 1) * early // steps > first_sig + i)
        assert AHEAD + ((i + 1) * TILE - 1) // WIDE + 1 <= at

    @pl.when(place < steps)
    def _():
        lax.fori_loop(place * early // steps, (place + 1) * early // steps, turn, 0)

    upper = triangle(False)

    @pl.when(place < AHEAD)
    def _():
        for i in range(GROUPS // AHEAD):
            chain(place * (GROUPS // AHEAD) + i)

    @pl.when(place == steps)
    def _():
        lax.fori_loop(early, turns, turn, 0)
        normed_copy = pltpu.make_async_copy(grad_normed, grad_normed_ref, done_sems.at[0])
        normed_copy.start()
        finish()
        normed_copy.wait()

        @pl.when(z > 0)
        def _():
            for k in range(GROUPS):
                to_previous(k).wait_send()
            for k in range(GROUPS + 1):
                edge_copy(k).wait_send()

    @pl.when(step == 0)
    def _():
        for c in range(blocks):
            at = slice(c * BLOCK, (c + 1) * BLOCK)
            maps = bc_ref[at, :].astype(low_type)
            inter[c] = dot_nt(maps[:, :STATE], maps[:, STATE:])
            out_t[:, at] = bc_ref[at, STATE:].T.astype(low_type)
        grad_inter[...] = jnp.zeros(grad_inter.shape, full_type)
        grad_maps[...] = jnp.zeros(grad_maps.shape, full_type)
        run_rows[...] = jnp.zeros(run_rows.shape, full_type)
        run_cols[...] = jnp.zeros(run_cols.shape, full_type)
        run_ends[...] = jnp.zeros(run_ends.shape, full_type)
        weighs[...] = jnp.zeros(weighs.shape, full_type)
        padded[...] = jnp.zeros(padded.shape, full_type)

    def conv_back(grad_pre):
        conv = conv_ref[...]
        grad_sig = conv[3:4] * padded[HALO : HALO + rows, :]
        edge = conv[3:4] * padded[8:HALO, :]
        for k in range(3):
            grad_sig = grad_sig + conv[k : k + 1] * padded[HALO + 3 - k : HALO + 3 - k + rows, :]
            edge = edge + conv[k : k + 1] * padded[11 - k : 19 - k, :]
        grad_pack[:, pl.ds(pl.multiple_of(step * WIDE, WIDE), WIDE)] = grad_sig.astype(low_type)
        lasts[step] = grad_sig[rows - 16 :]

        @pl.when(z > 0)
        def _():
            edges[step] = edge
            edge_copy(step).start()

        sums = [
            jnp.sum(grad_pre * sig[HALO - 3 + k : HALO - 3 + k + rows, :], axis=0, keepdims=True)
            for k in range(CONV_WIDTH)
        ]
        sums.append(jnp.sum(grad_pre, axis=0, keepdims=True))
        sums.append(jnp.zeros((3, WIDE), full_type))
        grad_conv_ref[...] = jnp.concatenate(sums, axis=0)

    @pl.when((step >= 0) & (step < GROUPS))
    def _():
        sig[...] = sig_ref[...].astype(full_type)
        lag = to_front(lag_ref[...], step)
        run_all = head_rows(run_t_ref, step)
        enter = to_front(enter_ref[...], step)
        tail = to_front(tail_ref[...], step)
        offs = to_front(offs_ref[...], step)
        skip = widen(to_front(head_ref[...], step)[2:3])
        left = lane_ids((BLOCK, LANES)) < HEAD_DIM
        heads_of = lax.broadcasted_iota(jnp.int32, (WIDE, LANES), 0) // HEAD_DIM + 4 * step
        picks = jnp.where(heads_of == lane_ids((WIDE, LANES)), 1.0, 0.0).astype(low_type)
        state_in = state_in_ref[...].astype(full_type)
        grad_state = land[step].astype(full_type)
        grad_skip = jnp.zeros((1, WIDE), full_type)
        pre_all = convolve(sig, conv_ref[...], rows)

        def head_sums(vals):
            high = vals.astype(low_type)
            rest = (vals - high.astype(full_type)).astype(low_type)
            return dot(high, picks) + dot(rest, picks)

        for c in reversed(range(blocks)):
            at = slice(c * BLOCK, (c + 1) * BLOCK)
            pre = pre_all[at]
            gate = sigmoid(pre)
            x = pre * gate
            x_low = x.astype(low_type)
            x_round = x_low.astype(full_type)
            grad_y = grad_y_ref[at, :]
            grad_y_full = grad_y.astype(full_type)
            in_map = bc_ref[at, :STATE].astype(low_type)
            out_map = bc_ref[at, STATE:].astype(low_type)
            tail_c = widen(tail[at])
            enter_c = widen(enter[at])
            entering = state_in * jnp.exp2(widen(offs[c : c + 1]))
            if c > 0:
                entering = entering + states_ref[c - 1].astype(full_type)
            leaving = states_ref[c].astype(full_type) + state_in * jnp.exp2(widen(offs[c + 1 : c + 2]))
            entering_low = entering.astype(low_type)
            grad_low = grad_state.astype(low_type)
            ends = jnp.sum(grad_state * leaving, axis=0, keepdims=True)
            run_ends[c : c + 1, :] += head_sums(jnp.concatenate([ends, jnp.zeros((7, WIDE), full_type)], axis=0))[0:1]
            grad_x = tail_c * dot(in_map, grad_low)
            grad_maps[at, :STATE] += dot_nt((x * tail_c).astype(low_type), grad_low)
            swept = grad_y_full * enter_c
            swept_low = swept.astype(low_type)
            through = swept * dot(out_map, entering_low)
            grad_maps[at, STATE:] += dot_nt(swept_low, entering_low)
            fade = jnp.exp2(widen(offs[c + 1 : c + 2] - offs[c : c + 1]))
            grad_state = grad_state * fade + dot(out_t[:, at], swept_low)
            parts = []
            sums = []
            for pair in range(2):
                half = slice(pair * LANES, (pair + 1) * LANES)
                grad_half = grad_y[:, half]
                zero = jnp.zeros_like(grad_half)
                stacked = jnp.concatenate(
                    [jnp.where(left, grad_half, zero), jnp.where(left, zero, grad_half)], axis=0
                )
                cross = dot_nt(x_low[:, half], stacked)
                mixes = []
                for i in range(2):
                    h = 2 * pair + i
                    run_row = run_all[h : h + 1, at]
                    power = jnp.where(upper, run_row - lag[at, h : h + 1], -1e30)
                    decay = jnp.exp2(power)
                    mix = (decay * inter[c]).astype(low_type)
                    mixes.append(mix)
                    cross_h = cross[:, i * LANES : (i + 1) * LANES]
                    grad_inter[c] += cross_h * decay
                    sums.append(jnp.sum(cross_h * mix.astype(full_type), axis=0, keepdims=True))
                parts.append(dot(jnp.concatenate(mixes, axis=1), stacked))
            sums.append(jnp.zeros((4, BLOCK), full_type))
            run_rows[pl.ds(pl.multiple_of(8 * step, 8), 8), at] = jnp.concatenate(sums, axis=0)
            grad_x = grad_x + jnp.concatenate(parts, axis=1)
            weigh = head_sums(x_round * grad_x)
            weighs[at, :] += weigh
            run_cols[at, :] += head_sums(through) - weigh
            grad_skip = grad_skip + jnp.sum(grad_y_full * x, axis=0, keepdims=True)
            grad_x = grad_x + skip * grad_y_full
            padded[HALO + c * BLOCK : HALO + (c + 1) * BLOCK, :] = grad_x * (gate + x * (1.0 - gate))
        grad_skip_ref[...] = jnp.broadcast_to(grad_skip, grad_skip_ref.shape)
        conv_back(padded[HALO : HALO + rows, :])

    @pl.when(step == GROUPS)
    def _():
        sig[...] = sig_ref[...].astype(full_type)
        pre_all = convolve(sig, conv_ref[...], rows)
        for c in range(blocks):
            at = slice(c * BLOCK, (c + 1) * BLOCK)
            maps = bc_ref[at, :].astype(low_type)
            grad_block = grad_inter[c]
            grad_bc = grad_maps[at, :] + jnp.concatenate(
                [
                    dot(grad_block.astype(low_type), maps[:, STATE:]),
                    dot(grad_block.T.astype(low_type), maps[:, :STATE]),
                ],
                axis=1,
            )
            pre = pre_all[at]
            gate = sigmoid(pre)
            padded[HALO + c * BLOCK : HALO + (c + 1) * BLOCK, :] = grad_bc * (gate + pre * gate * (1.0 - gate))
        conv_back(padded[HALO : HALO + rows, :])

    @pl.when(step == GROUPS + 1)
    def _():
        head = head_ref[...]
        step_sizes, slope, rate = step_terms(raw_ref[HALO:, :].astype(full_type), head)
        ratio = jnp.where(step_sizes > 1e-30, slope / jnp.maximum(step_sizes, 1e-30), 1.0)
        used = lane_ids((BLOCK, LANES)) < HEADS
        later = jnp.where(upper, 1.0, 0.0)
        rate_sum = jnp.zeros((1, LANES), full_type)
        bias_sum = jnp.zeros((1, LANES), full_type)
        for c in range(blocks):
            at = slice(c * BLOCK, (c + 1) * BLOCK)
            by_head = [run_rows[8 * j : 8 * j + 4, at] for j in range(GROUPS)]
            by_head.append(jnp.zeros((LANES - HEADS, BLOCK), full_type))
            grad_run = jnp.concatenate(by_head, axis=0).T + run_cols[at, :]
            grad_rates = dot(later, grad_run, precision=highest) + run_ends[c : c + 1, :]
            grad_raw = slope[at] * rate * grad_rates + ratio[at] * weighs[at, :]
            grad_raw = jnp.where(used, grad_raw, 0.0)
            grad_pack[at, CONV_CH:] = grad_raw.astype(low_type)
            rate_sum = rate_sum + jnp.sum(grad_rates * step_sizes[at], axis=0, keepdims=True)
            bias_sum = bias_sum + jnp.sum(grad_raw, axis=0, keepdims=True)
        grad_head_ref[...] = jnp.concatenate(
            [rate_sum * rate, bias_sum, jnp.zeros((6, LANES), full_type)], axis=0
        )


def run_states(packed, conv, head):
    rows = packed.shape[0] - HALO
    blocks = rows // BLOCK
    last = lambda j: jnp.minimum(j, GROUPS - 1)
    whole = lambda shape: pl.BlockSpec(shape, lambda j: (0,) * len(shape))
    small = jax.ShapeDtypeStruct((rows, LANES), full_type)
    small_t = jax.ShapeDtypeStruct((LANES, rows), full_type)
    return pl.pallas_call(
        states_kernel,
        grid=(GROUPS + CHAIN_LAG,),
        in_specs=[
            pl.BlockSpec((rows + HALO, WIDE), lambda j: (0, last(j))),
            pl.BlockSpec((rows + HALO, WIDE), lambda j: (0, GROUPS)),
            pl.BlockSpec((rows + HALO, LANES), lambda j: (0, CONV_CH // LANES)),
            pl.BlockSpec((8, WIDE), lambda j: (0, last(j))),
            pl.BlockSpec((8, WIDE), lambda j: (0, GROUPS)),
            whole((8, LANES)),
        ],
        out_specs=[
            pl.BlockSpec((rows, WIDE), lambda j: (0, last(j))),
            whole((rows, WIDE)),
            whole((rows, LANES)),
            whole((rows, LANES)),
            whole((LANES, rows)),
            whole((LANES, rows)),
            whole((rows, LANES)),
            whole((rows, LANES)),
            whole((rows, LANES)),
            whole((16, LANES)),
            pl.BlockSpec((blocks, STATE, WIDE), lambda j: (0, 0, last(j))),
            pl.BlockSpec((STATE, WIDE), lambda j: (0, jnp.maximum(j - CHAIN_LAG, 0))),
        ],
        out_shape=[
            jax.ShapeDtypeStruct((rows, INNER), full_type),
            jax.ShapeDtypeStruct((rows, WIDE), full_type),
            small, small, small_t, small_t, small, small, small,
            jax.ShapeDtypeStruct((16, LANES), full_type),
            jax.ShapeDtypeStruct((blocks, STATE, INNER), low_type),
            jax.ShapeDtypeStruct((STATE, INNER), low_type),
        ],
        scratch_shapes=[
            pltpu.VMEM((rows + HALO, WIDE), full_type),
            pltpu.VMEM((STATE, rows), low_type),
            pltpu.VMEM((GROUPS, STATE, WIDE), full_type),
            pltpu.VMEM((GROUPS, STATE, WIDE), low_type),
            pltpu.VMEM((GROUPS, STATE, WIDE), low_type),
            pltpu.SemaphoreType.DMA((2, GROUPS)),
        ],
        compiler_params=pltpu.CompilerParams(collective_id=1, has_side_effects=True, vmem_limit_bytes=VMEM_LIMIT),
        cost_estimate=pl.CostEstimate(flops=10**9, bytes_accessed=15 * 10**6, transcendentals=10**6),
        name="scan_states",
    )(packed, packed, packed, conv, conv, head)


def run_outputs(x, bc, run, lag_t, enter, states, head):
    rows = x.shape[0]
    blocks = rows // BLOCK
    whole = lambda shape: pl.BlockSpec(shape, lambda j: (0,) * len(shape))
    return pl.pallas_call(
        outputs_kernel,
        grid=(GROUPS,),
        in_specs=[
            pl.BlockSpec((rows, WIDE), lambda j: (0, j)),
            whole((rows, WIDE)),
            whole((rows, LANES)),
            whole((LANES, rows)),
            whole((rows, LANES)),
            pl.BlockSpec((blocks, STATE, WIDE), lambda j: (0, 0, j)),
            whole((8, LANES)),
        ],
        out_specs=pl.BlockSpec((rows, WIDE), lambda j: (0, j)),
        out_shape=jax.ShapeDtypeStruct((rows, INNER), full_type),
        scratch_shapes=[pltpu.VMEM((blocks, BLOCK, BLOCK), full_type)],
        compiler_params=pltpu.CompilerParams(vmem_limit_bytes=VMEM_LIMIT),
        cost_estimate=pl.CostEstimate(flops=10**10, bytes_accessed=15 * 10**6, transcendentals=3 * 10**6),
        name="scan_outputs",
    )(x, bc, run, lag_t, enter, states, head)


def run_norm(y, gate, back, gain, bc, enter, state):
    rows = y.shape[0]
    part = BLOCK
    by_rows = lambda cols: pl.BlockSpec((part, cols), lambda i: (i, 0))
    whole = lambda shape: pl.BlockSpec(shape, lambda i: (0,) * len(shape))
    return pl.pallas_call(
        norm_kernel,
        grid=(rows // part,),
        in_specs=[
            by_rows(INNER), by_rows(INNER), by_rows(INNER), whole((8, INNER)),
            by_rows(WIDE), by_rows(LANES), whole((STATE, INNER)),
        ],
        out_specs=[
            by_rows(INNER), pl.BlockSpec((INNER, part), lambda i: (0, i)), by_rows(INNER), by_rows(INNER),
            whole((8, INNER)), whole((STATE, INNER)),
        ],
        out_shape=[
            jax.ShapeDtypeStruct((rows, INNER), low_type),
            jax.ShapeDtypeStruct((INNER, rows), low_type),
            jax.ShapeDtypeStruct((rows, INNER), low_type),
            jax.ShapeDtypeStruct((rows, INNER), low_type),
            jax.ShapeDtypeStruct((8, INNER), full_type),
            jax.ShapeDtypeStruct((STATE, INNER), full_type),
        ],
        scratch_shapes=[pltpu.VMEM((part, INNER), full_type), pltpu.VMEM((part, INNER), low_type)],
        compiler_params=pltpu.CompilerParams(vmem_limit_bytes=VMEM_LIMIT),
        cost_estimate=pl.CostEstimate(flops=10**9, bytes_accessed=30 * 10**6, transcendentals=3 * 10**6),
        name="gated_norm",
    )(y, gate, back, gain, bc, enter, state)


def run_backward(
    packed, conv, head, grad_y, bc, lag, run_t, enter, tail, offs, states, state_in, grad_state, lefts, cot, grad_gate,
    full_gate, full_sig,
):
    rows = grad_y.shape[0]
    blocks = rows // BLOCK
    wsh_count, seq_count = lax.axis_size("wsh"), lax.axis_size("seq")
    groups = INNER // D
    n_out, n_gate, n_sig = cot.shape[1] // TILE, grad_gate.shape[1] // TILE, PACK // TILE
    first_gate, first_sig = n_out * groups, n_out * groups + n_gate
    spans = [(0, n_out, groups, 0), (first_gate, n_gate, 1, INNER), (first_sig, n_sig, 1, INNER)]
    chunks = first_sig + n_sig
    anywhere = pl.BlockSpec(memory_space=pl.ANY)
    low_at = lambda j, top: jnp.clip(j - AHEAD, 0, top)
    once = pl.Buffered(1)
    whole = lambda shape: pl.BlockSpec(shape, lambda j: (0,) * len(shape), pipeline_mode=once)
    kept = lambda shape: pl.BlockSpec(shape, lambda j: (0,) * len(shape))
    return pl.pallas_call(
        functools.partial(backward_kernel, (wsh_count, seq_count), spans),
        grid=(GROUPS + 3 + AHEAD,),
        in_specs=[
            pl.BlockSpec((rows + HALO, WIDE), lambda j: (0, low_at(j, GROUPS))),
            pl.BlockSpec((rows + HALO, LANES), lambda j: (0, CONV_CH // LANES), pipeline_mode=once),
            pl.BlockSpec((8, WIDE), lambda j: (0, low_at(j, GROUPS))),
            whole((8, LANES)),
            pl.BlockSpec((rows, WIDE), lambda j: (0, low_at(j, GROUPS - 1))),
            whole((rows, WIDE)),
            whole((rows, LANES)),
            whole((LANES, rows)),
            whole((rows, LANES)),
            whole((rows, LANES)),
            whole((16, LANES)),
            pl.BlockSpec((blocks, STATE, WIDE), lambda j: (0, 0, low_at(j, GROUPS - 1))),
            pl.BlockSpec((STATE, WIDE), lambda j: (0, low_at(j, GROUPS - 1))),
            whole((STATE, INNER)),
            whole(lefts.shape),
            whole(cot.shape),
            whole(grad_gate.shape),
            anywhere,
            anywhere,
        ],
        out_specs=[
            anywhere,
            pl.BlockSpec((8, WIDE), lambda j: (0, low_at(j, GROUPS))),
            pl.BlockSpec((8, WIDE), lambda j: (0, low_at(j, GROUPS - 1))),
            kept((8, LANES)),
            anywhere,
        ],
        out_shape=[
            jax.ShapeDtypeStruct((rows, D), full_type),
            jax.ShapeDtypeStruct((8, CONV_CH), full_type),
            jax.ShapeDtypeStruct((8, INNER), full_type),
            jax.ShapeDtypeStruct((8, LANES), full_type),
            jax.ShapeDtypeStruct((chunks, D // wsh_count, TILE), low_type),
        ],
        scratch_shapes=[
            pltpu.VMEM((rows + HALO, WIDE), full_type),
            pltpu.VMEM((rows + 2 * HALO, WIDE), full_type),
            pltpu.VMEM((blocks, BLOCK, BLOCK), full_type),
            pltpu.VMEM((blocks, BLOCK, BLOCK), full_type),
            pltpu.VMEM((rows, WIDE), full_type),
            pltpu.VMEM((STATE, rows), low_type),
            pltpu.VMEM((LANES, rows), full_type),
            pltpu.VMEM((rows, LANES), full_type),
            pltpu.VMEM((8, LANES), full_type),
            pltpu.VMEM((rows, LANES), full_type),
            pltpu.VMEM((GROUPS, STATE, WIDE), low_type),
            pltpu.VMEM((GROUPS, STATE, WIDE), low_type),
            pltpu.SemaphoreType.DMA((2, GROUPS)),
            pltpu.VMEM((rows, PACK), low_type),
            pltpu.VMEM((GROUPS + 1, 16, WIDE), full_type),
            pltpu.VMEM((GROUPS + 1, 8, WIDE), full_type),
            pltpu.VMEM((GROUPS + 1, 8, WIDE), full_type),
            pltpu.SemaphoreType.DMA((2, GROUPS + 1)),
            pltpu.VMEM((rows, D), full_type),
            pltpu.VMEM((2, D, TILE), low_type),
            pltpu.SemaphoreType.DMA((2,)),
            pltpu.SemaphoreType.DMA((1,)),
            *reduce_scratch(chunks, rows, wsh_count),
        ],
        compiler_params=pltpu.CompilerParams(collective_id=2, has_side_effects=True, vmem_limit_bytes=61 * 1024 * 1024),
        cost_estimate=pl.CostEstimate(flops=10**11, bytes_accessed=20 * 10**6, transcendentals=5 * 10**6),
        name="scan_backward",
    )(
        packed, packed, conv, head, grad_y, bc, lag, run_t, enter, tail, offs, states, state_in, grad_state,
        lefts, cot, grad_gate, full_gate, full_sig,
    )


def adam_update(weights, gradient, first_moment, second_moment, step_rate, decay_amount):
    next_first = beta_one * first_moment + (1.0 - beta_one) * gradient
    next_second = beta_two * second_moment + (1.0 - beta_two) * gradient * gradient
    corrected = (
        next_first
        / (1.0 - beta_one**STEP)
        / (jnp.sqrt(next_second / (1.0 - beta_two**STEP)) + adam_eps)
    )
    return (weights - step_rate * (corrected + decay_amount * weights), next_first, next_second)


def pad_rows(vals, rows):
    return jnp.pad(vals, ((0, rows - vals.shape[0]), (0, 0)))


def swap(vals, bit, axis="wsh"):
    return lax.ppermute(vals, axis, [(i, i ^ bit) for i in range(lax.axis_size(axis))])


def gather_pieces(own, count, also=None):
    rows = own.shape[0]
    far = [1 << b for b in range(1, count.bit_length() - 1)]
    pieces = [(0, 0, own)]
    if len(far) == 2:
        one, two = far
        half = rows // 2
        by_one = swap(own, one)
        by_two = swap(own, two)
        pieces += [(one, 0, by_one), (two, 0, by_two)]
        pieces += [(one | two, 0, swap(by_two[:half], one)), (one | two, half, swap(by_one[half:], two))]
    else:
        for bit in far:
            pieces += [(r ^ bit, first, swap(piece, bit)) for r, first, piece in pieces]
    marks = [piece for _, _, piece in pieces[-2:]]
    return pieces + [(r ^ 1, first, swap(piece, 1)) for r, first, piece in pieces], marks


def piece_kernel(spots, rows, me_ref, left_ref, *refs):
    sources, out_ref, whole_ref = refs[: len(spots)], refs[len(spots)], refs[len(spots) + 1]
    for source, (r, first) in zip(sources, spots):
        start = lax.bitwise_xor(me_ref[0], r) * rows + first
        whole_ref[pl.ds(pl.multiple_of(start, 16), source.shape[0]), :] = source[...]
    out_ref[...] = dot(left_ref[...], whole_ref[...]).astype(out_ref.dtype)


def multiply_pieces(left, pieces, count, out_type, name):
    rows, cols = pieces[0][2].shape
    tile = 512
    me = jnp.reshape(lax.axis_index("wsh"), (1,)).astype(jnp.int32)
    spots = [(r, first) for r, first, _ in pieces]
    return pl.pallas_call(
        functools.partial(piece_kernel, spots, rows),
        grid=(pl.cdiv(cols, tile),),
        in_specs=[pl.BlockSpec(memory_space=pltpu.SMEM), pl.BlockSpec(left.shape, lambda j: (0, 0))]
        + [pl.BlockSpec((piece.shape[0], tile), lambda j: (0, j)) for _, _, piece in pieces],
        out_specs=[
            pl.BlockSpec((left.shape[0], tile), lambda j: (0, j)),
            pl.BlockSpec((rows * count, tile), lambda j: (0, j)),
        ],
        out_shape=[
            jax.ShapeDtypeStruct((left.shape[0], cols), out_type),
            jax.ShapeDtypeStruct((rows * count, cols), low_type),
        ],
        compiler_params=pltpu.CompilerParams(vmem_limit_bytes=VMEM_LIMIT),
        cost_estimate=pl.CostEstimate(
            flops=2 * left.shape[0] * rows * count * cols, bytes_accessed=4 * rows * count * cols, transcendentals=0
        ),
        name=name,
    )(me, left, *[piece for _, _, piece in pieces])


def back_kernel(spots, me_ref, left_ref, *refs):
    sources, out_ref, whole_ref = refs[: len(spots)], refs[len(spots)], refs[len(spots) + 1]
    step = pl.program_id(0)
    for r in sorted({r for r, _ in spots}):

        @pl.when(step == r)
        def _():
            for source, (other, first) in zip(sources, spots):
                if other == r:
                    whole_ref[first : first + source.shape[0], :] = source[...]
            out_ref[...] = dot_nt(left_ref[...], whole_ref[...])


def multiply_back(left, pieces, count, name):
    rows, cols = pieces[0][2].shape
    if rows % LANES:
        whole = jnp.zeros((rows * count, cols), low_type)
        for r, first, piece in pieces:
            start = lax.bitwise_xor(lax.axis_index("wsh"), r) * rows + first
            whole = lax.dynamic_update_slice_in_dim(whole, piece, start, 0)
        return dot_nt(left, whole), whole
    me = jnp.reshape(lax.axis_index("wsh"), (1,)).astype(jnp.int32)
    spots = [(r, first) for r, first, _ in pieces]
    once = pl.Buffered(1)
    grid_spec = pltpu.PrefetchScalarGridSpec(
        num_scalar_prefetch=1,
        grid=(count,),
        in_specs=[pl.BlockSpec(left.shape, lambda j, me: (0, 0), pipeline_mode=once)]
        + [pl.BlockSpec(piece.shape, lambda j, me: (0, 0), pipeline_mode=once) for _, _, piece in pieces],
        out_specs=[
            pl.BlockSpec((left.shape[0], rows), lambda j, me: (0, lax.bitwise_xor(me[0], j))),
            pl.BlockSpec((rows, cols), lambda j, me: (lax.bitwise_xor(me[0], j), 0)),
        ],
    )
    return pl.pallas_call(
        functools.partial(back_kernel, spots),
        grid_spec=grid_spec,
        out_shape=[
            jax.ShapeDtypeStruct((left.shape[0], rows * count), full_type),
            jax.ShapeDtypeStruct((rows * count, cols), low_type),
        ],
        compiler_params=pltpu.CompilerParams(vmem_limit_bytes=VMEM_LIMIT),
        cost_estimate=pl.CostEstimate(
            flops=2 * left.shape[0] * rows * count * cols, bytes_accessed=4 * rows * count * cols, transcendentals=0
        ),
        name=name,
    )(me, left, *[piece for _, _, piece in pieces])


def sum_small(vals):
    for axis in ("wsh", "seq"):
        bit = 1
        while bit < lax.axis_size(axis):
            vals = vals + swap(vals, bit, axis)
            bit = 2 * bit
    return vals


TILE = 384
FAR_LAG = 2
UP_LAG = 1
LAND_SLOTS = 10
SLACK = 1


def part_orders(count):
    far = [b for b in range(count.bit_length() - 2)]
    return [far[p:] + far[:p] for p in range(len(far))]


def held(order, phase, bits):
    done = sum(1 << b for b in order[:phase])
    left = [m for m in range(1 << bits) if m & done == 0]
    bit = 1 << order[phase]
    return [m for m in left if m & bit == 0], [m for m in left if m & bit]


def greet():
    me, z = lax.axis_index("wsh"), lax.axis_index("seq")
    seq_count = lax.axis_size("seq")
    barrier = pltpu.get_barrier_semaphore()
    mesh_id = pl.DeviceIdType.MESH
    bits = lax.axis_size("wsh").bit_length() - 1
    for b in range(bits):
        pl.semaphore_signal(barrier, inc=1, device_id={"wsh": lax.bitwise_xor(me, 1 << b)}, device_id_type=mesh_id)

    @pl.when(z > 0)
    def _():
        pl.semaphore_signal(barrier, inc=1, device_id={"seq": z - 1}, device_id_type=mesh_id)

    @pl.when(z < seq_count - 1)
    def _():
        pl.semaphore_signal(barrier, inc=1, device_id={"seq": z + 1}, device_id_type=mesh_id)

    along = jnp.where(z > 0, 1, 0) + jnp.where(z < seq_count - 1, 1, 0)
    pl.semaphore_wait(barrier, bits + along)


def reduce_turns(wsh_count, seq_count, spans, left_ref, right_refs, out_ref, scratch, beside):
    orders = part_orders(wsh_count)
    bits = len(orders)
    tile, stage, pair, *rest = scratch
    lands, rest = rest[:bits], rest[bits:]
    from_left, from_right, pair_sems, far_sems, seq_sems, out_sems = rest
    chunks, blocks, rows, _ = pair.shape
    slots = lands[0].shape[0]
    part = rows // bits
    me = lax.axis_index("wsh")
    z = lax.axis_index("seq")
    root = seq_count // 2
    mesh_id = pl.DeviceIdType.MESH

    def pair_copy(k):
        return pltpu.make_async_remote_copy(
            src_ref=stage.at[lax.rem(k, 2)], dst_ref=pair.at[k],
            send_sem=pair_sems.at[0, k], recv_sem=pair_sems.at[1, k],
            device_id={"wsh": lax.bitwise_xor(me, 1)}, device_id_type=mesh_id,
        )

    spots = []
    for q in range(bits):
        for p, order in enumerate(orders):
            for i, m in enumerate(held(order, q, bits)[1]):
                spots.append((q, p, i, m, 2 << order[q]))

    def far_copies(k, phase):
        return [
            pltpu.make_async_remote_copy(
                src_ref=pair.at[k, m, pl.ds(p * part, part)], dst_ref=lands[q].at[lax.rem(k, slots), p, i],
                send_sem=far_sems.at[0, n, k], recv_sem=far_sems.at[1, n, k],
                device_id={"wsh": lax.bitwise_xor(me, bit)}, device_id_type=mesh_id,
            )
            for n, (q, p, i, m, bit) in enumerate(spots)
            if q == phase
        ]

    def to_right(k, source):
        return pltpu.make_async_remote_copy(
            src_ref=source, dst_ref=from_left.at[k],
            send_sem=seq_sems.at[0, k], recv_sem=seq_sems.at[1, k],
            device_id={"seq": z + 1}, device_id_type=mesh_id,
        )

    def to_left(k, source):
        return pltpu.make_async_remote_copy(
            src_ref=source, dst_ref=from_right.at[k],
            send_sem=seq_sems.at[2, k], recv_sem=seq_sems.at[3, k],
            device_id={"seq": z - 1}, device_id_type=mesh_id,
        )

    def out_copy(k, source):
        return pltpu.make_async_copy(source, out_ref.at[k], out_sems.at[k])

    def take_tile(k):
        for (start, tiles, groups, _), right_ref in zip(spans, right_refs):

            @pl.when((k >= start) & (k < start + tiles * groups))
            def _():
                col = lax.rem(k - start, tiles) * TILE
                tile[...] = right_ref[:, pl.ds(pl.multiple_of(col, LANES), TILE)]

    def product(k, b, core):
        owner = lax.bitwise_xor(me, 2 * b + core)
        first = jnp.zeros((), jnp.int32)
        for start, tiles, groups, base in spans:
            at = base + (owner * groups + (k - start) // tiles) * rows
            first = jnp.where((k >= start) & (k < start + tiles * groups), at, first)
        return dot(left_ref[pl.ds(pl.multiple_of(first, 16), rows), :], tile[...])

    def begin(k):
        @pl.when(k >= 2)
        def _():
            pair_copy(k - 2).wait_send()

        take_tile(k)
        for b in range(blocks):
            stage[lax.rem(k, 2), b] = product(k, b, 1).astype(low_type)
        pair_copy(k).start()
        beside(k, tile)

    def add_pair(k):
        take_tile(k)
        pair_copy(k).wait_recv()
        for b in range(blocks):
            pair[k, b] = (product(k, b, 0) + pair[k, b].astype(full_type)).astype(low_type)
        for copy in far_copies(k, 0):
            copy.start()

    def add_far(k, phase):
        for copy in far_copies(k, phase):
            copy.wait_recv()
        for p, order in enumerate(orders):
            at = pl.ds(p * part, part)
            for i, m in enumerate(held(order, phase, bits)[0]):
                total = pair[k, m, at].astype(full_type) + lands[phase][lax.rem(k, slots), p, i].astype(full_type)
                pair[k, m, at] = total.astype(low_type)
        if phase < bits - 1:
            for copy in far_copies(k, phase + 1):
                copy.start()

    def add_to(k, land):
        pair[k, 0] = (pair[k, 0].astype(full_type) + land[k].astype(full_type)).astype(low_type)

    def seq_up(k):
        mine = pair.at[k, 0]

        @pl.when((z > 0) & (z <= root))
        def _():
            to_right(k, mine).wait_recv()
            add_to(k, from_left)

        @pl.when((z < seq_count - 1) & (z >= root))
        def _():
            to_left(k, mine).wait_recv()
            add_to(k, from_right)

        @pl.when((z < seq_count - 1) & (z <= root))
        def _():
            to_right(k, mine).start()

        @pl.when((z > 0) & (z >= root))
        def _():
            to_left(k, mine).start()

    def seq_down(k):
        @pl.when(z == root)
        def _():
            out_copy(k, pair.at[k, 0]).start()

        @pl.when(z < root)
        def _():
            to_left(k, from_right.at[k]).wait_recv()
            out_copy(k, from_right.at[k]).start()
            pl.when(z > 0)(lambda: to_left(k, from_right.at[k]).start())

        @pl.when(z > root)
        def _():
            to_right(k, from_left.at[k]).wait_recv()
            out_copy(k, from_left.at[k]).start()
            pl.when(z < seq_count - 1)(lambda: to_right(k, from_left.at[k]).start())

    far = jnp.abs(z - root)
    farthest = max(root, seq_count - 1 - root)
    stages = [(0, begin), (1, add_pair)] + [
        (1 + FAR_LAG * (q + 1), functools.partial(add_far, phase=q)) for q in range(bits)
    ]
    up_at = 1 + FAR_LAG * bits + UP_LAG
    stages += [(up_at + SLACK * (farthest - far), seq_up), (up_at + 1 + SLACK * (farthest + far), seq_down)]
    turns = chunks + up_at + 2 + SLACK * 2 * farthest

    def turn(s, carry):
        for offset, run in stages:
            pl.when((s >= offset) & (s < chunks + offset))(lambda run=run, offset=offset: run(s - offset))
        return carry

    def finish():
        def wait_all(k, carry):
            for q in range(bits):
                for copy in far_copies(k, q):
                    copy.wait_send()
            pl.when(z < seq_count - 1)(lambda: to_right(k, pair.at[k, 0]).wait_send())
            pl.when(z > 0)(lambda: to_left(k, pair.at[k, 0]).wait_send())
            out_copy(k, pair.at[k, 0]).wait()
            return carry

        lax.fori_loop(0, chunks, wait_all, 0)
        for k in (chunks - 2, chunks - 1):
            pair_copy(k).wait_send()

    return turns, turn, finish


def reduce_scratch(chunks, depth, wsh_count):
    rows = D // wsh_count
    bits = len(part_orders(wsh_count))
    low = lambda *shape: pltpu.VMEM(shape, low_type)
    dma = pltpu.SemaphoreType.DMA
    return [
        low(depth, TILE),
        low(2, 1 << bits, rows, TILE),
        low(chunks, 1 << bits, rows, TILE),
        *[low(min(chunks, LAND_SLOTS), bits, 1 << (bits - 1 - q), rows // bits, TILE) for q in range(bits)],
        low(chunks, rows, TILE),
        low(chunks, rows, TILE),
        dma((2, chunks)),
        dma((2, bits * ((1 << bits) - 1), chunks)),
        dma((4, chunks)),
        dma((chunks,)),
    ]


def adam_kernel(start, rate, decay, *refs):
    share_ref, weight_ref, first_ref, second_ref, grad_ref, next_ref, next_first_ref, next_second_ref = refs
    grad = share_ref[0].astype(full_type)
    grad_ref[...] = grad
    next_ref[...], next_first_ref[...], next_second_ref[...] = adam_update(
        weight_ref[...], grad, first_ref[...], second_ref[...], rate, decay
    )


def adam_chunks(sums, start, weights, first_moment, second_moment, rate, decay, name):
    all_rows, cols = weights.shape
    rows = sums.shape[1]
    tiles = pl.cdiv(cols, TILE)
    block = pl.BlockSpec((rows, TILE), lambda i, j: (i, j))
    return pl.pallas_call(
        functools.partial(adam_kernel, start, rate, decay),
        grid=(all_rows // rows, tiles),
        in_specs=[pl.BlockSpec((1, rows, TILE), lambda i, j: (start + i * tiles + j, 0, 0))] + [block] * 3,
        out_specs=[block] * 4,
        out_shape=[jax.ShapeDtypeStruct(weights.shape, full_type)] * 4,
        compiler_params=pltpu.CompilerParams(vmem_limit_bytes=VMEM_LIMIT),
        cost_estimate=pl.CostEstimate(
            flops=20 * weights.size, bytes_accessed=30 * weights.size, transcendentals=weights.size
        ),
        name=name,
    )(sums, weights, first_moment, second_moment)


def after(vals, *others):
    return lax.optimization_barrier((vals,) + others)[0]


def shards(
    inputs, cotangent, w_in, w_dt, w_out, gain_pre, gain_norm, conv_param, head_param,
    first_w_in, second_w_in, first_w_dt, second_w_dt, first_w_out, second_w_out,
    first_gain_pre, second_gain_pre, first_gain_norm, second_gain_norm,
    first_conv, second_conv, first_head, second_head,
):
    wsh_count = lax.axis_size("wsh")
    seq_count = lax.axis_size("seq")
    seq_index = lax.axis_index("seq")
    wsh_index = lax.axis_index("wsh")
    rows_model = D // wsh_count
    rows_inner = INNER // wsh_count
    cols_conv = CONV_CH // wsh_count
    cols_head = HEADS // wsh_count
    flat = jnp.concatenate(
        [gain_pre, gain_norm, conv_param.reshape(-1), head_param.reshape(-1)]
    ).astype(low_type)
    count = flat.shape[0]
    flat = jnp.pad(flat, (0, -count % LANES))
    part_sig = jnp.concatenate(
        [w_in[:, INNER:].astype(low_type), w_dt.astype(low_type), jnp.zeros((rows_model, LANES - HEADS), low_type)],
        axis=1,
    )
    small = lax.all_gather(flat, "wsh", axis=0)
    part_sig = after(part_sig, small)
    sig_pieces, marks = gather_pieces(part_sig, wsh_count)
    gate_pieces, marks = gather_pieces(after(w_in[:, :INNER].astype(low_type), *marks), wsh_count)
    out_pieces, marks = gather_pieces(after(w_out.astype(low_type), *marks), wsh_count)
    small = small.astype(full_type)
    ends = [rows_model, rows_model + rows_inner, rows_model + rows_inner + 5 * cols_conv]
    gain_in = small[:, : ends[0]].reshape(-1)
    gain_out = small[:, ends[0] : ends[1]].reshape(1, -1)
    conv = small[:, ends[1] : ends[2]].reshape(wsh_count, 5, cols_conv).transpose(1, 0, 2).reshape(5, CONV_CH)
    head = small[:, ends[2] : ends[2] + 3 * cols_head].reshape(wsh_count, 3, cols_head)
    head = head.transpose(1, 0, 2).reshape(3, HEADS)
    conv = pad_rows(conv, 8)
    head = jnp.pad(head, ((0, 5), (0, LANES - HEADS)))
    tokens_low = inputs[0]
    cot_low = cotangent[0]
    rows = tokens_low.shape[0]
    before = lax.ppermute(tokens_low[rows - HALO :], "seq", [(i, i + 1) for i in range(seq_count - 1)])
    tokens = jnp.concatenate([before, tokens_low], axis=0).astype(full_type)
    inv_rms = lax.rsqrt(jnp.mean(tokens * tokens, axis=-1, keepdims=True) + norm_eps)
    normed_all = (tokens * inv_rms * gain_in).astype(low_type)
    packed, full_sig = multiply_pieces(normed_all, sig_pieces, wsh_count, low_type, "project_signal")
    tokens = tokens[HALO:]
    inv_rms = inv_rms[HALO:]
    normed = normed_all[HALO:]
    normed_t = normed.T
    x, bc, run, lag, run_t, lag_t, enter, enter_all, tail, offs, states, state_in = run_states(packed, conv, head)
    y = run_outputs(x, bc, run, lag_t, enter, states, head)
    gate_vals, full_gate = multiply_pieces(normed, gate_pieces, wsh_count, full_type, "project_gate")
    back, full_out = multiply_back(cot_low, out_pieces, wsh_count, "project_back")
    gain_rows = jnp.broadcast_to(gain_out, (8, INNER))
    normed_out, normed_out_t, grad_y, grad_gate, part_gnorm, grad_state = run_norm(
        y, gate_vals, back, gain_rows, bc, enter_all, state_in
    )
    block_out = (tokens + dot(normed_out, full_out)).astype(low_type)[None]
    lefts = jnp.concatenate([normed_out_t, normed_t], axis=0)
    grad_normed, part_conv, part_skip, part_head, sums = run_backward(
        packed, conv, head, grad_y, bc, lag, run_t, enter, tail, offs, states, state_in, grad_state,
        lefts, cot_low, grad_gate, full_gate, full_sig,
    )
    scaled = tokens * inv_rms
    part_gpre = jnp.sum(grad_normed * scaled, axis=0)
    pulled = grad_normed * gain_in
    grad_tokens = inv_rms * (pulled - scaled * jnp.mean(pulled * scaled, axis=-1, keepdims=True))
    input_grad = (cot_low.astype(full_type) + grad_tokens)[None]
    skip_sums = part_skip[0].reshape(HEADS, HEAD_DIM).sum(axis=1)
    small_parts = [
        part_gpre, part_gnorm[0], part_conv[:5].reshape(-1), part_head[0, :HEADS], part_head[1, :HEADS], skip_sums
    ]
    small_sums = sum_small(jnp.concatenate(small_parts))
    cuts = [D, D + INNER, D + INNER + 5 * CONV_CH]
    grad_gpre = lax.dynamic_slice_in_dim(small_sums[: cuts[0]], wsh_index * rows_model, rows_model, 0)
    grad_gnorm = lax.dynamic_slice_in_dim(small_sums[cuts[0] : cuts[1]], wsh_index * rows_inner, rows_inner, 0)
    grad_conv = lax.dynamic_slice_in_dim(
        small_sums[cuts[1] : cuts[2]].reshape(5, CONV_CH), wsh_index * cols_conv, cols_conv, 1
    )
    grad_head = lax.dynamic_slice_in_dim(
        small_sums[cuts[2] :].reshape(3, HEADS), wsh_index * cols_head, cols_head, 1
    )
    tiles_out = (INNER // D) * (D // TILE)
    grad_out, *new_out = adam_chunks(sums, 0, w_out, first_w_out, second_w_out, rate_matrix, weight_decay, "adam_w_out")
    grad_in_w, *new_in = adam_chunks(
        sums, tiles_out, w_in, first_w_in, second_w_in, rate_matrix, weight_decay, "adam_w_in"
    )
    at_dt = CONV_CH % TILE
    grad_dt = sums[-1, :, at_dt : at_dt + HEADS].astype(full_type)
    params = (w_in, w_dt, w_out, gain_pre, gain_norm, conv_param, head_param)
    gradients = (grad_in_w, grad_dt, grad_out, grad_gpre, grad_gnorm, grad_conv, grad_head)
    firsts = (first_w_in, first_w_dt, first_w_out, first_gain_pre, first_gain_norm, first_conv, first_head)
    seconds = (second_w_in, second_w_dt, second_w_out, second_gain_pre, second_gain_norm, second_conv, second_head)
    step_rates = (rate_matrix, rate_matrix, rate_matrix, rate_gain, rate_gain, rate_conv, rate_head)
    decays = (weight_decay, weight_decay, weight_decay, 0.0, 0.0, 0.0, 0.0)
    updated = [
        None if i in (0, 2) else adam_update(*items)
        for i, items in enumerate(zip(params, gradients, firsts, seconds, step_rates, decays))
    ]
    updated[0], updated[2] = new_in, new_out
    new_params = tuple(entry[0] for entry in updated)
    moments = []
    for entry in updated:
        moments.append(entry[1])
        moments.append(entry[2])
    return (block_out, input_grad) + gradients + new_params + tuple(moments)


def solution(mesh):
    rows, vec, cols = P("wsh", None), P("wsh"), P(None, "wsh")
    tokens = P("wsh", "seq", None)
    params = (rows, rows, rows, vec, vec, cols, cols)
    moments = tuple(spec for spec in params for _ in range(2))
    in_specs = (tokens, tokens) + params + moments
    out_specs = (tokens, tokens) + params + params + moments
    return jax.shard_map(shards, mesh=mesh, in_specs=in_specs, out_specs=out_specs, check_vma=False)
```

```python
import functools

import jax
import jax.numpy as jnp
from jax import lax
from jax.experimental import pallas as pl
from jax.experimental.pallas import tpu as pltpu
from jax.sharding import PartitionSpec as P

D = 1536
HEADS = 48
HEAD_DIM = 64
STATE = 128
CONV_WIDTH = 4
STEP = 2
INNER = 3072
CONV_CH = 3328
BLOCK = 128
LANES = 128
WIDE = 256
HALO = 16
GROUPS = INNER // WIDE
CHAIN_LAG = 2
AHEAD = 6
PACK = CONV_CH + LANES
LOG2E = 1.4426950408889634
VMEM_LIMIT = 56 * 1024 * 1024

norm_eps = 1e-05
beta_one = 0.9
beta_two = 0.999
adam_eps = 1e-08
rate_matrix = 0.01
rate_gain = 0.4
rate_conv = 0.1
rate_head = 1.0
weight_decay = 0.1
highest = lax.Precision.HIGHEST
low_type = jnp.bfloat16
full_type = jnp.float32


def dot(left_side, right_side, dims=((1,), (0,)), precision=None):
    return lax.dot_general(
        left_side, right_side, (dims, ((), ())), precision=precision, preferred_element_type=full_type
    )


def dot_nt(left_side, right_side):
    return dot(left_side, right_side, ((1,), (1,)))


def sigmoid(vals):
    return 0.5 * jnp.tanh(0.5 * vals) + 0.5


def lane_ids(shape):
    return lax.broadcasted_iota(jnp.int32, shape, len(shape) - 1)


def widen(vals, first=0):
    left = lane_ids((vals.shape[0], LANES)) < HEAD_DIM
    pairs = [
        jnp.where(left, vals[:, first + i : first + i + 1], vals[:, first + i + 1 : first + i + 2])
        for i in (0, 2)
    ]
    return jnp.concatenate(pairs, axis=1)


def to_front(vals, step):
    return pltpu.roll(vals, lax.rem(LANES - 4 * step, LANES), 1)


def head_rows(ref, step):
    eight = ref[pl.ds(pl.multiple_of(8 * (step // 2), 8), 8), :]
    return pltpu.roll(eight, 4 * lax.rem(step, 2), 0)


def step_terms(raw, head):
    shifted = raw + head[1:2]
    small = jnp.exp(-jnp.abs(shifted))
    log_part = jnp.where(
        small < 0.01, small * (1.0 - small * (0.5 - small * (1.0 / 3.0))), jnp.log(1.0 + small)
    )
    step_sizes = jnp.maximum(shifted, 0.0) + log_part
    slope = jnp.where(shifted >= 0.0, 1.0, small) / (1.0 + small)
    return step_sizes, slope, -jnp.exp(head[0:1])


def convolve(sig, conv, rows):
    total = conv[4:5] + conv[0:1] * sig[HALO - 3 : HALO - 3 + rows, :]
    for k in range(1, CONV_WIDTH):
        total = total + conv[k : k + 1] * sig[HALO - 3 + k : HALO - 3 + k + rows, :]
    return total


def triangle(lower):
    rows = lax.broadcasted_iota(jnp.int32, (BLOCK, BLOCK), 0)
    cols = lax.broadcasted_iota(jnp.int32, (BLOCK, BLOCK), 1)
    return rows >= cols if lower else rows <= cols


def gather_steps(count, own_ref, full_ref, far_sems, core_sems):
    orders = part_orders(count)
    bits = len(orders)
    rows = own_ref.shape[0]
    part = rows // bits
    me = lax.axis_index("wsh")
    mesh_id = pl.DeviceIdType.MESH

    def copy(m, first, size, bit, sems, n):
        start = lax.bitwise_xor(me, 2 * m) * rows + first
        at = full_ref.at[pl.ds(pl.multiple_of(start, 16), size)]
        return pltpu.make_async_remote_copy(
            src_ref=at, dst_ref=at, send_sem=sems.at[0, n], recv_sem=sems.at[1, n],
            device_id={"wsh": lax.bitwise_xor(me, bit)}, device_id_type=mesh_id,
        )

    far_spots = [
        (q, m, p * part, part, 2 << order[q])
        for q in range(bits)
        for p, order in enumerate(orders)
        for m in range(1 << bits)
        if m & ~sum(1 << b for b in order[:q]) == 0
    ]
    core_spots = [(0, 0, 0, rows, 1)] + [
        (q + 1, m, p * part, part, 1)
        for q in range(bits)
        for p, order in enumerate(orders)
        for m in range(1 << bits)
        if m >> order[q] & 1 and m & ~sum(1 << b for b in order[: q + 1]) == 0
    ]
    pick = lambda spots, sems, phase: [
        copy(m, first, size, bit, sems, n)
        for n, (q, m, first, size, bit) in enumerate(spots)
        if phase is None or q == phase
    ]

    def start():
        full_ref[pl.ds(pl.multiple_of(me * rows, 16), rows), :] = own_ref[...]
        for item in pick(far_spots, far_sems, 0) + pick(core_spots, core_sems, 0):
            item.start()

    def advance(phase):
        for item in pick(far_spots, far_sems, phase):
            item.wait_recv()
        later = pick(far_spots, far_sems, phase + 1) if phase + 1 < bits else []
        for item in later + pick(core_spots, core_sems, phase + 1):
            item.start()

    def done():
        for item in pick(core_spots, core_sems, None):
            item.wait_recv()

    def finish():
        for item in pick(far_spots, far_sems, None) + pick(core_spots, core_sems, None):
            item.wait_send()

    return start, advance, done, finish


def gather_sems(count):
    bits = len(part_orders(count))
    copies = bits * ((1 << bits) - 1)
    return [pltpu.SemaphoreType.DMA((2, copies)), pltpu.SemaphoreType.DMA((2, copies + 1))]


def forward_kernel(
    count,
    sig_ref, maps_ref, raw_ref, conv_ref, conv_maps_ref, head_ref, normed_ref, cot_ref, gate_own_ref, out_own_ref,
    y_ref, bc_ref, lag_ref, run_t_ref, enter_ref, enter_all_ref, tail_ref, offs_ref, states_ref, before_ref,
    gate_ref, back_ref, full_gate_ref, full_out_ref,
    sig, in_t, inter, run, lag_t, ends, stage, land, sems, gate_full, out_full,
    gate_far, gate_core, out_far, out_core, full_sems,
):
    step = pl.program_id(0)
    rows = y_ref.shape[0]
    blocks = rows // BLOCK
    z = lax.axis_index("seq")
    seq_count = lax.axis_size("seq")
    lower = triangle(True)
    bits = len(part_orders(count))
    gate_start, gate_advance, gate_done, gate_finish = gather_steps(count, gate_own_ref, gate_full, gate_far, gate_core)
    out_start, out_advance, out_done, out_finish = gather_steps(count, out_own_ref, out_full, out_far, out_core)
    gate_at, back_at = GROUPS + CHAIN_LAG, 2 * GROUPS + CHAIN_LAG

    def to_next(k):
        return pltpu.make_async_remote_copy(
            src_ref=stage.at[k], dst_ref=land.at[k], send_sem=sems.at[0, k], recv_sem=sems.at[1, k],
            device_id={"seq": z + 1}, device_id_type=pl.DeviceIdType.MESH,
        )

    @pl.when(step == 0)
    def _():
        greet()
        gate_start()
        out_start()
        sig[...] = maps_ref[...].astype(full_type)
        pre = convolve(sig, conv_maps_ref[...], rows)
        maps = pre * sigmoid(pre)
        bc_ref[...] = maps
        in_t[...] = maps[:, :STATE].T.astype(low_type)
        step_sizes, _, rate = step_terms(raw_ref[HALO:, :].astype(full_type), head_ref[...])
        rates = step_sizes * rate * LOG2E
        log_steps = jnp.log2(step_sizes)
        sums = jnp.where(lower, 1.0, 0.0)
        offset = jnp.zeros((1, LANES), full_type)
        offs_ref[...] = jnp.zeros(offs_ref.shape, full_type)
        for c in range(blocks):
            at = slice(c * BLOCK, (c + 1) * BLOCK)
            total = dot(sums, rates[at], precision=highest)
            lag = total - log_steps[at]
            run[at, :] = total
            lag_ref[at, :] = lag
            run_t_ref[:, at] = total.T
            lag_t[:, at] = lag.T
            enter_ref[at, :] = jnp.exp2(total)
            enter_all_ref[at, :] = jnp.exp2(total + offset)
            tail_ref[at, :] = jnp.exp2(total[BLOCK - 1 : BLOCK] - lag)
            offs_ref[c : c + 1, :] = offset
            offset = offset + total[BLOCK - 1 : BLOCK]
            low_maps = maps[at].astype(low_type)
            inter[c] = dot_nt(low_maps[:, STATE:], low_maps[:, :STATE])
        offs_ref[blocks : blocks + 1, :] = offset

    pl.when(step == GROUPS // 2)(lambda: gate_advance(0))
    pl.when(step == GROUPS)(lambda: out_advance(0))

    @pl.when(step < GROUPS)
    def _():
        sig[...] = sig_ref[...].astype(full_type)
        pre_all = convolve(sig, conv_ref[...], rows)
        tail = to_front(tail_ref[...], step)
        last = to_front(offs_ref[...], step)
        run_all = to_front(run[...], step)
        enter = to_front(enter_ref[...], step)
        lag_rows = head_rows(lag_t, step)
        skip = widen(to_front(head_ref[...], step)[2:3])
        left = lane_ids((BLOCK, LANES)) < HEAD_DIM
        state = jnp.zeros((STATE, WIDE), full_type)
        for c in range(blocks):
            at = slice(c * BLOCK, (c + 1) * BLOCK)
            pre = pre_all[at]
            x = pre * sigmoid(pre)
            parts = []
            for pair in range(2):
                mixes = []
                for i in range(2):
                    h = 2 * pair + i
                    power = jnp.where(lower, run_all[at, h : h + 1] - lag_rows[h : h + 1, at], -1e30)
                    mixes.append((jnp.exp2(power) * inter[c]).astype(low_type))
                half = x[:, pair * LANES : (pair + 1) * LANES].astype(low_type)
                zero = jnp.zeros_like(half)
                stacked = jnp.concatenate([jnp.where(left, half, zero), jnp.where(left, zero, half)], axis=0)
                parts.append(dot(jnp.concatenate(mixes, axis=1), stacked))
            y = jnp.concatenate(parts, axis=1) + skip * x
            if c > 0:
                out_map = bc_ref[at, STATE:].astype(low_type)
                y = y + widen(enter[at]) * dot(out_map, state.astype(low_type))
            y_ref[at, :] = y
            weighted = (x * widen(tail[at])).astype(low_type)
            fade = jnp.exp2(widen(last[c + 1 : c + 2] - last[c : c + 1]))
            state = state * fade + dot(in_t[:, at], weighted)
            states_ref[c] = state.astype(low_type)
        ends[step] = state

    @pl.when((step >= CHAIN_LAG) & (step < gate_at))
    def _():
        k = step - CHAIN_LAG

        @pl.when(z == 0)
        def _():
            land[k] = jnp.zeros((STATE, WIDE), low_type)

        @pl.when(z > 0)
        def _():
            to_next(k).wait_recv()

        before_ref[...] = land[k]

        @pl.when(z < seq_count - 1)
        def _():
            fade = jnp.exp2(widen(to_front(offs_ref[...], k)[blocks : blocks + 1]))
            stage[k] = (ends[k] + fade * land[k].astype(full_type)).astype(low_type)
            to_next(k).start()

    gate_out = pltpu.make_async_copy(gate_full, full_gate_ref, full_sems.at[0])
    out_out = pltpu.make_async_copy(out_full, full_out_ref, full_sems.at[1])

    @pl.when(step == gate_at)
    def _():
        for q in range(1, bits):
            gate_advance(q)
        gate_done()
        gate_out.start()

    @pl.when((step >= gate_at) & (step < back_at))
    def _():
        col = pl.multiple_of((step - gate_at) * WIDE, WIDE)
        gate_ref[...] = dot(normed_ref[...], gate_full[:, pl.ds(col, WIDE)])

    @pl.when(step == back_at)
    def _():
        for q in range(1, bits):
            out_advance(q)
        out_done()
        out_out.start()

    @pl.when(step >= back_at)
    def _():
        row = pl.multiple_of((step - back_at) * WIDE, WIDE)
        back_ref[...] = dot_nt(cot_ref[...], out_full[pl.ds(row, WIDE), :])

    @pl.when(step == back_at + GROUPS - 1)
    def _():
        gate_finish()
        out_finish()
        gate_out.wait()
        out_out.wait()

        @pl.when(z < seq_count - 1)
        def _():
            for k in range(GROUPS):
                to_next(k).wait_send()


def norm_kernel(
    y_ref, gate_ref, back_ref, gain_ref, bc_ref, enter_ref, state_ref,
    normed_ref, normed_t_ref, grad_y_ref, grad_gate_ref, grad_gain_ref, grad_state_ref,
    gated, low_y,
):
    step = pl.program_id(0)
    rows = y_ref.shape[0]

    @pl.when(step == 0)
    def _():
        grad_gain_ref[...] = jnp.zeros(grad_gain_ref.shape, full_type)
        grad_state_ref[...] = jnp.zeros(grad_state_ref.shape, full_type)

    out_map = bc_ref[:, STATE:]
    out_low = out_map.astype(low_type)
    out_t = out_map.T.astype(low_type)
    squares = jnp.zeros((rows, WIDE), full_type)
    cross = jnp.zeros((rows, WIDE), full_type)
    for j in range(GROUPS):
        at = slice(j * WIDE, (j + 1) * WIDE)
        enter = widen(enter_ref[...], 4 * j)
        y = y_ref[:, at] + enter * dot(out_low, state_ref[:, at])
        y_low = y.astype(low_type)
        low_y[:, at] = y_low
        gate = gate_ref[:, at]
        vals = y_low.astype(full_type) * (gate * sigmoid(gate))
        gated[:, at] = vals
        squares = squares + vals * vals
        cross = cross + vals * (back_ref[:, at] * gain_ref[0:1, at])
    inv = lax.rsqrt(jnp.sum(squares, axis=1, keepdims=True) * (1.0 / INNER) + norm_eps)
    pull = inv * inv * inv * (jnp.sum(cross, axis=1, keepdims=True) * (1.0 / INNER))
    for j in range(GROUPS):
        at = slice(j * WIDE, (j + 1) * WIDE)
        gain = gain_ref[0:1, at]
        back = back_ref[:, at]
        vals = gated[:, at]
        scaled = vals * inv
        normed = (scaled * gain).astype(low_type)
        normed_ref[:, at] = normed
        normed_t_ref[at, :] = normed.T
        grad_gain_ref[0:1, at] += jnp.sum(back * scaled, axis=0, keepdims=True)
        grad_vals = back * gain * inv - vals * pull
        gate = gate_ref[:, at]
        sig = sigmoid(gate)
        silu = gate * sig
        grad_y = (grad_vals * silu).astype(low_type)
        grad_y_ref[:, at] = grad_y
        slope = sig + silu * (1.0 - sig)
        grad_gate_ref[:, at] = (grad_vals * low_y[:, at].astype(full_type) * slope).astype(low_type)
        enter = widen(enter_ref[...], 4 * j)
        grad_state_ref[:, at] += dot(out_t, (grad_y.astype(full_type) * enter).astype(low_type))


def backward_kernel(
    counts, spans,
    sig_ref, raw_ref, conv_ref, head_ref, grad_y_ref, bc_ref,
    lag_ref, run_t_ref, enter_ref, tail_ref, offs_ref, states_ref, state_in_ref, grad_state_ref,
    lefts_ref, cot_ref, grad_gate_ref, full_gate_ref, full_sig_ref,
    grad_normed_ref, grad_conv_ref, grad_skip_ref, grad_head_ref, sums_ref,
    sig, padded, inter, grad_inter, grad_maps, out_t, run_rows, run_cols, run_ends, weighs,
    stage, land, chain_sems, grad_pack, lasts, edges, edge_land, edge_sems, grad_normed, weights, weight_sems, done_sems,
    *scratch,
):
    place = pl.program_id(0)
    step = place - AHEAD
    steps = GROUPS + 2 + AHEAD
    rows = grad_y_ref.shape[0]
    blocks = rows // BLOCK
    z = lax.axis_index("seq")
    seq_count = counts[1]
    mesh_id = pl.DeviceIdType.MESH
    first_gate, first_sig = spans[1][0], spans[2][0]
    chunks = first_sig + spans[2][1]

    def weight_copies(k):
        slot = lax.rem(k, 2)
        for ref, first, last in ((full_gate_ref, first_gate, first_sig), (full_sig_ref, first_sig, chunks)):
            col = pl.multiple_of(jnp.clip(k - first, 0, last - first - 1) * TILE, LANES)
            copy = pltpu.make_async_copy(ref.at[:, pl.ds(col, TILE)], weights.at[slot], weight_sems.at[slot])
            yield (k >= first) & (k < last), copy

    def beside(k, tile):
        for right, copy in weight_copies(k):
            pl.when(right)(copy.wait)
        for right, copy in weight_copies(k + 1):
            pl.when(right)(copy.start)

        @pl.when(k == first_gate)
        def _():
            grad_normed[...] = dot_nt(tile[...], weights[lax.rem(k, 2)])

        @pl.when(k > first_gate)
        def _():
            grad_normed[...] += dot_nt(tile[...], weights[lax.rem(k, 2)])

    turns, turn, finish = reduce_turns(
        *counts, spans, lefts_ref, [cot_ref, grad_gate_ref, grad_pack], sums_ref, scratch, beside
    )

    def to_previous(k):
        return pltpu.make_async_remote_copy(
            src_ref=stage.at[k], dst_ref=land.at[k], send_sem=chain_sems.at[0, k], recv_sem=chain_sems.at[1, k],
            device_id={"seq": z - 1}, device_id_type=mesh_id,
        )

    def edge_copy(k):
        return pltpu.make_async_remote_copy(
            src_ref=edges.at[k], dst_ref=edge_land.at[k], send_sem=edge_sems.at[0, k], recv_sem=edge_sems.at[1, k],
            device_id={"seq": z - 1}, device_id_type=mesh_id,
        )

    def chain(k):
        @pl.when(z == seq_count - 1)
        def _():
            land[k] = jnp.zeros((STATE, WIDE), low_type)

        @pl.when(z < seq_count - 1)
        def _():
            to_previous(k).wait_recv()

        @pl.when(z > 0)
        def _():
            fade = jnp.exp2(widen(to_front(offs_ref[...], k)[blocks : blocks + 1]))
            own = grad_state_ref[:, pl.ds(pl.multiple_of(k * WIDE, WIDE), WIDE)]
            stage[k] = (own + fade * land[k].astype(full_type)).astype(low_type)
            to_previous(k).start()

    def mend(k):
        @pl.when(z == seq_count - 1)
        def _():
            edge_land[k] = jnp.zeros((8, WIDE), full_type)

        @pl.when(z < seq_count - 1)
        def _():
            edge_copy(k).wait_recv()

        whole = lasts[k] + jnp.concatenate([jnp.zeros((8, WIDE), full_type), edge_land[k]], axis=0)
        grad_pack[rows - 16 :, pl.ds(pl.multiple_of(k * WIDE, WIDE), WIDE)] = whole.astype(low_type)

    @pl.when(place == 0)
    def _():
        greet()

    @pl.when((step >= 1) & (step <= GROUPS + 1))
    def _():
        mend(step - 1)

    early = chunks - 1
    for i in range(spans[2][1] - 1):
        at = next(p for p in range(steps) if (p + 1) * early // steps > first_sig + i)
        assert AHEAD + ((i + 1) * TILE - 1) // WIDE + 1 <= at

    @pl.when(place < steps)
    def _():
        lax.fori_loop(place * early // steps, (place + 1) * early // steps, turn, 0)

    upper = triangle(False)

    @pl.when(place < AHEAD)
    def _():
        for i in range(GROUPS // AHEAD):
            chain(place * (GROUPS // AHEAD) + i)

    @pl.when(place == steps)
    def _():
        lax.fori_loop(early, turns, turn, 0)
        normed_copy = pltpu.make_async_copy(grad_normed, grad_normed_ref, done_sems.at[0])
        normed_copy.start()
        finish()
        normed_copy.wait()

        @pl.when(z > 0)
        def _():
            for k in range(GROUPS):
                to_previous(k).wait_send()
            for k in range(GROUPS + 1):
                edge_copy(k).wait_send()

    @pl.when(step == 0)
    def _():
        for c in range(blocks):
            at = slice(c * BLOCK, (c + 1) * BLOCK)
            maps = bc_ref[at, :].astype(low_type)
            inter[c] = dot_nt(maps[:, :STATE], maps[:, STATE:])
            out_t[:, at] = bc_ref[at, STATE:].T.astype(low_type)
        grad_inter[...] = jnp.zeros(grad_inter.shape, full_type)
        grad_maps[...] = jnp.zeros(grad_maps.shape, full_type)
        run_rows[...] = jnp.zeros(run_rows.shape, full_type)
        run_cols[...] = jnp.zeros(run_cols.shape, full_type)
        run_ends[...] = jnp.zeros(run_ends.shape, full_type)
        weighs[...] = jnp.zeros(weighs.shape, full_type)
        padded[...] = jnp.zeros(padded.shape, full_type)

    def conv_back(grad_pre):
        conv = conv_ref[...]
        grad_sig = conv[3:4] * padded[HALO : HALO + rows, :]
        edge = conv[3:4] * padded[8:HALO, :]
        for k in range(3):
            grad_sig = grad_sig + conv[k : k + 1] * padded[HALO + 3 - k : HALO + 3 - k + rows, :]
            edge = edge + conv[k : k + 1] * padded[11 - k : 19 - k, :]
        grad_pack[:, pl.ds(pl.multiple_of(step * WIDE, WIDE), WIDE)] = grad_sig.astype(low_type)
        lasts[step] = grad_sig[rows - 16 :]

        @pl.when(z > 0)
        def _():
            edges[step] = edge
            edge_copy(step).start()

        sums = [
            jnp.sum(grad_pre * sig[HALO - 3 + k : HALO - 3 + k + rows, :], axis=0, keepdims=True)
            for k in range(CONV_WIDTH)
        ]
        sums.append(jnp.sum(grad_pre, axis=0, keepdims=True))
        sums.append(jnp.zeros((3, WIDE), full_type))
        grad_conv_ref[...] = jnp.concatenate(sums, axis=0)

    @pl.when((step >= 0) & (step < GROUPS))
    def _():
        sig[...] = sig_ref[...].astype(full_type)
        lag = to_front(lag_ref[...], step)
        run_all = head_rows(run_t_ref, step)
        enter = to_front(enter_ref[...], step)
        tail = to_front(tail_ref[...], step)
        offs = to_front(offs_ref[...], step)
        skip = widen(to_front(head_ref[...], step)[2:3])
        left = lane_ids((BLOCK, LANES)) < HEAD_DIM
        heads_of = lax.broadcasted_iota(jnp.int32, (WIDE, LANES), 0) // HEAD_DIM + 4 * step
        picks = jnp.where(heads_of == lane_ids((WIDE, LANES)), 1.0, 0.0).astype(low_type)
        state_in = state_in_ref[...].astype(full_type)
        grad_state = land[step].astype(full_type)
        grad_skip = jnp.zeros((1, WIDE), full_type)
        pre_all = convolve(sig, conv_ref[...], rows)

        def head_sums(vals):
            high = vals.astype(low_type)
            rest = (vals - high.astype(full_type)).astype(low_type)
            return dot(high, picks) + dot(rest, picks)

        for c in reversed(range(blocks)):
            at = slice(c * BLOCK, (c + 1) * BLOCK)
            pre = pre_all[at]
            gate = sigmoid(pre)
            x = pre * gate
            x_low = x.astype(low_type)
            x_round = x_low.astype(full_type)
            grad_y = grad_y_ref[at, :]
            grad_y_full = grad_y.astype(full_type)
            in_map = bc_ref[at, :STATE].astype(low_type)
            out_map = bc_ref[at, STATE:].astype(low_type)
            tail_c = widen(tail[at])
            enter_c = widen(enter[at])
            entering = state_in * jnp.exp2(widen(offs[c : c + 1]))
            if c > 0:
                entering = entering + states_ref[c - 1].astype(full_type)
            leaving = states_ref[c].astype(full_type) + state_in * jnp.exp2(widen(offs[c + 1 : c + 2]))
            entering_low = entering.astype(low_type)
            grad_low = grad_state.astype(low_type)
            ends = jnp.sum(grad_state * leaving, axis=0, keepdims=True)
            run_ends[c : c + 1, :] += head_sums(jnp.concatenate([ends, jnp.zeros((7, WIDE), full_type)], axis=0))[0:1]
            grad_x = tail_c * dot(in_map, grad_low)
            grad_maps[at, :STATE] += dot_nt((x * tail_c).astype(low_type), grad_low)
            swept = grad_y_full * enter_c
            swept_low = swept.astype(low_type)
            through = swept * dot(out_map, entering_low)
            grad_maps[at, STATE:] += dot_nt(swept_low, entering_low)
            fade = jnp.exp2(widen(offs[c + 1 : c + 2] - offs[c : c + 1]))
            grad_state = grad_state * fade + dot(out_t[:, at], swept_low)
            parts = []
            sums = []
            for pair in range(2):
                half = slice(pair * LANES, (pair + 1) * LANES)
                grad_half = grad_y[:, half]
                zero = jnp.zeros_like(grad_half)
                stacked = jnp.concatenate(
                    [jnp.where(left, grad_half, zero), jnp.where(left, zero, grad_half)], axis=0
                )
                cross = dot_nt(x_low[:, half], stacked)
                mixes = []
                for i in range(2):
                    h = 2 * pair + i
                    run_row = run_all[h : h + 1, at]
                    power = jnp.where(upper, run_row - lag[at, h : h + 1], -1e30)
                    decay = jnp.exp2(power)
                    mix = (decay * inter[c]).astype(low_type)
                    mixes.append(mix)
                    cross_h = cross[:, i * LANES : (i + 1) * LANES]
                    grad_inter[c] += cross_h * decay
                    sums.append(jnp.sum(cross_h * mix.astype(full_type), axis=0, keepdims=True))
                parts.append(dot(jnp.concatenate(mixes, axis=1), stacked))
            sums.append(jnp.zeros((4, BLOCK), full_type))
            run_rows[pl.ds(pl.multiple_of(8 * step, 8), 8), at] = jnp.concatenate(sums, axis=0)
            grad_x = grad_x + jnp.concatenate(parts, axis=1)
            weigh = head_sums(x_round * grad_x)
            weighs[at, :] += weigh
            run_cols[at, :] += head_sums(through) - weigh
            grad_skip = grad_skip + jnp.sum(grad_y_full * x, axis=0, keepdims=True)
            grad_x = grad_x + skip * grad_y_full
            padded[HALO + c * BLOCK : HALO + (c + 1) * BLOCK, :] = grad_x * (gate + x * (1.0 - gate))
        grad_skip_ref[...] = jnp.broadcast_to(grad_skip, grad_skip_ref.shape)
        conv_back(padded[HALO : HALO + rows, :])

    @pl.when(step == GROUPS)
    def _():
        sig[...] = sig_ref[...].astype(full_type)
        pre_all = convolve(sig, conv_ref[...], rows)
        for c in range(blocks):
            at = slice(c * BLOCK, (c + 1) * BLOCK)
            maps = bc_ref[at, :].astype(low_type)
            grad_block = grad_inter[c]
            grad_bc = grad_maps[at, :] + jnp.concatenate(
                [
                    dot(grad_block.astype(low_type), maps[:, STATE:]),
                    dot(grad_block.T.astype(low_type), maps[:, :STATE]),
                ],
                axis=1,
            )
            pre = pre_all[at]
            gate = sigmoid(pre)
            padded[HALO + c * BLOCK : HALO + (c + 1) * BLOCK, :] = grad_bc * (gate + pre * gate * (1.0 - gate))
        conv_back(padded[HALO : HALO + rows, :])

    @pl.when(step == GROUPS + 1)
    def _():
        head = head_ref[...]
        step_sizes, slope, rate = step_terms(raw_ref[HALO:, :].astype(full_type), head)
        ratio = jnp.where(step_sizes > 1e-30, slope / jnp.maximum(step_sizes, 1e-30), 1.0)
        used = lane_ids((BLOCK, LANES)) < HEADS
        later = jnp.where(upper, 1.0, 0.0)
        rate_sum = jnp.zeros((1, LANES), full_type)
        bias_sum = jnp.zeros((1, LANES), full_type)
        for c in range(blocks):
            at = slice(c * BLOCK, (c + 1) * BLOCK)
            by_head = [run_rows[8 * j : 8 * j + 4, at] for j in range(GROUPS)]
            by_head.append(jnp.zeros((LANES - HEADS, BLOCK), full_type))
            grad_run = jnp.concatenate(by_head, axis=0).T + run_cols[at, :]
            grad_rates = dot(later, grad_run, precision=highest) + run_ends[c : c + 1, :]
            grad_raw = slope[at] * rate * grad_rates + ratio[at] * weighs[at, :]
            grad_raw = jnp.where(used, grad_raw, 0.0)
            grad_pack[at, CONV_CH:] = grad_raw.astype(low_type)
            rate_sum = rate_sum + jnp.sum(grad_rates * step_sizes[at], axis=0, keepdims=True)
            bias_sum = bias_sum + jnp.sum(grad_raw, axis=0, keepdims=True)
        grad_head_ref[...] = jnp.concatenate(
            [rate_sum * rate, bias_sum, jnp.zeros((6, LANES), full_type)], axis=0
        )


def run_forward(packed, conv, head, normed, cot, gate_own, out_own):
    rows = packed.shape[0] - HALO
    blocks = rows // BLOCK
    count = lax.axis_size("wsh")
    gate_at, back_at = GROUPS + CHAIN_LAG, 2 * GROUPS + CHAIN_LAG
    at = lambda first: lambda j: jnp.clip(j - first, 0, GROUPS - 1)
    once = pl.Buffered(1)
    whole = lambda shape: pl.BlockSpec(shape, lambda j: (0,) * len(shape), pipeline_mode=once)
    kept = lambda shape: pl.BlockSpec(shape, lambda j: (0,) * len(shape))
    cols = lambda height, first: pl.BlockSpec((height, WIDE), lambda j: (0, at(first)(j)))
    anywhere = pl.BlockSpec(memory_space=pl.ANY)
    small = jax.ShapeDtypeStruct((rows, LANES), full_type)
    small_t = jax.ShapeDtypeStruct((LANES, rows), full_type)
    wide = jax.ShapeDtypeStruct((rows, INNER), full_type)
    vmem = pltpu.VMEM
    return pl.pallas_call(
        functools.partial(forward_kernel, count),
        grid=(back_at + GROUPS,),
        in_specs=[
            cols(rows + HALO, 0),
            pl.BlockSpec((rows + HALO, WIDE), lambda j: (0, GROUPS), pipeline_mode=once),
            pl.BlockSpec((rows + HALO, LANES), lambda j: (0, CONV_CH // LANES), pipeline_mode=once),
            cols(8, 0),
            pl.BlockSpec((8, WIDE), lambda j: (0, GROUPS), pipeline_mode=once),
            whole((8, LANES)),
            whole(normed.shape),
            whole(cot.shape),
            whole(gate_own.shape),
            whole(out_own.shape),
        ],
        out_specs=[
            cols(rows, 0),
            kept((rows, WIDE)),
            kept((rows, LANES)),
            kept((LANES, rows)),
            kept((rows, LANES)),
            kept((rows, LANES)),
            kept((rows, LANES)),
            kept((16, LANES)),
            pl.BlockSpec((blocks, STATE, WIDE), lambda j: (0, 0, at(0)(j))),
            cols(STATE, CHAIN_LAG),
            cols(rows, gate_at),
            cols(rows, back_at),
            anywhere,
            anywhere,
        ],
        out_shape=[
            wide,
            jax.ShapeDtypeStruct((rows, WIDE), full_type),
            small, small_t, small, small, small,
            jax.ShapeDtypeStruct((16, LANES), full_type),
            jax.ShapeDtypeStruct((blocks, STATE, INNER), low_type),
            jax.ShapeDtypeStruct((STATE, INNER), low_type),
            wide,
            wide,
            jax.ShapeDtypeStruct((D, INNER), low_type),
            jax.ShapeDtypeStruct((INNER, D), low_type),
        ],
        scratch_shapes=[
            vmem((rows + HALO, WIDE), full_type),
            vmem((STATE, rows), low_type),
            vmem((blocks, BLOCK, BLOCK), full_type),
            vmem((rows, LANES), full_type),
            vmem((LANES, rows), full_type),
            vmem((GROUPS, STATE, WIDE), full_type),
            vmem((GROUPS, STATE, WIDE), low_type),
            vmem((GROUPS, STATE, WIDE), low_type),
            pltpu.SemaphoreType.DMA((2, GROUPS)),
            vmem((D, INNER), low_type),
            vmem((INNER, D), low_type),
            *gather_sems(count),
            *gather_sems(count),
            pltpu.SemaphoreType.DMA((2,)),
        ],
        compiler_params=pltpu.CompilerParams(collective_id=1, has_side_effects=True, vmem_limit_bytes=VMEM_LIMIT),
        cost_estimate=pl.CostEstimate(flops=10**11, bytes_accessed=60 * 10**6, transcendentals=4 * 10**6),
        name="forward_scan",
    )(packed, packed, packed, conv, conv, head, normed, cot, gate_own, out_own)


def run_norm(y, gate, back, gain, bc, enter, state):
    rows = y.shape[0]
    part = BLOCK
    by_rows = lambda cols: pl.BlockSpec((part, cols), lambda i: (i, 0))
    whole = lambda shape: pl.BlockSpec(shape, lambda i: (0,) * len(shape))
    return pl.pallas_call(
        norm_kernel,
        grid=(rows // part,),
        in_specs=[
            by_rows(INNER), by_rows(INNER), by_rows(INNER), whole((8, INNER)),
            by_rows(WIDE), by_rows(LANES), whole((STATE, INNER)),
        ],
        out_specs=[
            by_rows(INNER), pl.BlockSpec((INNER, part), lambda i: (0, i)), by_rows(INNER), by_rows(INNER),
            whole((8, INNER)), whole((STATE, INNER)),
        ],
        out_shape=[
            jax.ShapeDtypeStruct((rows, INNER), low_type),
            jax.ShapeDtypeStruct((INNER, rows), low_type),
            jax.ShapeDtypeStruct((rows, INNER), low_type),
            jax.ShapeDtypeStruct((rows, INNER), low_type),
            jax.ShapeDtypeStruct((8, INNER), full_type),
            jax.ShapeDtypeStruct((STATE, INNER), full_type),
        ],
        scratch_shapes=[pltpu.VMEM((part, INNER), full_type), pltpu.VMEM((part, INNER), low_type)],
        compiler_params=pltpu.CompilerParams(vmem_limit_bytes=VMEM_LIMIT),
        cost_estimate=pl.CostEstimate(flops=10**9, bytes_accessed=30 * 10**6, transcendentals=3 * 10**6),
        name="gated_norm",
    )(y, gate, back, gain, bc, enter, state)


def run_backward(
    packed, conv, head, grad_y, bc, lag, run_t, enter, tail, offs, states, state_in, grad_state, lefts, cot, grad_gate,
    full_gate, full_sig,
):
    rows = grad_y.shape[0]
    blocks = rows // BLOCK
    wsh_count, seq_count = lax.axis_size("wsh"), lax.axis_size("seq")
    groups = INNER // D
    n_out, n_gate, n_sig = cot.shape[1] // TILE, grad_gate.shape[1] // TILE, PACK // TILE
    first_gate, first_sig = n_out * groups, n_out * groups + n_gate
    spans = [(0, n_out, groups, 0), (first_gate, n_gate, 1, INNER), (first_sig, n_sig, 1, INNER)]
    chunks = first_sig + n_sig
    anywhere = pl.BlockSpec(memory_space=pl.ANY)
    low_at = lambda j, top: jnp.clip(j - AHEAD, 0, top)
    once = pl.Buffered(1)
    whole = lambda shape: pl.BlockSpec(shape, lambda j: (0,) * len(shape), pipeline_mode=once)
    kept = lambda shape: pl.BlockSpec(shape, lambda j: (0,) * len(shape))
    return pl.pallas_call(
        functools.partial(backward_kernel, (wsh_count, seq_count), spans),
        grid=(GROUPS + 3 + AHEAD,),
        in_specs=[
            pl.BlockSpec((rows + HALO, WIDE), lambda j: (0, low_at(j, GROUPS))),
            pl.BlockSpec((rows + HALO, LANES), lambda j: (0, CONV_CH // LANES), pipeline_mode=once),
            pl.BlockSpec((8, WIDE), lambda j: (0, low_at(j, GROUPS))),
            whole((8, LANES)),
            pl.BlockSpec((rows, WIDE), lambda j: (0, low_at(j, GROUPS - 1))),
            whole((rows, WIDE)),
            whole((rows, LANES)),
            whole((LANES, rows)),
            whole((rows, LANES)),
            whole((rows, LANES)),
            whole((16, LANES)),
            pl.BlockSpec((blocks, STATE, WIDE), lambda j: (0, 0, low_at(j, GROUPS - 1))),
            pl.BlockSpec((STATE, WIDE), lambda j: (0, low_at(j, GROUPS - 1))),
            whole((STATE, INNER)),
            whole(lefts.shape),
            whole(cot.shape),
            whole(grad_gate.shape),
            anywhere,
            anywhere,
        ],
        out_specs=[
            anywhere,
            pl.BlockSpec((8, WIDE), lambda j: (0, low_at(j, GROUPS))),
            pl.BlockSpec((8, WIDE), lambda j: (0, low_at(j, GROUPS - 1))),
            kept((8, LANES)),
            anywhere,
        ],
        out_shape=[
            jax.ShapeDtypeStruct((rows, D), full_type),
            jax.ShapeDtypeStruct((8, CONV_CH), full_type),
            jax.ShapeDtypeStruct((8, INNER), full_type),
            jax.ShapeDtypeStruct((8, LANES), full_type),
            jax.ShapeDtypeStruct((chunks, D // wsh_count, TILE), low_type),
        ],
        scratch_shapes=[
            pltpu.VMEM((rows + HALO, WIDE), full_type),
            pltpu.VMEM((rows + 2 * HALO, WIDE), full_type),
            pltpu.VMEM((blocks, BLOCK, BLOCK), full_type),
            pltpu.VMEM((blocks, BLOCK, BLOCK), full_type),
            pltpu.VMEM((rows, WIDE), full_type),
            pltpu.VMEM((STATE, rows), low_type),
            pltpu.VMEM((LANES, rows), full_type),
            pltpu.VMEM((rows, LANES), full_type),
            pltpu.VMEM((8, LANES), full_type),
            pltpu.VMEM((rows, LANES), full_type),
            pltpu.VMEM((GROUPS, STATE, WIDE), low_type),
            pltpu.VMEM((GROUPS, STATE, WIDE), low_type),
            pltpu.SemaphoreType.DMA((2, GROUPS)),
            pltpu.VMEM((rows, PACK), low_type),
            pltpu.VMEM((GROUPS + 1, 16, WIDE), full_type),
            pltpu.VMEM((GROUPS + 1, 8, WIDE), full_type),
            pltpu.VMEM((GROUPS + 1, 8, WIDE), full_type),
            pltpu.SemaphoreType.DMA((2, GROUPS + 1)),
            pltpu.VMEM((rows, D), full_type),
            pltpu.VMEM((2, D, TILE), low_type),
            pltpu.SemaphoreType.DMA((2,)),
            pltpu.SemaphoreType.DMA((1,)),
            *reduce_scratch(chunks, rows, wsh_count),
        ],
        compiler_params=pltpu.CompilerParams(collective_id=2, has_side_effects=True, vmem_limit_bytes=61 * 1024 * 1024),
        cost_estimate=pl.CostEstimate(flops=10**11, bytes_accessed=20 * 10**6, transcendentals=5 * 10**6),
        name="scan_backward",
    )(
        packed, packed, conv, head, grad_y, bc, lag, run_t, enter, tail, offs, states, state_in, grad_state,
        lefts, cot, grad_gate, full_gate, full_sig,
    )


def adam_update(weights, gradient, first_moment, second_moment, step_rate, decay_amount):
    next_first = beta_one * first_moment + (1.0 - beta_one) * gradient
    next_second = beta_two * second_moment + (1.0 - beta_two) * gradient * gradient
    corrected = (
        next_first
        / (1.0 - beta_one**STEP)
        / (jnp.sqrt(next_second / (1.0 - beta_two**STEP)) + adam_eps)
    )
    return (weights - step_rate * (corrected + decay_amount * weights), next_first, next_second)


def pad_rows(vals, rows):
    return jnp.pad(vals, ((0, rows - vals.shape[0]), (0, 0)))


def swap(vals, bit, axis="wsh"):
    return lax.ppermute(vals, axis, [(i, i ^ bit) for i in range(lax.axis_size(axis))])


def gather_pieces(own, count, also=None):
    rows = own.shape[0]
    far = [1 << b for b in range(1, count.bit_length() - 1)]
    pieces = [(0, 0, own)]
    if len(far) == 2:
        one, two = far
        half = rows // 2
        by_one = swap(own, one)
        by_two = swap(own, two)
        pieces += [(one, 0, by_one), (two, 0, by_two)]
        pieces += [(one | two, 0, swap(by_two[:half], one)), (one | two, half, swap(by_one[half:], two))]
    else:
        for bit in far:
            pieces += [(r ^ bit, first, swap(piece, bit)) for r, first, piece in pieces]
    marks = [piece for _, _, piece in pieces[-2:]]
    return pieces + [(r ^ 1, first, swap(piece, 1)) for r, first, piece in pieces], marks


def piece_kernel(spots, rows, me_ref, left_ref, *refs):
    sources, out_ref, whole_ref = refs[: len(spots)], refs[len(spots)], refs[len(spots) + 1]
    for source, (r, first) in zip(sources, spots):
        start = lax.bitwise_xor(me_ref[0], r) * rows + first
        whole_ref[pl.ds(pl.multiple_of(start, 16), source.shape[0]), :] = source[...]
    out_ref[...] = dot(left_ref[...], whole_ref[...]).astype(out_ref.dtype)


def multiply_pieces(left, pieces, count, out_type, name):
    rows, cols = pieces[0][2].shape
    tile = 512
    me = jnp.reshape(lax.axis_index("wsh"), (1,)).astype(jnp.int32)
    spots = [(r, first) for r, first, _ in pieces]
    return pl.pallas_call(
        functools.partial(piece_kernel, spots, rows),
        grid=(pl.cdiv(cols, tile),),
        in_specs=[pl.BlockSpec(memory_space=pltpu.SMEM), pl.BlockSpec(left.shape, lambda j: (0, 0))]
        + [pl.BlockSpec((piece.shape[0], tile), lambda j: (0, j)) for _, _, piece in pieces],
        out_specs=[
            pl.BlockSpec((left.shape[0], tile), lambda j: (0, j)),
            pl.BlockSpec((rows * count, tile), lambda j: (0, j)),
        ],
        out_shape=[
            jax.ShapeDtypeStruct((left.shape[0], cols), out_type),
            jax.ShapeDtypeStruct((rows * count, cols), low_type),
        ],
        compiler_params=pltpu.CompilerParams(vmem_limit_bytes=VMEM_LIMIT),
        cost_estimate=pl.CostEstimate(
            flops=2 * left.shape[0] * rows * count * cols, bytes_accessed=4 * rows * count * cols, transcendentals=0
        ),
        name=name,
    )(me, left, *[piece for _, _, piece in pieces])


def sum_small(vals):
    for axis in ("wsh", "seq"):
        bit = 1
        while bit < lax.axis_size(axis):
            vals = vals + swap(vals, bit, axis)
            bit = 2 * bit
    return vals


TILE = 384
FAR_LAG = 2
UP_LAG = 1
LAND_SLOTS = 10
SLACK = 1


def part_orders(count):
    far = [b for b in range(count.bit_length() - 2)]
    return [far[p:] + far[:p] for p in range(len(far))]


def held(order, phase, bits):
    done = sum(1 << b for b in order[:phase])
    left = [m for m in range(1 << bits) if m & done == 0]
    bit = 1 << order[phase]
    return [m for m in left if m & bit == 0], [m for m in left if m & bit]


def greet():
    me, z = lax.axis_index("wsh"), lax.axis_index("seq")
    seq_count = lax.axis_size("seq")
    barrier = pltpu.get_barrier_semaphore()
    mesh_id = pl.DeviceIdType.MESH
    bits = lax.axis_size("wsh").bit_length() - 1
    for b in range(bits):
        pl.semaphore_signal(barrier, inc=1, device_id={"wsh": lax.bitwise_xor(me, 1 << b)}, device_id_type=mesh_id)

    @pl.when(z > 0)
    def _():
        pl.semaphore_signal(barrier, inc=1, device_id={"seq": z - 1}, device_id_type=mesh_id)

    @pl.when(z < seq_count - 1)
    def _():
        pl.semaphore_signal(barrier, inc=1, device_id={"seq": z + 1}, device_id_type=mesh_id)

    along = jnp.where(z > 0, 1, 0) + jnp.where(z < seq_count - 1, 1, 0)
    pl.semaphore_wait(barrier, bits + along)


def reduce_turns(wsh_count, seq_count, spans, left_ref, right_refs, out_ref, scratch, beside):
    orders = part_orders(wsh_count)
    bits = len(orders)
    tile, stage, pair, *rest = scratch
    lands, rest = rest[:bits], rest[bits:]
    from_left, from_right, pair_sems, far_sems, seq_sems, out_sems = rest
    chunks, blocks, rows, _ = pair.shape
    slots = lands[0].shape[0]
    part = rows // bits
    me = lax.axis_index("wsh")
    z = lax.axis_index("seq")
    root = seq_count // 2
    mesh_id = pl.DeviceIdType.MESH

    def pair_copy(k):
        return pltpu.make_async_remote_copy(
            src_ref=stage.at[lax.rem(k, 2)], dst_ref=pair.at[k],
            send_sem=pair_sems.at[0, k], recv_sem=pair_sems.at[1, k],
            device_id={"wsh": lax.bitwise_xor(me, 1)}, device_id_type=mesh_id,
        )

    spots = []
    for q in range(bits):
        for p, order in enumerate(orders):
            for i, m in enumerate(held(order, q, bits)[1]):
                spots.append((q, p, i, m, 2 << order[q]))

    def far_copies(k, phase):
        return [
            pltpu.make_async_remote_copy(
                src_ref=pair.at[k, m, pl.ds(p * part, part)], dst_ref=lands[q].at[lax.rem(k, slots), p, i],
                send_sem=far_sems.at[0, n, k], recv_sem=far_sems.at[1, n, k],
                device_id={"wsh": lax.bitwise_xor(me, bit)}, device_id_type=mesh_id,
            )
            for n, (q, p, i, m, bit) in enumerate(spots)
            if q == phase
        ]

    def to_right(k, source):
        return pltpu.make_async_remote_copy(
            src_ref=source, dst_ref=from_left.at[k],
            send_sem=seq_sems.at[0, k], recv_sem=seq_sems.at[1, k],
            device_id={"seq": z + 1}, device_id_type=mesh_id,
        )

    def to_left(k, source):
        return pltpu.make_async_remote_copy(
            src_ref=source, dst_ref=from_right.at[k],
            send_sem=seq_sems.at[2, k], recv_sem=seq_sems.at[3, k],
            device_id={"seq": z - 1}, device_id_type=mesh_id,
        )

    def out_copy(k, source):
        return pltpu.make_async_copy(source, out_ref.at[k], out_sems.at[k])

    def take_tile(k):
        for (start, tiles, groups, _), right_ref in zip(spans, right_refs):

            @pl.when((k >= start) & (k < start + tiles * groups))
            def _():
                col = lax.rem(k - start, tiles) * TILE
                tile[...] = right_ref[:, pl.ds(pl.multiple_of(col, LANES), TILE)]

    def product(k, b, core):
        owner = lax.bitwise_xor(me, 2 * b + core)
        first = jnp.zeros((), jnp.int32)
        for start, tiles, groups, base in spans:
            at = base + (owner * groups + (k - start) // tiles) * rows
            first = jnp.where((k >= start) & (k < start + tiles * groups), at, first)
        return dot(left_ref[pl.ds(pl.multiple_of(first, 16), rows), :], tile[...])

    def begin(k):
        @pl.when(k >= 2)
        def _():
            pair_copy(k - 2).wait_send()

        take_tile(k)
        for b in range(blocks):
            stage[lax.rem(k, 2), b] = product(k, b, 1).astype(low_type)
        pair_copy(k).start()
        beside(k, tile)

    def add_pair(k):
        take_tile(k)
        pair_copy(k).wait_recv()
        for b in range(blocks):
            pair[k, b] = (product(k, b, 0) + pair[k, b].astype(full_type)).astype(low_type)
        for copy in far_copies(k, 0):
            copy.start()

    def add_far(k, phase):
        for copy in far_copies(k, phase):
            copy.wait_recv()
        for p, order in enumerate(orders):
            at = pl.ds(p * part, part)
            for i, m in enumerate(held(order, phase, bits)[0]):
                total = pair[k, m, at].astype(full_type) + lands[phase][lax.rem(k, slots), p, i].astype(full_type)
                pair[k, m, at] = total.astype(low_type)
        if phase < bits - 1:
            for copy in far_copies(k, phase + 1):
                copy.start()

    def add_to(k, land):
        pair[k, 0] = (pair[k, 0].astype(full_type) + land[k].astype(full_type)).astype(low_type)

    def seq_up(k):
        mine = pair.at[k, 0]

        @pl.when((z > 0) & (z <= root))
        def _():
            to_right(k, mine).wait_recv()
            add_to(k, from_left)

        @pl.when((z < seq_count - 1) & (z >= root))
        def _():
            to_left(k, mine).wait_recv()
            add_to(k, from_right)

        @pl.when((z < seq_count - 1) & (z <= root))
        def _():
            to_right(k, mine).start()

        @pl.when((z > 0) & (z >= root))
        def _():
            to_left(k, mine).start()

    def seq_down(k):
        @pl.when(z == root)
        def _():
            out_copy(k, pair.at[k, 0]).start()

        @pl.when(z < root)
        def _():
            to_left(k, from_right.at[k]).wait_recv()
            out_copy(k, from_right.at[k]).start()
            pl.when(z > 0)(lambda: to_left(k, from_right.at[k]).start())

        @pl.when(z > root)
        def _():
            to_right(k, from_left.at[k]).wait_recv()
            out_copy(k, from_left.at[k]).start()
            pl.when(z < seq_count - 1)(lambda: to_right(k, from_left.at[k]).start())

    far = jnp.abs(z - root)
    farthest = max(root, seq_count - 1 - root)
    stages = [(0, begin), (1, add_pair)] + [
        (1 + FAR_LAG * (q + 1), functools.partial(add_far, phase=q)) for q in range(bits)
    ]
    up_at = 1 + FAR_LAG * bits + UP_LAG
    stages += [(up_at + SLACK * (farthest - far), seq_up), (up_at + 1 + SLACK * (farthest + far), seq_down)]
    turns = chunks + up_at + 2 + SLACK * 2 * farthest

    def turn(s, carry):
        for offset, run in stages:
            pl.when((s >= offset) & (s < chunks + offset))(lambda run=run, offset=offset: run(s - offset))
        return carry

    def finish():
        def wait_all(k, carry):
            for q in range(bits):
                for copy in far_copies(k, q):
                    copy.wait_send()
            pl.when(z < seq_count - 1)(lambda: to_right(k, pair.at[k, 0]).wait_send())
            pl.when(z > 0)(lambda: to_left(k, pair.at[k, 0]).wait_send())
            out_copy(k, pair.at[k, 0]).wait()
            return carry

        lax.fori_loop(0, chunks, wait_all, 0)
        for k in (chunks - 2, chunks - 1):
            pair_copy(k).wait_send()

    return turns, turn, finish


def reduce_scratch(chunks, depth, wsh_count):
    rows = D // wsh_count
    bits = len(part_orders(wsh_count))
    low = lambda *shape: pltpu.VMEM(shape, low_type)
    dma = pltpu.SemaphoreType.DMA
    return [
        low(depth, TILE),
        low(2, 1 << bits, rows, TILE),
        low(chunks, 1 << bits, rows, TILE),
        *[low(min(chunks, LAND_SLOTS), bits, 1 << (bits - 1 - q), rows // bits, TILE) for q in range(bits)],
        low(chunks, rows, TILE),
        low(chunks, rows, TILE),
        dma((2, chunks)),
        dma((2, bits * ((1 << bits) - 1), chunks)),
        dma((4, chunks)),
        dma((chunks,)),
    ]


def adam_kernel(start, rate, decay, *refs):
    share_ref, weight_ref, first_ref, second_ref, grad_ref, next_ref, next_first_ref, next_second_ref = refs
    grad = share_ref[0].astype(full_type)
    grad_ref[...] = grad
    next_ref[...], next_first_ref[...], next_second_ref[...] = adam_update(
        weight_ref[...], grad, first_ref[...], second_ref[...], rate, decay
    )


def adam_chunks(sums, start, weights, first_moment, second_moment, rate, decay, name):
    all_rows, cols = weights.shape
    rows = sums.shape[1]
    tiles = pl.cdiv(cols, TILE)
    block = pl.BlockSpec((rows, TILE), lambda i, j: (i, j))
    return pl.pallas_call(
        functools.partial(adam_kernel, start, rate, decay),
        grid=(all_rows // rows, tiles),
        in_specs=[pl.BlockSpec((1, rows, TILE), lambda i, j: (start + i * tiles + j, 0, 0))] + [block] * 3,
        out_specs=[block] * 4,
        out_shape=[jax.ShapeDtypeStruct(weights.shape, full_type)] * 4,
        compiler_params=pltpu.CompilerParams(vmem_limit_bytes=VMEM_LIMIT),
        cost_estimate=pl.CostEstimate(
            flops=20 * weights.size, bytes_accessed=30 * weights.size, transcendentals=weights.size
        ),
        name=name,
    )(sums, weights, first_moment, second_moment)


def after(vals, *others):
    return lax.optimization_barrier((vals,) + others)[0]


def shards(
    inputs, cotangent, w_in, w_dt, w_out, gain_pre, gain_norm, conv_param, head_param,
    first_w_in, second_w_in, first_w_dt, second_w_dt, first_w_out, second_w_out,
    first_gain_pre, second_gain_pre, first_gain_norm, second_gain_norm,
    first_conv, second_conv, first_head, second_head,
):
    wsh_count = lax.axis_size("wsh")
    seq_count = lax.axis_size("seq")
    seq_index = lax.axis_index("seq")
    wsh_index = lax.axis_index("wsh")
    rows_model = D // wsh_count
    rows_inner = INNER // wsh_count
    cols_conv = CONV_CH // wsh_count
    cols_head = HEADS // wsh_count
    flat = jnp.concatenate(
        [gain_pre, gain_norm, conv_param.reshape(-1), head_param.reshape(-1)]
    ).astype(low_type)
    count = flat.shape[0]
    flat = jnp.pad(flat, (0, -count % LANES))
    part_sig = jnp.concatenate(
        [w_in[:, INNER:].astype(low_type), w_dt.astype(low_type), jnp.zeros((rows_model, LANES - HEADS), low_type)],
        axis=1,
    )
    small = lax.all_gather(flat, "wsh", axis=0)
    part_sig = after(part_sig, small)
    sig_pieces, _ = gather_pieces(part_sig, wsh_count)
    small = small.astype(full_type)
    ends = [rows_model, rows_model + rows_inner, rows_model + rows_inner + 5 * cols_conv]
    gain_in = small[:, : ends[0]].reshape(-1)
    gain_out = small[:, ends[0] : ends[1]].reshape(1, -1)
    conv = small[:, ends[1] : ends[2]].reshape(wsh_count, 5, cols_conv).transpose(1, 0, 2).reshape(5, CONV_CH)
    head = small[:, ends[2] : ends[2] + 3 * cols_head].reshape(wsh_count, 3, cols_head)
    head = head.transpose(1, 0, 2).reshape(3, HEADS)
    conv = pad_rows(conv, 8)
    head = jnp.pad(head, ((0, 5), (0, LANES - HEADS)))
    tokens_low = inputs[0]
    cot_low = cotangent[0]
    rows = tokens_low.shape[0]
    before = lax.ppermute(tokens_low[rows - HALO :], "seq", [(i, i + 1) for i in range(seq_count - 1)])
    tokens = jnp.concatenate([before, tokens_low], axis=0).astype(full_type)
    inv_rms = lax.rsqrt(jnp.mean(tokens * tokens, axis=-1, keepdims=True) + norm_eps)
    normed_all = (tokens * inv_rms * gain_in).astype(low_type)
    packed, full_sig = multiply_pieces(normed_all, sig_pieces, wsh_count, low_type, "project_signal")
    tokens = tokens[HALO:]
    inv_rms = inv_rms[HALO:]
    normed = normed_all[HALO:]
    normed_t = normed.T
    (
        y, bc, lag, run_t, enter, enter_all, tail, offs, states, state_in, gate_vals, back, full_gate, full_out
    ) = run_forward(packed, conv, head, normed, cot_low, w_in[:, :INNER].astype(low_type), w_out.astype(low_type))
    gain_rows = jnp.broadcast_to(gain_out, (8, INNER))
    normed_out, normed_out_t, grad_y, grad_gate, part_gnorm, grad_state = run_norm(
        y, gate_vals, back, gain_rows, bc, enter_all, state_in
    )
    block_out = (tokens + dot(normed_out, full_out)).astype(low_type)[None]
    lefts = jnp.concatenate([normed_out_t, normed_t], axis=0)
    grad_normed, part_conv, part_skip, part_head, sums = run_backward(
        packed, conv, head, grad_y, bc, lag, run_t, enter, tail, offs, states, state_in, grad_state,
        lefts, cot_low, grad_gate, full_gate, full_sig,
    )
    scaled = tokens * inv_rms
    part_gpre = jnp.sum(grad_normed * scaled, axis=0)
    pulled = grad_normed * gain_in
    grad_tokens = inv_rms * (pulled - scaled * jnp.mean(pulled * scaled, axis=-1, keepdims=True))
    input_grad = (cot_low.astype(full_type) + grad_tokens)[None]
    skip_sums = part_skip[0].reshape(HEADS, HEAD_DIM).sum(axis=1)
    small_parts = [
        part_gpre, part_gnorm[0], part_conv[:5].reshape(-1), part_head[0, :HEADS], part_head[1, :HEADS], skip_sums
    ]
    small_sums = sum_small(jnp.concatenate(small_parts))
    cuts = [D, D + INNER, D + INNER + 5 * CONV_CH]
    grad_gpre = lax.dynamic_slice_in_dim(small_sums[: cuts[0]], wsh_index * rows_model, rows_model, 0)
    grad_gnorm = lax.dynamic_slice_in_dim(small_sums[cuts[0] : cuts[1]], wsh_index * rows_inner, rows_inner, 0)
    grad_conv = lax.dynamic_slice_in_dim(
        small_sums[cuts[1] : cuts[2]].reshape(5, CONV_CH), wsh_index * cols_conv, cols_conv, 1
    )
    grad_head = lax.dynamic_slice_in_dim(
        small_sums[cuts[2] :].reshape(3, HEADS), wsh_index * cols_head, cols_head, 1
    )
    tiles_out = (INNER // D) * (D // TILE)
    grad_out, *new_out = adam_chunks(sums, 0, w_out, first_w_out, second_w_out, rate_matrix, weight_decay, "adam_w_out")
    grad_in_w, *new_in = adam_chunks(
        sums, tiles_out, w_in, first_w_in, second_w_in, rate_matrix, weight_decay, "adam_w_in"
    )
    at_dt = CONV_CH % TILE
    grad_dt = sums[-1, :, at_dt : at_dt + HEADS].astype(full_type)
    params = (w_in, w_dt, w_out, gain_pre, gain_norm, conv_param, head_param)
    gradients = (grad_in_w, grad_dt, grad_out, grad_gpre, grad_gnorm, grad_conv, grad_head)
    firsts = (first_w_in, first_w_dt, first_w_out, first_gain_pre, first_gain_norm, first_conv, first_head)
    seconds = (second_w_in, second_w_dt, second_w_out, second_gain_pre, second_gain_norm, second_conv, second_head)
    step_rates = (rate_matrix, rate_matrix, rate_matrix, rate_gain, rate_gain, rate_conv, rate_head)
    decays = (weight_decay, weight_decay, weight_decay, 0.0, 0.0, 0.0, 0.0)
    updated = [
        None if i in (0, 2) else adam_update(*items)
        for i, items in enumerate(zip(params, gradients, firsts, seconds, step_rates, decays))
    ]
    updated[0], updated[2] = new_in, new_out
    new_params = tuple(entry[0] for entry in updated)
    moments = []
    for entry in updated:
        moments.append(entry[1])
        moments.append(entry[2])
    return (block_out, input_grad) + gradients + new_params + tuple(moments)


def solution(mesh):
    rows, vec, cols = P("wsh", None), P("wsh"), P(None, "wsh")
    tokens = P("wsh", "seq", None)
    params = (rows, rows, rows, vec, vec, cols, cols)
    moments = tuple(spec for spec in params for _ in range(2))
    in_specs = (tokens, tokens) + params + moments
    out_specs = (tokens, tokens) + params + params + moments
    return jax.shard_map(shards, mesh=mesh, in_specs=in_specs, out_specs=out_specs, check_vma=False)
```

```python
import functools

import jax
import jax.numpy as jnp
from jax import lax
from jax.experimental import pallas as pl
from jax.experimental.pallas import tpu as pltpu
from jax.sharding import PartitionSpec as P

D = 1536
HEADS = 48
HEAD_DIM = 64
STATE = 128
CONV_WIDTH = 4
STEP = 2
INNER = 3072
CONV_CH = 3328
BLOCK = 128
LANES = 128
WIDE = 256
HALO = 16
GROUPS = INNER // WIDE
CHAIN_LAG = 2
CHAIN_PER = 2
PACK = CONV_CH + LANES
LOG2E = 1.4426950408889634
VMEM_LIMIT = 56 * 1024 * 1024

norm_eps = 1e-05
beta_one = 0.9
beta_two = 0.999
adam_eps = 1e-08
rate_matrix = 0.01
rate_gain = 0.4
rate_conv = 0.1
rate_head = 1.0
weight_decay = 0.1
highest = lax.Precision.HIGHEST
low_type = jnp.bfloat16
full_type = jnp.float32


def dot(left_side, right_side, dims=((1,), (0,)), precision=None):
    return lax.dot_general(
        left_side, right_side, (dims, ((), ())), precision=precision, preferred_element_type=full_type
    )


def dot_nt(left_side, right_side):
    return dot(left_side, right_side, ((1,), (1,)))


def sigmoid(vals):
    return 0.5 * jnp.tanh(0.5 * vals) + 0.5


def lane_ids(shape):
    return lax.broadcasted_iota(jnp.int32, shape, len(shape) - 1)


def widen(vals, first=0):
    left = lane_ids((vals.shape[0], LANES)) < HEAD_DIM
    pairs = [
        jnp.where(left, vals[:, first + i : first + i + 1], vals[:, first + i + 1 : first + i + 2])
        for i in (0, 2)
    ]
    return jnp.concatenate(pairs, axis=1)


def to_front(vals, step):
    return pltpu.roll(vals, lax.rem(LANES - 4 * step, LANES), 1)


def head_rows(ref, step):
    eight = ref[pl.ds(pl.multiple_of(8 * (step // 2), 8), 8), :]
    return pltpu.roll(eight, 4 * lax.rem(step, 2), 0)


def step_terms(raw, head):
    shifted = raw + head[1:2]
    small = jnp.exp(-jnp.abs(shifted))
    log_part = jnp.where(
        small < 0.01, small * (1.0 - small * (0.5 - small * (1.0 / 3.0))), jnp.log(1.0 + small)
    )
    step_sizes = jnp.maximum(shifted, 0.0) + log_part
    slope = jnp.where(shifted >= 0.0, 1.0, small) / (1.0 + small)
    return step_sizes, slope, -jnp.exp(head[0:1])


def convolve(sig, conv, rows):
    total = conv[4:5] + conv[0:1] * sig[HALO - 3 : HALO - 3 + rows, :]
    for k in range(1, CONV_WIDTH):
        total = total + conv[k : k + 1] * sig[HALO - 3 + k : HALO - 3 + k + rows, :]
    return total


def triangle(lower):
    rows = lax.broadcasted_iota(jnp.int32, (BLOCK, BLOCK), 0)
    cols = lax.broadcasted_iota(jnp.int32, (BLOCK, BLOCK), 1)
    return rows >= cols if lower else rows <= cols


def gather_steps(count, own_ref, full_ref, far_sems, core_sems, cols=None, split=True):
    orders = part_orders(count)
    bits = len(orders)
    orders = orders if split else orders[:1]
    rows = own_ref.shape[0]
    part = rows // len(orders)
    cols = cols or (0, own_ref.shape[1])
    me = lax.axis_index("wsh")
    mesh_id = pl.DeviceIdType.MESH

    def copy(m, first, size, bit, sems, n):
        start = lax.bitwise_xor(me, 2 * m) * rows + first
        at = full_ref.at[pl.ds(pl.multiple_of(start, 16), size), pl.ds(*cols)]
        return pltpu.make_async_remote_copy(
            src_ref=at, dst_ref=at, send_sem=sems.at[0, n], recv_sem=sems.at[1, n],
            device_id={"wsh": lax.bitwise_xor(me, bit)}, device_id_type=mesh_id,
        )

    far_spots = [
        (q, m, p * part, part, 2 << order[q])
        for q in range(bits)
        for p, order in enumerate(orders)
        for m in range(1 << bits)
        if m & ~sum(1 << b for b in order[:q]) == 0
    ]
    core_spots = [(0, 0, 0, rows, 1)] + [
        (q + 1, m, p * part, part, 1)
        for q in range(bits)
        for p, order in enumerate(orders)
        for m in range(1 << bits)
        if m >> order[q] & 1 and m & ~sum(1 << b for b in order[: q + 1]) == 0
    ]
    pick = lambda spots, sems, phase: [
        copy(m, first, size, bit, sems, n)
        for n, (q, m, first, size, bit) in enumerate(spots)
        if phase is None or q == phase
    ]

    def start():
        full_ref[pl.ds(pl.multiple_of(me * rows, 16), rows), pl.ds(*cols)] = own_ref[:, pl.ds(*cols)]
        for item in pick(far_spots, far_sems, 0) + pick(core_spots, core_sems, 0):
            item.start()

    def advance(phase):
        for item in pick(far_spots, far_sems, phase):
            item.wait_recv()
        later = pick(far_spots, far_sems, phase + 1) if phase + 1 < bits else []
        for item in later + pick(core_spots, core_sems, phase + 1):
            item.start()

    def done():
        for item in pick(core_spots, core_sems, None):
            item.wait_recv()

    def finish():
        for item in pick(far_spots, far_sems, None) + pick(core_spots, core_sems, None):
            item.wait_send()

    return start, advance, done, finish


def gather_sems(count, split=True):
    bits = len(part_orders(count))
    copies = (bits if split else 1) * ((1 << bits) - 1)
    return [pltpu.SemaphoreType.DMA((2, copies)), pltpu.SemaphoreType.DMA((2, copies + 1))]


def signal_kernel(
    count, tokens_ref, own_ref, small_ref,
    packed_ref, normed_ref, inv_ref, gain_in_ref, gain_out_ref, conv_ref, head_ref, full_ref,
    normed, full, small_full, small_far, small_core, out_sems, *sems,
):
    bits = len(part_orders(count))
    pieces = len(sems) // 2
    width = own_ref.shape[1] // pieces
    small_start, small_advance, small_done, small_finish = gather_steps(
        count, small_ref, small_full, small_far, small_core, split=False
    )
    gathers = [
        gather_steps(count, own_ref, full, sems[2 * c], sems[2 * c + 1], cols=(c * width, width)) for c in range(pieces)
    ]
    greet()
    small_start()
    for start, _, _, _ in gathers:
        start()
    for q in range(bits):
        small_advance(q)
    small_done()
    height = small_ref.shape[0]
    small = small_full[:height, :].astype(full_type)
    for d in range(1, count):
        small = small + small_full[d * height : (d + 1) * height, :].astype(full_type)
    gain_in_ref[...] = jnp.broadcast_to(small[0:1, :D], gain_in_ref.shape)
    gain_out_ref[...] = jnp.broadcast_to(small[1:2, :INNER], gain_out_ref.shape)
    conv_ref[...] = jnp.concatenate([small[2:7], jnp.zeros((3, CONV_CH), full_type)], axis=0)
    head_ref[...] = jnp.concatenate([small[7:10, :LANES], jnp.zeros((5, LANES), full_type)], axis=0)
    gathers[0][1](0)
    all_rows = tokens_ref.shape[0]
    for first in range(0, all_rows, BLOCK):
        size = min(BLOCK, all_rows - first)
        tokens = tokens_ref[first : first + size, :].astype(full_type)
        inv = lax.rsqrt(jnp.sum(tokens * tokens, axis=1, keepdims=True) * (1.0 / D) + norm_eps)
        low = (tokens * inv * gain_in_ref[0:1, :]).astype(low_type)
        normed[first : first + size, :] = low
        skip = max(HALO - first, 0)
        at = slice(first + skip - HALO, first + size - HALO)
        normed_ref[at, :] = low[skip:]
        inv_ref[at, :] = jnp.broadcast_to(inv[skip:], (size - skip, LANES))
    for _, advance, _, _ in gathers[1:]:
        advance(0)
    outs = []
    for c, (_, advance, done, _) in enumerate(gathers):
        for q in range(1, bits):
            advance(q)
        done()
        cols = pl.ds(c * width, width)
        outs.append(pltpu.make_async_copy(full.at[:, cols], full_ref.at[:, cols], out_sems.at[c]))
        outs[-1].start()

        def multiply(t, carry, c=c):
            col = pl.multiple_of(c * width + t * TILE, LANES)
            packed_ref[:, pl.ds(col, TILE)] = dot(normed[...], full[:, pl.ds(col, TILE)]).astype(low_type)
            return carry

        lax.fori_loop(0, width // TILE, multiply, 0)
    for out in outs:
        out.wait()
    small_finish()
    for _, _, _, finish in gathers:
        finish()


def project_signal(tokens, own, small):
    count = lax.axis_size("wsh")
    all_rows = tokens.shape[0]
    rows = all_rows - HALO
    pieces = 3
    vmem = pl.BlockSpec(memory_space=pltpu.VMEM)
    wide = lambda cols: jax.ShapeDtypeStruct((8, cols), full_type)
    sems = [sem for _ in range(pieces) for sem in gather_sems(count)]
    return pl.pallas_call(
        functools.partial(signal_kernel, count),
        in_specs=[vmem] * 3,
        out_specs=[vmem] * 7 + [pl.BlockSpec(memory_space=pl.ANY)],
        out_shape=[
            jax.ShapeDtypeStruct((all_rows, PACK), low_type),
            jax.ShapeDtypeStruct((rows, D), low_type),
            jax.ShapeDtypeStruct((rows, LANES), full_type),
            wide(D), wide(INNER), wide(CONV_CH), wide(LANES),
            jax.ShapeDtypeStruct((D, PACK), low_type),
        ],
        scratch_shapes=[
            pltpu.VMEM((all_rows, D), low_type),
            pltpu.VMEM((D, PACK), low_type),
            pltpu.VMEM((count * small.shape[0], CONV_CH), low_type),
            *gather_sems(count, split=False),
            pltpu.SemaphoreType.DMA((pieces,)),
            *sems,
        ],
        compiler_params=pltpu.CompilerParams(collective_id=0, has_side_effects=True, vmem_limit_bytes=VMEM_LIMIT),
        cost_estimate=pl.CostEstimate(flops=6 * 10**10, bytes_accessed=30 * 10**6, transcendentals=0),
        name="project_signal",
    )(tokens, own, small)


def forward_kernel(
    count,
    sig_ref, maps_ref, raw_ref, conv_ref, conv_maps_ref, head_ref, normed_ref, cot_ref, gate_own_ref, out_own_ref,
    y_ref, bc_ref, lag_ref, run_t_ref, enter_ref, enter_all_ref, tail_ref, offs_ref, states_ref, before_ref,
    gate_ref, back_ref, full_gate_ref, full_out_ref,
    sig, in_t, inter, run, lag_t, ends, stage, land, sems, gate_full, out_full,
    gate_far, gate_core, out_far, out_core, full_sems,
):
    step = pl.program_id(0)
    rows = y_ref.shape[0]
    blocks = rows // BLOCK
    z = lax.axis_index("seq")
    seq_count = lax.axis_size("seq")
    lower = triangle(True)
    bits = len(part_orders(count))
    gate_start, gate_advance, gate_done, gate_finish = gather_steps(count, gate_own_ref, gate_full, gate_far, gate_core)
    out_start, out_advance, out_done, out_finish = gather_steps(count, out_own_ref, out_full, out_far, out_core)
    gate_at, back_at = GROUPS + CHAIN_LAG, 2 * GROUPS + CHAIN_LAG

    def to_next(k):
        return pltpu.make_async_remote_copy(
            src_ref=stage.at[k], dst_ref=land.at[k], send_sem=sems.at[0, k], recv_sem=sems.at[1, k],
            device_id={"seq": z + 1}, device_id_type=pl.DeviceIdType.MESH,
        )

    @pl.when(step == 0)
    def _():
        greet()
        gate_start()
        out_start()
        sig[...] = maps_ref[...].astype(full_type)
        pre = convolve(sig, conv_maps_ref[...], rows)
        maps = pre * sigmoid(pre)
        bc_ref[...] = maps
        in_t[...] = maps[:, :STATE].T.astype(low_type)
        step_sizes, _, rate = step_terms(raw_ref[HALO:, :].astype(full_type), head_ref[...])
        rates = step_sizes * rate * LOG2E
        log_steps = jnp.log2(step_sizes)
        sums = jnp.where(lower, 1.0, 0.0)
        offset = jnp.zeros((1, LANES), full_type)
        offs_ref[...] = jnp.zeros(offs_ref.shape, full_type)
        for c in range(blocks):
            at = slice(c * BLOCK, (c + 1) * BLOCK)
            total = dot(sums, rates[at], precision=highest)
            lag = total - log_steps[at]
            run[at, :] = total
            lag_ref[at, :] = lag
            run_t_ref[:, at] = total.T
            lag_t[:, at] = lag.T
            enter_ref[at, :] = jnp.exp2(total)
            enter_all_ref[at, :] = jnp.exp2(total + offset)
            tail_ref[at, :] = jnp.exp2(total[BLOCK - 1 : BLOCK] - lag)
            offs_ref[c : c + 1, :] = offset
            offset = offset + total[BLOCK - 1 : BLOCK]
            low_maps = maps[at].astype(low_type)
            inter[c] = dot_nt(low_maps[:, STATE:], low_maps[:, :STATE])
        offs_ref[blocks : blocks + 1, :] = offset

    pl.when(step == GROUPS // 2)(lambda: gate_advance(0))
    pl.when(step == GROUPS)(lambda: out_advance(0))

    @pl.when(step < GROUPS)
    def _():
        sig[...] = sig_ref[...].astype(full_type)
        pre_all = convolve(sig, conv_ref[...], rows)
        tail = to_front(tail_ref[...], step)
        last = to_front(offs_ref[...], step)
        run_all = to_front(run[...], step)
        enter = to_front(enter_ref[...], step)
        lag_rows = head_rows(lag_t, step)
        skip = widen(to_front(head_ref[...], step)[2:3])
        left = lane_ids((BLOCK, LANES)) < HEAD_DIM
        state = jnp.zeros((STATE, WIDE), full_type)
        for c in range(blocks):
            at = slice(c * BLOCK, (c + 1) * BLOCK)
            pre = pre_all[at]
            x = pre * sigmoid(pre)
            parts = []
            for pair in range(2):
                mixes = []
                for i in range(2):
                    h = 2 * pair + i
                    power = jnp.where(lower, run_all[at, h : h + 1] - lag_rows[h : h + 1, at], -1e30)
                    mixes.append((jnp.exp2(power) * inter[c]).astype(low_type))
                half = x[:, pair * LANES : (pair + 1) * LANES].astype(low_type)
                zero = jnp.zeros_like(half)
                stacked = jnp.concatenate([jnp.where(left, half, zero), jnp.where(left, zero, half)], axis=0)
                parts.append(dot(jnp.concatenate(mixes, axis=1), stacked))
            y = jnp.concatenate(parts, axis=1) + skip * x
            if c > 0:
                out_map = bc_ref[at, STATE:].astype(low_type)
                y = y + widen(enter[at]) * dot(out_map, state.astype(low_type))
            y_ref[at, :] = y
            weighted = (x * widen(tail[at])).astype(low_type)
            fade = jnp.exp2(widen(last[c + 1 : c + 2] - last[c : c + 1]))
            state = state * fade + dot(in_t[:, at], weighted)
            states_ref[c] = state.astype(low_type)
        ends[step] = state

    @pl.when((step >= CHAIN_LAG) & (step < gate_at))
    def _():
        k = step - CHAIN_LAG

        @pl.when(z == 0)
        def _():
            land[k] = jnp.zeros((STATE, WIDE), low_type)

        @pl.when(z > 0)
        def _():
            to_next(k).wait_recv()

        before_ref[...] = land[k]

        @pl.when(z < seq_count - 1)
        def _():
            fade = jnp.exp2(widen(to_front(offs_ref[...], k)[blocks : blocks + 1]))
            stage[k] = (ends[k] + fade * land[k].astype(full_type)).astype(low_type)
            to_next(k).start()

    gate_out = pltpu.make_async_copy(gate_full, full_gate_ref, full_sems.at[0])
    out_out = pltpu.make_async_copy(out_full, full_out_ref, full_sems.at[1])

    @pl.when(step == gate_at)
    def _():
        for q in range(1, bits):
            gate_advance(q)
        gate_done()
        gate_out.start()

    @pl.when((step >= gate_at) & (step < back_at))
    def _():
        col = pl.multiple_of((step - gate_at) * WIDE, WIDE)
        gate_ref[...] = dot(normed_ref[...], gate_full[:, pl.ds(col, WIDE)])

    @pl.when(step == back_at)
    def _():
        for q in range(1, bits):
            out_advance(q)
        out_done()
        out_out.start()

    @pl.when(step >= back_at)
    def _():
        row = pl.multiple_of((step - back_at) * WIDE, WIDE)
        back_ref[...] = dot_nt(cot_ref[...], out_full[pl.ds(row, WIDE), :])

    @pl.when(step == back_at + GROUPS - 1)
    def _():
        gate_finish()
        out_finish()
        gate_out.wait()
        out_out.wait()

        @pl.when(z < seq_count - 1)
        def _():
            for k in range(GROUPS):
                to_next(k).wait_send()


def norm_kernel(
    y_ref, gate_ref, back_ref, gain_ref, bc_ref, enter_ref, state_ref, inner_ref,
    normed_ref, lefts_ref, grad_y_ref, grad_gate_ref, grad_gain_ref, grad_state_ref,
    gated, low_y,
):
    step = pl.program_id(0)
    rows = y_ref.shape[0]

    @pl.when(step == 0)
    def _():
        grad_gain_ref[...] = jnp.zeros(grad_gain_ref.shape, full_type)
        grad_state_ref[...] = jnp.zeros(grad_state_ref.shape, full_type)

    for j in range(D // WIDE):
        lefts_ref[INNER + j * WIDE : INNER + (j + 1) * WIDE, :] = inner_ref[:, j * WIDE : (j + 1) * WIDE].T
    out_map = bc_ref[:, STATE:]
    out_low = out_map.astype(low_type)
    out_t = out_map.T.astype(low_type)
    squares = jnp.zeros((rows, WIDE), full_type)
    cross = jnp.zeros((rows, WIDE), full_type)
    for j in range(GROUPS):
        at = slice(j * WIDE, (j + 1) * WIDE)
        enter = widen(enter_ref[...], 4 * j)
        y = y_ref[:, at] + enter * dot(out_low, state_ref[:, at])
        y_low = y.astype(low_type)
        low_y[:, at] = y_low
        gate = gate_ref[:, at]
        vals = y_low.astype(full_type) * (gate * sigmoid(gate))
        gated[:, at] = vals
        squares = squares + vals * vals
        cross = cross + vals * (back_ref[:, at] * gain_ref[0:1, at])
    inv = lax.rsqrt(jnp.sum(squares, axis=1, keepdims=True) * (1.0 / INNER) + norm_eps)
    pull = inv * inv * inv * (jnp.sum(cross, axis=1, keepdims=True) * (1.0 / INNER))
    for j in range(GROUPS):
        at = slice(j * WIDE, (j + 1) * WIDE)
        gain = gain_ref[0:1, at]
        back = back_ref[:, at]
        vals = gated[:, at]
        scaled = vals * inv
        normed = (scaled * gain).astype(low_type)
        normed_ref[:, at] = normed
        lefts_ref[at, :] = normed.T
        grad_gain_ref[0:1, at] += jnp.sum(back * scaled, axis=0, keepdims=True)
        grad_vals = back * gain * inv - vals * pull
        gate = gate_ref[:, at]
        sig = sigmoid(gate)
        silu = gate * sig
        grad_y = (grad_vals * silu).astype(low_type)
        grad_y_ref[:, at] = grad_y
        slope = sig + silu * (1.0 - sig)
        grad_gate_ref[:, at] = (grad_vals * low_y[:, at].astype(full_type) * slope).astype(low_type)
        enter = widen(enter_ref[...], 4 * j)
        grad_state_ref[:, at] += dot(out_t, (grad_y.astype(full_type) * enter).astype(low_type))


def steps_ahead(seq_count):
    return GROUPS // CHAIN_PER + seq_count - 1


def backward_kernel(
    counts, spans,
    sig_ref, raw_ref, conv_ref, head_ref, grad_y_ref, bc_ref,
    lag_ref, run_t_ref, enter_ref, tail_ref, offs_ref, states_ref, state_in_ref, grad_state_ref,
    lefts_ref, cot_ref, grad_gate_ref, full_gate_ref, full_sig_ref,
    grad_normed_ref, grad_conv_ref, grad_skip_ref, grad_head_ref, sums_ref,
    sig, padded, inter, grad_inter, grad_maps, out_t, run_rows, run_cols, run_ends, weighs,
    stage, land, chain_sems, grad_pack, lasts, edges, edge_land, edge_sems, grad_normed, weights, weight_sems, done_sems,
    *scratch,
):
    ahead = steps_ahead(counts[1])
    place = pl.program_id(0)
    step = place - ahead
    steps = GROUPS + 2 + ahead
    rows = grad_y_ref.shape[0]
    blocks = rows // BLOCK
    z = lax.axis_index("seq")
    seq_count = counts[1]
    mesh_id = pl.DeviceIdType.MESH
    first_gate, first_sig = spans[1][0], spans[2][0]
    chunks = first_sig + spans[2][1]

    def weight_copies(k):
        slot = lax.rem(k, 2)
        for ref, first, last in ((full_gate_ref, first_gate, first_sig), (full_sig_ref, first_sig, chunks)):
            col = pl.multiple_of(jnp.clip(k - first, 0, last - first - 1) * TILE, LANES)
            copy = pltpu.make_async_copy(ref.at[:, pl.ds(col, TILE)], weights.at[slot], weight_sems.at[slot])
            yield (k >= first) & (k < last), copy

    def add_normed(k, right_ref, first):
        col = pl.multiple_of((k - first) * TILE, LANES)
        for right, copy in weight_copies(k):
            pl.when(right)(copy.wait)
        for right, copy in weight_copies(k + 1):
            pl.when(right)(copy.start)

        part = dot_nt(right_ref[:, pl.ds(col, TILE)], weights[lax.rem(k, 2)])

        @pl.when(k == first_gate)
        def _():
            grad_normed[...] = part

        @pl.when(k > first_gate)
        def _():
            grad_normed[...] += part

    def late_turn(s, carry):
        turn(s, 0)
        per = -(-(chunks - first_gate) // (turns - early))
        for i in range(per):
            k = first_gate + (s - early) * per + i
            pl.when(k < first_sig)(lambda k=k: add_normed(k, grad_gate_ref, first_gate))
            pl.when((k >= first_sig) & (k < chunks))(lambda k=k: add_normed(k, grad_pack, first_sig))
        return carry

    turns, turn, finish = reduce_turns(
        *counts, spans, lefts_ref, [cot_ref, grad_gate_ref, grad_pack], sums_ref, scratch
    )

    def to_previous(k):
        return pltpu.make_async_remote_copy(
            src_ref=stage.at[k], dst_ref=land.at[k], send_sem=chain_sems.at[0, k], recv_sem=chain_sems.at[1, k],
            device_id={"seq": z - 1}, device_id_type=mesh_id,
        )

    def edge_copy(k):
        return pltpu.make_async_remote_copy(
            src_ref=edges.at[k], dst_ref=edge_land.at[k], send_sem=edge_sems.at[0, k], recv_sem=edge_sems.at[1, k],
            device_id={"seq": z - 1}, device_id_type=mesh_id,
        )

    def chain(k):
        @pl.when(z == seq_count - 1)
        def _():
            land[k] = jnp.zeros((STATE, WIDE), low_type)

        @pl.when(z < seq_count - 1)
        def _():
            to_previous(k).wait_recv()

        @pl.when(z > 0)
        def _():
            fade = jnp.exp2(widen(to_front(offs_ref[...], k)[blocks : blocks + 1]))
            own = grad_state_ref[:, pl.ds(pl.multiple_of(k * WIDE, WIDE), WIDE)]
            stage[k] = (own + fade * land[k].astype(full_type)).astype(low_type)
            to_previous(k).start()

    def mend(k):
        @pl.when(z == seq_count - 1)
        def _():
            edge_land[k] = jnp.zeros((8, WIDE), full_type)

        @pl.when(z < seq_count - 1)
        def _():
            edge_copy(k).wait_recv()

        whole = lasts[k] + jnp.concatenate([jnp.zeros((8, WIDE), full_type), edge_land[k]], axis=0)
        grad_pack[rows - 16 :, pl.ds(pl.multiple_of(k * WIDE, WIDE), WIDE)] = whole.astype(low_type)

    @pl.when(place == 0)
    def _():
        greet()
        next(copy for _, copy in weight_copies(first_gate)).start()

    @pl.when((step >= 1) & (step <= GROUPS + 1))
    def _():
        mend(step - 1)

    early = chunks - 1
    for i in range(spans[2][1] - 1):
        at = next(p for p in range(steps) if (p + 1) * early // steps > first_sig + i)
        assert ahead + ((i + 1) * TILE - 1) // WIDE + 1 <= at

    @pl.when(place < steps)
    def _():
        lax.fori_loop(place * early // steps, (place + 1) * early // steps, turn, 0)

    upper = triangle(False)

    turn_of = place - (seq_count - 1 - z)

    @pl.when((turn_of >= 0) & (turn_of < GROUPS // CHAIN_PER))
    def _():
        for i in range(CHAIN_PER):
            chain(turn_of * CHAIN_PER + i)

    @pl.when(place == steps)
    def _():
        lax.fori_loop(early, turns, late_turn, 0)
        normed_copy = pltpu.make_async_copy(grad_normed, grad_normed_ref, done_sems.at[0])
        normed_copy.start()
        finish()
        normed_copy.wait()

        @pl.when(z > 0)
        def _():
            for k in range(GROUPS):
                to_previous(k).wait_send()
            for k in range(GROUPS + 1):
                edge_copy(k).wait_send()

    @pl.when(step == 0)
    def _():
        for c in range(blocks):
            at = slice(c * BLOCK, (c + 1) * BLOCK)
            maps = bc_ref[at, :].astype(low_type)
            inter[c] = dot_nt(maps[:, :STATE], maps[:, STATE:])
            out_t[:, at] = bc_ref[at, STATE:].T.astype(low_type)
        grad_inter[...] = jnp.zeros(grad_inter.shape, full_type)
        grad_maps[...] = jnp.zeros(grad_maps.shape, full_type)
        run_rows[...] = jnp.zeros(run_rows.shape, full_type)
        run_cols[...] = jnp.zeros(run_cols.shape, full_type)
        run_ends[...] = jnp.zeros(run_ends.shape, full_type)
        weighs[...] = jnp.zeros(weighs.shape, full_type)
        padded[...] = jnp.zeros(padded.shape, full_type)

    def conv_back(grad_pre):
        conv = conv_ref[...]
        grad_sig = conv[3:4] * padded[HALO : HALO + rows, :]
        edge = conv[3:4] * padded[8:HALO, :]
        for k in range(3):
            grad_sig = grad_sig + conv[k : k + 1] * padded[HALO + 3 - k : HALO + 3 - k + rows, :]
            edge = edge + conv[k : k + 1] * padded[11 - k : 19 - k, :]
        grad_pack[:, pl.ds(pl.multiple_of(step * WIDE, WIDE), WIDE)] = grad_sig.astype(low_type)
        lasts[step] = grad_sig[rows - 16 :]

        @pl.when(z > 0)
        def _():
            edges[step] = edge
            edge_copy(step).start()

        sums = [
            jnp.sum(grad_pre * sig[HALO - 3 + k : HALO - 3 + k + rows, :], axis=0, keepdims=True)
            for k in range(CONV_WIDTH)
        ]
        sums.append(jnp.sum(grad_pre, axis=0, keepdims=True))
        sums.append(jnp.zeros((3, WIDE), full_type))
        grad_conv_ref[...] = jnp.concatenate(sums, axis=0)

    @pl.when((step >= 0) & (step < GROUPS))
    def _():
        sig[...] = sig_ref[...].astype(full_type)
        lag = to_front(lag_ref[...], step)
        run_all = head_rows(run_t_ref, step)
        enter = to_front(enter_ref[...], step)
        tail = to_front(tail_ref[...], step)
        offs = to_front(offs_ref[...], step)
        skip = widen(to_front(head_ref[...], step)[2:3])
        left = lane_ids((BLOCK, LANES)) < HEAD_DIM
        heads_of = lax.broadcasted_iota(jnp.int32, (WIDE, LANES), 0) // HEAD_DIM + 4 * step
        picks = jnp.where(heads_of == lane_ids((WIDE, LANES)), 1.0, 0.0).astype(low_type)
        state_in = state_in_ref[...].astype(full_type)
        grad_state = land[step].astype(full_type)
        grad_skip = jnp.zeros((1, WIDE), full_type)
        pre_all = convolve(sig, conv_ref[...], rows)

        def head_sums(vals):
            high = vals.astype(low_type)
            rest = (vals - high.astype(full_type)).astype(low_type)
            return dot(high, picks) + dot(rest, picks)

        for c in reversed(range(blocks)):
            at = slice(c * BLOCK, (c + 1) * BLOCK)
            pre = pre_all[at]
            gate = sigmoid(pre)
            x = pre * gate
            x_low = x.astype(low_type)
            x_round = x_low.astype(full_type)
            grad_y = grad_y_ref[at, :]
            grad_y_full = grad_y.astype(full_type)
            in_map = bc_ref[at, :STATE].astype(low_type)
            out_map = bc_ref[at, STATE:].astype(low_type)
            tail_c = widen(tail[at])
            enter_c = widen(enter[at])
            entering = state_in * jnp.exp2(widen(offs[c : c + 1]))
            if c > 0:
                entering = entering + states_ref[c - 1].astype(full_type)
            leaving = states_ref[c].astype(full_type) + state_in * jnp.exp2(widen(offs[c + 1 : c + 2]))
            entering_low = entering.astype(low_type)
            grad_low = grad_state.astype(low_type)
            ends = jnp.sum(grad_state * leaving, axis=0, keepdims=True)
            run_ends[c : c + 1, :] += head_sums(jnp.concatenate([ends, jnp.zeros((7, WIDE), full_type)], axis=0))[0:1]
            grad_x = tail_c * dot(in_map, grad_low)
            grad_maps[at, :STATE] += dot_nt((x * tail_c).astype(low_type), grad_low)
            swept = grad_y_full * enter_c
            swept_low = swept.astype(low_type)
            through = swept * dot(out_map, entering_low)
            grad_maps[at, STATE:] += dot_nt(swept_low, entering_low)
            fade = jnp.exp2(widen(offs[c + 1 : c + 2] - offs[c : c + 1]))
            grad_state = grad_state * fade + dot(out_t[:, at], swept_low)
            parts = []
            sums = []
            for pair in range(2):
                half = slice(pair * LANES, (pair + 1) * LANES)
                grad_half = grad_y[:, half]
                zero = jnp.zeros_like(grad_half)
                stacked = jnp.concatenate(
                    [jnp.where(left, grad_half, zero), jnp.where(left, zero, grad_half)], axis=0
                )
                cross = dot_nt(x_low[:, half], stacked)
                mixes = []
                for i in range(2):
                    h = 2 * pair + i
                    run_row = run_all[h : h + 1, at]
                    power = jnp.where(upper, run_row - lag[at, h : h + 1], -1e30)
                    decay = jnp.exp2(power)
                    mix = (decay * inter[c]).astype(low_type)
                    mixes.append(mix)
                    cross_h = cross[:, i * LANES : (i + 1) * LANES]
                    grad_inter[c] += cross_h * decay
                    sums.append(jnp.sum(cross_h * mix.astype(full_type), axis=0, keepdims=True))
                parts.append(dot(jnp.concatenate(mixes, axis=1), stacked))
            sums.append(jnp.zeros((4, BLOCK), full_type))
            run_rows[pl.ds(pl.multiple_of(8 * step, 8), 8), at] = jnp.concatenate(sums, axis=0)
            grad_x = grad_x + jnp.concatenate(parts, axis=1)
            weigh = head_sums(x_round * grad_x)
            weighs[at, :] += weigh
            run_cols[at, :] += head_sums(through) - weigh
            grad_skip = grad_skip + jnp.sum(grad_y_full * x, axis=0, keepdims=True)
            grad_x = grad_x + skip * grad_y_full
            padded[HALO + c * BLOCK : HALO + (c + 1) * BLOCK, :] = grad_x * (gate + x * (1.0 - gate))
        grad_skip_ref[...] = jnp.broadcast_to(grad_skip, grad_skip_ref.shape)
        conv_back(padded[HALO : HALO + rows, :])

    @pl.when(step == GROUPS)
    def _():
        sig[...] = sig_ref[...].astype(full_type)
        pre_all = convolve(sig, conv_ref[...], rows)
        for c in range(blocks):
            at = slice(c * BLOCK, (c + 1) * BLOCK)
            maps = bc_ref[at, :].astype(low_type)
            grad_block = grad_inter[c]
            grad_bc = grad_maps[at, :] + jnp.concatenate(
                [
                    dot(grad_block.astype(low_type), maps[:, STATE:]),
                    dot(grad_block.T.astype(low_type), maps[:, :STATE]),
                ],
                axis=1,
            )
            pre = pre_all[at]
            gate = sigmoid(pre)
            padded[HALO + c * BLOCK : HALO + (c + 1) * BLOCK, :] = grad_bc * (gate + pre * gate * (1.0 - gate))
        conv_back(padded[HALO : HALO + rows, :])

    @pl.when(step == GROUPS + 1)
    def _():
        head = head_ref[...]
        step_sizes, slope, rate = step_terms(raw_ref[HALO:, :].astype(full_type), head)
        ratio = jnp.where(step_sizes > 1e-30, slope / jnp.maximum(step_sizes, 1e-30), 1.0)
        used = lane_ids((BLOCK, LANES)) < HEADS
        later = jnp.where(upper, 1.0, 0.0)
        rate_sum = jnp.zeros((1, LANES), full_type)
        bias_sum = jnp.zeros((1, LANES), full_type)
        for c in range(blocks):
            at = slice(c * BLOCK, (c + 1) * BLOCK)
            by_head = [run_rows[8 * j : 8 * j + 4, at] for j in range(GROUPS)]
            by_head.append(jnp.zeros((LANES - HEADS, BLOCK), full_type))
            grad_run = jnp.concatenate(by_head, axis=0).T + run_cols[at, :]
            grad_rates = dot(later, grad_run, precision=highest) + run_ends[c : c + 1, :]
            grad_raw = slope[at] * rate * grad_rates + ratio[at] * weighs[at, :]
            grad_raw = jnp.where(used, grad_raw, 0.0)
            grad_pack[at, CONV_CH:] = grad_raw.astype(low_type)
            rate_sum = rate_sum + jnp.sum(grad_rates * step_sizes[at], axis=0, keepdims=True)
            bias_sum = bias_sum + jnp.sum(grad_raw, axis=0, keepdims=True)
        grad_head_ref[...] = jnp.concatenate(
            [rate_sum * rate, bias_sum, jnp.zeros((6, LANES), full_type)], axis=0
        )


def run_forward(packed, conv, head, normed, cot, gate_own, out_own):
    rows = packed.shape[0] - HALO
    blocks = rows // BLOCK
    count = lax.axis_size("wsh")
    gate_at, back_at = GROUPS + CHAIN_LAG, 2 * GROUPS + CHAIN_LAG
    at = lambda first: lambda j: jnp.clip(j - first, 0, GROUPS - 1)
    once = pl.Buffered(1)
    whole = lambda shape: pl.BlockSpec(shape, lambda j: (0,) * len(shape), pipeline_mode=once)
    kept = lambda shape: pl.BlockSpec(shape, lambda j: (0,) * len(shape))
    cols = lambda height, first: pl.BlockSpec((height, WIDE), lambda j: (0, at(first)(j)))
    anywhere = pl.BlockSpec(memory_space=pl.ANY)
    small = jax.ShapeDtypeStruct((rows, LANES), full_type)
    small_t = jax.ShapeDtypeStruct((LANES, rows), full_type)
    wide = jax.ShapeDtypeStruct((rows, INNER), full_type)
    vmem = pltpu.VMEM
    return pl.pallas_call(
        functools.partial(forward_kernel, count),
        grid=(back_at + GROUPS,),
        in_specs=[
            cols(rows + HALO, 0),
            pl.BlockSpec((rows + HALO, WIDE), lambda j: (0, GROUPS), pipeline_mode=once),
            pl.BlockSpec((rows + HALO, LANES), lambda j: (0, CONV_CH // LANES), pipeline_mode=once),
            cols(8, 0),
            pl.BlockSpec((8, WIDE), lambda j: (0, GROUPS), pipeline_mode=once),
            whole((8, LANES)),
            whole(normed.shape),
            whole(cot.shape),
            whole(gate_own.shape),
            whole(out_own.shape),
        ],
        out_specs=[
            cols(rows, 0),
            kept((rows, WIDE)),
            kept((rows, LANES)),
            kept((LANES, rows)),
            kept((rows, LANES)),
            kept((rows, LANES)),
            kept((rows, LANES)),
            kept((16, LANES)),
            pl.BlockSpec((blocks, STATE, WIDE), lambda j: (0, 0, at(0)(j))),
            cols(STATE, CHAIN_LAG),
            cols(rows, gate_at),
            cols(rows, back_at),
            anywhere,
            anywhere,
        ],
        out_shape=[
            wide,
            jax.ShapeDtypeStruct((rows, WIDE), full_type),
            small, small_t, small, small, small,
            jax.ShapeDtypeStruct((16, LANES), full_type),
            jax.ShapeDtypeStruct((blocks, STATE, INNER), low_type),
            jax.ShapeDtypeStruct((STATE, INNER), low_type),
            wide,
            wide,
            jax.ShapeDtypeStruct((D, INNER), low_type),
            jax.ShapeDtypeStruct((INNER, D), low_type),
        ],
        scratch_shapes=[
            vmem((rows + HALO, WIDE), full_type),
            vmem((STATE, rows), low_type),
            vmem((blocks, BLOCK, BLOCK), full_type),
            vmem((rows, LANES), full_type),
            vmem((LANES, rows), full_type),
            vmem((GROUPS, STATE, WIDE), full_type),
            vmem((GROUPS, STATE, WIDE), low_type),
            vmem((GROUPS, STATE, WIDE), low_type),
            pltpu.SemaphoreType.DMA((2, GROUPS)),
            vmem((D, INNER), low_type),
            vmem((INNER, D), low_type),
            *gather_sems(count),
            *gather_sems(count),
            pltpu.SemaphoreType.DMA((2,)),
        ],
        compiler_params=pltpu.CompilerParams(collective_id=1, has_side_effects=True, vmem_limit_bytes=VMEM_LIMIT),
        cost_estimate=pl.CostEstimate(flops=10**11, bytes_accessed=60 * 10**6, transcendentals=4 * 10**6),
        name="forward_scan",
    )(packed, packed, packed, conv, conv, head, normed, cot, gate_own, out_own)


def run_norm(y, gate, back, gain, bc, enter, state, normed):
    rows = y.shape[0]
    part = BLOCK
    by_rows = lambda cols: pl.BlockSpec((part, cols), lambda i: (i, 0))
    whole = lambda shape: pl.BlockSpec(shape, lambda i: (0,) * len(shape))
    return pl.pallas_call(
        norm_kernel,
        grid=(rows // part,),
        in_specs=[
            by_rows(INNER), by_rows(INNER), by_rows(INNER), whole((8, INNER)),
            by_rows(WIDE), by_rows(LANES), whole((STATE, INNER)), by_rows(D),
        ],
        out_specs=[
            by_rows(INNER), pl.BlockSpec((INNER + D, part), lambda i: (0, i)), by_rows(INNER), by_rows(INNER),
            whole((8, INNER)), whole((STATE, INNER)),
        ],
        out_shape=[
            jax.ShapeDtypeStruct((rows, INNER), low_type),
            jax.ShapeDtypeStruct((INNER + D, rows), low_type),
            jax.ShapeDtypeStruct((rows, INNER), low_type),
            jax.ShapeDtypeStruct((rows, INNER), low_type),
            jax.ShapeDtypeStruct((8, INNER), full_type),
            jax.ShapeDtypeStruct((STATE, INNER), full_type),
        ],
        scratch_shapes=[pltpu.VMEM((part, INNER), full_type), pltpu.VMEM((part, INNER), low_type)],
        compiler_params=pltpu.CompilerParams(vmem_limit_bytes=VMEM_LIMIT),
        cost_estimate=pl.CostEstimate(flops=10**9, bytes_accessed=30 * 10**6, transcendentals=3 * 10**6),
        name="gated_norm",
    )(y, gate, back, gain, bc, enter, state, normed)


def run_backward(
    packed, conv, head, grad_y, bc, lag, run_t, enter, tail, offs, states, state_in, grad_state, lefts, cot, grad_gate,
    full_gate, full_sig,
):
    rows = grad_y.shape[0]
    blocks = rows // BLOCK
    wsh_count, seq_count = lax.axis_size("wsh"), lax.axis_size("seq")
    groups = INNER // D
    n_out, n_gate, n_sig = cot.shape[1] // TILE, grad_gate.shape[1] // TILE, PACK // TILE
    first_gate, first_sig = n_out * groups, n_out * groups + n_gate
    spans = [(0, n_out, groups, 0), (first_gate, n_gate, 1, INNER), (first_sig, n_sig, 1, INNER)]
    chunks = first_sig + n_sig
    anywhere = pl.BlockSpec(memory_space=pl.ANY)
    ahead = steps_ahead(seq_count)
    low_at = lambda j, top: jnp.clip(j - ahead, 0, top)
    once = pl.Buffered(1)
    whole = lambda shape: pl.BlockSpec(shape, lambda j: (0,) * len(shape), pipeline_mode=once)
    kept = lambda shape: pl.BlockSpec(shape, lambda j: (0,) * len(shape))
    return pl.pallas_call(
        functools.partial(backward_kernel, (wsh_count, seq_count), spans),
        grid=(GROUPS + 3 + ahead,),
        in_specs=[
            pl.BlockSpec((rows + HALO, WIDE), lambda j: (0, low_at(j, GROUPS))),
            pl.BlockSpec((rows + HALO, LANES), lambda j: (0, CONV_CH // LANES), pipeline_mode=once),
            pl.BlockSpec((8, WIDE), lambda j: (0, low_at(j, GROUPS))),
            whole((8, LANES)),
            pl.BlockSpec((rows, WIDE), lambda j: (0, low_at(j, GROUPS - 1))),
            whole((rows, WIDE)),
            whole((rows, LANES)),
            whole((LANES, rows)),
            whole((rows, LANES)),
            whole((rows, LANES)),
            whole((16, LANES)),
            pl.BlockSpec((blocks, STATE, WIDE), lambda j: (0, 0, low_at(j, GROUPS - 1))),
            pl.BlockSpec((STATE, WIDE), lambda j: (0, low_at(j, GROUPS - 1))),
            whole((STATE, INNER)),
            whole(lefts.shape),
            whole(cot.shape),
            whole(grad_gate.shape),
            anywhere,
            anywhere,
        ],
        out_specs=[
            anywhere,
            pl.BlockSpec((8, WIDE), lambda j: (0, low_at(j, GROUPS))),
            pl.BlockSpec((8, WIDE), lambda j: (0, low_at(j, GROUPS - 1))),
            kept((8, LANES)),
            anywhere,
        ],
        out_shape=[
            jax.ShapeDtypeStruct((rows, D), full_type),
            jax.ShapeDtypeStruct((8, CONV_CH), full_type),
            jax.ShapeDtypeStruct((8, INNER), full_type),
            jax.ShapeDtypeStruct((8, LANES), full_type),
            jax.ShapeDtypeStruct((chunks, D // wsh_count, TILE), low_type),
        ],
        scratch_shapes=[
            pltpu.VMEM((rows + HALO, WIDE), full_type),
            pltpu.VMEM((rows + 2 * HALO, WIDE), full_type),
            pltpu.VMEM((blocks, BLOCK, BLOCK), full_type),
            pltpu.VMEM((blocks, BLOCK, BLOCK), full_type),
            pltpu.VMEM((rows, WIDE), full_type),
            pltpu.VMEM((STATE, rows), low_type),
            pltpu.VMEM((LANES, rows), full_type),
            pltpu.VMEM((rows, LANES), full_type),
            pltpu.VMEM((8, LANES), full_type),
            pltpu.VMEM((rows, LANES), full_type),
            pltpu.VMEM((GROUPS, STATE, WIDE), low_type),
            pltpu.VMEM((GROUPS, STATE, WIDE), low_type),
            pltpu.SemaphoreType.DMA((2, GROUPS)),
            pltpu.VMEM((rows, PACK), low_type),
            pltpu.VMEM((GROUPS + 1, 16, WIDE), full_type),
            pltpu.VMEM((GROUPS + 1, 8, WIDE), full_type),
            pltpu.VMEM((GROUPS + 1, 8, WIDE), full_type),
            pltpu.SemaphoreType.DMA((2, GROUPS + 1)),
            pltpu.VMEM((rows, D), full_type),
            pltpu.VMEM((2, D, TILE), low_type),
            pltpu.SemaphoreType.DMA((2,)),
            pltpu.SemaphoreType.DMA((1,)),
            *reduce_scratch(chunks, rows, wsh_count),
        ],
        compiler_params=pltpu.CompilerParams(collective_id=2, has_side_effects=True, vmem_limit_bytes=61 * 1024 * 1024),
        cost_estimate=pl.CostEstimate(flops=10**11, bytes_accessed=20 * 10**6, transcendentals=5 * 10**6),
        name="scan_backward",
    )(
        packed, packed, conv, head, grad_y, bc, lag, run_t, enter, tail, offs, states, state_in, grad_state,
        lefts, cot, grad_gate, full_gate, full_sig,
    )


def adam_update(weights, gradient, first_moment, second_moment, step_rate, decay_amount):
    next_first = beta_one * first_moment + (1.0 - beta_one) * gradient
    next_second = beta_two * second_moment + (1.0 - beta_two) * (gradient * gradient)
    spread = jnp.sqrt(next_second * (1.0 / (1.0 - beta_two**STEP))) + adam_eps
    change = next_first * (step_rate / (1.0 - beta_one**STEP)) / spread
    return (weights * (1.0 - step_rate * decay_amount) - change, next_first, next_second)


def swap(vals, bit, axis="wsh"):
    return lax.ppermute(vals, axis, [(i, i ^ bit) for i in range(lax.axis_size(axis))])


def sum_small(vals, beside):
    hops = [
        (axis, 1 << b) for axis in ("wsh", "seq") for b in range(lax.axis_size(axis).bit_length() - 1)
    ]
    for i, (axis, bit) in enumerate(hops):
        got = swap(vals, bit, axis)
        if i < len(beside):
            got = after(got, beside[i])
        vals = vals + got
    return vals


TILE = 384
FAR_LAG = 2
UP_LAG = 1
LAND_SLOTS = 10
SLACK = 1


def part_orders(count):
    far = [b for b in range(count.bit_length() - 2)]
    return [far[p:] + far[:p] for p in range(len(far))]


def held(order, phase, bits):
    done = sum(1 << b for b in order[:phase])
    left = [m for m in range(1 << bits) if m & done == 0]
    bit = 1 << order[phase]
    return [m for m in left if m & bit == 0], [m for m in left if m & bit]


def greet():
    me, z = lax.axis_index("wsh"), lax.axis_index("seq")
    seq_count = lax.axis_size("seq")
    barrier = pltpu.get_barrier_semaphore()
    mesh_id = pl.DeviceIdType.MESH
    bits = lax.axis_size("wsh").bit_length() - 1
    for b in range(bits):
        pl.semaphore_signal(barrier, inc=1, device_id={"wsh": lax.bitwise_xor(me, 1 << b)}, device_id_type=mesh_id)

    @pl.when(z > 0)
    def _():
        pl.semaphore_signal(barrier, inc=1, device_id={"seq": z - 1}, device_id_type=mesh_id)

    @pl.when(z < seq_count - 1)
    def _():
        pl.semaphore_signal(barrier, inc=1, device_id={"seq": z + 1}, device_id_type=mesh_id)

    along = jnp.where(z > 0, 1, 0) + jnp.where(z < seq_count - 1, 1, 0)
    pl.semaphore_wait(barrier, bits + along)


def reduce_turns(wsh_count, seq_count, spans, left_ref, right_refs, out_ref, scratch):
    orders = part_orders(wsh_count)
    bits = len(orders)
    tile, stage, pair, *rest = scratch
    lands, rest = rest[:bits], rest[bits:]
    from_left, from_right, pair_sems, far_sems, seq_sems, out_sems = rest
    chunks, blocks, rows, _ = pair.shape
    slots = lands[0].shape[0]
    part = rows // bits
    me = lax.axis_index("wsh")
    z = lax.axis_index("seq")
    root = seq_count // 2
    mesh_id = pl.DeviceIdType.MESH

    def pair_copy(k):
        return pltpu.make_async_remote_copy(
            src_ref=stage.at[lax.rem(k, 2)], dst_ref=pair.at[k],
            send_sem=pair_sems.at[0, k], recv_sem=pair_sems.at[1, k],
            device_id={"wsh": lax.bitwise_xor(me, 1)}, device_id_type=mesh_id,
        )

    spots = []
    for q in range(bits):
        for p, order in enumerate(orders):
            for i, m in enumerate(held(order, q, bits)[1]):
                spots.append((q, p, i, m, 2 << order[q]))

    def far_copies(k, phase):
        return [
            pltpu.make_async_remote_copy(
                src_ref=pair.at[k, m, pl.ds(p * part, part)], dst_ref=lands[q].at[lax.rem(k, slots), p, i],
                send_sem=far_sems.at[0, n, k], recv_sem=far_sems.at[1, n, k],
                device_id={"wsh": lax.bitwise_xor(me, bit)}, device_id_type=mesh_id,
            )
            for n, (q, p, i, m, bit) in enumerate(spots)
            if q == phase
        ]

    def to_right(k, source):
        return pltpu.make_async_remote_copy(
            src_ref=source, dst_ref=from_left.at[k],
            send_sem=seq_sems.at[0, k], recv_sem=seq_sems.at[1, k],
            device_id={"seq": z + 1}, device_id_type=mesh_id,
        )

    def to_left(k, source):
        return pltpu.make_async_remote_copy(
            src_ref=source, dst_ref=from_right.at[k],
            send_sem=seq_sems.at[2, k], recv_sem=seq_sems.at[3, k],
            device_id={"seq": z - 1}, device_id_type=mesh_id,
        )

    def out_copy(k, source):
        return pltpu.make_async_copy(source, out_ref.at[k], out_sems.at[k])

    def take_tile(k):
        for (start, tiles, groups, _), right_ref in zip(spans, right_refs):

            @pl.when((k >= start) & (k < start + tiles * groups))
            def _():
                col = lax.rem(k - start, tiles) * TILE
                tile[...] = right_ref[:, pl.ds(pl.multiple_of(col, LANES), TILE)]

    def product(k, b, core):
        owner = lax.bitwise_xor(me, 2 * b + core)
        first = jnp.zeros((), jnp.int32)
        for start, tiles, groups, base in spans:
            at = base + (owner * groups + (k - start) // tiles) * rows
            first = jnp.where((k >= start) & (k < start + tiles * groups), at, first)
        return dot(left_ref[pl.ds(pl.multiple_of(first, 16), rows), :], tile[...])

    def begin(k):
        @pl.when(k >= 2)
        def _():
            pair_copy(k - 2).wait_send()

        take_tile(k)
        for b in range(blocks):
            stage[lax.rem(k, 2), b] = product(k, b, 1).astype(low_type)
        pair_copy(k).start()

    def add_pair(k):
        take_tile(k)
        pair_copy(k).wait_recv()
        for b in range(blocks):
            pair[k, b] = (product(k, b, 0) + pair[k, b].astype(full_type)).astype(low_type)
        for copy in far_copies(k, 0):
            copy.start()

    def add_far(k, phase):
        for copy in far_copies(k, phase):
            copy.wait_recv()
        for p, order in enumerate(orders):
            at = pl.ds(p * part, part)
            for i, m in enumerate(held(order, phase, bits)[0]):
                total = pair[k, m, at].astype(full_type) + lands[phase][lax.rem(k, slots), p, i].astype(full_type)
                pair[k, m, at] = total.astype(low_type)
        if phase < bits - 1:
            for copy in far_copies(k, phase + 1):
                copy.start()

    def add_to(k, land):
        pair[k, 0] = (pair[k, 0].astype(full_type) + land[k].astype(full_type)).astype(low_type)

    def seq_up(k):
        mine = pair.at[k, 0]

        @pl.when((z > 0) & (z <= root))
        def _():
            to_right(k, mine).wait_recv()
            add_to(k, from_left)

        @pl.when((z < seq_count - 1) & (z >= root))
        def _():
            to_left(k, mine).wait_recv()
            add_to(k, from_right)

        @pl.when((z < seq_count - 1) & (z <= root))
        def _():
            to_right(k, mine).start()

        @pl.when((z > 0) & (z >= root))
        def _():
            to_left(k, mine).start()

    def seq_down(k):
        @pl.when(z == root)
        def _():
            out_copy(k, pair.at[k, 0]).start()

        @pl.when(z < root)
        def _():
            to_left(k, from_right.at[k]).wait_recv()
            out_copy(k, from_right.at[k]).start()
            pl.when(z > 0)(lambda: to_left(k, from_right.at[k]).start())

        @pl.when(z > root)
        def _():
            to_right(k, from_left.at[k]).wait_recv()
            out_copy(k, from_left.at[k]).start()
            pl.when(z < seq_count - 1)(lambda: to_right(k, from_left.at[k]).start())

    far = jnp.abs(z - root)
    farthest = max(root, seq_count - 1 - root)
    stages = [(0, begin), (1, add_pair)] + [
        (1 + FAR_LAG * (q + 1), functools.partial(add_far, phase=q)) for q in range(bits)
    ]
    up_at = 1 + FAR_LAG * bits + UP_LAG
    stages += [(up_at + SLACK * (farthest - far), seq_up), (up_at + 1 + SLACK * (farthest + far), seq_down)]
    turns = chunks + up_at + 2 + SLACK * 2 * farthest

    def turn(s, carry):
        for offset, run in stages:
            pl.when((s >= offset) & (s < chunks + offset))(lambda run=run, offset=offset: run(s - offset))
        return carry

    def finish():
        def wait_all(k, carry):
            for q in range(bits):
                for copy in far_copies(k, q):
                    copy.wait_send()
            pl.when(z < seq_count - 1)(lambda: to_right(k, pair.at[k, 0]).wait_send())
            pl.when(z > 0)(lambda: to_left(k, pair.at[k, 0]).wait_send())
            out_copy(k, pair.at[k, 0]).wait()
            return carry

        lax.fori_loop(0, chunks, wait_all, 0)
        for k in (chunks - 2, chunks - 1):
            pair_copy(k).wait_send()

    return turns, turn, finish


def reduce_scratch(chunks, depth, wsh_count):
    rows = D // wsh_count
    bits = len(part_orders(wsh_count))
    low = lambda *shape: pltpu.VMEM(shape, low_type)
    dma = pltpu.SemaphoreType.DMA
    return [
        low(depth, TILE),
        low(2, 1 << bits, rows, TILE),
        low(chunks, 1 << bits, rows, TILE),
        *[low(min(chunks, LAND_SLOTS), bits, 1 << (bits - 1 - q), rows // bits, TILE) for q in range(bits)],
        low(chunks, rows, TILE),
        low(chunks, rows, TILE),
        dma((2, chunks)),
        dma((2, bits * ((1 << bits) - 1), chunks)),
        dma((4, chunks)),
        dma((chunks,)),
    ]


def adam_kernel(rate, decay, share_ref, weight_ref, first_ref, second_ref, *outs):
    grad_ref, next_ref, next_first_ref, next_second_ref = outs
    for i in range(share_ref.shape[0]):
        at = slice(i * TILE, (i + 1) * TILE)
        grad = share_ref[i].astype(full_type)
        grad_ref[:, at] = grad
        next_ref[:, at], next_first_ref[:, at], next_second_ref[:, at] = adam_update(
            weight_ref[:, at], grad, first_ref[:, at], second_ref[:, at], rate, decay
        )


def adam_chunks(sums, start, weights, first_moment, second_moment, rate, decay, name):
    all_rows, cols = weights.shape
    rows = sums.shape[1]
    tiles = pl.cdiv(cols, 2 * TILE)
    block = pl.BlockSpec((rows, 2 * TILE), lambda i, j: (i, j))
    return pl.pallas_call(
        functools.partial(adam_kernel, rate, decay),
        grid=(all_rows // rows, tiles),
        in_specs=[pl.BlockSpec((2, rows, TILE), lambda i, j: (start // 2 + i * tiles + j, 0, 0))] + [block] * 3,
        out_specs=[block] * 4,
        out_shape=[jax.ShapeDtypeStruct(weights.shape, full_type)] * 4,
        compiler_params=pltpu.CompilerParams(vmem_limit_bytes=VMEM_LIMIT),
        cost_estimate=pl.CostEstimate(
            flops=20 * weights.size, bytes_accessed=30 * weights.size, transcendentals=weights.size
        ),
        name=name,
    )(sums, weights, first_moment, second_moment)


def after(vals, *others):
    return lax.optimization_barrier((vals,) + others)[0]


def shards(
    inputs, cotangent, w_in, w_dt, w_out, gain_pre, gain_norm, conv_param, head_param,
    first_w_in, second_w_in, first_w_dt, second_w_dt, first_w_out, second_w_out,
    first_gain_pre, second_gain_pre, first_gain_norm, second_gain_norm,
    first_conv, second_conv, first_head, second_head,
):
    wsh_count = lax.axis_size("wsh")
    seq_count = lax.axis_size("seq")
    seq_index = lax.axis_index("seq")
    wsh_index = lax.axis_index("wsh")
    rows_model = D // wsh_count
    rows_inner = INNER // wsh_count
    cols_conv = CONV_CH // wsh_count
    cols_head = HEADS // wsh_count
    small = jnp.zeros((16, CONV_CH), full_type)
    for row, part in ((0, gain_pre[None]), (1, gain_norm[None]), (2, conv_param), (7, head_param)):
        small = lax.dynamic_update_slice(small, part, (row, wsh_index * part.shape[1]))
    part_sig = jnp.concatenate(
        [w_in[:, INNER:].astype(low_type), w_dt.astype(low_type), jnp.zeros((rows_model, LANES - HEADS), low_type)],
        axis=1,
    )
    tokens_low = inputs[0]
    cot_low = cotangent[0]
    rows = tokens_low.shape[0]
    before = lax.ppermute(tokens_low[rows - HALO :], "seq", [(i, i + 1) for i in range(seq_count - 1)])
    packed, normed, inv_wide, gain_in_rows, gain_rows, conv, head, full_sig = project_signal(
        jnp.concatenate([before, tokens_low], axis=0), part_sig, small.astype(low_type)
    )
    tokens = tokens_low.astype(full_type)
    inv_rms = inv_wide[:, :1]
    gain_in = gain_in_rows[0]
    (
        y, bc, lag, run_t, enter, enter_all, tail, offs, states, state_in, gate_vals, back, full_gate, full_out
    ) = run_forward(packed, conv, head, normed, cot_low, w_in[:, :INNER].astype(low_type), w_out.astype(low_type))
    normed_out, lefts, grad_y, grad_gate, part_gnorm, grad_state = run_norm(
        y, gate_vals, back, gain_rows, bc, enter_all, state_in, normed
    )
    block_out = (tokens + dot(normed_out, full_out)).astype(low_type)[None]
    grad_normed, part_conv, part_skip, part_head, sums = run_backward(
        packed, conv, head, grad_y, bc, lag, run_t, enter, tail, offs, states, state_in, grad_state,
        lefts, cot_low, grad_gate, full_gate, full_sig,
    )
    scaled = tokens * inv_rms
    part_gpre = jnp.sum(grad_normed * scaled, axis=0)
    pulled = grad_normed * gain_in
    grad_tokens = inv_rms * (pulled - scaled * jnp.mean(pulled * scaled, axis=-1, keepdims=True))
    input_grad = (cot_low.astype(full_type) + grad_tokens)[None]
    skip_sums = part_skip[0].reshape(HEADS, HEAD_DIM).sum(axis=1)
    small_parts = [
        part_gpre, part_gnorm[0], part_conv[:5].reshape(-1), part_head[0, :HEADS], part_head[1, :HEADS], skip_sums
    ]
    tiles_out = (INNER // D) * (D // TILE)
    grad_out, *new_out = adam_chunks(sums, 0, w_out, first_w_out, second_w_out, rate_matrix, weight_decay, "adam_w_out")
    grad_in_w, *new_in = adam_chunks(
        sums, tiles_out, w_in, first_w_in, second_w_in, rate_matrix, weight_decay, "adam_w_in"
    )
    at_dt = CONV_CH % TILE
    grad_dt = sums[-1, :, at_dt : at_dt + HEADS].astype(full_type)
    small_sums = sum_small(jnp.concatenate(small_parts), [block_out, new_out[0], new_in[0]])
    cuts = [D, D + INNER, D + INNER + 5 * CONV_CH]
    grad_gpre = lax.dynamic_slice_in_dim(small_sums[: cuts[0]], wsh_index * rows_model, rows_model, 0)
    grad_gnorm = lax.dynamic_slice_in_dim(small_sums[cuts[0] : cuts[1]], wsh_index * rows_inner, rows_inner, 0)
    grad_conv = lax.dynamic_slice_in_dim(
        small_sums[cuts[1] : cuts[2]].reshape(5, CONV_CH), wsh_index * cols_conv, cols_conv, 1
    )
    grad_head = lax.dynamic_slice_in_dim(
        small_sums[cuts[2] :].reshape(3, HEADS), wsh_index * cols_head, cols_head, 1
    )
    params = (w_in, w_dt, w_out, gain_pre, gain_norm, conv_param, head_param)
    gradients = (grad_in_w, grad_dt, grad_out, grad_gpre, grad_gnorm, grad_conv, grad_head)
    firsts = (first_w_in, first_w_dt, first_w_out, first_gain_pre, first_gain_norm, first_conv, first_head)
    seconds = (second_w_in, second_w_dt, second_w_out, second_gain_pre, second_gain_norm, second_conv, second_head)
    step_rates = (rate_matrix, rate_matrix, rate_matrix, rate_gain, rate_gain, rate_conv, rate_head)
    decays = (weight_decay, weight_decay, weight_decay, 0.0, 0.0, 0.0, 0.0)
    updated = [
        None if i in (0, 2) else adam_update(*items)
        for i, items in enumerate(zip(params, gradients, firsts, seconds, step_rates, decays))
    ]
    updated[0], updated[2] = new_in, new_out
    new_params = tuple(entry[0] for entry in updated)
    moments = []
    for entry in updated:
        moments.append(entry[1])
        moments.append(entry[2])
    return (block_out, input_grad) + gradients + new_params + tuple(moments)


def solution(mesh):
    rows, vec, cols = P("wsh", None), P("wsh"), P(None, "wsh")
    tokens = P("wsh", "seq", None)
    params = (rows, rows, rows, vec, vec, cols, cols)
    moments = tuple(spec for spec in params for _ in range(2))
    in_specs = (tokens, tokens) + params + moments
    out_specs = (tokens, tokens) + params + params + moments
    return jax.shard_map(shards, mesh=mesh, in_specs=in_specs, out_specs=out_specs, check_vma=False)
```

```python
import functools

import jax
import jax.numpy as jnp
from jax import lax
from jax.experimental import pallas as pl
from jax.experimental.pallas import tpu as pltpu
from jax.sharding import PartitionSpec as P

D = 1536
HEADS = 48
HEAD_DIM = 64
STATE = 128
CONV_WIDTH = 4
STEP = 2
INNER = 3072
CONV_CH = 3328
BLOCK = 128
LANES = 128
WIDE = 256
SIG_PIECES = 3
HALO = 16
GROUPS = INNER // WIDE
CHAIN_LAG = 2
CHAIN_PER = 2
PACK = CONV_CH + LANES
LOG2E = 1.4426950408889634
VMEM_LIMIT = 56 * 1024 * 1024

norm_eps = 1e-05
beta_one = 0.9
beta_two = 0.999
adam_eps = 1e-08
rate_matrix = 0.01
rate_gain = 0.4
rate_conv = 0.1
rate_head = 1.0
weight_decay = 0.1
highest = lax.Precision.HIGHEST
low_type = jnp.bfloat16
full_type = jnp.float32


def dot(left_side, right_side, dims=((1,), (0,)), precision=None):
    return lax.dot_general(
        left_side, right_side, (dims, ((), ())), precision=precision, preferred_element_type=full_type
    )


def dot_nt(left_side, right_side):
    return dot(left_side, right_side, ((1,), (1,)))


def sigmoid(vals):
    return 0.5 * jnp.tanh(0.5 * vals) + 0.5


def lane_ids(shape):
    return lax.broadcasted_iota(jnp.int32, shape, len(shape) - 1)


def widen(vals, first=0):
    left = lane_ids((vals.shape[0], LANES)) < HEAD_DIM
    pairs = [
        jnp.where(left, vals[:, first + i : first + i + 1], vals[:, first + i + 1 : first + i + 2])
        for i in (0, 2)
    ]
    return jnp.concatenate(pairs, axis=1)


def to_front(vals, step):
    return pltpu.roll(vals, lax.rem(LANES - 4 * step, LANES), 1)


def head_rows(ref, step):
    eight = ref[pl.ds(pl.multiple_of(8 * (step // 2), 8), 8), :]
    return pltpu.roll(eight, 4 * lax.rem(step, 2), 0)


def step_terms(raw, head):
    shifted = raw + head[1:2]
    small = jnp.exp(-jnp.abs(shifted))
    log_part = jnp.where(
        small < 0.01, small * (1.0 - small * (0.5 - small * (1.0 / 3.0))), jnp.log(1.0 + small)
    )
    step_sizes = jnp.maximum(shifted, 0.0) + log_part
    slope = jnp.where(shifted >= 0.0, 1.0, small) / (1.0 + small)
    return step_sizes, slope, -jnp.exp(head[0:1])


def convolve(sig, conv, rows):
    total = conv[4:5] + conv[0:1] * sig[HALO - 3 : HALO - 3 + rows, :]
    for k in range(1, CONV_WIDTH):
        total = total + conv[k : k + 1] * sig[HALO - 3 + k : HALO - 3 + k + rows, :]
    return total


def triangle(lower):
    rows = lax.broadcasted_iota(jnp.int32, (BLOCK, BLOCK), 0)
    cols = lax.broadcasted_iota(jnp.int32, (BLOCK, BLOCK), 1)
    return rows >= cols if lower else rows <= cols


def gather_steps(count, own_ref, full_ref, far_sems, core_sems, cols=None, split=True):
    orders = part_orders(count)
    bits = len(orders)
    orders = orders if split else orders[:1]
    rows = own_ref.shape[0]
    part = rows // len(orders)
    cols = cols or (0, own_ref.shape[1])
    me = lax.axis_index("wsh")
    mesh_id = pl.DeviceIdType.MESH

    def copy(m, first, size, bit, sems, n):
        start = lax.bitwise_xor(me, 2 * m) * rows + first
        at = full_ref.at[pl.ds(pl.multiple_of(start, 16), size), pl.ds(*cols)]
        return pltpu.make_async_remote_copy(
            src_ref=at, dst_ref=at, send_sem=sems.at[0, n], recv_sem=sems.at[1, n],
            device_id={"wsh": lax.bitwise_xor(me, bit)}, device_id_type=mesh_id,
        )

    far_spots = [
        (q, m, p * part, part, 2 << order[q])
        for q in range(bits)
        for p, order in enumerate(orders)
        for m in range(1 << bits)
        if m & ~sum(1 << b for b in order[:q]) == 0
    ]
    core_spots = [(0, 0, 0, rows, 1)] + [
        (q + 1, m, p * part, part, 1)
        for q in range(bits)
        for p, order in enumerate(orders)
        for m in range(1 << bits)
        if m >> order[q] & 1 and m & ~sum(1 << b for b in order[: q + 1]) == 0
    ]
    pick = lambda spots, sems, phase: [
        copy(m, first, size, bit, sems, n)
        for n, (q, m, first, size, bit) in enumerate(spots)
        if phase is None or q == phase
    ]

    def start():
        full_ref[pl.ds(pl.multiple_of(me * rows, 16), rows), pl.ds(*cols)] = own_ref[:, pl.ds(*cols)]
        for item in pick(far_spots, far_sems, 0) + pick(core_spots, core_sems, 0):
            item.start()

    def advance(phase):
        for item in pick(far_spots, far_sems, phase):
            item.wait_recv()
        later = pick(far_spots, far_sems, phase + 1) if phase + 1 < bits else []
        for item in later + pick(core_spots, core_sems, phase + 1):
            item.start()

    def done():
        for item in pick(core_spots, core_sems, None):
            item.wait_recv()

    def finish():
        for item in pick(far_spots, far_sems, None) + pick(core_spots, core_sems, None):
            item.wait_send()

    return start, advance, done, finish


def gather_sems(count, split=True):
    bits = len(part_orders(count))
    copies = (bits if split else 1) * ((1 << bits) - 1)
    return [pltpu.SemaphoreType.DMA((2, copies)), pltpu.SemaphoreType.DMA((2, copies + 1))]


def forward_kernel(
    count,
    tokens_ref, sig_own_ref, small_ref, cot_ref, gate_own_ref, out_own_ref,
    packed_ref, normed_ref, inv_ref, gain_in_ref, gain_out_ref, conv_ref, head_ref, full_sig_ref,
    y_ref, bc_ref, lag_ref, run_t_ref, enter_ref, enter_all_ref, tail_ref, offs_ref, states_ref, before_ref,
    gate_ref, back_ref, full_gate_ref, full_out_ref,
    sig, in_t, inter, run, lag_t, ends, stage, land, sems, gate_full, out_full,
    gate_far, gate_core, out_far, out_core, full_sems,
    packed, normed, sig_full, small_full, small_far, small_core, *sig_sems,
):
    step = pl.program_id(0)
    rows = y_ref.shape[0]
    blocks = rows // BLOCK
    z = lax.axis_index("seq")
    seq_count = lax.axis_size("seq")
    lower = triangle(True)
    bits = len(part_orders(count))
    gate_start, gate_advance, gate_done, gate_finish = gather_steps(count, gate_own_ref, gate_full, gate_far, gate_core)
    out_start, out_advance, out_done, out_finish = gather_steps(count, out_own_ref, out_full, out_far, out_core)
    gate_at, back_at = GROUPS + CHAIN_LAG, 2 * GROUPS + CHAIN_LAG
    small_start, small_advance, small_done, small_finish = gather_steps(
        count, small_ref, small_full, small_far, small_core, split=False
    )
    width = PACK // SIG_PIECES
    gathers = [
        gather_steps(count, sig_own_ref, sig_full, sig_sems[2 * c], sig_sems[2 * c + 1], cols=(c * width, width))
        for c in range(SIG_PIECES)
    ]
    sig_out = pltpu.make_async_copy(sig_full, full_sig_ref, full_sems.at[2])
    packed_out = pltpu.make_async_copy(packed, packed_ref, full_sems.at[3])
    normed_out = pltpu.make_async_copy(normed.at[pl.ds(HALO, rows)], normed_ref, full_sems.at[4])

    def project_signal():
        small_start()
        for start, _, _, _ in gathers:
            start()
        for q in range(bits):
            small_advance(q)
        small_done()
        height = small_ref.shape[0]
        small = small_full[:height, :].astype(full_type)
        for d in range(1, count):
            small = small + small_full[d * height : (d + 1) * height, :].astype(full_type)
        gain_in_ref[...] = jnp.broadcast_to(small[0:1, :D], gain_in_ref.shape)
        gain_out_ref[...] = jnp.broadcast_to(small[1:2, :INNER], gain_out_ref.shape)
        conv_ref[...] = jnp.concatenate([small[2:7], jnp.zeros((3, CONV_CH), full_type)], axis=0)
        head_ref[...] = jnp.concatenate([small[7:10, :LANES], jnp.zeros((5, LANES), full_type)], axis=0)
        gathers[0][1](0)
        all_rows = tokens_ref.shape[0]
        for first in range(0, all_rows, BLOCK):
            size = min(BLOCK, all_rows - first)
            tokens = tokens_ref[first : first + size, :].astype(full_type)
            inv = lax.rsqrt(jnp.sum(tokens * tokens, axis=1, keepdims=True) * (1.0 / D) + norm_eps)
            normed[first : first + size, :] = (tokens * inv * gain_in_ref[0:1, :]).astype(low_type)
            skip = max(HALO - first, 0)
            at = slice(first + skip - HALO, first + size - HALO)
            inv_ref[at, :] = jnp.broadcast_to(inv[skip:], (size - skip, LANES))
        normed_out.start()
        for _, advance, _, _ in gathers[1:]:
            advance(0)
        gate_start()
        out_start()
        for c, (_, advance, done, _) in enumerate(gathers):
            for q in range(1, bits):
                advance(q)
            done()

            def multiply(t, carry, c=c):
                col = pl.multiple_of(c * width + t * TILE, LANES)
                packed[:, pl.ds(col, TILE)] = dot(normed[...], sig_full[:, pl.ds(col, TILE)]).astype(low_type)
                return carry

            lax.fori_loop(0, width // TILE, multiply, 0)
        sig_out.start()
        packed_out.start()

    def to_next(k):
        return pltpu.make_async_remote_copy(
            src_ref=stage.at[k], dst_ref=land.at[k], send_sem=sems.at[0, k], recv_sem=sems.at[1, k],
            device_id={"seq": z + 1}, device_id_type=pl.DeviceIdType.MESH,
        )

    @pl.when(step == 0)
    def _():
        greet()
        project_signal()
        sig[...] = packed[:, INNER:CONV_CH].astype(full_type)
        pre = convolve(sig, conv_ref[:, INNER:], rows)
        maps = pre * sigmoid(pre)
        bc_ref[...] = maps
        in_t[...] = maps[:, :STATE].T.astype(low_type)
        step_sizes, _, rate = step_terms(packed[HALO:, CONV_CH:].astype(full_type), head_ref[...])
        rates = step_sizes * rate * LOG2E
        log_steps = jnp.log2(step_sizes)
        sums = jnp.where(lower, 1.0, 0.0)
        offset = jnp.zeros((1, LANES), full_type)
        offs_ref[...] = jnp.zeros(offs_ref.shape, full_type)
        for c in range(blocks):
            at = slice(c * BLOCK, (c + 1) * BLOCK)
            total = dot(sums, rates[at], precision=highest)
            lag = total - log_steps[at]
            run[at, :] = total
            lag_ref[at, :] = lag
            run_t_ref[:, at] = total.T
            lag_t[:, at] = lag.T
            enter_ref[at, :] = jnp.exp2(total)
            enter_all_ref[at, :] = jnp.exp2(total + offset)
            tail_ref[at, :] = jnp.exp2(total[BLOCK - 1 : BLOCK] - lag)
            offs_ref[c : c + 1, :] = offset
            offset = offset + total[BLOCK - 1 : BLOCK]
            low_maps = maps[at].astype(low_type)
            inter[c] = dot_nt(low_maps[:, STATE:], low_maps[:, :STATE])
        offs_ref[blocks : blocks + 1, :] = offset

    pl.when(step == GROUPS // 2)(lambda: gate_advance(0))
    pl.when(step == GROUPS)(lambda: out_advance(0))

    @pl.when(step < GROUPS)
    def _():
        cols = pl.ds(pl.multiple_of(step * WIDE, WIDE), WIDE)
        sig[...] = packed[:, cols].astype(full_type)
        pre_all = convolve(sig, conv_ref[:, cols], rows)
        tail = to_front(tail_ref[...], step)
        last = to_front(offs_ref[...], step)
        run_all = to_front(run[...], step)
        enter = to_front(enter_ref[...], step)
        lag_rows = head_rows(lag_t, step)
        skip = widen(to_front(head_ref[...], step)[2:3])
        left = lane_ids((BLOCK, LANES)) < HEAD_DIM
        state = jnp.zeros((STATE, WIDE), full_type)
        for c in range(blocks):
            at = slice(c * BLOCK, (c + 1) * BLOCK)
            pre = pre_all[at]
            x = pre * sigmoid(pre)
            parts = []
            for pair in range(2):
                mixes = []
                for i in range(2):
                    h = 2 * pair + i
                    power = jnp.where(lower, run_all[at, h : h + 1] - lag_rows[h : h + 1, at], -1e30)
                    mixes.append((jnp.exp2(power) * inter[c]).astype(low_type))
                half = x[:, pair * LANES : (pair + 1) * LANES].astype(low_type)
                zero = jnp.zeros_like(half)
                stacked = jnp.concatenate([jnp.where(left, half, zero), jnp.where(left, zero, half)], axis=0)
                parts.append(dot(jnp.concatenate(mixes, axis=1), stacked))
            y = jnp.concatenate(parts, axis=1) + skip * x
            if c > 0:
                out_map = bc_ref[at, STATE:].astype(low_type)
                y = y + widen(enter[at]) * dot(out_map, state.astype(low_type))
            y_ref[at, :] = y
            weighted = (x * widen(tail[at])).astype(low_type)
            fade = jnp.exp2(widen(last[c + 1 : c + 2] - last[c : c + 1]))
            state = state * fade + dot(in_t[:, at], weighted)
            states_ref[c] = state.astype(low_type)
        ends[step] = state

    @pl.when((step >= CHAIN_LAG) & (step < gate_at))
    def _():
        k = step - CHAIN_LAG

        @pl.when(z == 0)
        def _():
            land[k] = jnp.zeros((STATE, WIDE), low_type)

        @pl.when(z > 0)
        def _():
            to_next(k).wait_recv()

        before_ref[...] = land[k]

        @pl.when(z < seq_count - 1)
        def _():
            fade = jnp.exp2(widen(to_front(offs_ref[...], k)[blocks : blocks + 1]))
            stage[k] = (ends[k] + fade * land[k].astype(full_type)).astype(low_type)
            to_next(k).start()

    gate_out = pltpu.make_async_copy(gate_full, full_gate_ref, full_sems.at[0])
    out_out = pltpu.make_async_copy(out_full, full_out_ref, full_sems.at[1])

    @pl.when(step == gate_at)
    def _():
        for q in range(1, bits):
            gate_advance(q)
        gate_done()
        gate_out.start()

    @pl.when((step >= gate_at) & (step < back_at))
    def _():
        col = pl.multiple_of((step - gate_at) * WIDE, WIDE)
        gate_ref[...] = dot(normed[HALO:, :], gate_full[:, pl.ds(col, WIDE)])

    @pl.when(step == back_at)
    def _():
        for q in range(1, bits):
            out_advance(q)
        out_done()
        out_out.start()

    @pl.when(step >= back_at)
    def _():
        row = pl.multiple_of((step - back_at) * WIDE, WIDE)
        back_ref[...] = dot_nt(cot_ref[...], out_full[pl.ds(row, WIDE), :])

    @pl.when(step == back_at + GROUPS - 1)
    def _():
        for _, _, _, end in gathers:
            end()
        small_finish()
        gate_finish()
        out_finish()
        sig_out.wait()
        packed_out.wait()
        normed_out.wait()
        gate_out.wait()
        out_out.wait()

        @pl.when(z < seq_count - 1)
        def _():
            for k in range(GROUPS):
                to_next(k).wait_send()


def norm_kernel(
    y_ref, gate_ref, back_ref, gain_ref, bc_ref, enter_ref, state_ref, inner_ref,
    normed_ref, lefts_ref, grad_y_ref, grad_gate_ref, grad_gain_ref, grad_state_ref,
    gated, low_y,
):
    step = pl.program_id(0)
    rows = y_ref.shape[0]

    @pl.when(step == 0)
    def _():
        grad_gain_ref[...] = jnp.zeros(grad_gain_ref.shape, full_type)
        grad_state_ref[...] = jnp.zeros(grad_state_ref.shape, full_type)

    for j in range(D // WIDE):
        lefts_ref[INNER + j * WIDE : INNER + (j + 1) * WIDE, :] = inner_ref[:, j * WIDE : (j + 1) * WIDE].T
    out_map = bc_ref[:, STATE:]
    out_low = out_map.astype(low_type)
    out_t = out_map.T.astype(low_type)
    squares = jnp.zeros((rows, WIDE), full_type)
    cross = jnp.zeros((rows, WIDE), full_type)
    for j in range(GROUPS):
        at = slice(j * WIDE, (j + 1) * WIDE)
        enter = widen(enter_ref[...], 4 * j)
        y = y_ref[:, at] + enter * dot(out_low, state_ref[:, at])
        y_low = y.astype(low_type)
        low_y[:, at] = y_low
        gate = gate_ref[:, at]
        vals = y_low.astype(full_type) * (gate * sigmoid(gate))
        gated[:, at] = vals
        squares = squares + vals * vals
        cross = cross + vals * (back_ref[:, at] * gain_ref[0:1, at])
    inv = lax.rsqrt(jnp.sum(squares, axis=1, keepdims=True) * (1.0 / INNER) + norm_eps)
    pull = inv * inv * inv * (jnp.sum(cross, axis=1, keepdims=True) * (1.0 / INNER))
    for j in range(GROUPS):
        at = slice(j * WIDE, (j + 1) * WIDE)
        gain = gain_ref[0:1, at]
        back = back_ref[:, at]
        vals = gated[:, at]
        scaled = vals * inv
        normed = (scaled * gain).astype(low_type)
        normed_ref[:, at] = normed
        lefts_ref[at, :] = normed.T
        grad_gain_ref[0:1, at] += jnp.sum(back * scaled, axis=0, keepdims=True)
        grad_vals = back * gain * inv - vals * pull
        gate = gate_ref[:, at]
        sig = sigmoid(gate)
        silu = gate * sig
        grad_y = (grad_vals * silu).astype(low_type)
        grad_y_ref[:, at] = grad_y
        slope = sig + silu * (1.0 - sig)
        grad_gate_ref[:, at] = (grad_vals * low_y[:, at].astype(full_type) * slope).astype(low_type)
        enter = widen(enter_ref[...], 4 * j)
        grad_state_ref[:, at] += dot(out_t, (grad_y.astype(full_type) * enter).astype(low_type))


def steps_ahead(seq_count):
    return GROUPS // CHAIN_PER + seq_count - 1


def backward_kernel(
    counts, spans,
    sig_ref, raw_ref, conv_ref, head_ref, grad_y_ref, bc_ref,
    lag_ref, run_t_ref, enter_ref, tail_ref, offs_ref, states_ref, state_in_ref, grad_state_ref,
    lefts_ref, cot_ref, grad_gate_ref, full_gate_ref, full_sig_ref,
    grad_normed_ref, grad_conv_ref, grad_skip_ref, grad_head_ref, sums_ref,
    sig, padded, inter, grad_inter, grad_maps, out_t, run_rows, run_cols, run_ends, weighs,
    stage, land, chain_sems, grad_pack, lasts, edges, edge_land, edge_sems, grad_normed, weights, weight_sems, done_sems,
    *scratch,
):
    ahead = steps_ahead(counts[1])
    place = pl.program_id(0)
    step = place - ahead
    steps = GROUPS + 2 + ahead
    rows = grad_y_ref.shape[0]
    blocks = rows // BLOCK
    z = lax.axis_index("seq")
    seq_count = counts[1]
    mesh_id = pl.DeviceIdType.MESH
    first_gate, first_sig = spans[1][0], spans[2][0]
    chunks = first_sig + spans[2][1]

    def weight_copies(k):
        slot = lax.rem(k, 2)
        for ref, first, last in ((full_gate_ref, first_gate, first_sig), (full_sig_ref, first_sig, chunks)):
            col = pl.multiple_of(jnp.clip(k - first, 0, last - first - 1) * TILE, LANES)
            copy = pltpu.make_async_copy(ref.at[:, pl.ds(col, TILE)], weights.at[slot], weight_sems.at[slot])
            yield (k >= first) & (k < last), copy

    def add_normed(k, right_ref, first):
        col = pl.multiple_of((k - first) * TILE, LANES)
        for right, copy in weight_copies(k):
            pl.when(right)(copy.wait)
        for right, copy in weight_copies(k + 1):
            pl.when(right)(copy.start)

        part = dot_nt(right_ref[:, pl.ds(col, TILE)], weights[lax.rem(k, 2)])

        @pl.when(k == first_gate)
        def _():
            grad_normed[...] = part

        @pl.when(k > first_gate)
        def _():
            grad_normed[...] += part

    def late_turn(s, carry):
        turn(s, 0)
        per = -(-(chunks - first_gate) // (turns - early))
        for i in range(per):
            k = first_gate + (s - early) * per + i
            pl.when(k < first_sig)(lambda k=k: add_normed(k, grad_gate_ref, first_gate))
            pl.when((k >= first_sig) & (k < chunks))(lambda k=k: add_normed(k, grad_pack, first_sig))
        return carry

    turns, turn, finish = reduce_turns(
        *counts, spans, lefts_ref, [cot_ref, grad_gate_ref, grad_pack], sums_ref, scratch
    )

    def to_previous(k):
        return pltpu.make_async_remote_copy(
            src_ref=stage.at[k], dst_ref=land.at[k], send_sem=chain_sems.at[0, k], recv_sem=chain_sems.at[1, k],
            device_id={"seq": z - 1}, device_id_type=mesh_id,
        )

    def edge_copy(k):
        return pltpu.make_async_remote_copy(
            src_ref=edges.at[k], dst_ref=edge_land.at[k], send_sem=edge_sems.at[0, k], recv_sem=edge_sems.at[1, k],
            device_id={"seq": z - 1}, device_id_type=mesh_id,
        )

    def chain(k):
        @pl.when(z == seq_count - 1)
        def _():
            land[k] = jnp.zeros((STATE, WIDE), low_type)

        @pl.when(z < seq_count - 1)
        def _():
            to_previous(k).wait_recv()

        @pl.when(z > 0)
        def _():
            fade = jnp.exp2(widen(to_front(offs_ref[...], k)[blocks : blocks + 1]))
            own = grad_state_ref[:, pl.ds(pl.multiple_of(k * WIDE, WIDE), WIDE)]
            stage[k] = (own + fade * land[k].astype(full_type)).astype(low_type)
            to_previous(k).start()

    def mend(k):
        @pl.when(z == seq_count - 1)
        def _():
            edge_land[k] = jnp.zeros((8, WIDE), full_type)

        @pl.when(z < seq_count - 1)
        def _():
            edge_copy(k).wait_recv()

        whole = lasts[k] + jnp.concatenate([jnp.zeros((8, WIDE), full_type), edge_land[k]], axis=0)
        grad_pack[rows - 16 :, pl.ds(pl.multiple_of(k * WIDE, WIDE), WIDE)] = whole.astype(low_type)

    @pl.when(place == 0)
    def _():
        greet()
        next(copy for _, copy in weight_copies(first_gate)).start()

    @pl.when((step >= 1) & (step <= GROUPS + 1))
    def _():
        mend(step - 1)

    early = chunks - 1
    for i in range(spans[2][1] - 1):
        at = next(p for p in range(steps) if (p + 1) * early // steps > first_sig + i)
        assert ahead + ((i + 1) * TILE - 1) // WIDE + 1 <= at

    @pl.when(place < steps)
    def _():
        lax.fori_loop(place * early // steps, (place + 1) * early // steps, turn, 0)

    upper = triangle(False)

    turn_of = place - (seq_count - 1 - z)

    @pl.when((turn_of >= 0) & (turn_of < GROUPS // CHAIN_PER))
    def _():
        for i in range(CHAIN_PER):
            chain(turn_of * CHAIN_PER + i)

    @pl.when(place == steps)
    def _():
        lax.fori_loop(early, turns, late_turn, 0)
        normed_copy = pltpu.make_async_copy(grad_normed, grad_normed_ref, done_sems.at[0])
        normed_copy.start()
        finish()
        normed_copy.wait()

        @pl.when(z > 0)
        def _():
            for k in range(GROUPS):
                to_previous(k).wait_send()
            for k in range(GROUPS + 1):
                edge_copy(k).wait_send()

    @pl.when(step == 0)
    def _():
        for c in range(blocks):
            at = slice(c * BLOCK, (c + 1) * BLOCK)
            maps = bc_ref[at, :].astype(low_type)
            inter[c] = dot_nt(maps[:, :STATE], maps[:, STATE:])
            out_t[:, at] = bc_ref[at, STATE:].T.astype(low_type)
        grad_inter[...] = jnp.zeros(grad_inter.shape, full_type)
        grad_maps[...] = jnp.zeros(grad_maps.shape, full_type)
        run_rows[...] = jnp.zeros(run_rows.shape, full_type)
        run_cols[...] = jnp.zeros(run_cols.shape, full_type)
        run_ends[...] = jnp.zeros(run_ends.shape, full_type)
        weighs[...] = jnp.zeros(weighs.shape, full_type)
        padded[...] = jnp.zeros(padded.shape, full_type)

    def conv_back(grad_pre):
        conv = conv_ref[...]
        grad_sig = conv[3:4] * padded[HALO : HALO + rows, :]
        edge = conv[3:4] * padded[8:HALO, :]
        for k in range(3):
            grad_sig = grad_sig + conv[k : k + 1] * padded[HALO + 3 - k : HALO + 3 - k + rows, :]
            edge = edge + conv[k : k + 1] * padded[11 - k : 19 - k, :]
        grad_pack[:, pl.ds(pl.multiple_of(step * WIDE, WIDE), WIDE)] = grad_sig.astype(low_type)
        lasts[step] = grad_sig[rows - 16 :]

        @pl.when(z > 0)
        def _():
            edges[step] = edge
            edge_copy(step).start()

        sums = [
            jnp.sum(grad_pre * sig[HALO - 3 + k : HALO - 3 + k + rows, :], axis=0, keepdims=True)
            for k in range(CONV_WIDTH)
        ]
        sums.append(jnp.sum(grad_pre, axis=0, keepdims=True))
        sums.append(jnp.zeros((3, WIDE), full_type))
        grad_conv_ref[...] = jnp.concatenate(sums, axis=0)

    @pl.when((step >= 0) & (step < GROUPS))
    def _():
        sig[...] = sig_ref[...].astype(full_type)
        lag = to_front(lag_ref[...], step)
        run_all = head_rows(run_t_ref, step)
        enter = to_front(enter_ref[...], step)
        tail = to_front(tail_ref[...], step)
        offs = to_front(offs_ref[...], step)
        skip = widen(to_front(head_ref[...], step)[2:3])
        left = lane_ids((BLOCK, LANES)) < HEAD_DIM
        heads_of = lax.broadcasted_iota(jnp.int32, (WIDE, LANES), 0) // HEAD_DIM + 4 * step
        picks = jnp.where(heads_of == lane_ids((WIDE, LANES)), 1.0, 0.0).astype(low_type)
        state_in = state_in_ref[...].astype(full_type)
        grad_state = land[step].astype(full_type)
        grad_skip = jnp.zeros((1, WIDE), full_type)
        pre_all = convolve(sig, conv_ref[...], rows)

        def head_sums(vals):
            high = vals.astype(low_type)
            rest = (vals - high.astype(full_type)).astype(low_type)
            return dot(high, picks) + dot(rest, picks)

        for c in reversed(range(blocks)):
            at = slice(c * BLOCK, (c + 1) * BLOCK)
            pre = pre_all[at]
            gate = sigmoid(pre)
            x = pre * gate
            x_low = x.astype(low_type)
            x_round = x_low.astype(full_type)
            grad_y = grad_y_ref[at, :]
            grad_y_full = grad_y.astype(full_type)
            in_map = bc_ref[at, :STATE].astype(low_type)
            out_map = bc_ref[at, STATE:].astype(low_type)
            tail_c = widen(tail[at])
            enter_c = widen(enter[at])
            entering = state_in * jnp.exp2(widen(offs[c : c + 1]))
            if c > 0:
                entering = entering + states_ref[c - 1].astype(full_type)
            leaving = states_ref[c].astype(full_type) + state_in * jnp.exp2(widen(offs[c + 1 : c + 2]))
            entering_low = entering.astype(low_type)
            grad_low = grad_state.astype(low_type)
            ends = jnp.sum(grad_state * leaving, axis=0, keepdims=True)
            run_ends[c : c + 1, :] += head_sums(jnp.concatenate([ends, jnp.zeros((7, WIDE), full_type)], axis=0))[0:1]
            grad_x = tail_c * dot(in_map, grad_low)
            grad_maps[at, :STATE] += dot_nt((x * tail_c).astype(low_type), grad_low)
            swept = grad_y_full * enter_c
            swept_low = swept.astype(low_type)
            through = swept * dot(out_map, entering_low)
            grad_maps[at, STATE:] += dot_nt(swept_low, entering_low)
            fade = jnp.exp2(widen(offs[c + 1 : c + 2] - offs[c : c + 1]))
            grad_state = grad_state * fade + dot(out_t[:, at], swept_low)
            parts = []
            sums = []
            for pair in range(2):
                half = slice(pair * LANES, (pair + 1) * LANES)
                grad_half = grad_y[:, half]
                zero = jnp.zeros_like(grad_half)
                stacked = jnp.concatenate(
                    [jnp.where(left, grad_half, zero), jnp.where(left, zero, grad_half)], axis=0
                )
                cross = dot_nt(x_low[:, half], stacked)
                mixes = []
                for i in range(2):
                    h = 2 * pair + i
                    run_row = run_all[h : h + 1, at]
                    power = jnp.where(upper, run_row - lag[at, h : h + 1], -1e30)
                    decay = jnp.exp2(power)
                    mix = (decay * inter[c]).astype(low_type)
                    mixes.append(mix)
                    cross_h = cross[:, i * LANES : (i + 1) * LANES]
                    grad_inter[c] += cross_h * decay
                    sums.append(jnp.sum(cross_h * mix.astype(full_type), axis=0, keepdims=True))
                parts.append(dot(jnp.concatenate(mixes, axis=1), stacked))
            sums.append(jnp.zeros((4, BLOCK), full_type))
            run_rows[pl.ds(pl.multiple_of(8 * step, 8), 8), at] = jnp.concatenate(sums, axis=0)
            grad_x = grad_x + jnp.concatenate(parts, axis=1)
            weigh = head_sums(x_round * grad_x)
            weighs[at, :] += weigh
            run_cols[at, :] += head_sums(through) - weigh
            grad_skip = grad_skip + jnp.sum(grad_y_full * x, axis=0, keepdims=True)
            grad_x = grad_x + skip * grad_y_full
            padded[HALO + c * BLOCK : HALO + (c + 1) * BLOCK, :] = grad_x * (gate + x * (1.0 - gate))
        grad_skip_ref[...] = jnp.broadcast_to(grad_skip, grad_skip_ref.shape)
        conv_back(padded[HALO : HALO + rows, :])

    @pl.when(step == GROUPS)
    def _():
        sig[...] = sig_ref[...].astype(full_type)
        pre_all = convolve(sig, conv_ref[...], rows)
        for c in range(blocks):
            at = slice(c * BLOCK, (c + 1) * BLOCK)
            maps = bc_ref[at, :].astype(low_type)
            grad_block = grad_inter[c]
            grad_bc = grad_maps[at, :] + jnp.concatenate(
                [
                    dot(grad_block.astype(low_type), maps[:, STATE:]),
                    dot(grad_block.T.astype(low_type), maps[:, :STATE]),
                ],
                axis=1,
            )
            pre = pre_all[at]
            gate = sigmoid(pre)
            padded[HALO + c * BLOCK : HALO + (c + 1) * BLOCK, :] = grad_bc * (gate + pre * gate * (1.0 - gate))
        conv_back(padded[HALO : HALO + rows, :])

    @pl.when(step == GROUPS + 1)
    def _():
        head = head_ref[...]
        step_sizes, slope, rate = step_terms(raw_ref[HALO:, :].astype(full_type), head)
        ratio = jnp.where(step_sizes > 1e-30, slope / jnp.maximum(step_sizes, 1e-30), 1.0)
        used = lane_ids((BLOCK, LANES)) < HEADS
        later = jnp.where(upper, 1.0, 0.0)
        rate_sum = jnp.zeros((1, LANES), full_type)
        bias_sum = jnp.zeros((1, LANES), full_type)
        for c in range(blocks):
            at = slice(c * BLOCK, (c + 1) * BLOCK)
            by_head = [run_rows[8 * j : 8 * j + 4, at] for j in range(GROUPS)]
            by_head.append(jnp.zeros((LANES - HEADS, BLOCK), full_type))
            grad_run = jnp.concatenate(by_head, axis=0).T + run_cols[at, :]
            grad_rates = dot(later, grad_run, precision=highest) + run_ends[c : c + 1, :]
            grad_raw = slope[at] * rate * grad_rates + ratio[at] * weighs[at, :]
            grad_raw = jnp.where(used, grad_raw, 0.0)
            grad_pack[at, CONV_CH:] = grad_raw.astype(low_type)
            rate_sum = rate_sum + jnp.sum(grad_rates * step_sizes[at], axis=0, keepdims=True)
            bias_sum = bias_sum + jnp.sum(grad_raw, axis=0, keepdims=True)
        grad_head_ref[...] = jnp.concatenate(
            [rate_sum * rate, bias_sum, jnp.zeros((6, LANES), full_type)], axis=0
        )


def run_forward(tokens, sig_own, small, cot, gate_own, out_own):
    all_rows = tokens.shape[0]
    rows = all_rows - HALO
    blocks = rows // BLOCK
    count = lax.axis_size("wsh")
    gate_at, back_at = GROUPS + CHAIN_LAG, 2 * GROUPS + CHAIN_LAG
    at = lambda first: lambda j: jnp.clip(j - first, 0, GROUPS - 1)
    once = pl.Buffered(1)
    whole = lambda shape: pl.BlockSpec(shape, lambda j: (0,) * len(shape), pipeline_mode=once)
    kept = lambda shape: pl.BlockSpec(shape, lambda j: (0,) * len(shape))
    cols = lambda height, first: pl.BlockSpec((height, WIDE), lambda j: (0, at(first)(j)))
    anywhere = pl.BlockSpec(memory_space=pl.ANY)
    small_out = jax.ShapeDtypeStruct((rows, LANES), full_type)
    eight = lambda width: jax.ShapeDtypeStruct((8, width), full_type)
    small_t = jax.ShapeDtypeStruct((LANES, rows), full_type)
    wide = jax.ShapeDtypeStruct((rows, INNER), full_type)
    vmem = pltpu.VMEM
    return pl.pallas_call(
        functools.partial(forward_kernel, count),
        grid=(back_at + GROUPS,),
        in_specs=[whole(item.shape) for item in (tokens, sig_own, small, cot, gate_own, out_own)],
        out_specs=[
            anywhere,
            anywhere,
            kept((rows, LANES)),
            kept((8, D)),
            kept((8, INNER)),
            kept((8, CONV_CH)),
            kept((8, LANES)),
            anywhere,
            cols(rows, 0),
            kept((rows, WIDE)),
            kept((rows, LANES)),
            kept((LANES, rows)),
            kept((rows, LANES)),
            kept((rows, LANES)),
            kept((rows, LANES)),
            kept((16, LANES)),
            pl.BlockSpec((blocks, STATE, WIDE), lambda j: (0, 0, at(0)(j))),
            cols(STATE, CHAIN_LAG),
            cols(rows, gate_at),
            cols(rows, back_at),
            anywhere,
            anywhere,
        ],
        out_shape=[
            jax.ShapeDtypeStruct((all_rows, PACK), low_type),
            jax.ShapeDtypeStruct((rows, D), low_type),
            small_out,
            eight(D), eight(INNER), eight(CONV_CH), eight(LANES),
            jax.ShapeDtypeStruct((D, PACK), low_type),
            wide,
            jax.ShapeDtypeStruct((rows, WIDE), full_type),
            small_out, small_t, small_out, small_out, small_out,
            jax.ShapeDtypeStruct((16, LANES), full_type),
            jax.ShapeDtypeStruct((blocks, STATE, INNER), low_type),
            jax.ShapeDtypeStruct((STATE, INNER), low_type),
            wide,
            wide,
            jax.ShapeDtypeStruct((D, INNER), low_type),
            jax.ShapeDtypeStruct((INNER, D), low_type),
        ],
        scratch_shapes=[
            vmem((rows + HALO, WIDE), full_type),
            vmem((STATE, rows), low_type),
            vmem((blocks, BLOCK, BLOCK), full_type),
            vmem((rows, LANES), full_type),
            vmem((LANES, rows), full_type),
            vmem((GROUPS, STATE, WIDE), full_type),
            vmem((GROUPS, STATE, WIDE), low_type),
            vmem((GROUPS, STATE, WIDE), low_type),
            pltpu.SemaphoreType.DMA((2, GROUPS)),
            vmem((D, INNER), low_type),
            vmem((INNER, D), low_type),
            *gather_sems(count),
            *gather_sems(count),
            pltpu.SemaphoreType.DMA((5,)),
            vmem((all_rows, PACK), low_type),
            vmem((all_rows, D), low_type),
            vmem((D, PACK), low_type),
            vmem((count * small.shape[0], CONV_CH), low_type),
            *gather_sems(count, split=False),
            *[sem for _ in range(SIG_PIECES) for sem in gather_sems(count)],
        ],
        compiler_params=pltpu.CompilerParams(collective_id=1, has_side_effects=True, vmem_limit_bytes=61 * 1024 * 1024),
        cost_estimate=pl.CostEstimate(flops=10**11, bytes_accessed=60 * 10**6, transcendentals=4 * 10**6),
        name="forward_scan",
    )(tokens, sig_own, small, cot, gate_own, out_own)


def run_norm(y, gate, back, gain, bc, enter, state, normed):
    rows = y.shape[0]
    part = BLOCK
    by_rows = lambda cols: pl.BlockSpec((part, cols), lambda i: (i, 0))
    whole = lambda shape: pl.BlockSpec(shape, lambda i: (0,) * len(shape))
    return pl.pallas_call(
        norm_kernel,
        grid=(rows // part,),
        in_specs=[
            by_rows(INNER), by_rows(INNER), by_rows(INNER), whole((8, INNER)),
            by_rows(WIDE), by_rows(LANES), whole((STATE, INNER)), by_rows(D),
        ],
        out_specs=[
            by_rows(INNER), pl.BlockSpec((INNER + D, part), lambda i: (0, i)), by_rows(INNER), by_rows(INNER),
            whole((8, INNER)), whole((STATE, INNER)),
        ],
        out_shape=[
            jax.ShapeDtypeStruct((rows, INNER), low_type),
            jax.ShapeDtypeStruct((INNER + D, rows), low_type),
            jax.ShapeDtypeStruct((rows, INNER), low_type),
            jax.ShapeDtypeStruct((rows, INNER), low_type),
            jax.ShapeDtypeStruct((8, INNER), full_type),
            jax.ShapeDtypeStruct((STATE, INNER), full_type),
        ],
        scratch_shapes=[pltpu.VMEM((part, INNER), full_type), pltpu.VMEM((part, INNER), low_type)],
        compiler_params=pltpu.CompilerParams(vmem_limit_bytes=VMEM_LIMIT),
        cost_estimate=pl.CostEstimate(flops=10**9, bytes_accessed=30 * 10**6, transcendentals=3 * 10**6),
        name="gated_norm",
    )(y, gate, back, gain, bc, enter, state, normed)


def run_backward(
    packed, conv, head, grad_y, bc, lag, run_t, enter, tail, offs, states, state_in, grad_state, lefts, cot, grad_gate,
    full_gate, full_sig,
):
    rows = grad_y.shape[0]
    blocks = rows // BLOCK
    wsh_count, seq_count = lax.axis_size("wsh"), lax.axis_size("seq")
    groups = INNER // D
    n_out, n_gate, n_sig = cot.shape[1] // TILE, grad_gate.shape[1] // TILE, PACK // TILE
    first_gate, first_sig = n_out * groups, n_out * groups + n_gate
    spans = [(0, n_out, groups, 0), (first_gate, n_gate, 1, INNER), (first_sig, n_sig, 1, INNER)]
    chunks = first_sig + n_sig
    anywhere = pl.BlockSpec(memory_space=pl.ANY)
    ahead = steps_ahead(seq_count)
    low_at = lambda j, top: jnp.clip(j - ahead, 0, top)
    once = pl.Buffered(1)
    whole = lambda shape: pl.BlockSpec(shape, lambda j: (0,) * len(shape), pipeline_mode=once)
    kept = lambda shape: pl.BlockSpec(shape, lambda j: (0,) * len(shape))
    return pl.pallas_call(
        functools.partial(backward_kernel, (wsh_count, seq_count), spans),
        grid=(GROUPS + 3 + ahead,),
        in_specs=[
            pl.BlockSpec((rows + HALO, WIDE), lambda j: (0, low_at(j, GROUPS))),
            pl.BlockSpec((rows + HALO, LANES), lambda j: (0, CONV_CH // LANES), pipeline_mode=once),
            pl.BlockSpec((8, WIDE), lambda j: (0, low_at(j, GROUPS))),
            whole((8, LANES)),
            pl.BlockSpec((rows, WIDE), lambda j: (0, low_at(j, GROUPS - 1))),
            whole((rows, WIDE)),
            whole((rows, LANES)),
            whole((LANES, rows)),
            whole((rows, LANES)),
            whole((rows, LANES)),
            whole((16, LANES)),
            pl.BlockSpec((blocks, STATE, WIDE), lambda j: (0, 0, low_at(j, GROUPS - 1))),
            pl.BlockSpec((STATE, WIDE), lambda j: (0, low_at(j, GROUPS - 1))),
            whole((STATE, INNER)),
            whole(lefts.shape),
            whole(cot.shape),
            whole(grad_gate.shape),
            anywhere,
            anywhere,
        ],
        out_specs=[
            anywhere,
            pl.BlockSpec((8, WIDE), lambda j: (0, low_at(j, GROUPS))),
            pl.BlockSpec((8, WIDE), lambda j: (0, low_at(j, GROUPS - 1))),
            kept((8, LANES)),
            anywhere,
        ],
        out_shape=[
            jax.ShapeDtypeStruct((rows, D), full_type),
            jax.ShapeDtypeStruct((8, CONV_CH), full_type),
            jax.ShapeDtypeStruct((8, INNER), full_type),
            jax.ShapeDtypeStruct((8, LANES), full_type),
            jax.ShapeDtypeStruct((chunks, D // wsh_count, TILE), low_type),
        ],
        scratch_shapes=[
            pltpu.VMEM((rows + HALO, WIDE), full_type),
            pltpu.VMEM((rows + 2 * HALO, WIDE), full_type),
            pltpu.VMEM((blocks, BLOCK, BLOCK), full_type),
            pltpu.VMEM((blocks, BLOCK, BLOCK), full_type),
            pltpu.VMEM((rows, WIDE), full_type),
            pltpu.VMEM((STATE, rows), low_type),
            pltpu.VMEM((LANES, rows), full_type),
            pltpu.VMEM((rows, LANES), full_type),
            pltpu.VMEM((8, LANES), full_type),
            pltpu.VMEM((rows, LANES), full_type),
            pltpu.VMEM((GROUPS, STATE, WIDE), low_type),
            pltpu.VMEM((GROUPS, STATE, WIDE), low_type),
            pltpu.SemaphoreType.DMA((2, GROUPS)),
            pltpu.VMEM((rows, PACK), low_type),
            pltpu.VMEM((GROUPS + 1, 16, WIDE), full_type),
            pltpu.VMEM((GROUPS + 1, 8, WIDE), full_type),
            pltpu.VMEM((GROUPS + 1, 8, WIDE), full_type),
            pltpu.SemaphoreType.DMA((2, GROUPS + 1)),
            pltpu.VMEM((rows, D), full_type),
            pltpu.VMEM((2, D, TILE), low_type),
            pltpu.SemaphoreType.DMA((2,)),
            pltpu.SemaphoreType.DMA((1,)),
            *reduce_scratch(chunks, rows, wsh_count),
        ],
        compiler_params=pltpu.CompilerParams(collective_id=2, has_side_effects=True, vmem_limit_bytes=61 * 1024 * 1024),
        cost_estimate=pl.CostEstimate(flops=10**11, bytes_accessed=20 * 10**6, transcendentals=5 * 10**6),
        name="scan_backward",
    )(
        packed, packed, conv, head, grad_y, bc, lag, run_t, enter, tail, offs, states, state_in, grad_state,
        lefts, cot, grad_gate, full_gate, full_sig,
    )


def adam_update(weights, gradient, first_moment, second_moment, step_rate, decay_amount):
    next_first = beta_one * first_moment + (1.0 - beta_one) * gradient
    next_second = beta_two * second_moment + (1.0 - beta_two) * (gradient * gradient)
    spread = jnp.sqrt(next_second * (1.0 / (1.0 - beta_two**STEP))) + adam_eps
    change = next_first * (step_rate / (1.0 - beta_one**STEP)) / spread
    return (weights * (1.0 - step_rate * decay_amount) - change, next_first, next_second)


def swap(vals, bit, axis="wsh"):
    return lax.ppermute(vals, axis, [(i, i ^ bit) for i in range(lax.axis_size(axis))])


def sum_small(vals, beside):
    hops = [
        (axis, 1 << b) for axis in ("wsh", "seq") for b in range(lax.axis_size(axis).bit_length() - 1)
    ]
    for i, (axis, bit) in enumerate(hops):
        got = swap(vals, bit, axis)
        if i < len(beside):
            got = after(got, beside[i])
        vals = vals + got
    return vals


TILE = 384
FAR_LAG = 2
UP_LAG = 1
LAND_SLOTS = 10
SLACK = 1


def part_orders(count):
    far = [b for b in range(count.bit_length() - 2)]
    return [far[p:] + far[:p] for p in range(len(far))]


def held(order, phase, bits):
    done = sum(1 << b for b in order[:phase])
    left = [m for m in range(1 << bits) if m & done == 0]
    bit = 1 << order[phase]
    return [m for m in left if m & bit == 0], [m for m in left if m & bit]


def greet():
    me, z = lax.axis_index("wsh"), lax.axis_index("seq")
    seq_count = lax.axis_size("seq")
    barrier = pltpu.get_barrier_semaphore()
    mesh_id = pl.DeviceIdType.MESH
    bits = lax.axis_size("wsh").bit_length() - 1
    for b in range(bits):
        pl.semaphore_signal(barrier, inc=1, device_id={"wsh": lax.bitwise_xor(me, 1 << b)}, device_id_type=mesh_id)

    @pl.when(z > 0)
    def _():
        pl.semaphore_signal(barrier, inc=1, device_id={"seq": z - 1}, device_id_type=mesh_id)

    @pl.when(z < seq_count - 1)
    def _():
        pl.semaphore_signal(barrier, inc=1, device_id={"seq": z + 1}, device_id_type=mesh_id)

    along = jnp.where(z > 0, 1, 0) + jnp.where(z < seq_count - 1, 1, 0)
    pl.semaphore_wait(barrier, bits + along)


def reduce_turns(wsh_count, seq_count, spans, left_ref, right_refs, out_ref, scratch):
    orders = part_orders(wsh_count)
    bits = len(orders)
    tile, stage, pair, *rest = scratch
    lands, rest = rest[:bits], rest[bits:]
    from_left, from_right, pair_sems, far_sems, seq_sems, out_sems = rest
    chunks, blocks, rows, _ = pair.shape
    slots = lands[0].shape[0]
    part = rows // bits
    me = lax.axis_index("wsh")
    z = lax.axis_index("seq")
    root = seq_count // 2
    mesh_id = pl.DeviceIdType.MESH

    def pair_copy(k):
        return pltpu.make_async_remote_copy(
            src_ref=stage.at[lax.rem(k, 2)], dst_ref=pair.at[k],
            send_sem=pair_sems.at[0, k], recv_sem=pair_sems.at[1, k],
            device_id={"wsh": lax.bitwise_xor(me, 1)}, device_id_type=mesh_id,
        )

    spots = []
    for q in range(bits):
        for p, order in enumerate(orders):
            for i, m in enumerate(held(order, q, bits)[1]):
                spots.append((q, p, i, m, 2 << order[q]))

    def far_copies(k, phase):
        return [
            pltpu.make_async_remote_copy(
                src_ref=pair.at[k, m, pl.ds(p * part, part)], dst_ref=lands[q].at[lax.rem(k, slots), p, i],
                send_sem=far_sems.at[0, n, k], recv_sem=far_sems.at[1, n, k],
                device_id={"wsh": lax.bitwise_xor(me, bit)}, device_id_type=mesh_id,
            )
            for n, (q, p, i, m, bit) in enumerate(spots)
            if q == phase
        ]

    def to_right(k, source):
        return pltpu.make_async_remote_copy(
            src_ref=source, dst_ref=from_left.at[k],
            send_sem=seq_sems.at[0, k], recv_sem=seq_sems.at[1, k],
            device_id={"seq": z + 1}, device_id_type=mesh_id,
        )

    def to_left(k, source):
        return pltpu.make_async_remote_copy(
            src_ref=source, dst_ref=from_right.at[k],
            send_sem=seq_sems.at[2, k], recv_sem=seq_sems.at[3, k],
            device_id={"seq": z - 1}, device_id_type=mesh_id,
        )

    def out_copy(k, source):
        return pltpu.make_async_copy(source, out_ref.at[k], out_sems.at[k])

    def take_tile(k):
        for (start, tiles, groups, _), right_ref in zip(spans, right_refs):

            @pl.when((k >= start) & (k < start + tiles * groups))
            def _():
                col = lax.rem(k - start, tiles) * TILE
                tile[...] = right_ref[:, pl.ds(pl.multiple_of(col, LANES), TILE)]

    def product(k, b, core):
        owner = lax.bitwise_xor(me, 2 * b + core)
        first = jnp.zeros((), jnp.int32)
        for start, tiles, groups, base in spans:
            at = base + (owner * groups + (k - start) // tiles) * rows
            first = jnp.where((k >= start) & (k < start + tiles * groups), at, first)
        return dot(left_ref[pl.ds(pl.multiple_of(first, 16), rows), :], tile[...])

    def begin(k):
        @pl.when(k >= 2)
        def _():
            pair_copy(k - 2).wait_send()

        take_tile(k)
        for b in range(blocks):
            stage[lax.rem(k, 2), b] = product(k, b, 1).astype(low_type)
        pair_copy(k).start()

    def add_pair(k):
        take_tile(k)
        pair_copy(k).wait_recv()
        for b in range(blocks):
            pair[k, b] = (product(k, b, 0) + pair[k, b].astype(full_type)).astype(low_type)
        for copy in far_copies(k, 0):
            copy.start()

    def add_far(k, phase):
        for copy in far_copies(k, phase):
            copy.wait_recv()
        for p, order in enumerate(orders):
            at = pl.ds(p * part, part)
            for i, m in enumerate(held(order, phase, bits)[0]):
                total = pair[k, m, at].astype(full_type) + lands[phase][lax.rem(k, slots), p, i].astype(full_type)
                pair[k, m, at] = total.astype(low_type)
        if phase < bits - 1:
            for copy in far_copies(k, phase + 1):
                copy.start()

    def add_to(k, land):
        pair[k, 0] = (pair[k, 0].astype(full_type) + land[k].astype(full_type)).astype(low_type)

    def seq_up(k):
        mine = pair.at[k, 0]

        @pl.when((z > 0) & (z <= root))
        def _():
            to_right(k, mine).wait_recv()
            add_to(k, from_left)

        @pl.when((z < seq_count - 1) & (z >= root))
        def _():
            to_left(k, mine).wait_recv()
            add_to(k, from_right)

        @pl.when((z < seq_count - 1) & (z <= root))
        def _():
            to_right(k, mine).start()

        @pl.when((z > 0) & (z >= root))
        def _():
            to_left(k, mine).start()

    def seq_down(k):
        @pl.when(z == root)
        def _():
            out_copy(k, pair.at[k, 0]).start()

        @pl.when(z < root)
        def _():
            to_left(k, from_right.at[k]).wait_recv()
            out_copy(k, from_right.at[k]).start()
            pl.when(z > 0)(lambda: to_left(k, from_right.at[k]).start())

        @pl.when(z > root)
        def _():
            to_right(k, from_left.at[k]).wait_recv()
            out_copy(k, from_left.at[k]).start()
            pl.when(z < seq_count - 1)(lambda: to_right(k, from_left.at[k]).start())

    far = jnp.abs(z - root)
    farthest = max(root, seq_count - 1 - root)
    stages = [(0, begin), (1, add_pair)] + [
        (1 + FAR_LAG * (q + 1), functools.partial(add_far, phase=q)) for q in range(bits)
    ]
    up_at = 1 + FAR_LAG * bits + UP_LAG
    stages += [(up_at + SLACK * (farthest - far), seq_up), (up_at + 1 + SLACK * (farthest + far), seq_down)]
    turns = chunks + up_at + 2 + SLACK * 2 * farthest

    def turn(s, carry):
        for offset, run in stages:
            pl.when((s >= offset) & (s < chunks + offset))(lambda run=run, offset=offset: run(s - offset))
        return carry

    def finish():
        def wait_all(k, carry):
            for q in range(bits):
                for copy in far_copies(k, q):
                    copy.wait_send()
            pl.when(z < seq_count - 1)(lambda: to_right(k, pair.at[k, 0]).wait_send())
            pl.when(z > 0)(lambda: to_left(k, pair.at[k, 0]).wait_send())
            out_copy(k, pair.at[k, 0]).wait()
            return carry

        lax.fori_loop(0, chunks, wait_all, 0)
        for k in (chunks - 2, chunks - 1):
            pair_copy(k).wait_send()

    return turns, turn, finish


def reduce_scratch(chunks, depth, wsh_count):
    rows = D // wsh_count
    bits = len(part_orders(wsh_count))
    low = lambda *shape: pltpu.VMEM(shape, low_type)
    dma = pltpu.SemaphoreType.DMA
    return [
        low(depth, TILE),
        low(2, 1 << bits, rows, TILE),
        low(chunks, 1 << bits, rows, TILE),
        *[low(min(chunks, LAND_SLOTS), bits, 1 << (bits - 1 - q), rows // bits, TILE) for q in range(bits)],
        low(chunks, rows, TILE),
        low(chunks, rows, TILE),
        dma((2, chunks)),
        dma((2, bits * ((1 << bits) - 1), chunks)),
        dma((4, chunks)),
        dma((chunks,)),
    ]


def adam_kernel(rate, decay, share_ref, weight_ref, first_ref, second_ref, *outs):
    grad_ref, next_ref, next_first_ref, next_second_ref = outs
    for i in range(share_ref.shape[0]):
        at = slice(i * TILE, (i + 1) * TILE)
        grad = share_ref[i].astype(full_type)
        grad_ref[:, at] = grad
        next_ref[:, at], next_first_ref[:, at], next_second_ref[:, at] = adam_update(
            weight_ref[:, at], grad, first_ref[:, at], second_ref[:, at], rate, decay
        )


def adam_chunks(sums, start, weights, first_moment, second_moment, rate, decay, name):
    all_rows, cols = weights.shape
    rows = sums.shape[1]
    tiles = pl.cdiv(cols, 2 * TILE)
    block = pl.BlockSpec((rows, 2 * TILE), lambda i, j: (i, j))
    return pl.pallas_call(
        functools.partial(adam_kernel, rate, decay),
        grid=(all_rows // rows, tiles),
        in_specs=[pl.BlockSpec((2, rows, TILE), lambda i, j: (start // 2 + i * tiles + j, 0, 0))] + [block] * 3,
        out_specs=[block] * 4,
        out_shape=[jax.ShapeDtypeStruct(weights.shape, full_type)] * 4,
        compiler_params=pltpu.CompilerParams(vmem_limit_bytes=VMEM_LIMIT),
        cost_estimate=pl.CostEstimate(
            flops=20 * weights.size, bytes_accessed=30 * weights.size, transcendentals=weights.size
        ),
        name=name,
    )(sums, weights, first_moment, second_moment)


def after(vals, *others):
    return lax.optimization_barrier((vals,) + others)[0]


def shards(
    inputs, cotangent, w_in, w_dt, w_out, gain_pre, gain_norm, conv_param, head_param,
    first_w_in, second_w_in, first_w_dt, second_w_dt, first_w_out, second_w_out,
    first_gain_pre, second_gain_pre, first_gain_norm, second_gain_norm,
    first_conv, second_conv, first_head, second_head,
):
    wsh_count = lax.axis_size("wsh")
    seq_count = lax.axis_size("seq")
    seq_index = lax.axis_index("seq")
    wsh_index = lax.axis_index("wsh")
    rows_model = D // wsh_count
    rows_inner = INNER // wsh_count
    cols_conv = CONV_CH // wsh_count
    cols_head = HEADS // wsh_count
    small = jnp.zeros((16, CONV_CH), full_type)
    for row, part in ((0, gain_pre[None]), (1, gain_norm[None]), (2, conv_param), (7, head_param)):
        small = lax.dynamic_update_slice(small, part, (row, wsh_index * part.shape[1]))
    part_sig = jnp.concatenate(
        [w_in[:, INNER:].astype(low_type), w_dt.astype(low_type), jnp.zeros((rows_model, LANES - HEADS), low_type)],
        axis=1,
    )
    tokens_low = inputs[0]
    cot_low = cotangent[0]
    rows = tokens_low.shape[0]
    before = lax.ppermute(tokens_low[rows - HALO :], "seq", [(i, i + 1) for i in range(seq_count - 1)])
    (
        packed, normed, inv_wide, gain_in_rows, gain_rows, conv, head, full_sig,
        y, bc, lag, run_t, enter, enter_all, tail, offs, states, state_in, gate_vals, back, full_gate, full_out,
    ) = run_forward(
        jnp.concatenate([before, tokens_low], axis=0), part_sig, small.astype(low_type), cot_low,
        w_in[:, :INNER].astype(low_type), w_out.astype(low_type),
    )
    tokens = tokens_low.astype(full_type)
    inv_rms = inv_wide[:, :1]
    gain_in = gain_in_rows[0]
    normed_out, lefts, grad_y, grad_gate, part_gnorm, grad_state = run_norm(
        y, gate_vals, back, gain_rows, bc, enter_all, state_in, normed
    )
    block_out = (tokens + dot(normed_out, full_out)).astype(low_type)[None]
    grad_normed, part_conv, part_skip, part_head, sums = run_backward(
        packed, conv, head, grad_y, bc, lag, run_t, enter, tail, offs, states, state_in, grad_state,
        lefts, cot_low, grad_gate, full_gate, full_sig,
    )
    scaled = tokens * inv_rms
    part_gpre = jnp.sum(grad_normed * scaled, axis=0)
    pulled = grad_normed * gain_in
    grad_tokens = inv_rms * (pulled - scaled * jnp.mean(pulled * scaled, axis=-1, keepdims=True))
    input_grad = (cot_low.astype(full_type) + grad_tokens)[None]
    skip_sums = part_skip[0].reshape(HEADS, HEAD_DIM).sum(axis=1)
    small_parts = [
        part_gpre, part_gnorm[0], part_conv[:5].reshape(-1), part_head[0, :HEADS], part_head[1, :HEADS], skip_sums
    ]
    tiles_out = (INNER // D) * (D // TILE)
    grad_out, *new_out = adam_chunks(sums, 0, w_out, first_w_out, second_w_out, rate_matrix, weight_decay, "adam_w_out")
    grad_in_w, *new_in = adam_chunks(
        sums, tiles_out, w_in, first_w_in, second_w_in, rate_matrix, weight_decay, "adam_w_in"
    )
    at_dt = CONV_CH % TILE
    grad_dt = sums[-1, :, at_dt : at_dt + HEADS].astype(full_type)
    small_sums = sum_small(jnp.concatenate(small_parts), [block_out, new_out[0], new_in[0]])
    cuts = [D, D + INNER, D + INNER + 5 * CONV_CH]
    grad_gpre = lax.dynamic_slice_in_dim(small_sums[: cuts[0]], wsh_index * rows_model, rows_model, 0)
    grad_gnorm = lax.dynamic_slice_in_dim(small_sums[cuts[0] : cuts[1]], wsh_index * rows_inner, rows_inner, 0)
    grad_conv = lax.dynamic_slice_in_dim(
        small_sums[cuts[1] : cuts[2]].reshape(5, CONV_CH), wsh_index * cols_conv, cols_conv, 1
    )
    grad_head = lax.dynamic_slice_in_dim(
        small_sums[cuts[2] :].reshape(3, HEADS), wsh_index * cols_head, cols_head, 1
    )
    params = (w_in, w_dt, w_out, gain_pre, gain_norm, conv_param, head_param)
    gradients = (grad_in_w, grad_dt, grad_out, grad_gpre, grad_gnorm, grad_conv, grad_head)
    firsts = (first_w_in, first_w_dt, first_w_out, first_gain_pre, first_gain_norm, first_conv, first_head)
    seconds = (second_w_in, second_w_dt, second_w_out, second_gain_pre, second_gain_norm, second_conv, second_head)
    step_rates = (rate_matrix, rate_matrix, rate_matrix, rate_gain, rate_gain, rate_conv, rate_head)
    decays = (weight_decay, weight_decay, weight_decay, 0.0, 0.0, 0.0, 0.0)
    updated = [
        None if i in (0, 2) else adam_update(*items)
        for i, items in enumerate(zip(params, gradients, firsts, seconds, step_rates, decays))
    ]
    updated[0], updated[2] = new_in, new_out
    new_params = tuple(entry[0] for entry in updated)
    moments = []
    for entry in updated:
        moments.append(entry[1])
        moments.append(entry[2])
    return (block_out, input_grad) + gradients + new_params + tuple(moments)


def solution(mesh):
    rows, vec, cols = P("wsh", None), P("wsh"), P(None, "wsh")
    tokens = P("wsh", "seq", None)
    params = (rows, rows, rows, vec, vec, cols, cols)
    moments = tuple(spec for spec in params for _ in range(2))
    in_specs = (tokens, tokens) + params + moments
    out_specs = (tokens, tokens) + params + params + moments
    return jax.shard_map(shards, mesh=mesh, in_specs=in_specs, out_specs=out_specs, check_vma=False)
```
